128 devices in a mesh: fsdp: 32 (over x, y, core), ctx: 2 (over z_hi), tp: 2 (over z_lo).
Axes of the slice: x: 4, y: 4, z: 4 (z_hi: 2, z_lo: 2; z = z_hi * 2 + z_lo), core: 2. Of those that a mesh axis runs over, the one named last changes fastest.
Arguments:
- tokens: bfloat16 [32, 1024, 1536], P('fsdp', 'ctx'), may hold values from -6 to 6
- segments: int32 [32, 1024], P('fsdp'), may hold values from 0 to 2, as said below
- routes: int32 [32, 1024, 4], P('fsdp', 'ctx'), may hold values from 0 to 7, all different within a row; in each aligned block of 512 rows (0 to 511, 512 to 1023, ..., all dimensions but the last counted through in order) at most 320 rows name the same one
- attn_gain: bfloat16 [1536], P(('fsdp', 'ctx')), may hold values from 0.25 to 1.75
- w_query: bfloat16 [1536, 1536], P(('fsdp', 'ctx'), 'tp'), may hold values from -0.15625 to 0.15625
- key_matrix: bfloat16 [1536, 256], P(('fsdp', 'ctx'), 'tp'), may hold values from -0.15625 to 0.15625
- value_matrix: bfloat16 [1536, 256], P(('fsdp', 'ctx'), 'tp'), may hold values from -0.15625 to 0.15625
- w_output: bfloat16 [1536, 1536], P('tp', ('fsdp', 'ctx')), may hold values from -1.75 to 1.75
- mix_gain: bfloat16 [1536], P(('fsdp', 'ctx')), may hold values from 0.25 to 1.75
- w_router: bfloat16 [1536, 8], P(('fsdp', 'ctx')), may hold values from -0.078125 to 0.078125
- w_gate: bfloat16 [8, 1536, 768], P(None, ('fsdp', 'ctx'), 'tp'), may hold values from -0.15625 to 0.15625
- w_up: bfloat16 [8, 1536, 768], P(None, ('fsdp', 'ctx'), 'tp'), may hold values from -0.15625 to 0.15625
- w_down: bfloat16 [8, 1536, 768], P(None, ('fsdp', 'ctx'), 'tp'), may hold values from -0.21875 to 0.21875
- block_cotangent: bfloat16 [32, 1024, 1536], P('fsdp', 'ctx'), may hold values from -6 to 6
Outputs:
- block_out: bfloat16 [32, 1024, 1536], P('fsdp', 'ctx')
- tokens_grad: float32 [32, 1024, 1536], P('fsdp', 'ctx')
- grad_attn_gain: float32 [1536], P(('fsdp', 'ctx'))
- grad_query: float32 [1536, 1536], P(('fsdp', 'ctx'), 'tp')
- grad_key: float32 [1536, 256], P(('fsdp', 'ctx'), 'tp')
- grad_value: float32 [1536, 256], P(('fsdp', 'ctx'), 'tp')
- grad_output: float32 [1536, 1536], P('tp', ('fsdp', 'ctx'))
- grad_mix_gain: float32 [1536], P(('fsdp', 'ctx'))
- grad_router: float32 [1536, 8], P(('fsdp', 'ctx'))
- grad_gate: float32 [8, 1536, 768], P(None, ('fsdp', 'ctx'), 'tp')
- grad_up: float32 [8, 1536, 768], P(None, ('fsdp', 'ctx'), 'tp')
- grad_down: float32 [8, 1536, 768], P(None, ('fsdp', 'ctx'), 'tp')
The draws below stay inside these ranges and needn't reach their ends.
Inputs may be any that keep to these rules, and one draw needn't show every extreme that they name: `segments`: segment numbers never fall along a sequence; every sequence holds documents 0, 1 and 2, the first and the last of 128 to 384 positions. `routes`: each row names 4 different experts; in the 512 rows of one index of ctx no expert is named more than 320 times.
All inputs are finite; a program needn't handle non-finite values.
Results may differ from the reference program's by a relative error of at most 0.015.
Values may be sent and summed in bfloat16 or wider, within the bound.
A program may use at most 256 MiB of HBM per device.

```python
import math
import jax
import jax.numpy as jnp
import numpy as np
from jax import lax

MODEL_DIM = 1536
QUERY_HEADS = 12
KEY_VALUE_HEADS = 2
HEAD_SIZE = 128
FF = 768
TOP = 4
EXPERTS = 8
LEN = 1024
SEQS = 32
ROWS = 512
CAP = 320
N_CTX = 2


def draw_segments(key, part):
    key = jax.random.fold_in(key, 11)
    first_key, second_key = jax.random.split(key)
    first_cut = jax.random.randint(first_key, (SEQS, 1), LEN // 8, 3 * LEN // 8)
    second_cut = jax.random.randint(second_key, (SEQS, 1), 5 * LEN // 8, 7 * LEN // 8)
    positions = jnp.arange(LEN, dtype=jnp.int32)[None, :]
    return (positions >= first_cut).astype(jnp.int32) + (positions >= second_cut).astype(jnp.int32)


def level_of(stream_key, extent, cuts, least, top_value):
    level = 1.0
    for dim, blocks in cuts:
        draws = jax.random.uniform(jax.random.fold_in(jax.random.fold_in(stream_key, 6), dim), (blocks,), jnp.float32, least / len(cuts), top_value / len(cuts))
        level = level * jnp.repeat(jnp.exp(draws), extent[dim] // blocks).reshape((-1,) + (1,) * (len(extent) - 1 - dim))
    return level


def assign_block(rng, own, number, rows, count, top, limit, lean):
    order = jax.random.permutation(rng, count)
    crowded, ordinary = portions_of(count, rows * top, limit, lean, True), portions_of(count, rows * top, limit, lean, False)
    places = jnp.arange(count)

    def named(sizes, offset_by):
        used = int((sizes > 0).sum())
        fixed = max(1, used // 4)
        shifted = fixed + (places - fixed + offset_by * (used - fixed)) % max(1, count - fixed)
        return jnp.zeros((count,), jnp.int32).at[order[jnp.where(places < fixed, places, shifted)]].set(jnp.asarray(sizes, jnp.int32))

    sizes = jnp.where(number % 4 == 0, named(crowded, number // 4), named(ordinary, number - number // 4 - 1))
    mixed = jax.random.permutation(jax.random.fold_in(own, 3), count)
    donor, taker = mixed[0:count // 2 * 2:2], mixed[1:count // 2 * 2:2]
    slack = jnp.minimum(sizes[donor] - 1, limit - sizes[taker]) // 2
    slack = jnp.where((donor == order[0]) | (taker == order[0]) | (sizes[taker] == 0), 0, jnp.maximum(slack, 0))
    shifted = jax.random.randint(jax.random.fold_in(own, 4), (count // 2,), 0, 1 << 20) % (slack + 1)
    sizes = sizes.at[donor].add(-shifted).at[taker].add(shifted)
    items = jnp.searchsorted(jnp.cumsum(sizes), jnp.arange(rows * top), side="right").astype(jnp.int32)
    table = items.reshape(top, rows).T
    table = table[jax.random.permutation(jax.random.fold_in(own, 1), rows)]
    offset_by = jax.random.randint(jax.random.fold_in(own, 2), (rows, 1), 0, top)
    return jnp.take_along_axis(table, (jnp.arange(top)[None, :] + offset_by) % top, axis=1)


def portions_of(count, total, reach, skew, full):
    portions = [(1 << 20) // math.isqrt(rank ** skew) + 1 for rank in range(1, count + 1)]
    largest = reach if full else min(reach, max(-(-total // count), total * portions[0] // sum(portions)))
    least = 1 if total - largest >= count - 1 else 0
    given, rest = [largest] + [least] * (count - 1), total - largest - least * (count - 1)
    while rest > 0:
        candidates = [i for i in range(1, count) if given[i] < largest] or [i for i in range(1, count) if given[i] < reach]
        mass, left = sum([portions[i] for i in candidates]), rest
        for i in candidates:
            extra = min(reach - given[i], max(1, left * portions[i] // mass), rest)
            given[i] = given[i] + extra
            rest = rest - extra
    return np.array(given)


def scatter_about(key, extent, spread, reach, cuts=(), kind=jnp.bfloat16):
    drawn = spread * jax.random.normal(key, extent, jnp.float32)
    if cuts:
        drawn = drawn * level_of(key, extent, cuts, -0.22, 0.18)
    return jnp.clip(drawn, -reach, reach).astype(kind)


def setup_inputs(seed: int = 0) -> dict:
    streams_of = jax.random.split(jax.random.key(seed), 15)
    tokens = scatter_about(streams_of[0], (SEQS, LEN, MODEL_DIM), 1.0, 6.0, ((0, 32), (1, 2)))
    segments = draw_segments(jax.random.fold_in(streams_of[14], 71), 0)
    routes_keys = jax.random.split(jax.random.fold_in(streams_of[2], 1), SEQS * LEN // ROWS)
    routes_turns = jax.random.permutation(jax.random.fold_in(streams_of[2], 3), SEQS * LEN // ROWS)
    routes = jax.vmap(lambda own, number: assign_block(jax.random.fold_in(streams_of[2], 2), own, number, ROWS, EXPERTS, TOP, CAP, 1))(routes_keys, routes_turns).reshape((SEQS, LEN, TOP))
    attn_gain = jnp.clip(1.0 + 0.15 * jax.random.normal(streams_of[3], (MODEL_DIM,), jnp.float32), 0.25, 1.75).astype(jnp.bfloat16)
    w_query = scatter_about(streams_of[4], (MODEL_DIM, QUERY_HEADS * HEAD_SIZE), MODEL_DIM ** -0.5, 0.15625, ((0, 64), (1, 2)))
    key_matrix = scatter_about(streams_of[5], (MODEL_DIM, KEY_VALUE_HEADS * HEAD_SIZE), MODEL_DIM ** -0.5, 0.15625, ((0, 64), (1, 2)))
    value_matrix = scatter_about(streams_of[6], (MODEL_DIM, KEY_VALUE_HEADS * HEAD_SIZE), MODEL_DIM ** -0.5, 0.15625, ((0, 64), (1, 2)))
    w_output = scatter_about(streams_of[7], (QUERY_HEADS * HEAD_SIZE, MODEL_DIM), (max(QUERY_HEADS * HEAD_SIZE // 128, 2)) ** -0.5, 1.75, ((0, 2), (1, 64)))
    mix_gain = jnp.clip(1.0 + 0.15 * jax.random.normal(streams_of[8], (MODEL_DIM,), jnp.float32), 0.25, 1.75).astype(jnp.bfloat16)
    w_router = scatter_about(streams_of[9], (MODEL_DIM, EXPERTS), (4 * MODEL_DIM) ** -0.5, 0.078125, ((0, 64),))
    w_gate = scatter_about(streams_of[10], (EXPERTS, MODEL_DIM, FF), MODEL_DIM ** -0.5, 0.15625, ((1, 64), (2, 2)))
    w_up = scatter_about(streams_of[11], (EXPERTS, MODEL_DIM, FF), MODEL_DIM ** -0.5, 0.15625, ((1, 64), (2, 2)))
    w_down = scatter_about(streams_of[12], (EXPERTS, MODEL_DIM, FF), FF ** -0.5, 0.21875, ((1, 64), (2, 2)))
    block_cotangent = scatter_about(streams_of[13], (SEQS, LEN, MODEL_DIM), 1.0, 6.0, ((0, 32), (1, 2)))
    return {"tokens": tokens, "segments": segments, "routes": routes, "attn_gain": attn_gain, "w_query": w_query, "key_matrix": key_matrix, "value_matrix": value_matrix, "w_output": w_output, "mix_gain": mix_gain, "w_router": w_router, "w_gate": w_gate, "w_up": w_up, "w_down": w_down, "block_cotangent": block_cotangent}


EPS = 1e-06
ROPE_BASE = 1000000.0
NEG_FILL = -1e+30
FULL_PRECISION = lax.Precision.HIGHEST

@jax.custom_vjp
def reduced_cast(v):
    return lax.optimization_barrier(v.astype(jnp.bfloat16)).astype(jnp.float32)

@jax.custom_vjp
def reduced_cast_backward(v):
    return v

def low_keep(v):
    return (reduced_cast(v), None)

def low_pass(kept, grad):
    return (grad,)

def back_keep(v):
    return (v, None)

def back_low(kept, grad):
    return (reduced_cast(grad),)
reduced_cast.defvjp(low_keep, low_pass)
reduced_cast_backward.defvjp(back_keep, back_low)

def rope_tables(positions):
    half_dim = HEAD_SIZE // 2
    frequency = ROPE_BASE ** (-jnp.arange(half_dim, dtype=jnp.float32) * (2.0 / HEAD_SIZE))
    angles = positions.astype(jnp.float32)[:, None] * frequency[None, :]
    angles = jnp.concatenate([angles, angles], axis=1)
    return (jnp.cos(angles)[:, None, :], jnp.sin(angles)[:, None, :])

def rotary_embed(value_rows, cosine_table, sine_table):
    half_dim = HEAD_SIZE // 2
    turned = jnp.concatenate([-value_rows[..., half_dim:], value_rows[..., :half_dim]], axis=-1)
    return value_rows * cosine_table + turned * sine_table

def slot_tables(route_rows, experts, capacity, top_k):
    flat_routes = route_rows.reshape(-1)
    hot_slots = (flat_routes[:, None] == jnp.arange(experts, dtype=jnp.int32)[None, :]).astype(jnp.int32)
    before = jnp.cumsum(hot_slots, axis=0) - hot_slots
    slot_pos = lax.optimization_barrier(jnp.sum(before * hot_slots, axis=1))
    slot_place = (flat_routes * capacity + slot_pos).astype(jnp.int32)
    pair_ids = jnp.arange(flat_routes.shape[0], dtype=jnp.int32)
    slot_owner = jnp.zeros((experts * capacity,), jnp.int32).at[slot_place].set(pair_ids // top_k)
    slot_pair = jnp.zeros((experts * capacity,), jnp.int32).at[slot_place].set(pair_ids)
    filled = jnp.zeros((experts * capacity,), jnp.float32).at[slot_place].set(1.0)
    return (slot_place, slot_owner, slot_pair, filled)

def mix_block(normed_rows, route_rows, gate_weights, w_gate, w_up, w_down):
    slot_place, slot_owner, slot_pair, filled = slot_tables(route_rows, EXPERTS, CAP, TOP)
    dispatched = (normed_rows[slot_owner] * filled[:, None]).reshape(EXPERTS, CAP, MODEL_DIM)
    gate_act = reduced_cast_backward(jnp.einsum('ecd,edf->ecf', dispatched, w_gate, precision=FULL_PRECISION))
    up_act = reduced_cast_backward(jnp.einsum('ecd,edf->ecf', dispatched, w_up, precision=FULL_PRECISION))
    hidden = reduced_cast(jax.nn.silu(gate_act) * up_act)
    result = reduced_cast_backward(jnp.einsum('ecf,edf->ecd', hidden, w_down, precision=FULL_PRECISION))
    gathered_out = result.reshape(EXPERTS * CAP, MODEL_DIM)[slot_place].reshape(ROWS, TOP, MODEL_DIM)
    return lax.optimization_barrier(jnp.sum(gate_weights[:, :, None] * gathered_out, axis=1))

def layer(tokens_row, seg_row, route_row, attn_gain, w_query, key_matrix, value_matrix, w_output, mix_gain, w_router, w_gate, w_up, w_down):
    token_length = tokens_row.shape[0]
    heads_per_group = QUERY_HEADS // KEY_VALUE_HEADS
    positions = jnp.arange(token_length, dtype=jnp.int32)
    cosine_table, sine_table = rope_tables(positions)
    inv_norm = lax.rsqrt(lax.optimization_barrier(jnp.mean(tokens_row * tokens_row, axis=1, keepdims=True)) + EPS)
    normalized_input = reduced_cast(tokens_row * inv_norm * attn_gain)
    query_rows = reduced_cast(rotary_embed(reduced_cast_backward(jnp.dot(normalized_input, w_query, precision=FULL_PRECISION)).reshape(token_length, QUERY_HEADS, HEAD_SIZE), cosine_table, sine_table))
    key_rows = reduced_cast(rotary_embed(reduced_cast_backward(jnp.dot(normalized_input, key_matrix, precision=FULL_PRECISION)).reshape(token_length, KEY_VALUE_HEADS, HEAD_SIZE), cosine_table, sine_table))
    value_rows = reduced_cast(reduced_cast_backward(jnp.dot(normalized_input, value_matrix, precision=FULL_PRECISION)).reshape(token_length, KEY_VALUE_HEADS, HEAD_SIZE))
    attention_scores = reduced_cast_backward(jnp.einsum('wmnz,smz->mnws', query_rows.reshape(token_length, KEY_VALUE_HEADS, heads_per_group, HEAD_SIZE), key_rows, precision=FULL_PRECISION) * HEAD_SIZE ** (-0.5))
    allowed = (seg_row[:, None] == seg_row[None, :]) & (positions[:, None] >= positions[None, :])
    masked = jnp.where(allowed[None, None], attention_scores, NEG_FILL)
    row_peak = lax.optimization_barrier(jnp.max(masked, axis=-1, keepdims=True))
    expo_vals = jnp.exp(masked - row_peak)
    prob_vals = expo_vals / lax.optimization_barrier(jnp.sum(expo_vals, axis=-1, keepdims=True))
    mixed_out = jnp.einsum('gajk,kgd->jgad', reduced_cast(prob_vals), value_rows, precision=FULL_PRECISION)
    attended = reduced_cast(reduced_cast_backward(mixed_out.reshape(token_length, QUERY_HEADS * HEAD_SIZE)))
    branch = reduced_cast_backward(jnp.dot(attended, w_output, precision=FULL_PRECISION))
    residual = tokens_row + branch
    inv_mix = lax.rsqrt(lax.optimization_barrier(jnp.mean(residual * residual, axis=1, keepdims=True)) + EPS)
    normed_mix = reduced_cast(residual * inv_mix * mix_gain)
    logits = reduced_cast_backward(jnp.dot(normed_mix, w_router, precision=FULL_PRECISION))
    hot_routes = (route_row[:, :, None] == jnp.arange(EXPERTS, dtype=jnp.int32)[None, None, :]).astype(jnp.float32)
    chosen = lax.optimization_barrier(jnp.sum(hot_routes * logits[:, None, :], axis=-1))
    gate_expo = jnp.exp(chosen - lax.optimization_barrier(jnp.max(chosen, axis=1, keepdims=True)))
    gate_weights = gate_expo / lax.optimization_barrier(jnp.sum(gate_expo, axis=1, keepdims=True))
    mix_out = jax.vmap(mix_block, in_axes=(0, 0, 0, None, None, None))(normed_mix.reshape(N_CTX, ROWS, MODEL_DIM), route_row.reshape(N_CTX, ROWS, TOP), gate_weights.reshape(N_CTX, ROWS, TOP), w_gate, w_up, w_down).reshape(token_length, MODEL_DIM)
    return residual + mix_out

def reference(tokens, segments, routes, attn_gain, w_query, key_matrix, value_matrix, w_output, mix_gain, w_router, w_gate, w_up, w_down, block_cotangent):
    weights = tuple((item.astype(jnp.float32) for item in (attn_gain, w_query, key_matrix, value_matrix, w_output, mix_gain, w_router, w_gate, w_up, w_down)))

    def one_sequence(summed, sequence_items):
        row_tokens, row_segments, row_routes, row_cotangent = sequence_items

        def apply_layer(token_vals, *weight_list):
            return layer(token_vals, row_segments, row_routes, *weight_list)
        result, pull_back = jax.vjp(apply_layer, row_tokens.astype(jnp.float32), *weights)
        grad_list = pull_back(row_cotangent.astype(jnp.float32))
        summed = tuple((total_now + grad_now for total_now, grad_now in zip(summed, grad_list[1:])))
        return (summed, (result.astype(jnp.bfloat16), grad_list[0]))
    zero_grads = tuple((jnp.zeros_like(item) for item in weights))
    totals, (block_outs, token_grads) = lax.scan(one_sequence, zero_grads, (tokens, segments, routes, block_cotangent))
    return (block_outs, token_grads, totals[0], totals[1], totals[2], totals[3], totals[4], totals[5], totals[6], totals[7], totals[8], totals[9])
```

```python
import functools

import jax
import jax.numpy as jnp
from jax import lax
from jax.experimental import pallas as pl
from jax.experimental.pallas import tpu as pltpu
from jax.sharding import Mesh
from jax.sharding import PartitionSpec as P

QUERY_HEADS = 12
KEY_VALUE_HEADS = 2
HEAD_SIZE = 128
GROUP = QUERY_HEADS // KEY_VALUE_HEADS
EPS = 1e-06
ROPE_BASE = 1000000.0
NEG_FILL = -1e30
MISC = 128
SLOTS = 320
PAD = 32
MESH = pl.DeviceIdType.MESH
ANY = pl.BlockSpec(memory_space=pl.ANY)
VMEM = pl.BlockSpec(memory_space=pltpu.VMEM)
f32 = jnp.float32
bf16 = jnp.bfloat16


def rope_tables(positions):
    half_dim = HEAD_SIZE // 2
    frequency = ROPE_BASE ** (-jnp.arange(half_dim, dtype=f32) * (2.0 / HEAD_SIZE))
    angles = positions.astype(f32)[:, None] * frequency[None, :]
    angles = jnp.concatenate([angles, angles], axis=1)
    return (jnp.cos(angles)[:, None, :], jnp.sin(angles)[:, None, :])


def rotary_embed(value_rows, cosine_table, sine_table):
    half_dim = HEAD_SIZE // 2
    turned = jnp.concatenate([-value_rows[..., half_dim:], value_rows[..., :half_dim]], axis=-1)
    return value_rows * cosine_table + turned * sine_table


def rotate_back(grad_vals, cosine_table, sine_table):
    half_dim = HEAD_SIZE // 2
    scaled = grad_vals * sine_table
    turned = jnp.concatenate([scaled[..., half_dim:], -scaled[..., :half_dim]], axis=-1)
    return grad_vals * cosine_table + turned


def place():
    return lax.axis_index("c"), lax.axis_index("h"), lax.axis_index("l")


def column_peer(core_step, z_step):
    c, h, l = place()
    z = lax.rem(h * 2 + l + z_step, 4)
    return {"c": lax.rem(c + core_step, 2), "h": z // 2, "l": lax.rem(z, 2)}


def at_z(core, z):
    return {"c": core, "h": z // 2, "l": lax.rem(z, 2)}


def greet(steps):
    barrier = pltpu.get_barrier_semaphore()
    for core_step, z_step in steps:
        pl.semaphore_signal(
            barrier, inc=1, device_id=column_peer(core_step, (4 - z_step) % 4), device_id_type=MESH
        )
    pl.semaphore_wait(barrier, len(steps))


def send(src, dst, send_sem, recv_sem, peer):
    copy = pltpu.make_async_remote_copy(
        src_ref=src,
        dst_ref=dst,
        send_sem=send_sem,
        recv_sem=recv_sem,
        device_id=peer,
        device_id_type=MESH,
    )
    copy.start()
    return copy


COLUMN = [(0, 1), (0, 2), (0, 3), (1, 0), (1, 1), (1, 2), (1, 3)]
ALONG_Z = [(0, 1), (0, 2), (0, 3)]


def spread_kernel(attn_ref, expert_ref, attn_out, expert_out, s_sem, r_sem, as_sem, ar_sem, own):
    c, h, l = place()
    me = (c * 2 + h) * 2 + l
    greet(COLUMN)
    copies = []
    own_copy = pltpu.make_async_copy(expert_ref.at[me], expert_out.at[me], own.at[0])
    own_copy.start()
    slot = c * 2 + h
    for z_step in range(4):
        if z_step == 0:
            here = pltpu.make_async_copy(attn_ref, attn_out.at[slot], own.at[1])
            pl.when(c == l)(here.start)
            there = pltpu.make_async_remote_copy(
                src_ref=attn_ref,
                dst_ref=attn_out.at[slot],
                send_sem=as_sem.at[0],
                recv_sem=ar_sem.at[slot],
                device_id=column_peer(1, 0),
                device_id_type=MESH,
            )
            pl.when(c != l)(there.start)
        else:
            z = lax.rem(h * 2 + l + z_step, 4)
            send(attn_ref, attn_out.at[slot], as_sem.at[z_step], ar_sem.at[slot], at_z(l, z))
    for i, (core_step, z_step) in enumerate(COLUMN):
        peer = column_peer(core_step, z_step)
        to = (peer["c"] * 2 + peer["h"]) * 2 + peer["l"]
        copies.append(
            send(expert_ref.at[to], expert_out.at[me], s_sem.at[i], r_sem.at[i], peer)
        )
    for source in range(4):
        mine = (c == l) & (slot == source)

        def landed(source=source):
            pltpu.make_async_remote_copy(
                src_ref=attn_ref,
                dst_ref=attn_out.at[source],
                send_sem=as_sem.at[0],
                recv_sem=ar_sem.at[source],
                device_id=column_peer(1, 0),
                device_id_type=MESH,
            ).wait_recv()

        pl.when(jnp.logical_not(mine))(landed)
    pl.when(c == l)(here.wait)
    pl.when(c != l)(there.wait_send)
    for z_step in range(1, 4):
        pltpu.make_async_remote_copy(
            src_ref=attn_ref,
            dst_ref=attn_out.at[slot],
            send_sem=as_sem.at[z_step],
            recv_sem=ar_sem.at[slot],
            device_id=column_peer(0, z_step),
            device_id_type=MESH,
        ).wait_send()
    own_copy.wait()
    for copy in copies:
        copy.wait()


def spread(attn_block, expert_pieces):
    return pl.pallas_call(
        spread_kernel,
        name="spread_weights",
        out_shape=(
            jax.ShapeDtypeStruct((4,) + attn_block.shape, attn_block.dtype),
            jax.ShapeDtypeStruct(expert_pieces.shape, expert_pieces.dtype),
        ),
        in_specs=[ANY, ANY],
        out_specs=(ANY, ANY),
        scratch_shapes=[
            pltpu.SemaphoreType.DMA((7,)),
            pltpu.SemaphoreType.DMA((7,)),
            pltpu.SemaphoreType.DMA((4,)),
            pltpu.SemaphoreType.DMA((4,)),
            pltpu.SemaphoreType.DMA((2,)),
        ],
        compiler_params=pltpu.CompilerParams(collective_id=1, has_side_effects=True),
    )(attn_block, expert_pieces)


def along_z_kernel(block_ref, out_ref, s_sem, r_sem, own):
    c, h, l = place()
    z = h * 2 + l
    greet(ALONG_Z)
    own_copy = pltpu.make_async_copy(block_ref, out_ref.at[z], own)
    own_copy.start()
    copies = [
        send(block_ref, out_ref.at[z], s_sem.at[i], r_sem.at[i], column_peer(*step))
        for i, step in enumerate(ALONG_Z)
    ]
    own_copy.wait()
    for copy in copies:
        copy.wait()


def gather_along_z(block):
    return pl.pallas_call(
        along_z_kernel,
        name="gather_keys_values",
        out_shape=jax.ShapeDtypeStruct((4,) + block.shape, block.dtype),
        in_specs=[VMEM],
        out_specs=VMEM,
        scratch_shapes=[
            pltpu.SemaphoreType.DMA((3,)),
            pltpu.SemaphoreType.DMA((3,)),
            pltpu.SemaphoreType.DMA(()),
        ],
        compiler_params=pltpu.CompilerParams(collective_id=2, has_side_effects=True),
    )(block)


def sum_along_z_kernel(parts_ref, out_ref, held, s_sem, r_sem):
    c, h, l = place()
    z = h * 2 + l
    greet(ALONG_Z)
    copies = [
        send(
            parts_ref.at[lax.rem(z + step[1], 4)],
            held.at[i],
            s_sem.at[i],
            r_sem.at[i],
            column_peer(*step),
        )
        for i, step in enumerate(ALONG_Z)
    ]
    for copy in copies:
        copy.wait()
    total = parts_ref[z].astype(f32)
    for i in range(3):
        total = total + held[i].astype(f32)
    out_ref[...] = total


def sum_along_z(parts):
    shape = parts.shape[1:]
    return pl.pallas_call(
        sum_along_z_kernel,
        name="sum_key_value_gradients",
        out_shape=jax.ShapeDtypeStruct(shape, f32),
        in_specs=[VMEM],
        out_specs=VMEM,
        scratch_shapes=[
            pltpu.VMEM((3,) + shape, parts.dtype),
            pltpu.SemaphoreType.DMA((3,)),
            pltpu.SemaphoreType.DMA((3,)),
        ],
        compiler_params=pltpu.CompilerParams(collective_id=3, has_side_effects=True),
    )(parts)


def column_gather_kernel(
    rows_ref, gate_ref, rows_out, gates_out, s_sem, r_sem, fs_sem, fr_sem, gs_sem, gr_sem, own
):
    c, h, l = place()
    z = h * 2 + l
    me = c * 4 + z
    greet(COLUMN)
    own_copies = [
        pltpu.make_async_copy(rows_ref, rows_out.at[me], own.at[0]),
        pltpu.make_async_copy(gate_ref, gates_out.at[me], own.at[1]),
    ]
    for copy in own_copies:
        copy.start()
    order = [(0, 2), (0, 1), (0, 3)]
    copies = [
        send(gate_ref, gates_out.at[me], gs_sem.at[i], gr_sem.at[i], column_peer(*step))
        for i, step in enumerate(COLUMN)
    ]
    rounds = [
        send(rows_ref, rows_out.at[me], s_sem.at[i], r_sem.at[i], column_peer(*step))
        for i, step in enumerate(order)
    ]
    other = column_peer(1, 0)
    forwards = [send(rows_ref, rows_out.at[me], fs_sem.at[3], fr_sem.at[3], other)]
    for i in (1, 2, 0):
        rounds[i].wait_recv()
        origin = c * 4 + lax.rem(z + 4 - order[i][1], 4)
        block = rows_out.at[origin]
        forwards.append(send(block, block, fs_sem.at[i], fr_sem.at[i], other))
    for copy in rounds:
        copy.wait_send()
    for copy in own_copies:
        copy.wait()
    for copy in copies + forwards:
        copy.wait()


def column_gather(rows, gates):
    return pl.pallas_call(
        column_gather_kernel,
        name="gather_normed_rows",
        out_shape=(
            jax.ShapeDtypeStruct((8,) + rows.shape, rows.dtype),
            jax.ShapeDtypeStruct((8,) + gates.shape, gates.dtype),
        ),
        in_specs=[ANY, ANY],
        out_specs=(ANY, ANY),
        scratch_shapes=[
            pltpu.SemaphoreType.DMA((3,)),
            pltpu.SemaphoreType.DMA((3,)),
            pltpu.SemaphoreType.DMA((4,)),
            pltpu.SemaphoreType.DMA((4,)),
            pltpu.SemaphoreType.DMA((7,)),
            pltpu.SemaphoreType.DMA((7,)),
            pltpu.SemaphoreType.DMA((2,)),
        ],
        compiler_params=pltpu.CompilerParams(collective_id=4, has_side_effects=True),
    )(rows, gates)


def column_sum_kernel(
    parts_ref, small_ref, out_ref, small_out, near, chip, far, cs, cr, zs, zr, ss, sr, own
):
    c, h, l = place()
    z = h * 2 + l
    me = c * 4 + z
    greet(COLUMN)
    other = column_peer(1, 0)
    order = [2, 1, 3, 0]
    near_copies = [
        send(
            parts_ref.at[(1 - c) * 4 + lax.rem(z + step, 4)],
            near.at[i],
            cs.at[i],
            cr.at[i],
            other,
        )
        for i, step in enumerate(order)
    ]
    own_copy = pltpu.make_async_copy(small_ref.at[me], small_out.at[me], own)
    own_copy.start()
    small_copies = []
    for i, step in enumerate(COLUMN):
        peer = column_peer(*step)
        to = (peer["c"] * 2 + peer["h"]) * 2 + peer["l"]
        small_copies.append(send(small_ref.at[to], small_out.at[me], ss.at[i], sr.at[i], peer))
    rows = parts_ref.shape[1]
    chunk = 32
    far_copies = []
    for i, step in enumerate(order):
        near_copies[i].wait_recv()
        mine = c * 4 + lax.rem(z + step, 4)

        def add(k, carry, i=i, mine=mine, step=step):
            here = pl.ds(pl.multiple_of(k * chunk, chunk), chunk)
            total = parts_ref[mine, here, :].astype(f32) + near[i, here, :].astype(f32)
            if step == 0:
                out_ref[here, :] = total
            else:
                chip[i, here, :] = total.astype(chip.dtype)
            return carry

        lax.fori_loop(0, rows // chunk, add, 0)
        if step:
            far_copies.append(
                send(chip.at[i], far.at[i], zs.at[i], zr.at[i], column_peer(0, step))
            )
    for copy in far_copies:
        copy.wait()

    def finish(k, carry):
        here = pl.ds(pl.multiple_of(k * chunk, chunk), chunk)
        total = out_ref[here, :]
        for i in range(3):
            total = total + far[i, here, :].astype(f32)
        out_ref[here, :] = total
        return carry

    lax.fori_loop(0, rows // chunk, finish, 0)
    for copy in near_copies:
        copy.wait_send()
    own_copy.wait()
    for copy in small_copies:
        copy.wait()


def column_sum(parts, small, number):
    rows, width = parts.shape[1:]
    return pl.pallas_call(
        column_sum_kernel,
        name="sum_over_experts",
        out_shape=(
            jax.ShapeDtypeStruct((rows, width), f32),
            jax.ShapeDtypeStruct(small.shape, small.dtype),
        ),
        in_specs=[VMEM, VMEM],
        out_specs=(VMEM, VMEM),
        scratch_shapes=[
            pltpu.VMEM((4, rows, width), parts.dtype),
            pltpu.VMEM((3, rows, width), parts.dtype),
            pltpu.VMEM((3, rows, width), parts.dtype),
            pltpu.SemaphoreType.DMA((4,)),
            pltpu.SemaphoreType.DMA((4,)),
            pltpu.SemaphoreType.DMA((3,)),
            pltpu.SemaphoreType.DMA((3,)),
            pltpu.SemaphoreType.DMA((7,)),
            pltpu.SemaphoreType.DMA((7,)),
            pltpu.SemaphoreType.DMA(()),
        ],
        compiler_params=pltpu.CompilerParams(
            collective_id=number, has_side_effects=True, vmem_limit_bytes=40 * 2**20
        ),
    )(parts, small)


def expert_return_kernel(pieces_ref, out_ref, s_sem, r_sem, own):
    c, h, l = place()
    me = (c * 2 + h) * 2 + l
    greet(COLUMN)
    own_copy = pltpu.make_async_copy(pieces_ref.at[me], out_ref.at[me], own)
    own_copy.start()
    copies = []
    for i, step in enumerate(COLUMN):
        peer = column_peer(*step)
        to = (peer["c"] * 2 + peer["h"]) * 2 + peer["l"]
        copies.append(send(pieces_ref.at[to], out_ref.at[me], s_sem.at[i], r_sem.at[i], peer))
    own_copy.wait()
    for copy in copies:
        copy.wait()


def expert_return(pieces):
    return pl.pallas_call(
        expert_return_kernel,
        name="return_expert_gradients",
        out_shape=jax.ShapeDtypeStruct(pieces.shape, pieces.dtype),
        in_specs=[ANY],
        out_specs=ANY,
        scratch_shapes=[
            pltpu.SemaphoreType.DMA((7,)),
            pltpu.SemaphoreType.DMA((7,)),
            pltpu.SemaphoreType.DMA(()),
        ],
        compiler_params=pltpu.CompilerParams(collective_id=7, has_side_effects=True),
    )(pieces)


def attn_return_kernel(pieces_ref, misc_ref, out_ref, misc_out, ps, pr, ms, mr, own):
    c, h, l = place()
    z = h * 2 + l
    greet(COLUMN)
    for target in range(4):
        owner = {"c": target // 2, "h": target % 2, "l": c}
        is_me = (owner["c"] == c) & (owner["h"] == h) & (owner["l"] == l)
        there = pltpu.make_async_remote_copy(
            src_ref=pieces_ref.at[target],
            dst_ref=out_ref.at[z],
            send_sem=ps.at[target],
            recv_sem=pr.at[z],
            device_id=owner,
            device_id_type=MESH,
        )
        here = pltpu.make_async_copy(pieces_ref.at[target], out_ref.at[z], pr.at[z])
        pl.when(jnp.logical_not(is_me))(there.start)
        pl.when(is_me)(here.start)
    for target in range(8):
        owner = {"c": target // 4, "h": (target // 2) % 2, "l": target % 2}
        is_me = (owner["c"] == c) & (owner["h"] == h) & (owner["l"] == l)
        there = pltpu.make_async_remote_copy(
            src_ref=misc_ref.at[target // 2],
            dst_ref=misc_out.at[z],
            send_sem=ms.at[target],
            recv_sem=mr.at[z],
            device_id=owner,
            device_id_type=MESH,
        )
        here = pltpu.make_async_copy(misc_ref.at[target // 2], misc_out.at[z], mr.at[z])
        pl.when((c == 0) & jnp.logical_not(is_me))(there.start)
        pl.when((c == 0) & is_me)(here.start)
    for source in range(4):
        pltpu.make_async_copy(pieces_ref.at[0], out_ref.at[source], pr.at[source]).wait()
        pltpu.make_async_copy(misc_ref.at[0], misc_out.at[source], mr.at[source]).wait()
    for target in range(4):
        owner = {"c": target // 2, "h": target % 2, "l": c}
        is_me = (owner["c"] == c) & (owner["h"] == h) & (owner["l"] == l)
        sent = pltpu.make_async_copy(pieces_ref.at[0], out_ref.at[0], ps.at[target])
        pl.when(jnp.logical_not(is_me))(sent.wait)
    for target in range(8):
        owner = {"c": target // 4, "h": (target // 2) % 2, "l": target % 2}
        is_me = (owner["c"] == c) & (owner["h"] == h) & (owner["l"] == l)
        sent = pltpu.make_async_copy(misc_ref.at[0], misc_out.at[0], ms.at[target])
        pl.when((c == 0) & jnp.logical_not(is_me))(sent.wait)


def attn_return(pieces, misc):
    return pl.pallas_call(
        attn_return_kernel,
        name="return_attention_gradients",
        out_shape=(
            jax.ShapeDtypeStruct((4,) + pieces.shape[1:], pieces.dtype),
            jax.ShapeDtypeStruct((4,) + misc.shape[1:], misc.dtype),
        ),
        in_specs=[ANY, ANY],
        out_specs=(ANY, ANY),
        scratch_shapes=[
            pltpu.SemaphoreType.DMA((4,)),
            pltpu.SemaphoreType.DMA((4,)),
            pltpu.SemaphoreType.DMA((8,)),
            pltpu.SemaphoreType.DMA((4,)),
            pltpu.SemaphoreType.DMA(()),
        ],
        compiler_params=pltpu.CompilerParams(collective_id=8, has_side_effects=True),
    )(pieces, misc)


def dot(a, b):
    return jnp.dot(a, b, preferred_element_type=f32)


def dot_nt(a, b):
    return lax.dot_general(a, b, (((1,), (1,)), ((), ())), preferred_element_type=f32)


def dot_tn(a, b):
    return lax.dot_general(a, b, (((0,), (0,)), ((), ())), preferred_element_type=f32)


def exchange_halves(own, l):
    other = lax.ppermute(own, "l", [(0, 1), (1, 0)])
    first = jnp.where(l == 0, own, other)
    second = jnp.where(l == 0, other, own)
    return jnp.concatenate([first, second], axis=0)


def body(
    tokens,
    segments,
    routes,
    attn_gain,
    w_query,
    key_matrix,
    value_matrix,
    w_output,
    mix_gain,
    w_router,
    w_gate,
    w_up,
    w_down,
    block_cotangent,
):
    c, h, l = place()
    model_width = tokens.shape[2]
    rows = tokens.shape[1] // 2
    seq_length = segments.shape[1]
    experts, part, ff_half = w_gate.shape
    q_half = w_query.shape[1]
    score_scale = HEAD_SIZE ** (-0.5)

    misc = jnp.concatenate([attn_gain[:, None], mix_gain[:, None], w_router], axis=1)
    misc = jnp.pad(misc, ((0, 0), (0, MISC - misc.shape[1])))
    attn_block = jnp.concatenate(
        [w_query, key_matrix, value_matrix, misc, w_output.T], axis=1
    )
    attn_block = jnp.pad(attn_block, ((0, PAD - part), (0, 0)))
    expert_pieces = jnp.pad(
        jnp.stack([w_gate, w_up, w_down], axis=1), ((0, 0), (0, 0), (0, PAD - part), (0, 0))
    )
    attn_col, expert_col = spread(attn_block, expert_pieces)
    attn_col = attn_col[:, :part].reshape(4 * part, attn_block.shape[1])
    expert_col = (
        expert_col[:, :, :part]
        .reshape(4, 2, 3, part, ff_half)
        .transpose(2, 0, 3, 1, 4)
        .reshape(3, 4 * part, 2 * ff_half)
    )
    kv_width = key_matrix.shape[1]
    in_width = q_half + 2 * kv_width + MISC
    w_in = lax.all_gather(attn_col[:, :in_width], ("c", "x", "y"), axis=0, tiled=True).reshape(
        2, model_width, in_width
    )
    w_out = lax.all_gather(attn_col[:, in_width:], ("c", "x", "y"), axis=0, tiled=True).reshape(
        2, model_width, q_half
    )
    expert_full = lax.all_gather(expert_col, ("x", "y"), axis=1, tiled=True)
    gate_w, up_w, down_w = expert_full[0], expert_full[1], expert_full[2]
    qkv_w = w_in[:, :, : q_half + 2 * kv_width]
    misc_full = w_in[0, :, q_half + 2 * kv_width :]
    attn_scale = misc_full[:, 0].astype(f32)
    mix_scale = misc_full[:, 1].astype(f32)
    router_w = misc_full[:, 2 : 2 + experts]

    first = l * rows
    inputs = lax.dynamic_slice_in_dim(tokens[0], first, rows).astype(f32)
    upstream_low = lax.dynamic_slice_in_dim(block_cotangent[0], first, rows)
    upstream = upstream_low.astype(f32)
    route_rows = lax.dynamic_slice_in_dim(routes[0], first, rows)
    z = h * 2 + l
    positions = z * rows + jnp.arange(rows, dtype=jnp.int32)
    key_positions = jnp.arange(seq_length, dtype=jnp.int32)
    seg_all = segments[0]
    seg_local = lax.dynamic_slice_in_dim(seg_all, z * rows, rows)
    allowed = (seg_local[:, None] == seg_all[None, :]) & (
        positions[:, None] >= key_positions[None, :]
    )
    cosine_table, sine_table = rope_tables(positions)

    inv_attn = lax.rsqrt(jnp.mean(inputs * inputs, axis=1, keepdims=True) + EPS)
    scaled_in = inputs * inv_attn
    normalized_input = (scaled_in * attn_scale).astype(bf16)
    halves = [dot(normalized_input, qkv_w[i]) for i in range(2)]
    q_heads = [
        rotary_embed(p[:, :q_half].reshape(rows, GROUP, HEAD_SIZE), cosine_table, sine_table)
        .astype(bf16)
        .transpose(1, 0, 2)
        for p in halves
    ]
    k_own = [
        rotary_embed(
            p[:, None, q_half : q_half + kv_width], cosine_table, sine_table
        ).astype(bf16)[:, 0]
        for p in halves
    ]
    v_own = [p[:, q_half + kv_width :].astype(bf16) for p in halves]
    kv_all = gather_along_z(jnp.concatenate(k_own + v_own, axis=1)).reshape(
        seq_length, 4 * kv_width
    )
    keys = [kv_all[:, i * kv_width : (i + 1) * kv_width] for i in range(2)]
    values = [kv_all[:, (2 + i) * kv_width : (3 + i) * kv_width] for i in range(2)]

    def scores_of(i):
        scores = dot_nt(q_heads[i].reshape(GROUP * rows, HEAD_SIZE), keys[i]) * score_scale
        return jnp.where(
            allowed[None], scores.reshape(GROUP, rows, seq_length), NEG_FILL
        )

    attended, log_totals = [], []
    for i in range(2):
        masked = scores_of(i)
        row_peak = jnp.max(masked, axis=-1, keepdims=True)
        expo_vals = jnp.exp(masked - row_peak)
        row_total = jnp.sum(expo_vals, axis=-1, keepdims=True)
        weights_low = (expo_vals / row_total).astype(bf16)
        mixed = dot(weights_low.reshape(GROUP * rows, seq_length), values[i])
        attended.append(
            mixed.astype(bf16)
            .reshape(GROUP, rows, HEAD_SIZE)
            .transpose(1, 0, 2)
            .reshape(rows, q_half)
        )
        log_totals.append(row_peak + jnp.log(row_total))
    branch = dot_nt(attended[0], w_out[0]) + dot_nt(attended[1], w_out[1])
    residual = inputs + branch

    inv_mix = lax.rsqrt(jnp.mean(residual * residual, axis=1, keepdims=True) + EPS)
    scaled_mix = residual * inv_mix
    normed_mix = (scaled_mix * mix_scale).astype(bf16)
    logits = dot(normed_mix, router_w)
    hot_routes = (
        route_rows[:, :, None] == jnp.arange(experts, dtype=jnp.int32)[None, None, :]
    ).astype(f32)
    chosen = jnp.sum(hot_routes * logits[:, None, :], axis=-1)
    gate_expo = jnp.exp(chosen - jnp.max(chosen, axis=1, keepdims=True))
    gate_weights = gate_expo / jnp.sum(gate_expo, axis=1, keepdims=True)
    named = jnp.sum(hot_routes, axis=1)
    gate_rows = jnp.sum(gate_weights[:, :, None] * hot_routes, axis=1)
    gate_sent = jnp.where(named > 0, gate_rows, -1.0).T

    rows_all, gates_all = column_gather(normed_mix, gate_sent)
    grads_all = lax.all_gather(
        lax.all_gather(block_cotangent[0], "h", axis=0, tiled=True), "c", axis=0, tiled=True
    )
    expert = (c * 2 + h) * 2 + l
    block = 2 * rows
    rows_all = rows_all.reshape(4, block, model_width)
    grads_all = grads_all.reshape(4, block, model_width)
    gate_own = lax.dynamic_index_in_dim(gates_all, expert, axis=1, keepdims=False).reshape(
        4, block
    )
    taken = gate_own >= 0
    taken_low = taken.astype(jnp.int32)
    slot_of = jnp.cumsum(taken_low, axis=1) - taken_low
    hot_slots = (slot_of[:, None, :] == jnp.arange(SLOTS, dtype=jnp.int32)[None, :, None]) & taken[
        :, None, :
    ]
    pick = hot_slots.astype(bf16)
    slot_gate = jnp.sum(jnp.where(hot_slots, gate_own[:, None, :], 0.0), axis=2).reshape(
        4 * SLOTS, 1
    )

    def to_slots(values_all):
        return (
            jnp.einsum("kst,ktd->ksd", pick, values_all, preferred_element_type=f32)
            .astype(bf16)
            .reshape(4 * SLOTS, model_width)
        )

    def to_rows(slot_values):
        return (
            jnp.einsum(
                "kst,ksd->ktd",
                pick,
                slot_values.astype(bf16).reshape(4, SLOTS, model_width),
                preferred_element_type=f32,
            )
            .astype(bf16)
            .reshape(8, rows, model_width)
        )

    dispatched = to_slots(rows_all)
    slot_grad = to_slots(grads_all)
    gate_act = dot(dispatched, gate_w)
    up_act = dot(dispatched, up_w)
    sigmoid_act = jax.nn.sigmoid(gate_act)
    silu_act = gate_act * sigmoid_act
    hidden = silu_act * up_act
    hidden_gated = (hidden * slot_gate).astype(bf16)
    mix_parts = to_rows(dot_nt(hidden_gated, down_w))
    hidden_grad = dot(slot_grad, down_w)
    gate_back_slots = jnp.sum(hidden * hidden_grad, axis=1).reshape(4, SLOTS)
    gate_back_rows = jnp.sum(
        jnp.where(hot_slots, gate_back_slots[:, :, None], 0.0), axis=1
    ).reshape(8, 2, rows // 2)
    hidden_grad = hidden_grad * slot_gate
    gate_low = (hidden_grad * up_act * (sigmoid_act * (1.0 + gate_act * (1.0 - sigmoid_act)))).astype(
        bf16
    )
    up_low = (hidden_grad * silu_act).astype(bf16)
    grad_down = dot_tn(slot_grad, hidden_gated).astype(bf16)
    grad_gate = dot_tn(dispatched, gate_low).astype(bf16)
    grad_up = dot_tn(dispatched, up_low).astype(bf16)
    back_parts = to_rows(dot_nt(gate_low, gate_w) + dot_nt(up_low, up_w))

    mix_back, gate_back = column_sum(back_parts, gate_back_rows, 5)
    mix_out, unused = column_sum(mix_parts, gate_back_rows, 6)
    expert_sum = lax.psum_scatter(
        jnp.stack([grad_gate, grad_up, grad_down]), ("x", "y"), scatter_dimension=1, tiled=True
    )
    block_out = exchange_halves((residual + mix_out).astype(bf16), l)

    gate_back = jnp.sum(hot_routes * gate_back.reshape(experts, rows).T[:, None, :], axis=-1)
    gate_mean = jnp.sum(gate_weights * gate_back, axis=1, keepdims=True)
    chosen_grad = gate_weights * (gate_back - gate_mean)
    logit_grad = jnp.sum(chosen_grad[:, :, None] * hot_routes, axis=1).astype(bf16)
    grad_router = dot_tn(normed_mix, logit_grad)
    normed_grad = mix_back + dot_nt(logit_grad, router_w)
    grad_mix_gain = jnp.sum(normed_grad * scaled_mix, axis=0)
    scaled_grad = normed_grad * mix_scale
    resid_grad = (
        upstream
        + inv_mix * scaled_grad
        - residual * inv_mix**3 * jnp.mean(scaled_grad * residual, axis=1, keepdims=True)
    )

    branch_low = resid_grad.astype(bf16)
    grad_out = jnp.stack([dot_tn(branch_low, attended[i]) for i in range(2)]).astype(bf16)
    query_low, key_parts, value_parts = [], [], []
    for i in range(2):
        back_low = (
            dot(branch_low, w_out[i])
            .astype(bf16)
            .reshape(rows, GROUP, HEAD_SIZE)
            .transpose(1, 0, 2)
            .reshape(GROUP * rows, HEAD_SIZE)
        )
        prob_vals = jnp.exp(scores_of(i) - log_totals[i]).reshape(GROUP * rows, seq_length)
        prob_low = prob_vals.astype(bf16)
        prob_grad = dot_nt(back_low, values[i])
        row_dot = jnp.sum(prob_vals * prob_grad, axis=-1, keepdims=True)
        score_grad = (prob_vals * (prob_grad - row_dot)).astype(bf16)
        query_grad = dot(score_grad, keys[i]) * score_scale
        key_parts.append(
            dot_tn(score_grad, q_heads[i].reshape(GROUP * rows, HEAD_SIZE)) * score_scale
        )
        value_parts.append(dot_tn(prob_low, back_low))
        query_low.append(
            rotate_back(
                query_grad.reshape(GROUP, rows, HEAD_SIZE).transpose(1, 0, 2),
                cosine_table,
                sine_table,
            )
            .astype(bf16)
            .reshape(rows, q_half)
        )
    kv_back = sum_along_z(
        jnp.concatenate(key_parts + value_parts, axis=1)
        .astype(bf16)
        .reshape(4, rows, 4 * kv_width)
    )
    grad_in, normed_back = [], 0.0
    for i in range(2):
        key_low = rotate_back(
            kv_back[:, None, i * kv_width : (i + 1) * kv_width], cosine_table, sine_table
        ).astype(bf16)[:, 0]
        value_low = kv_back[:, (2 + i) * kv_width : (3 + i) * kv_width].astype(bf16)
        back_rows = jnp.concatenate([query_low[i], key_low, value_low], axis=1)
        grad_in.append(dot_tn(normalized_input, back_rows))
        normed_back = normed_back + dot_nt(back_rows, qkv_w[i])
    grad_attn_gain = jnp.sum(normed_back * scaled_in, axis=0)
    scaled_back = normed_back * attn_scale
    input_grad = (
        resid_grad
        + inv_attn * scaled_back
        - inputs * inv_attn**3 * jnp.mean(scaled_back * inputs, axis=1, keepdims=True)
    )
    input_grad = exchange_halves(input_grad.astype(bf16), l).astype(f32)

    misc_grad = jnp.concatenate(
        [grad_attn_gain[:, None], grad_mix_gain[:, None], grad_router], axis=1
    )
    misc_grad = jnp.pad(misc_grad, ((0, 0), (0, MISC - misc_grad.shape[1])))
    misc_grad = jnp.stack([misc_grad, jnp.zeros_like(misc_grad)]).astype(bf16)
    attn_grads = jnp.concatenate([jnp.stack(grad_in).astype(bf16), misc_grad], axis=2)

    def to_columns(grads):
        chip_sum = lax.psum_scatter(grads, "c", scatter_dimension=0, tiled=True)[0]
        return lax.psum_scatter(chip_sum, ("x", "y"), scatter_dimension=0, tiled=True)

    sums = jnp.concatenate([to_columns(attn_grads), to_columns(grad_out)], axis=1).astype(f32)
    sums = sums.reshape(4, part, sums.shape[1])
    returned, misc_back = attn_return(
        sums, sums[:, :, q_half + 2 * kv_width : in_width]
    )
    returned = jnp.sum(returned, axis=0)
    misc_back = jnp.sum(misc_back, axis=0)
    expert_back = expert_return(
        expert_sum.astype(f32)
        .reshape(3, 4, part, 2, ff_half)
        .transpose(1, 3, 0, 2, 4)
        .reshape(8, 3, part, ff_half)
    )
    return (
        block_out[None],
        input_grad[None],
        misc_back[:, 0],
        returned[:, :q_half],
        returned[:, q_half : q_half + kv_width],
        returned[:, q_half + kv_width : q_half + 2 * kv_width],
        returned[:, in_width:].T,
        misc_back[:, 1],
        misc_back[:, 2 : 2 + experts],
        expert_back[:, 0],
        expert_back[:, 1],
        expert_back[:, 2],
    )


def solution(mesh):
    split = Mesh(mesh.devices.reshape(4, 4, 2, 2, 2), ("x", "y", "c", "h", "l"))
    fsdp = ("x", "y", "c")
    owner = ("x", "y", "c", "h")
    return jax.shard_map(
        body,
        mesh=split,
        in_specs=(
            P(fsdp, "h", None),
            P(fsdp, None),
            P(fsdp, "h", None),
            P(owner),
            P(owner, "l"),
            P(owner, "l"),
            P(owner, "l"),
            P("l", owner),
            P(owner),
            P(owner, None),
            P(None, owner, "l"),
            P(None, owner, "l"),
            P(None, owner, "l"),
            P(fsdp, "h", None),
        ),
        out_specs=(
            P(fsdp, "h", None),
            P(fsdp, "h", None),
            P(owner),
            P(owner, "l"),
            P(owner, "l"),
            P(owner, "l"),
            P("l", owner),
            P(owner),
            P(owner, None),
            P(None, owner, "l"),
            P(None, owner, "l"),
            P(None, owner, "l"),
        ),
        check_vma=False,
    )
```

```python
import functools

import jax
import jax.numpy as jnp
from jax import lax
from jax.experimental import pallas as pl
from jax.experimental.pallas import tpu as pltpu
from jax.sharding import Mesh
from jax.sharding import PartitionSpec as P

QUERY_HEADS = 12
KEY_VALUE_HEADS = 2
HEAD_SIZE = 128
GROUP = QUERY_HEADS // KEY_VALUE_HEADS
EPS = 1e-06
ROPE_BASE = 1000000.0
NEG_FILL = -1e30
MISC = 128
SLOTS = 320
PAD = 32
MESH = pl.DeviceIdType.MESH
ANY = pl.BlockSpec(memory_space=pl.ANY)
VMEM = pl.BlockSpec(memory_space=pltpu.VMEM)
f32 = jnp.float32
bf16 = jnp.bfloat16


def rope_tables(positions):
    half_dim = HEAD_SIZE // 2
    frequency = ROPE_BASE ** (-jnp.arange(half_dim, dtype=f32) * (2.0 / HEAD_SIZE))
    angles = positions.astype(f32)[:, None] * frequency[None, :]
    angles = jnp.concatenate([angles, angles], axis=1)
    return (jnp.cos(angles)[:, None, :], jnp.sin(angles)[:, None, :])


def rotary_embed(value_rows, cosine_table, sine_table):
    half_dim = HEAD_SIZE // 2
    turned = jnp.concatenate([-value_rows[..., half_dim:], value_rows[..., :half_dim]], axis=-1)
    return value_rows * cosine_table + turned * sine_table


def rotate_back(grad_vals, cosine_table, sine_table):
    half_dim = HEAD_SIZE // 2
    scaled = grad_vals * sine_table
    turned = jnp.concatenate([scaled[..., half_dim:], -scaled[..., :half_dim]], axis=-1)
    return grad_vals * cosine_table + turned


def place():
    return lax.axis_index("c"), lax.axis_index("h"), lax.axis_index("l")


def column_peer(core_step, z_step):
    c, h, l = place()
    z = lax.rem(h * 2 + l + z_step, 4)
    return {"c": lax.rem(c + core_step, 2), "h": z // 2, "l": lax.rem(z, 2)}


def at_z(core, z):
    return {"c": core, "h": z // 2, "l": lax.rem(z, 2)}


def greet(steps):
    barrier = pltpu.get_barrier_semaphore()
    for core_step, z_step in steps:
        pl.semaphore_signal(
            barrier, inc=1, device_id=column_peer(core_step, (4 - z_step) % 4), device_id_type=MESH
        )
    pl.semaphore_wait(barrier, len(steps))


def send(src, dst, send_sem, recv_sem, peer):
    copy = pltpu.make_async_remote_copy(
        src_ref=src,
        dst_ref=dst,
        send_sem=send_sem,
        recv_sem=recv_sem,
        device_id=peer,
        device_id_type=MESH,
    )
    copy.start()
    return copy


COLUMN = [(0, 1), (0, 2), (0, 3), (1, 0), (1, 1), (1, 2), (1, 3)]
ALONG_Z = [(0, 1), (0, 2), (0, 3)]


class Lanes:
    def __init__(self, send_sem, recv_sem):
        self.send_sem, self.recv_sem, self.used = send_sem, recv_sem, 0

    def send(self, src, dst, peer):
        i = self.used
        self.used += 1
        return send(src, dst, self.send_sem.at[i], self.recv_sem.at[i], peer)


def lanes_scratch(count):
    return [pltpu.SemaphoreType.DMA((count,)), pltpu.SemaphoreType.DMA((count,))]


def chip_peer(axis, step):
    return {axis: lax.rem(lax.axis_index(axis) + step + 4, 4)}


def greet_chips(barrier):
    for axis in ("x", "y"):
        for step in (1, 3):
            pl.semaphore_signal(
                barrier, inc=1, device_id=chip_peer(axis, step), device_id_type=MESH
            )
    return 4


def greet_column(barrier):
    for step in COLUMN:
        pl.semaphore_signal(barrier, inc=1, device_id=column_peer(*step), device_id_type=MESH)
    return len(COLUMN)


class ColumnRing:
    def __init__(self, lanes, rows_ref, out_ref):
        c, h, l = place()
        self.lanes, self.rows, self.out = lanes, rows_ref, out_ref
        self.c, self.z = c, h * 2 + l
        self.half = rows_ref.shape[0] // 2
        self.copies = []

    def at(self, step):
        return self.c * 4 + lax.rem(self.z + step + 4, 4)

    def forward(self, step):
        block = self.out.at[self.at(step)]
        self.copies.append(self.lanes.send(block, block, column_peer(1, 0)))

    def start(self):
        here = self.out.at[self.at(0)]
        self.up = self.lanes.send(self.rows, here, column_peer(0, 1))
        self.down = self.lanes.send(self.rows, here, column_peer(0, 3))
        self.copies.append(self.lanes.send(self.rows, here, column_peer(1, 0)))

    def relay(self):
        lower, upper = pl.ds(0, self.half), pl.ds(self.half, self.half)
        self.up.wait_recv()
        block = self.out.at[self.at(-1), lower]
        self.up_far = self.lanes.send(block, block, column_peer(0, 1))
        self.down.wait_recv()
        block = self.out.at[self.at(1), upper]
        self.down_far = self.lanes.send(block, block, column_peer(0, 3))
        self.forward(-1)
        self.forward(1)

    def finish(self):
        self.up_far.wait_recv()
        self.down_far.wait_recv()
        self.forward(2)
        for copy in (self.up, self.down, self.up_far, self.down_far):
            copy.wait_send()
        for copy in self.copies:
            copy.wait()


class ChipRing:
    def __init__(self, lanes, w_out, block, low, rows, a, b):
        self.lanes, self.w_out, self.block = lanes, w_out, block
        self.rows, self.a, self.b = pl.ds(low, rows), a, b
        self.c = lax.axis_index("c")
        self.split = 1024
        self.sent, self.near = [], []

    def ref(self, da, db, columns=None):
        steps = {self.a: da, self.b: db}
        x = lax.rem(lax.axis_index("x") + steps["x"] + 4, 4)
        y = lax.rem(lax.axis_index("y") + steps["y"] + 4, 4)
        if columns is None:
            return self.w_out.at[self.c, x * 4 + y, self.rows]
        return self.w_out.at[self.c, x * 4 + y, self.rows, columns]

    def copy(self, src, dst, axis, step):
        made = self.lanes.send(src, dst, chip_peer(axis, step))
        self.sent.append(made)
        return made

    def share(self, da, db):
        block = self.ref(da, db)
        self.near.append(self.lanes.send(block, block, column_peer(1, 0)))

    def start(self):
        own = self.block.at[self.rows]
        here = self.ref(0, 0)
        self.first = [self.copy(own, here, self.a, step) for step in (1, -1)]
        self.turn = {0: [self.copy(own, here, self.b, step) for step in (1, -1)]}
        self.near.append(self.lanes.send(own, here, column_peer(1, 0)))

    def pass_on(self, da):
        block = self.ref(da, 0)
        self.turn[da] = [self.copy(block, block, self.b, step) for step in (1, -1)]
        self.share(da, 0)

    def relay_first(self):
        width = self.w_out.shape[3]
        low, high = pl.ds(0, self.split), pl.ds(self.split, width - self.split)
        for copy in self.first:
            copy.wait_recv()
        block = self.ref(-1, 0, low)
        one = self.copy(block, block, self.a, 1)
        block = self.ref(1, 0, high)
        self.second = [one, self.copy(block, block, self.a, -1)]
        self.pass_on(-1)
        self.pass_on(1)

    def relay_turn(self, da):
        for copy in self.turn[da]:
            copy.wait_recv()
        step = 1 if da in (0, -1) else -1
        block = self.ref(da, -step)
        self.last[da] = self.copy(block, block, self.b, step)
        self.share(da, 1)
        self.share(da, -1)

    def relay_second(self):
        for copy in self.second:
            copy.wait_recv()
        self.pass_on(2)

    def finish(self):
        for da in (0, -1, 1, 2):
            self.last[da].wait_recv()
            self.share(da, 2)

    def drain(self):
        for copy in self.sent:
            copy.wait_send()
        for copy in self.near:
            copy.wait()


def weights_kernel(
    part,
    attn_ref,
    expert_ref,
    rows_ref,
    w_out,
    expert_out,
    rows_out,
    attn_in,
    expert_in,
    block,
    s_sem,
    r_sem,
    as_sem,
    ar_sem,
    own,
):
    c, h, l = place()
    me = (c * 2 + h) * 2 + l
    barrier = pltpu.get_barrier_semaphore()
    pl.semaphore_wait(barrier, greet_column(barrier) + greet_chips(barrier))
    lanes = Lanes(s_sem, r_sem)
    slot = c * 2 + h
    here = pltpu.make_async_copy(attn_ref, attn_in.at[slot], own.at[1])
    there = pltpu.make_async_remote_copy(
        src_ref=attn_ref,
        dst_ref=attn_in.at[slot],
        send_sem=as_sem.at[0],
        recv_sem=ar_sem.at[slot],
        device_id=column_peer(1, 0),
        device_id_type=MESH,
    )
    pl.when(c == l)(here.start)
    pl.when(c != l)(there.start)
    for z_step in range(1, 4):
        z = lax.rem(h * 2 + l + z_step, 4)
        send(attn_ref, attn_in.at[slot], as_sem.at[z_step], ar_sem.at[slot], at_z(l, z))
    own_copy = pltpu.make_async_copy(expert_ref.at[me], expert_in.at[me], own.at[0])
    own_copy.start()
    pieces = []
    for step in COLUMN:
        peer = column_peer(*step)
        to = (peer["c"] * 2 + peer["h"]) * 2 + peer["l"]
        pieces.append(lanes.send(expert_ref.at[to], expert_in.at[me], peer))
    own_rows = pltpu.make_async_copy(rows_ref, rows_out.at[me], own.at[2])
    own_rows.start()
    ring = ColumnRing(lanes, rows_ref, rows_out)
    ring.start()

    for source in range(4):
        mine = (c == l) & (slot == source)

        def landed(source=source):
            pltpu.make_async_remote_copy(
                src_ref=attn_ref,
                dst_ref=attn_in.at[source],
                send_sem=as_sem.at[0],
                recv_sem=ar_sem.at[source],
                device_id=column_peer(1, 0),
                device_id_type=MESH,
            ).wait_recv()

        pl.when(jnp.logical_not(mine))(landed)
    pl.when(c == l)(here.wait)
    block[...] = jnp.concatenate(
        [attn_in[i].astype(f32)[:part] for i in range(4)], axis=0
    ).astype(block.dtype)
    x, y = lax.axis_index("x"), lax.axis_index("y")
    keep = pltpu.make_async_copy(block, w_out.at[c, x * 4 + y], own.at[3])
    keep.start()
    half = block.shape[0] // 2
    halves = [
        ChipRing(lanes, w_out, block, 0, half, "x", "y"),
        ChipRing(lanes, w_out, block, half, half, "y", "x"),
    ]
    for ring_half in halves:
        ring_half.last = {}
        ring_half.start()

    own_copy.wait()
    for copy in pieces:
        copy.wait()
    for i in range(3):
        for l_side in range(2):
            expert_out[i, :, l_side * 384 : (l_side + 1) * 384] = jnp.concatenate(
                [expert_in[2 * j + l_side, i].astype(f32)[:part] for j in range(4)], axis=0
            ).astype(expert_out.dtype)

    for ring_half in halves:
        ring_half.relay_first()
    for ring_half in halves:
        ring_half.relay_turn(0)
    for ring_half in halves:
        ring_half.relay_second()
    ring.relay()
    for da in (-1, 1, 2):
        for ring_half in halves:
            ring_half.relay_turn(da)
    ring.finish()
    for ring_half in halves:
        ring_half.finish()
    for ring_half in halves:
        ring_half.drain()
    keep.wait()
    own_rows.wait()
    pl.when(c != l)(there.wait_send)
    for z_step in range(1, 4):
        pltpu.make_async_remote_copy(
            src_ref=attn_ref,
            dst_ref=attn_in.at[slot],
            send_sem=as_sem.at[z_step],
            recv_sem=ar_sem.at[slot],
            device_id=column_peer(0, z_step),
            device_id_type=MESH,
        ).wait_send()


def gather_weights(attn_block, expert_pieces, rows, part):
    width = attn_block.shape[1]
    ff_half = expert_pieces.shape[3]
    return pl.pallas_call(
        functools.partial(weights_kernel, part),
        name="gather_weights",
        out_shape=(
            jax.ShapeDtypeStruct((2, 16, 4 * part, width), bf16),
            jax.ShapeDtypeStruct((3, 4 * part, 2 * ff_half), bf16),
            jax.ShapeDtypeStruct((8,) + rows.shape, bf16),
        ),
        in_specs=[VMEM, ANY, ANY],
        out_specs=(ANY, VMEM, ANY),
        scratch_shapes=[
            pltpu.VMEM((4,) + attn_block.shape, bf16),
            pltpu.VMEM(expert_pieces.shape, bf16),
            pltpu.VMEM((4 * part, width), bf16),
        ]
        + lanes_scratch(90)
        + [
            pltpu.SemaphoreType.DMA((4,)),
            pltpu.SemaphoreType.DMA((4,)),
            pltpu.SemaphoreType.DMA((4,)),
        ],
        compiler_params=pltpu.CompilerParams(
            collective_id=1, has_side_effects=True, vmem_limit_bytes=32 * 2**20
        ),
    )(attn_block, expert_pieces, rows)


def along_z_kernel(block_ref, out_ref, s_sem, r_sem, own):
    c, h, l = place()
    z = h * 2 + l
    greet(ALONG_Z)
    own_copy = pltpu.make_async_copy(block_ref, out_ref.at[z], own)
    own_copy.start()
    copies = [
        send(block_ref, out_ref.at[z], s_sem.at[i], r_sem.at[i], column_peer(*step))
        for i, step in enumerate(ALONG_Z)
    ]
    own_copy.wait()
    for copy in copies:
        copy.wait()


def gather_along_z(block):
    return pl.pallas_call(
        along_z_kernel,
        name="gather_keys_values",
        out_shape=jax.ShapeDtypeStruct((4,) + block.shape, block.dtype),
        in_specs=[VMEM],
        out_specs=VMEM,
        scratch_shapes=[
            pltpu.SemaphoreType.DMA((3,)),
            pltpu.SemaphoreType.DMA((3,)),
            pltpu.SemaphoreType.DMA(()),
        ],
        compiler_params=pltpu.CompilerParams(collective_id=2, has_side_effects=True),
    )(block)


def sum_along_z_kernel(parts_ref, out_ref, held, s_sem, r_sem):
    c, h, l = place()
    z = h * 2 + l
    greet(ALONG_Z)
    copies = [
        send(
            parts_ref.at[lax.rem(z + step[1], 4)],
            held.at[i],
            s_sem.at[i],
            r_sem.at[i],
            column_peer(*step),
        )
        for i, step in enumerate(ALONG_Z)
    ]
    for copy in copies:
        copy.wait()
    total = parts_ref[z].astype(f32)
    for i in range(3):
        total = total + held[i].astype(f32)
    out_ref[...] = total


def sum_along_z(parts):
    shape = parts.shape[1:]
    return pl.pallas_call(
        sum_along_z_kernel,
        name="sum_key_value_gradients",
        out_shape=jax.ShapeDtypeStruct(shape, f32),
        in_specs=[VMEM],
        out_specs=VMEM,
        scratch_shapes=[
            pltpu.VMEM((3,) + shape, parts.dtype),
            pltpu.SemaphoreType.DMA((3,)),
            pltpu.SemaphoreType.DMA((3,)),
        ],
        compiler_params=pltpu.CompilerParams(collective_id=3, has_side_effects=True),
    )(parts)


def column_gather_kernel(rows_ref, gate_ref, rows_out, gates_out, s_sem, r_sem, own):
    c, h, l = place()
    me = c * 4 + h * 2 + l
    barrier = pltpu.get_barrier_semaphore()
    pl.semaphore_wait(barrier, greet_column(barrier))
    lanes = Lanes(s_sem, r_sem)
    ring = ColumnRing(lanes, rows_ref, rows_out)
    ring.start()
    own_copies = [
        pltpu.make_async_copy(rows_ref, rows_out.at[me], own.at[0]),
        pltpu.make_async_copy(gate_ref, gates_out.at[me], own.at[1]),
    ]
    for copy in own_copies:
        copy.start()
    copies = [lanes.send(gate_ref, gates_out.at[me], column_peer(*step)) for step in COLUMN]
    ring.relay()
    ring.finish()
    for copy in own_copies + copies:
        copy.wait()


def column_gather(rows, gates):
    return pl.pallas_call(
        column_gather_kernel,
        name="gather_normed_rows",
        out_shape=(
            jax.ShapeDtypeStruct((8,) + rows.shape, rows.dtype),
            jax.ShapeDtypeStruct((8,) + gates.shape, gates.dtype),
        ),
        in_specs=[ANY, ANY],
        out_specs=(ANY, ANY),
        scratch_shapes=lanes_scratch(16) + [pltpu.SemaphoreType.DMA((2,))],
        compiler_params=pltpu.CompilerParams(collective_id=4, has_side_effects=True),
    )(rows, gates)


def column_sum_kernel(
    parts_ref, small_ref, out_ref, small_out, near, chip, far, cs, cr, zs, zr, ss, sr, own
):
    c, h, l = place()
    z = h * 2 + l
    me = c * 4 + z
    greet(COLUMN)
    other = column_peer(1, 0)
    order = [2, 1, 3, 0]
    near_copies = [
        send(
            parts_ref.at[(1 - c) * 4 + lax.rem(z + step, 4)],
            near.at[i],
            cs.at[i],
            cr.at[i],
            other,
        )
        for i, step in enumerate(order)
    ]
    own_copy = pltpu.make_async_copy(small_ref.at[me], small_out.at[me], own)
    own_copy.start()
    small_copies = []
    for i, step in enumerate(COLUMN):
        peer = column_peer(*step)
        to = (peer["c"] * 2 + peer["h"]) * 2 + peer["l"]
        small_copies.append(send(small_ref.at[to], small_out.at[me], ss.at[i], sr.at[i], peer))
    rows = parts_ref.shape[1]
    chunk = 32
    far_copies = []
    for i, step in enumerate(order):
        near_copies[i].wait_recv()
        mine = c * 4 + lax.rem(z + step, 4)

        def add(k, carry, i=i, mine=mine, step=step):
            here = pl.ds(pl.multiple_of(k * chunk, chunk), chunk)
            total = parts_ref[mine, here, :].astype(f32) + near[i, here, :].astype(f32)
            if step == 0:
                out_ref[here, :] = total
            else:
                chip[i, here, :] = total.astype(chip.dtype)
            return carry

        lax.fori_loop(0, rows // chunk, add, 0)
        if step:
            far_copies.append(
                send(chip.at[i], far.at[i], zs.at[i], zr.at[i], column_peer(0, step))
            )
    for copy in far_copies:
        copy.wait()

    def finish(k, carry):
        here = pl.ds(pl.multiple_of(k * chunk, chunk), chunk)
        total = out_ref[here, :]
        for i in range(3):
            total = total + far[i, here, :].astype(f32)
        out_ref[here, :] = total
        return carry

    lax.fori_loop(0, rows // chunk, finish, 0)
    for copy in near_copies:
        copy.wait_send()
    own_copy.wait()
    for copy in small_copies:
        copy.wait()


def column_sum(parts, small, number):
    rows, width = parts.shape[1:]
    return pl.pallas_call(
        column_sum_kernel,
        name="sum_over_experts",
        out_shape=(
            jax.ShapeDtypeStruct((rows, width), f32),
            jax.ShapeDtypeStruct(small.shape, small.dtype),
        ),
        in_specs=[VMEM, VMEM],
        out_specs=(VMEM, VMEM),
        scratch_shapes=[
            pltpu.VMEM((4, rows, width), parts.dtype),
            pltpu.VMEM((3, rows, width), parts.dtype),
            pltpu.VMEM((3, rows, width), parts.dtype),
            pltpu.SemaphoreType.DMA((4,)),
            pltpu.SemaphoreType.DMA((4,)),
            pltpu.SemaphoreType.DMA((3,)),
            pltpu.SemaphoreType.DMA((3,)),
            pltpu.SemaphoreType.DMA((7,)),
            pltpu.SemaphoreType.DMA((7,)),
            pltpu.SemaphoreType.DMA(()),
        ],
        compiler_params=pltpu.CompilerParams(
            collective_id=number, has_side_effects=True, vmem_limit_bytes=40 * 2**20
        ),
    )(parts, small)


class ChipSum:
    def __init__(self, lanes, chip, low, rows, p, q, near_p, rest_p, near_q):
        self.lanes, self.chip = lanes, chip
        self.rows, self.p, self.q = pl.ds(low, rows), p, q
        self.near_p, self.rest_p, self.near_q = near_p, rest_p, near_q
        self.sent = []

    def index(self, dp, dq):
        steps = {self.p: dp, self.q: dq}
        x = lax.rem(lax.axis_index("x") + steps["x"] + 4, 4)
        y = lax.rem(lax.axis_index("y") + steps["y"] + 4, 4)
        return x * 4 + y

    def copy(self, src, dst, axis, step):
        made = self.lanes.send(src, dst, chip_peer(axis, step))
        self.sent.append(made)
        return made

    def own(self, dp, dq):
        return self.chip.at[self.index(dp, dq), self.rows]

    def far(self):
        self.far_copies = {}
        for dq, step, i in ((2, 1, 0), (3, -1, 0), (1, 1, 1), (0, -1, 1)):
            direction = 0 if step == 1 else 1
            self.far_copies[direction, i] = self.copy(
                self.own(2, dq), self.near_p.at[direction, i], self.p, step
            )

    def plain(self):
        self.next_copies = {}
        for dq, step in ((2, -1), (3, 1), (1, -1), (0, 1)):
            self.next_to(dq, step)

    def next_to(self, dq, step):
        direction = 0 if step == 1 else 1
        self.next_copies[direction, dq] = self.copy(
            self.own(step, dq), self.rest_p.at[direction, dq], self.p, step
        )

    def joined(self):
        for dq, step, i in ((2, 1, 0), (3, -1, 0), (1, 1, 1), (0, -1, 1)):
            direction = 0 if step == 1 else 1
            self.far_copies[direction, i].wait_recv()
            mine = self.own(step, dq)
            mine[...] = mine[...] + self.near_p[direction, i]
            self.next_to(dq, step)

    def collect(self, dq):
        for direction in range(2):
            self.next_copies[direction, dq].wait_recv()
        mine = self.own(0, dq)
        total = mine[...].astype(f32)
        for direction in range(2):
            total = total + self.rest_p[direction, dq].astype(f32)
        mine[...] = total.astype(mine.dtype)

    def far_q(self):
        width = self.chip.shape[2]
        self.low, self.high = pl.ds(0, 1024), pl.ds(1024, width - 1024)
        self.collect(2)
        block = self.index(0, 2)
        self.far_q_copies = [
            self.copy(
                self.chip.at[block, self.rows, self.low], self.near_q.at[0, :, self.low], self.q, 1
            ),
            self.copy(
                self.chip.at[block, self.rows, self.high], self.near_q.at[1, :, self.high], self.q, -1
            ),
        ]

    def next_q(self):
        self.next_q_copies = []
        for i, (dq, columns) in enumerate(((1, self.low), (3, self.high))):
            self.collect(dq)
            self.far_q_copies[i].wait_recv()
            block = self.index(0, dq)
            self.chip[block, self.rows, columns] = (
                self.chip[block, self.rows, columns] + self.near_q[i, :, columns]
            )
            self.next_q_copies.append(
                self.copy(
                    self.chip.at[block, self.rows],
                    self.near_q.at[2 + i],
                    self.q,
                    1 if i == 0 else -1,
                )
            )

    def total(self):
        self.collect(0)
        total = self.chip[self.index(0, 0), self.rows, :].astype(f32)
        for i in range(2):
            self.next_q_copies[i].wait_recv()
            total = total + self.near_q[2 + i].astype(f32)
        return total

    def drain(self):
        for copy in self.sent:
            copy.wait_send()


def return_kernel(
    part,
    misc_at,
    in_ref,
    out_ref,
    expert_ref,
    grads_out,
    misc_out,
    expert_out,
    near,
    near_p0,
    rest_p0,
    near_q0,
    near_p1,
    rest_p1,
    near_q1,
    pieces,
    landed,
    misc_landed,
    s_sem,
    r_sem,
    ps,
    pr,
    ms,
    mr,
    own,
):
    c, h, l = place()
    z = h * 2 + l
    me = c * 4 + z
    barrier = pltpu.get_barrier_semaphore()
    pl.semaphore_wait(barrier, greet_column(barrier) + greet_chips(barrier))
    lanes = Lanes(s_sem, r_sem)
    in_width = in_ref.shape[3]
    width = near.shape[2]
    half = near.shape[1] // 2
    other = column_peer(1, 0)
    x, y = lax.axis_index("x"), lax.axis_index("y")
    sums = [
        ChipSum(lanes, near, 0, half, "y", "x", near_p0, rest_p0, near_q0),
        ChipSum(lanes, near, half, half, "x", "y", near_p1, rest_p1, near_q1),
    ]
    order = [2, 1, 3, 0]
    arrive = {}
    for step in order:
        for which in range(2):
            for dq in range(4):
                block = sums[which].index(step, dq)
                rows = pl.ds(which * half, half)
                arrive[step, which, dq] = [
                    lanes.send(
                        in_ref.at[1 - c, block, rows],
                        near.at[block, rows, pl.ds(0, in_width)],
                        other,
                    ),
                    lanes.send(
                        out_ref.at[1 - c, block, rows],
                        near.at[block, rows, pl.ds(in_width, width - in_width)],
                        other,
                    ),
                ]
    own_copy = pltpu.make_async_copy(expert_ref.at[me], expert_out.at[me], own.at[0])
    own_copy.start()
    expert_copies = []
    for step in COLUMN:
        peer = column_peer(*step)
        to = (peer["c"] * 2 + peer["h"]) * 2 + peer["l"]
        expert_copies.append(lanes.send(expert_ref.at[to], expert_out.at[me], peer))

    def add_own(step, which):
        for dq in range(4):
            for copy in arrive[step, which, dq]:
                copy.wait_recv()
            block = sums[which].index(step, dq)
            rows = pl.ds(which * half, half)
            near[block, rows, pl.ds(0, in_width)] = (
                near[block, rows, pl.ds(0, in_width)] + in_ref[c, block, rows, :]
            )
            near[block, rows, pl.ds(in_width, width - in_width)] = (
                near[block, rows, pl.ds(in_width, width - in_width)] + out_ref[c, block, rows, :]
            )

    for which in range(2):
        add_own(2, which)
        sums[which].far()
    for step in (1, 3):
        for which in range(2):
            add_own(step, which)
    for each in sums:
        each.plain()
    for each in sums:
        each.joined()
    for which in range(2):
        add_own(0, which)
    for each in sums:
        each.far_q()
    for each in sums:
        each.next_q()
    for which in range(2):
        total = sums[which].total()
        for i in range(2):
            pieces[2 * which + i] = total[i * part : (i + 1) * part]

    def to_owner(target, owner, src, dst, send_sem, recv_sem, asked):
        is_me = (owner["c"] == c) & (owner["h"] == h) & (owner["l"] == l)
        there = pltpu.make_async_remote_copy(
            src_ref=src,
            dst_ref=dst,
            send_sem=send_sem,
            recv_sem=recv_sem,
            device_id=owner,
            device_id_type=MESH,
        )
        here = pltpu.make_async_copy(src, dst, recv_sem)
        pl.when(asked & jnp.logical_not(is_me))(there.start)
        pl.when(asked & is_me)(here.start)
        return asked & jnp.logical_not(is_me), there

    sent = []
    everyone = c < 2
    for target in range(4):
        owner = {"c": target // 2, "h": target % 2, "l": c}
        sent.append(
            to_owner(
                target, owner, pieces.at[target], landed.at[z], ps.at[target], pr.at[z], everyone
            )
        )
    misc = pl.ds(misc_at, MISC)
    for target in range(4):
        owner = {"c": target // 2, "h": target % 2, "l": 1}
        sent.append(
            to_owner(
                target,
                owner,
                pieces.at[target, :, misc],
                misc_landed.at[z],
                ms.at[target],
                mr.at[z],
                c == 0,
            )
        )
    for source in range(4):
        pltpu.make_async_copy(pieces.at[0], landed.at[source], pr.at[source]).wait()
    grads_out[...] = (landed[0] + landed[1]) + (landed[2] + landed[3])

    def from_core():
        for source in range(4):
            pltpu.make_async_copy(
                pieces.at[0, :, misc], misc_landed.at[source], mr.at[source]
            ).wait()
        misc_out[...] = (misc_landed[0] + misc_landed[1]) + (misc_landed[2] + misc_landed[3])

    def from_piece():
        misc_out[...] = (landed[0, :, misc] + landed[1, :, misc]) + (
            landed[2, :, misc] + landed[3, :, misc]
        )

    pl.when(l == 1)(from_core)
    pl.when(l == 0)(from_piece)
    for asked, there in sent:
        pl.when(asked)(there.wait_send)
    for copies in arrive.values():
        for copy in copies:
            copy.wait_send()
    for each in sums:
        each.drain()
    own_copy.wait()
    for copy in expert_copies:
        copy.wait()


def return_gradients(grad_in, grad_out, expert_pieces, part, misc_at):
    in_width, out_width = grad_in.shape[3], grad_out.shape[3]
    width, rows = in_width + out_width, grad_in.shape[2]
    half = rows // 2
    ring = [
        pltpu.VMEM((2, 2, half, width), bf16),
        pltpu.VMEM((2, 4, half, width), bf16),
        pltpu.VMEM((4, half, width), bf16),
    ]
    return pl.pallas_call(
        functools.partial(return_kernel, part, misc_at),
        name="return_gradients",
        out_shape=(
            jax.ShapeDtypeStruct((part, width), f32),
            jax.ShapeDtypeStruct((part, MISC), f32),
            jax.ShapeDtypeStruct(expert_pieces.shape, expert_pieces.dtype),
        ),
        in_specs=[VMEM, VMEM, ANY],
        out_specs=(VMEM, VMEM, ANY),
        scratch_shapes=[pltpu.VMEM((16, rows, width), bf16)]
        + ring
        + ring
        + [
            pltpu.VMEM((4, part, width), f32),
            pltpu.VMEM((4, part, width), f32),
            pltpu.VMEM((4, part, MISC), f32),
        ]
        + lanes_scratch(130)
        + [
            pltpu.SemaphoreType.DMA((4,)),
            pltpu.SemaphoreType.DMA((4,)),
            pltpu.SemaphoreType.DMA((4,)),
            pltpu.SemaphoreType.DMA((4,)),
            pltpu.SemaphoreType.DMA((1,)),
        ],
        compiler_params=pltpu.CompilerParams(
            collective_id=7, has_side_effects=True, vmem_limit_bytes=48 * 2**20
        ),
    )(grad_in, grad_out, expert_pieces)


def dot(a, b):
    return jnp.dot(a, b, preferred_element_type=f32)


def dot_nt(a, b):
    return lax.dot_general(a, b, (((1,), (1,)), ((), ())), preferred_element_type=f32)


def dot_tn(a, b):
    return lax.dot_general(a, b, (((0,), (0,)), ((), ())), preferred_element_type=f32)


def exchange_halves(own, l):
    other = lax.ppermute(own, "l", [(0, 1), (1, 0)])
    first = jnp.where(l == 0, own, other)
    second = jnp.where(l == 0, other, own)
    return jnp.concatenate([first, second], axis=0)


def body(
    tokens,
    segments,
    routes,
    attn_gain,
    w_query,
    key_matrix,
    value_matrix,
    w_output,
    mix_gain,
    w_router,
    w_gate,
    w_up,
    w_down,
    block_cotangent,
):
    c, h, l = place()
    model_width = tokens.shape[2]
    rows = tokens.shape[1] // 2
    seq_length = segments.shape[1]
    experts, part, ff_half = w_gate.shape
    q_half = w_query.shape[1]
    score_scale = HEAD_SIZE ** (-0.5)

    misc = jnp.concatenate([attn_gain[:, None], mix_gain[:, None], w_router], axis=1)
    misc = jnp.pad(misc, ((0, 0), (0, MISC - misc.shape[1])))
    attn_block = jnp.concatenate(
        [w_query, key_matrix, value_matrix, misc, w_output.T], axis=1
    )
    attn_block = jnp.pad(attn_block, ((0, PAD - part), (0, 0)))
    expert_pieces = jnp.pad(
        jnp.stack([w_gate, w_up, w_down], axis=1), ((0, 0), (0, 0), (0, PAD - part), (0, 0))
    )
    upstream_low = lax.dynamic_slice_in_dim(block_cotangent[0], l * rows, rows)
    w_attn, expert_col, grads_all = gather_weights(attn_block, expert_pieces, upstream_low, part)
    kv_width = key_matrix.shape[1]
    in_width = q_half + 2 * kv_width + MISC
    w_attn = w_attn.reshape(2, model_width, attn_block.shape[1])
    w_out = w_attn[:, :, in_width:]
    expert_full = lax.all_gather(expert_col, ("x", "y"), axis=1, tiled=True)
    gate_w, up_w, down_w = expert_full[0], expert_full[1], expert_full[2]
    qkv_w = w_attn[:, :, : q_half + 2 * kv_width]
    misc_full = w_attn[0, :, q_half + 2 * kv_width : in_width]
    attn_scale = misc_full[:, 0].astype(f32)
    mix_scale = misc_full[:, 1].astype(f32)
    router_w = misc_full[:, 2 : 2 + experts]

    first = l * rows
    inputs = lax.dynamic_slice_in_dim(tokens[0], first, rows).astype(f32)
    upstream = upstream_low.astype(f32)
    route_rows = lax.dynamic_slice_in_dim(routes[0], first, rows)
    z = h * 2 + l
    positions = z * rows + jnp.arange(rows, dtype=jnp.int32)
    key_positions = jnp.arange(seq_length, dtype=jnp.int32)
    seg_all = segments[0]
    seg_local = lax.dynamic_slice_in_dim(seg_all, z * rows, rows)
    allowed = (seg_local[:, None] == seg_all[None, :]) & (
        positions[:, None] >= key_positions[None, :]
    )
    cosine_table, sine_table = rope_tables(positions)

    inv_attn = lax.rsqrt(jnp.mean(inputs * inputs, axis=1, keepdims=True) + EPS)
    scaled_in = inputs * inv_attn
    normalized_input = (scaled_in * attn_scale).astype(bf16)
    halves = [dot(normalized_input, qkv_w[i]) for i in range(2)]
    q_heads = [
        rotary_embed(p[:, :q_half].reshape(rows, GROUP, HEAD_SIZE), cosine_table, sine_table)
        .astype(bf16)
        .transpose(1, 0, 2)
        for p in halves
    ]
    k_own = [
        rotary_embed(
            p[:, None, q_half : q_half + kv_width], cosine_table, sine_table
        ).astype(bf16)[:, 0]
        for p in halves
    ]
    v_own = [p[:, q_half + kv_width :].astype(bf16) for p in halves]
    kv_all = gather_along_z(jnp.concatenate(k_own + v_own, axis=1)).reshape(
        seq_length, 4 * kv_width
    )
    keys = [kv_all[:, i * kv_width : (i + 1) * kv_width] for i in range(2)]
    values = [kv_all[:, (2 + i) * kv_width : (3 + i) * kv_width] for i in range(2)]

    def scores_of(i):
        scores = dot_nt(q_heads[i].reshape(GROUP * rows, HEAD_SIZE), keys[i]) * score_scale
        return jnp.where(
            allowed[None], scores.reshape(GROUP, rows, seq_length), NEG_FILL
        )

    attended, log_totals = [], []
    for i in range(2):
        masked = scores_of(i)
        row_peak = jnp.max(masked, axis=-1, keepdims=True)
        expo_vals = jnp.exp(masked - row_peak)
        row_total = jnp.sum(expo_vals, axis=-1, keepdims=True)
        weights_low = (expo_vals / row_total).astype(bf16)
        mixed = dot(weights_low.reshape(GROUP * rows, seq_length), values[i])
        attended.append(
            mixed.astype(bf16)
            .reshape(GROUP, rows, HEAD_SIZE)
            .transpose(1, 0, 2)
            .reshape(rows, q_half)
        )
        log_totals.append(row_peak + jnp.log(row_total))
    branch = dot_nt(attended[0], w_out[0]) + dot_nt(attended[1], w_out[1])
    residual = inputs + branch

    inv_mix = lax.rsqrt(jnp.mean(residual * residual, axis=1, keepdims=True) + EPS)
    scaled_mix = residual * inv_mix
    normed_mix = (scaled_mix * mix_scale).astype(bf16)
    logits = dot(normed_mix, router_w)
    hot_routes = (
        route_rows[:, :, None] == jnp.arange(experts, dtype=jnp.int32)[None, None, :]
    ).astype(f32)
    chosen = jnp.sum(hot_routes * logits[:, None, :], axis=-1)
    gate_expo = jnp.exp(chosen - jnp.max(chosen, axis=1, keepdims=True))
    gate_weights = gate_expo / jnp.sum(gate_expo, axis=1, keepdims=True)
    named = jnp.sum(hot_routes, axis=1)
    gate_rows = jnp.sum(gate_weights[:, :, None] * hot_routes, axis=1)
    gate_sent = jnp.where(named > 0, gate_rows, -1.0).T

    rows_all, gates_all = column_gather(normed_mix, gate_sent)
    expert = (c * 2 + h) * 2 + l
    block = 2 * rows
    rows_all = rows_all.reshape(4, block, model_width)
    grads_all = grads_all.reshape(4, block, model_width)
    gate_own = lax.dynamic_index_in_dim(gates_all, expert, axis=1, keepdims=False).reshape(
        4, block
    )
    taken = gate_own >= 0
    taken_low = taken.astype(jnp.int32)
    slot_of = jnp.cumsum(taken_low, axis=1) - taken_low
    hot_slots = (slot_of[:, None, :] == jnp.arange(SLOTS, dtype=jnp.int32)[None, :, None]) & taken[
        :, None, :
    ]
    pick = hot_slots.astype(bf16)
    slot_gate = jnp.sum(jnp.where(hot_slots, gate_own[:, None, :], 0.0), axis=2).reshape(
        4 * SLOTS, 1
    )

    def to_slots(values_all):
        return (
            jnp.einsum("kst,ktd->ksd", pick, values_all, preferred_element_type=f32)
            .astype(bf16)
            .reshape(4 * SLOTS, model_width)
        )

    def to_rows(slot_values):
        return (
            jnp.einsum(
                "kst,ksd->ktd",
                pick,
                slot_values.astype(bf16).reshape(4, SLOTS, model_width),
                preferred_element_type=f32,
            )
            .astype(bf16)
            .reshape(8, rows, model_width)
        )

    dispatched = to_slots(rows_all)
    slot_grad = to_slots(grads_all)
    gate_act = dot(dispatched, gate_w)
    up_act = dot(dispatched, up_w)
    sigmoid_act = jax.nn.sigmoid(gate_act)
    silu_act = gate_act * sigmoid_act
    hidden = silu_act * up_act
    hidden_gated = (hidden * slot_gate).astype(bf16)
    mix_parts = to_rows(dot_nt(hidden_gated, down_w))
    hidden_grad = dot(slot_grad, down_w)
    gate_back_slots = jnp.sum(hidden * hidden_grad, axis=1).reshape(4, SLOTS)
    gate_back_rows = jnp.sum(
        jnp.where(hot_slots, gate_back_slots[:, :, None], 0.0), axis=1
    ).reshape(8, 2, rows // 2)
    hidden_grad = hidden_grad * slot_gate
    gate_low = (hidden_grad * up_act * (sigmoid_act * (1.0 + gate_act * (1.0 - sigmoid_act)))).astype(
        bf16
    )
    up_low = (hidden_grad * silu_act).astype(bf16)
    grad_down = dot_tn(slot_grad, hidden_gated).astype(bf16)
    grad_gate = dot_tn(dispatched, gate_low).astype(bf16)
    grad_up = dot_tn(dispatched, up_low).astype(bf16)
    back_parts = to_rows(dot_nt(gate_low, gate_w) + dot_nt(up_low, up_w))

    mix_back, gate_back = column_sum(back_parts, gate_back_rows, 5)
    mix_out, unused = column_sum(mix_parts, gate_back_rows, 6)
    expert_sum = lax.psum_scatter(
        jnp.stack([grad_gate, grad_up, grad_down]), ("x", "y"), scatter_dimension=1, tiled=True
    )
    block_out = exchange_halves((residual + mix_out).astype(bf16), l)

    gate_back = jnp.sum(hot_routes * gate_back.reshape(experts, rows).T[:, None, :], axis=-1)
    gate_mean = jnp.sum(gate_weights * gate_back, axis=1, keepdims=True)
    chosen_grad = gate_weights * (gate_back - gate_mean)
    logit_grad = jnp.sum(chosen_grad[:, :, None] * hot_routes, axis=1).astype(bf16)
    grad_router = dot_tn(normed_mix, logit_grad)
    normed_grad = mix_back + dot_nt(logit_grad, router_w)
    grad_mix_gain = jnp.sum(normed_grad * scaled_mix, axis=0)
    scaled_grad = normed_grad * mix_scale
    resid_grad = (
        upstream
        + inv_mix * scaled_grad
        - residual * inv_mix**3 * jnp.mean(scaled_grad * residual, axis=1, keepdims=True)
    )

    branch_low = resid_grad.astype(bf16)
    grad_out = jnp.stack([dot_tn(branch_low, attended[i]) for i in range(2)]).astype(bf16)
    query_low, key_parts, value_parts = [], [], []
    for i in range(2):
        back_low = (
            dot(branch_low, w_out[i])
            .astype(bf16)
            .reshape(rows, GROUP, HEAD_SIZE)
            .transpose(1, 0, 2)
            .reshape(GROUP * rows, HEAD_SIZE)
        )
        prob_vals = jnp.exp(scores_of(i) - log_totals[i]).reshape(GROUP * rows, seq_length)
        prob_low = prob_vals.astype(bf16)
        prob_grad = dot_nt(back_low, values[i])
        row_dot = jnp.sum(prob_vals * prob_grad, axis=-1, keepdims=True)
        score_grad = (prob_vals * (prob_grad - row_dot)).astype(bf16)
        query_grad = dot(score_grad, keys[i]) * score_scale
        key_parts.append(
            dot_tn(score_grad, q_heads[i].reshape(GROUP * rows, HEAD_SIZE)) * score_scale
        )
        value_parts.append(dot_tn(prob_low, back_low))
        query_low.append(
            rotate_back(
                query_grad.reshape(GROUP, rows, HEAD_SIZE).transpose(1, 0, 2),
                cosine_table,
                sine_table,
            )
            .astype(bf16)
            .reshape(rows, q_half)
        )
    kv_back = sum_along_z(
        jnp.concatenate(key_parts + value_parts, axis=1)
        .astype(bf16)
        .reshape(4, rows, 4 * kv_width)
    )
    grad_in, normed_back = [], 0.0
    for i in range(2):
        key_low = rotate_back(
            kv_back[:, None, i * kv_width : (i + 1) * kv_width], cosine_table, sine_table
        ).astype(bf16)[:, 0]
        value_low = kv_back[:, (2 + i) * kv_width : (3 + i) * kv_width].astype(bf16)
        back_rows = jnp.concatenate([query_low[i], key_low, value_low], axis=1)
        grad_in.append(dot_tn(normalized_input, back_rows))
        normed_back = normed_back + dot_nt(back_rows, qkv_w[i])
    grad_attn_gain = jnp.sum(normed_back * scaled_in, axis=0)
    scaled_back = normed_back * attn_scale
    input_grad = (
        resid_grad
        + inv_attn * scaled_back
        - inputs * inv_attn**3 * jnp.mean(scaled_back * inputs, axis=1, keepdims=True)
    )
    input_grad = exchange_halves(input_grad.astype(bf16), l).astype(f32)

    misc_grad = jnp.concatenate(
        [grad_attn_gain[:, None], grad_mix_gain[:, None], grad_router], axis=1
    )
    misc_grad = jnp.pad(misc_grad, ((0, 0), (0, MISC - misc_grad.shape[1])))
    misc_grad = jnp.stack([misc_grad, jnp.zeros_like(misc_grad)]).astype(bf16)
    attn_grads = jnp.concatenate([jnp.stack(grad_in).astype(bf16), misc_grad], axis=2)

    pieces = (
        jnp.pad(expert_sum.reshape(3, 4, part, 2, ff_half), ((0, 0), (0, 0), (0, PAD - part), (0, 0), (0, 0)))
        .transpose(1, 3, 0, 2, 4)
        .reshape(8, 3, PAD, ff_half)
    )
    returned, misc_back, expert_back = return_gradients(
        attn_grads.reshape(2, 16, 4 * part, in_width),
        grad_out.reshape(2, 16, 4 * part, q_half),
        pieces,
        part,
        in_width - MISC,
    )
    expert_back = expert_back[:, :, :part].astype(f32)
    return (
        block_out[None],
        input_grad[None],
        misc_back[:, 0],
        returned[:, :q_half],
        returned[:, q_half : q_half + kv_width],
        returned[:, q_half + kv_width : q_half + 2 * kv_width],
        returned[:, in_width:].T,
        misc_back[:, 1],
        misc_back[:, 2 : 2 + experts],
        expert_back[:, 0],
        expert_back[:, 1],
        expert_back[:, 2],
    )


def solution(mesh):
    split = Mesh(mesh.devices.reshape(4, 4, 2, 2, 2), ("x", "y", "c", "h", "l"))
    fsdp = ("x", "y", "c")
    owner = ("x", "y", "c", "h")
    return jax.shard_map(
        body,
        mesh=split,
        in_specs=(
            P(fsdp, "h", None),
            P(fsdp, None),
            P(fsdp, "h", None),
            P(owner),
            P(owner, "l"),
            P(owner, "l"),
            P(owner, "l"),
            P("l", owner),
            P(owner),
            P(owner, None),
            P(None, owner, "l"),
            P(None, owner, "l"),
            P(None, owner, "l"),
            P(fsdp, "h", None),
        ),
        out_specs=(
            P(fsdp, "h", None),
            P(fsdp, "h", None),
            P(owner),
            P(owner, "l"),
            P(owner, "l"),
            P(owner, "l"),
            P("l", owner),
            P(owner),
            P(owner, None),
            P(None, owner, "l"),
            P(None, owner, "l"),
            P(None, owner, "l"),
        ),
        check_vma=False,
    )
```

```python
import functools

import jax
import jax.numpy as jnp
from jax import lax
from jax.experimental import pallas as pl
from jax.experimental.pallas import tpu as pltpu
from jax.sharding import Mesh
from jax.sharding import PartitionSpec as P

QUERY_HEADS = 12
KEY_VALUE_HEADS = 2
HEAD_SIZE = 128
GROUP = QUERY_HEADS // KEY_VALUE_HEADS
EPS = 1e-06
ROPE_BASE = 1000000.0
NEG_FILL = -1e30
MISC = 128
SLOTS = 320
PAD = 32
MESH = pl.DeviceIdType.MESH
ANY = pl.BlockSpec(memory_space=pl.ANY)
VMEM = pl.BlockSpec(memory_space=pltpu.VMEM)
f32 = jnp.float32
bf16 = jnp.bfloat16


def rope_tables(positions):
    half_dim = HEAD_SIZE // 2
    frequency = ROPE_BASE ** (-jnp.arange(half_dim, dtype=f32) * (2.0 / HEAD_SIZE))
    angles = positions.astype(f32)[:, None] * frequency[None, :]
    angles = jnp.concatenate([angles, angles], axis=1)
    return (jnp.cos(angles)[:, None, :], jnp.sin(angles)[:, None, :])


def rotary_embed(value_rows, cosine_table, sine_table):
    half_dim = HEAD_SIZE // 2
    turned = jnp.concatenate([-value_rows[..., half_dim:], value_rows[..., :half_dim]], axis=-1)
    return value_rows * cosine_table + turned * sine_table


def rotate_back(grad_vals, cosine_table, sine_table):
    half_dim = HEAD_SIZE // 2
    scaled = grad_vals * sine_table
    turned = jnp.concatenate([scaled[..., half_dim:], -scaled[..., :half_dim]], axis=-1)
    return grad_vals * cosine_table + turned


def place():
    return lax.axis_index("c"), lax.axis_index("h"), lax.axis_index("l")


def column_peer(core_step, z_step):
    c, h, l = place()
    z = lax.rem(h * 2 + l + z_step, 4)
    return {"c": lax.rem(c + core_step, 2), "h": z // 2, "l": lax.rem(z, 2)}


def at_z(core, z):
    return {"c": core, "h": z // 2, "l": lax.rem(z, 2)}


def greet(steps):
    barrier = pltpu.get_barrier_semaphore()
    for core_step, z_step in steps:
        pl.semaphore_signal(
            barrier, inc=1, device_id=column_peer(core_step, (4 - z_step) % 4), device_id_type=MESH
        )
    pl.semaphore_wait(barrier, len(steps))


def send(src, dst, send_sem, recv_sem, peer):
    copy = pltpu.make_async_remote_copy(
        src_ref=src,
        dst_ref=dst,
        send_sem=send_sem,
        recv_sem=recv_sem,
        device_id=peer,
        device_id_type=MESH,
    )
    copy.start()
    return copy


COLUMN = [(0, 1), (0, 2), (0, 3), (1, 0), (1, 1), (1, 2), (1, 3)]
ALONG_Z = [(0, 1), (0, 2), (0, 3)]


class Lanes:
    def __init__(self, send_sem, recv_sem):
        self.send_sem, self.recv_sem, self.used = send_sem, recv_sem, 0

    def send(self, src, dst, peer):
        i = self.used
        self.used += 1
        return send(src, dst, self.send_sem.at[i], self.recv_sem.at[i], peer)


def lanes_scratch(count):
    return [pltpu.SemaphoreType.DMA((count,)), pltpu.SemaphoreType.DMA((count,))]


def chip_peer(axis, step):
    return {axis: lax.rem(lax.axis_index(axis) + step + 4, 4)}


def greet_chips(barrier):
    for axis in ("x", "y"):
        for step in (1, 3):
            pl.semaphore_signal(
                barrier, inc=1, device_id=chip_peer(axis, step), device_id_type=MESH
            )
    return 4


def greet_column(barrier):
    for step in COLUMN:
        pl.semaphore_signal(barrier, inc=1, device_id=column_peer(*step), device_id_type=MESH)
    return len(COLUMN)


def partner():
    return {"l": 1 - lax.axis_index("l")}


def cross():
    return {"h": 1 - lax.axis_index("h"), "l": 1 - lax.axis_index("l")}


def other_core():
    return {"c": 1 - lax.axis_index("c")}


class ColumnRing:
    def __init__(self, lanes, rows_ref, out_ref):
        c, h, l = place()
        self.lanes, self.rows, self.out = lanes, rows_ref, out_ref
        half = rows_ref.shape[0] // 2
        self.first, self.second = pl.ds(0, half), pl.ds(half, half)
        self.at = {
            "own": c * 4 + h * 2 + l,
            "partner": c * 4 + h * 2 + 1 - l,
            "cross": c * 4 + (1 - h) * 2 + 1 - l,
            "far": c * 4 + (1 - h) * 2 + l,
        }
        self.shared = {}

    def share(self, which):
        block = self.out.at[self.at[which]]
        self.shared[which] = self.lanes.send(block, block, other_core())

    def start(self):
        here = self.out.at[self.at["own"]]
        self.to_partner = self.lanes.send(self.rows, here, partner())
        self.to_cross = self.lanes.send(self.rows, here, cross())
        self.shared["own"] = self.lanes.send(self.rows, here, other_core())

    def relay(self):
        self.to_partner.wait_recv()
        block = self.out.at[self.at["partner"], self.first]
        self.far_cross = self.lanes.send(block, block, cross())
        self.to_cross.wait_recv()
        block = self.out.at[self.at["cross"], self.second]
        self.far_partner = self.lanes.send(block, block, partner())
        self.share("partner")
        self.share("cross")

    def far(self):
        self.far_cross.wait_recv()
        self.far_partner.wait_recv()
        self.share("far")

    def drain(self):
        for copy in (self.to_partner, self.to_cross, self.far_cross, self.far_partner):
            copy.wait_send()
        for copy in self.shared.values():
            copy.wait_send()

    def finish(self):
        self.far()
        for copy in self.shared.values():
            copy.wait_recv()
        self.drain()


class ChipRing:
    def __init__(self, lanes, w_out, block, low, rows, a, b):
        self.lanes, self.w_out, self.block = lanes, w_out, block
        self.rows, self.a, self.b = pl.ds(low, rows), a, b
        self.c = lax.axis_index("c")
        self.split = 1024
        self.sent, self.near = [], []

    def ref(self, da, db, columns=None):
        steps = {self.a: da, self.b: db}
        x = lax.rem(lax.axis_index("x") + steps["x"] + 4, 4)
        y = lax.rem(lax.axis_index("y") + steps["y"] + 4, 4)
        if columns is None:
            return self.w_out.at[self.c, x * 4 + y, self.rows]
        return self.w_out.at[self.c, x * 4 + y, self.rows, columns]

    def copy(self, src, dst, axis, step):
        made = self.lanes.send(src, dst, chip_peer(axis, step))
        self.sent.append(made)
        return made

    def share(self, da, db):
        block = self.ref(da, db)
        self.near.append(self.lanes.send(block, block, column_peer(1, 0)))

    def start(self):
        own = self.block.at[self.rows]
        here = self.ref(0, 0)
        self.first = [self.copy(own, here, self.a, step) for step in (1, -1)]
        self.turn = {0: [self.copy(own, here, self.b, step) for step in (1, -1)]}
        self.near.append(self.lanes.send(own, here, column_peer(1, 0)))

    def pass_on(self, da):
        block = self.ref(da, 0)
        self.turn[da] = [self.copy(block, block, self.b, step) for step in (1, -1)]
        self.share(da, 0)

    def relay_first(self):
        width = self.w_out.shape[3]
        low, high = pl.ds(0, self.split), pl.ds(self.split, width - self.split)
        for copy in self.first:
            copy.wait_recv()
        block = self.ref(-1, 0, low)
        one = self.copy(block, block, self.a, 1)
        block = self.ref(1, 0, high)
        self.second = [one, self.copy(block, block, self.a, -1)]
        self.pass_on(-1)
        self.pass_on(1)

    def relay_turn(self, da):
        for copy in self.turn[da]:
            copy.wait_recv()
        step = 1 if da in (0, -1) else -1
        block = self.ref(da, -step)
        self.last[da] = self.copy(block, block, self.b, step)
        self.share(da, 1)
        self.share(da, -1)

    def relay_second(self):
        for copy in self.second:
            copy.wait_recv()
        self.pass_on(2)

    def finish(self):
        for da in (0, -1, 1, 2):
            self.last[da].wait_recv()
            self.share(da, 2)

    def drain(self):
        for copy in self.sent:
            copy.wait_send()
        for copy in self.near:
            copy.wait()


def weights_kernel(
    part,
    attn_ref,
    expert_ref,
    rows_ref,
    slots_ref,
    w_out,
    expert_out,
    rows_out,
    slots_out,
    attn_in,
    expert_in,
    block,
    s_sem,
    r_sem,
    as_sem,
    ar_sem,
    own,
):
    c, h, l = place()
    me = (c * 2 + h) * 2 + l
    barrier = pltpu.get_barrier_semaphore()
    pl.semaphore_wait(barrier, greet_column(barrier) + greet_chips(barrier))
    lanes = Lanes(s_sem, r_sem)
    slot = c * 2 + h
    here = pltpu.make_async_copy(attn_ref, attn_in.at[slot], own.at[1])
    there = pltpu.make_async_remote_copy(
        src_ref=attn_ref,
        dst_ref=attn_in.at[slot],
        send_sem=as_sem.at[0],
        recv_sem=ar_sem.at[slot],
        device_id=column_peer(1, 0),
        device_id_type=MESH,
    )
    pl.when(c == l)(here.start)
    pl.when(c != l)(there.start)
    for z_step in range(1, 4):
        z = lax.rem(h * 2 + l + z_step, 4)
        send(attn_ref, attn_in.at[slot], as_sem.at[z_step], ar_sem.at[slot], at_z(l, z))
    own_copy = pltpu.make_async_copy(expert_ref.at[me], expert_in.at[me], own.at[0])
    own_copy.start()
    pieces = []
    for step in COLUMN:
        peer = column_peer(*step)
        to = (peer["c"] * 2 + peer["h"]) * 2 + peer["l"]
        pieces.append(lanes.send(expert_ref.at[to], expert_in.at[me], peer))
        pieces.append(lanes.send(slots_ref.at[to], slots_out.at[me], peer))
    own_rows = pltpu.make_async_copy(rows_ref, rows_out.at[me], own.at[2])
    own_rows.start()
    own_slots = pltpu.make_async_copy(slots_ref.at[me], slots_out.at[me], own.at[4])
    own_slots.start()
    ring = ColumnRing(lanes, rows_ref, rows_out)
    ring.start()

    for source in range(4):
        mine = (c == l) & (slot == source)

        def landed(source=source):
            pltpu.make_async_remote_copy(
                src_ref=attn_ref,
                dst_ref=attn_in.at[source],
                send_sem=as_sem.at[0],
                recv_sem=ar_sem.at[source],
                device_id=column_peer(1, 0),
                device_id_type=MESH,
            ).wait_recv()

        pl.when(jnp.logical_not(mine))(landed)
    pl.when(c == l)(here.wait)
    block[...] = jnp.concatenate(
        [attn_in[i].astype(f32)[:part] for i in range(4)], axis=0
    ).astype(block.dtype)
    x, y = lax.axis_index("x"), lax.axis_index("y")
    keep = pltpu.make_async_copy(block, w_out.at[c, x * 4 + y], own.at[3])
    keep.start()
    half = block.shape[0] // 2
    halves = [
        ChipRing(lanes, w_out, block, 0, half, "x", "y"),
        ChipRing(lanes, w_out, block, half, half, "y", "x"),
    ]
    for ring_half in halves:
        ring_half.last = {}
        ring_half.start()

    own_copy.wait()
    for copy in pieces:
        copy.wait()
    for i in range(3):
        for l_side in range(2):
            expert_out[i, :, l_side * 384 : (l_side + 1) * 384] = jnp.concatenate(
                [expert_in[2 * j + l_side, i].astype(f32)[:part] for j in range(4)], axis=0
            ).astype(expert_out.dtype)

    for ring_half in halves:
        ring_half.relay_first()
    for ring_half in halves:
        ring_half.relay_turn(0)
    for ring_half in halves:
        ring_half.relay_second()
    ring.relay()
    for da in (-1, 1, 2):
        for ring_half in halves:
            ring_half.relay_turn(da)
    ring.finish()
    for ring_half in halves:
        ring_half.finish()
    for ring_half in halves:
        ring_half.drain()
    keep.wait()
    own_rows.wait()
    own_slots.wait()
    pl.when(c != l)(there.wait_send)
    for z_step in range(1, 4):
        pltpu.make_async_remote_copy(
            src_ref=attn_ref,
            dst_ref=attn_in.at[slot],
            send_sem=as_sem.at[z_step],
            recv_sem=ar_sem.at[slot],
            device_id=column_peer(0, z_step),
            device_id_type=MESH,
        ).wait_send()


def gather_weights(attn_block, expert_pieces, rows, slots, part):
    width = attn_block.shape[1]
    ff_half = expert_pieces.shape[3]
    return pl.pallas_call(
        functools.partial(weights_kernel, part),
        name="gather_weights",
        out_shape=(
            jax.ShapeDtypeStruct((2, 16, 4 * part, width), bf16),
            jax.ShapeDtypeStruct((3, 4 * part, 2 * ff_half), bf16),
            jax.ShapeDtypeStruct((8,) + rows.shape, bf16),
            jax.ShapeDtypeStruct(slots.shape, f32),
        ),
        in_specs=[VMEM, ANY, ANY, ANY],
        out_specs=(ANY, VMEM, ANY, ANY),
        scratch_shapes=[
            pltpu.VMEM((4,) + attn_block.shape, bf16),
            pltpu.VMEM(expert_pieces.shape, bf16),
            pltpu.VMEM((4 * part, width), bf16),
        ]
        + lanes_scratch(100)
        + [
            pltpu.SemaphoreType.DMA((4,)),
            pltpu.SemaphoreType.DMA((4,)),
            pltpu.SemaphoreType.DMA((5,)),
        ],
        compiler_params=pltpu.CompilerParams(
            collective_id=1, has_side_effects=True, vmem_limit_bytes=32 * 2**20
        ),
    )(attn_block, expert_pieces, rows, slots)


def along_z_kernel(block_ref, out_ref, s_sem, r_sem, own):
    c, h, l = place()
    z = h * 2 + l
    greet(ALONG_Z)
    own_copy = pltpu.make_async_copy(block_ref, out_ref.at[z], own)
    own_copy.start()
    copies = [
        send(block_ref, out_ref.at[z], s_sem.at[i], r_sem.at[i], column_peer(*step))
        for i, step in enumerate(ALONG_Z)
    ]
    own_copy.wait()
    for copy in copies:
        copy.wait()


def gather_along_z(block):
    return pl.pallas_call(
        along_z_kernel,
        name="gather_keys_values",
        out_shape=jax.ShapeDtypeStruct((4,) + block.shape, block.dtype),
        in_specs=[VMEM],
        out_specs=VMEM,
        scratch_shapes=[
            pltpu.SemaphoreType.DMA((3,)),
            pltpu.SemaphoreType.DMA((3,)),
            pltpu.SemaphoreType.DMA(()),
        ],
        compiler_params=pltpu.CompilerParams(collective_id=2, has_side_effects=True),
    )(block)


def sum_along_z_kernel(parts_ref, out_ref, held, s_sem, r_sem):
    c, h, l = place()
    z = h * 2 + l
    greet(ALONG_Z)
    copies = [
        send(
            parts_ref.at[lax.rem(z + step[1], 4)],
            held.at[i],
            s_sem.at[i],
            r_sem.at[i],
            column_peer(*step),
        )
        for i, step in enumerate(ALONG_Z)
    ]
    for copy in copies:
        copy.wait()
    total = parts_ref[z].astype(f32)
    for i in range(3):
        total = total + held[i].astype(f32)
    out_ref[...] = total


def sum_along_z(parts):
    shape = parts.shape[1:]
    return pl.pallas_call(
        sum_along_z_kernel,
        name="sum_key_value_gradients",
        out_shape=jax.ShapeDtypeStruct(shape, f32),
        in_specs=[VMEM],
        out_specs=VMEM,
        scratch_shapes=[
            pltpu.VMEM((3,) + shape, parts.dtype),
            pltpu.SemaphoreType.DMA((3,)),
            pltpu.SemaphoreType.DMA((3,)),
        ],
        compiler_params=pltpu.CompilerParams(collective_id=3, has_side_effects=True),
    )(parts)


def experts_kernel(
    rows_ref,
    gate_ref,
    grads_ref,
    slot_rows,
    slot_columns,
    weights_ref,
    mix_out,
    weight_grads,
    back_out,
    gate_back_out,
    rows_all,
    held,
    w_gate,
    w_up,
    w_down,
    picked,
    picked_grads,
    hidden_back,
    hidden_gated,
    gate_low,
    up_low,
    mix_stage,
    near,
    far,
    nearest,
    gates_in,
    gate_back,
    s_sem,
    r_sem,
    own,
    stage_sem,
    near_send,
    near_recv,
):
    c, h, l = place()
    me = (c * 2 + h) * 2 + l
    barrier = pltpu.get_barrier_semaphore()
    pl.semaphore_wait(barrier, greet_column(barrier))
    lanes = Lanes(s_sem, r_sem)
    rows, width = rows_ref.shape
    slots = picked.shape[1]
    ff = w_gate.shape[1]
    block = 2 * rows

    ring = ColumnRing(lanes, rows_ref, rows_all)
    ring.start()
    local = [
        pltpu.make_async_copy(grads_ref, held, own.at[0]),
        pltpu.make_async_copy(weights_ref.at[2], w_down, own.at[1]),
        pltpu.make_async_copy(weights_ref.at[0], w_gate, own.at[2]),
        pltpu.make_async_copy(weights_ref.at[1], w_up, own.at[3]),
        pltpu.make_async_copy(rows_ref, rows_all.at[me], own.at[4]),
        pltpu.make_async_copy(gate_ref.at[me], gates_in.at[me], own.at[5]),
    ]
    for copy in local:
        copy.start()
    gate_copies = []
    for step in COLUMN:
        peer = column_peer(*step)
        to = (peer["c"] * 2 + peer["h"]) * 2 + peer["l"]
        gate_copies.append(lanes.send(gate_ref.at[to], gates_in.at[me], peer))

    def pick_of(k):
        number = lax.broadcasted_iota(jnp.int32, (slots, block), 0).astype(f32)
        return slot_rows[k] == number

    def spread_of(k):
        number = lax.broadcasted_iota(jnp.int32, (block, slots), 1).astype(f32)
        return (slot_columns[k] == number).astype(f32).astype(bf16)

    def low(mask):
        return mask.astype(f32).astype(bf16)

    def both(ref, k, columns=None):
        if columns is None:
            return ref[pl.ds(2 * k, 2)].reshape(block, width)
        return ref[pl.ds(2 * k, 2), :, columns].reshape(block, -1)

    wide = 512
    narrow = 256

    def at(i, size):
        return pl.ds(pl.multiple_of(i * size, size), size)

    local[0].wait()
    local[1].wait()

    def prepare(k, carry):
        pick = low(pick_of(k))

        def gather(i, carry):
            columns = at(i, wide)
            values = ref_dot(pick, held[pl.ds(2 * k, 2), :, columns].reshape(block, wide))
            picked_grads[k, :, columns] = values.astype(bf16)
            return carry

        lax.fori_loop(0, width // wide, gather, 0)

        def down(i, carry):
            columns = at(i, narrow)
            hidden_back[k, :, columns] = ref_dot(picked_grads[k], w_down[:, columns])
            return carry

        lax.fori_loop(0, ff // narrow, down, 0)
        return carry

    lax.fori_loop(0, 4, prepare, 0)
    ring.relay()
    for copy in local[2:]:
        copy.wait()
    for copy in gate_copies:
        copy.wait()
    ring.shared["own"].wait_recv()
    ring.shared["partner"].wait_recv()

    def expert(k, stage):
        pick = pick_of(k)
        pick_low = low(pick)
        spread = spread_of(k)
        gates = gates_in[pl.ds(2 * k, 2)]
        gate_row = jnp.concatenate([gates[0], gates[1]], axis=1)
        gate = jnp.sum(jnp.where(pick, gate_row, 0.0), axis=1, keepdims=True)

        def gather(i, carry):
            columns = at(i, wide)
            values = ref_dot(pick_low, rows_all[pl.ds(2 * k, 2), :, columns].reshape(block, wide))
            picked[k, :, columns] = values.astype(bf16)
            return carry

        lax.fori_loop(0, width // wide, gather, 0)

        def hide(i, total):
            columns = at(i, narrow)
            gate_act = ref_dot(picked[k], w_gate[:, columns])
            up_act = ref_dot(picked[k], w_up[:, columns])
            back = hidden_back[k, :, columns]
            sigmoid_act = 1.0 / (1.0 + jnp.exp(-gate_act))
            silu_act = gate_act * sigmoid_act
            hidden = silu_act * up_act
            hidden_gated[k, :, columns] = (hidden * gate).astype(bf16)
            total = total + jnp.sum(hidden * back, axis=1, keepdims=True)
            back = back * gate
            slope = sigmoid_act * (1.0 + gate_act * (1.0 - sigmoid_act))
            gate_low[k, :, columns] = (back * up_act * slope).astype(bf16)
            up_low[k, :, columns] = (back * silu_act).astype(bf16)
            return total

        gate_slots = lax.fori_loop(0, ff // narrow, hide, jnp.zeros((slots, 1), f32))
        back_row = jnp.sum(jnp.where(pick, gate_slots, 0.0), axis=0, keepdims=True)
        gate_back[2 * k] = back_row[:, :rows]
        gate_back[2 * k + 1] = back_row[:, rows:]

        def leave(i, carry):
            columns = at(i, wide)
            out = ref_dot_nt(hidden_gated[k], w_down[columns, :]).astype(bf16)
            mix_stage[stage, :, :, columns] = (
                ref_dot(spread, out).astype(bf16).reshape(2, rows, wide)
            )
            back = ref_dot_nt(gate_low[k], w_gate[columns, :])
            back = (back + ref_dot_nt(up_low[k], w_up[columns, :])).astype(bf16)
            held[pl.ds(2 * k, 2), :, columns] = (
                ref_dot(spread, back).astype(bf16).reshape(2, rows, wide)
            )
            return carry

        lax.fori_loop(0, width // wide, leave, 0)

    def stage_copy(k, stage):
        return pltpu.make_async_copy(
            mix_stage.at[stage], mix_out.at[pl.ds(2 * k, 2)], stage_sem.at[stage]
        )

    def near_copy(side, i):
        return pltpu.make_async_remote_copy(
            src_ref=held.at[pl.ds(((1 - c) * 2 + side) * 2, 2)],
            dst_ref=near.at[pl.ds(side * 2, 2)],
            send_sem=near_send.at[i],
            recv_sem=near_recv.at[i],
            device_id=other_core(),
            device_id_type=MESH,
        )

    expert((1 - c) * 2 + h, 0)
    near_copy(h, 0).start()
    stage_copy((1 - c) * 2 + h, 0).start()
    ring.far()
    expert(c * 2 + h, 1)
    stage_copy(c * 2 + h, 1).start()

    def add_near(z):
        mine = held.at[c * 4 + z]

        def add(i, carry):
            here = at(i, 64)
            mine[here] = mine[here] + near[z, here]
            return carry

        lax.fori_loop(0, rows // 64, add, 0)

    half = rows // 2
    first, second = pl.ds(0, half), pl.ds(half, half)
    z = {
        "own": h * 2 + l,
        "partner": h * 2 + 1 - l,
        "cross": (1 - h) * 2 + 1 - l,
        "far": (1 - h) * 2 + l,
    }

    def block_at(which, part):
        return held.at[c * 4 + z[which], part]

    near_copy(h, 0).wait_recv()
    add_near(z["partner"])
    sends = []
    early_partner = lanes.send(
        block_at("partner", first), nearest.at[0, first], partner()
    )
    add_near(z["own"])
    ring.shared["cross"].wait_recv()
    ring.shared["far"].wait_recv()

    for stage, k in ((0, (1 - c) * 2 + 1 - h), (1, c * 2 + 1 - h)):
        stage_copy(k, stage).wait()
        expert(k, stage)
        stage_copy(k, stage).start()
        if stage == 0:
            near_copy(1 - h, 1).start()
    gate_own = pltpu.make_async_copy(gate_back.at[me], gate_back_out.at[me], own.at[6])
    gate_own.start()
    for step in COLUMN:
        peer = column_peer(*step)
        to = (peer["c"] * 2 + peer["h"]) * 2 + peer["l"]
        sends.append(lanes.send(gate_back.at[to], gate_back_out.at[me], peer))
    near_copy(1 - h, 1).wait_recv()
    add_near(z["far"])
    far_partner = lanes.send(block_at("far", first), far.at[0], partner())
    far_cross = lanes.send(block_at("far", second), far.at[1], cross())
    add_near(z["cross"])
    early_cross = lanes.send(block_at("cross", second), nearest.at[1, second], cross())

    def weight_grad(values, others, target, number):
        def rows_of(i, carry):
            columns = at(i, narrow)
            left = values[:, :, columns].reshape(4 * slots, narrow)
            target[columns, :] = ref_dot_tn(left, others[...].reshape(4 * slots, ff)).astype(bf16)
            return carry

        lax.fori_loop(0, width // narrow, rows_of, 0)
        copy = pltpu.make_async_copy(target, weight_grads.at[number], own.at[1 + number])
        copy.start()
        return copy

    grad_copies = [weight_grad(picked_grads, hidden_gated, w_down, 2)]
    far_partner.wait_recv()
    mine = block_at("cross", first)
    mine[...] = mine[...] + far[0]
    late_cross = lanes.send(mine, nearest.at[1, first], cross())
    far_cross.wait_recv()
    mine = block_at("partner", second)
    mine[...] = mine[...] + far[1]
    late_partner = lanes.send(mine, nearest.at[0, second], partner())
    grad_copies.append(weight_grad(picked, gate_low, w_gate, 0))
    grad_copies.append(weight_grad(picked, up_low, w_up, 1))
    for copy in (early_partner, early_cross, late_cross, late_partner):
        copy.wait_recv()

    def finish(i, carry):
        here = at(i, 64)
        total = held[c * 4 + z["own"], here].astype(f32)
        back_out[here, :] = (
            total + nearest[0, here].astype(f32) + nearest[1, here].astype(f32)
        )
        return carry

    lax.fori_loop(0, rows // 64, finish, 0)
    for copy in (early_partner, early_cross, late_cross, late_partner, far_partner, far_cross):
        copy.wait_send()
    for i, side in ((0, h), (1, 1 - h)):
        near_copy(side, i).wait_send()
    for copy in sends + grad_copies + [gate_own]:
        copy.wait()
    for stage, k in ((0, (1 - c) * 2 + 1 - h), (1, c * 2 + 1 - h)):
        stage_copy(k, stage).wait()
    ring.drain()


def ref_dot(a, b):
    return jnp.dot(a, b, preferred_element_type=f32)


def ref_dot_nt(a, b):
    return lax.dot_general(a, b, (((1,), (1,)), ((), ())), preferred_element_type=f32)


def ref_dot_tn(a, b):
    return lax.dot_general(a, b, (((0,), (0,)), ((), ())), preferred_element_type=f32)


def experts_of_column(rows, gates, grads_all, slots, weights):
    count, width = rows.shape
    ff = weights.shape[2]
    return pl.pallas_call(
        experts_kernel,
        name="experts",
        out_shape=(
            jax.ShapeDtypeStruct((8, count, width), bf16),
            jax.ShapeDtypeStruct(weights.shape, bf16),
            jax.ShapeDtypeStruct((count, width), f32),
            jax.ShapeDtypeStruct(gates.shape, f32),
        ),
        in_specs=[VMEM, VMEM, ANY, VMEM, VMEM, ANY],
        out_specs=(ANY, ANY, VMEM, VMEM),
        scratch_shapes=[
            pltpu.VMEM((8, count, width), bf16),
            pltpu.VMEM((8, count, width), bf16),
            pltpu.VMEM((width, ff), bf16),
            pltpu.VMEM((width, ff), bf16),
            pltpu.VMEM((width, ff), bf16),
            pltpu.VMEM((4, SLOTS, width), bf16),
            pltpu.VMEM((4, SLOTS, width), bf16),
            pltpu.VMEM((4, SLOTS, ff), f32),
            pltpu.VMEM((4, SLOTS, ff), bf16),
            pltpu.VMEM((4, SLOTS, ff), bf16),
            pltpu.VMEM((4, SLOTS, ff), bf16),
            pltpu.VMEM((2, 2, count, width), bf16),
            pltpu.VMEM((4, count, width), bf16),
            pltpu.VMEM((2, count // 2, width), bf16),
            pltpu.VMEM((2, count, width), bf16),
            pltpu.VMEM(gates.shape, f32),
            pltpu.VMEM(gates.shape, f32),
        ]
        + lanes_scratch(32)
        + [
            pltpu.SemaphoreType.DMA((7,)),
            pltpu.SemaphoreType.DMA((2,)),
            pltpu.SemaphoreType.DMA((2,)),
            pltpu.SemaphoreType.DMA((2,)),
        ],
        compiler_params=pltpu.CompilerParams(
            collective_id=4, has_side_effects=True, vmem_limit_bytes=60 * 2**20
        ),
    )(rows, gates, grads_all, slots[:, None, :], slots[:, :, None], weights)


def column_sum_kernel(
    parts_ref, small_ref, out_ref, small_out, near, chip, far, cs, cr, zs, zr, ss, sr, own
):
    c, h, l = place()
    z = h * 2 + l
    me = c * 4 + z
    greet(COLUMN)
    other = column_peer(1, 0)
    order = [2, 1, 3, 0]
    near_copies = [
        send(
            parts_ref.at[(1 - c) * 4 + lax.rem(z + step, 4)],
            near.at[i],
            cs.at[i],
            cr.at[i],
            other,
        )
        for i, step in enumerate(order)
    ]
    own_copy = pltpu.make_async_copy(small_ref.at[me], small_out.at[me], own)
    own_copy.start()
    small_copies = []
    for i, step in enumerate(COLUMN):
        peer = column_peer(*step)
        to = (peer["c"] * 2 + peer["h"]) * 2 + peer["l"]
        small_copies.append(send(small_ref.at[to], small_out.at[me], ss.at[i], sr.at[i], peer))
    rows = parts_ref.shape[1]
    chunk = 32
    far_copies = []
    for i, step in enumerate(order):
        near_copies[i].wait_recv()
        mine = c * 4 + lax.rem(z + step, 4)

        def add(k, carry, i=i, mine=mine, step=step):
            here = pl.ds(pl.multiple_of(k * chunk, chunk), chunk)
            total = parts_ref[mine, here, :].astype(f32) + near[i, here, :].astype(f32)
            if step == 0:
                out_ref[here, :] = total
            else:
                chip[i, here, :] = total.astype(chip.dtype)
            return carry

        lax.fori_loop(0, rows // chunk, add, 0)
        if step:
            far_copies.append(
                send(chip.at[i], far.at[i], zs.at[i], zr.at[i], column_peer(0, step))
            )
    for copy in far_copies:
        copy.wait()

    def finish(k, carry):
        here = pl.ds(pl.multiple_of(k * chunk, chunk), chunk)
        total = out_ref[here, :]
        for i in range(3):
            total = total + far[i, here, :].astype(f32)
        out_ref[here, :] = total
        return carry

    lax.fori_loop(0, rows // chunk, finish, 0)
    for copy in near_copies:
        copy.wait_send()
    own_copy.wait()
    for copy in small_copies:
        copy.wait()


def column_sum(parts, small, number):
    rows, width = parts.shape[1:]
    return pl.pallas_call(
        column_sum_kernel,
        name="sum_over_experts",
        out_shape=(
            jax.ShapeDtypeStruct((rows, width), f32),
            jax.ShapeDtypeStruct(small.shape, small.dtype),
        ),
        in_specs=[VMEM, VMEM],
        out_specs=(VMEM, VMEM),
        scratch_shapes=[
            pltpu.VMEM((4, rows, width), parts.dtype),
            pltpu.VMEM((3, rows, width), parts.dtype),
            pltpu.VMEM((3, rows, width), parts.dtype),
            pltpu.SemaphoreType.DMA((4,)),
            pltpu.SemaphoreType.DMA((4,)),
            pltpu.SemaphoreType.DMA((3,)),
            pltpu.SemaphoreType.DMA((3,)),
            pltpu.SemaphoreType.DMA((7,)),
            pltpu.SemaphoreType.DMA((7,)),
            pltpu.SemaphoreType.DMA(()),
        ],
        compiler_params=pltpu.CompilerParams(
            collective_id=number, has_side_effects=True, vmem_limit_bytes=40 * 2**20
        ),
    )(parts, small)


class ChipSum:
    def __init__(self, lanes, chip, low, rows, p, q, near_p, rest_p, near_q):
        self.lanes, self.chip = lanes, chip
        self.rows, self.p, self.q = pl.ds(low, rows), p, q
        self.near_p, self.rest_p, self.near_q = near_p, rest_p, near_q
        self.sent = []

    def index(self, dp, dq):
        steps = {self.p: dp, self.q: dq}
        x = lax.rem(lax.axis_index("x") + steps["x"] + 4, 4)
        y = lax.rem(lax.axis_index("y") + steps["y"] + 4, 4)
        return x * 4 + y

    def copy(self, src, dst, axis, step):
        made = self.lanes.send(src, dst, chip_peer(axis, step))
        self.sent.append(made)
        return made

    def own(self, dp, dq):
        return self.chip.at[self.index(dp, dq), self.rows]

    def far(self):
        self.far_copies = {}
        for dq, step, i in ((2, 1, 0), (3, -1, 0), (1, 1, 1), (0, -1, 1)):
            direction = 0 if step == 1 else 1
            self.far_copies[direction, i] = self.copy(
                self.own(2, dq), self.near_p.at[direction, i], self.p, step
            )

    def plain(self):
        self.next_copies = {}
        for dq, step in ((2, -1), (3, 1), (1, -1), (0, 1)):
            self.next_to(dq, step)

    def next_to(self, dq, step):
        direction = 0 if step == 1 else 1
        self.next_copies[direction, dq] = self.copy(
            self.own(step, dq), self.rest_p.at[direction, dq], self.p, step
        )

    def joined(self):
        for dq, step, i in ((2, 1, 0), (3, -1, 0), (1, 1, 1), (0, -1, 1)):
            direction = 0 if step == 1 else 1
            self.far_copies[direction, i].wait_recv()
            mine = self.own(step, dq)
            mine[...] = mine[...] + self.near_p[direction, i]
            self.next_to(dq, step)

    def collect(self, dq):
        for direction in range(2):
            self.next_copies[direction, dq].wait_recv()
        mine = self.own(0, dq)
        total = mine[...].astype(f32)
        for direction in range(2):
            total = total + self.rest_p[direction, dq].astype(f32)
        mine[...] = total.astype(mine.dtype)

    def far_q(self):
        width = self.chip.shape[2]
        self.low, self.high = pl.ds(0, 1024), pl.ds(1024, width - 1024)
        self.collect(2)
        block = self.index(0, 2)
        self.far_q_copies = [
            self.copy(
                self.chip.at[block, self.rows, self.low], self.near_q.at[0, :, self.low], self.q, 1
            ),
            self.copy(
                self.chip.at[block, self.rows, self.high], self.near_q.at[1, :, self.high], self.q, -1
            ),
        ]

    def next_q(self):
        self.next_q_copies = []
        for i, (dq, columns) in enumerate(((1, self.low), (3, self.high))):
            self.collect(dq)
            self.far_q_copies[i].wait_recv()
            block = self.index(0, dq)
            self.chip[block, self.rows, columns] = (
                self.chip[block, self.rows, columns] + self.near_q[i, :, columns]
            )
            self.next_q_copies.append(
                self.copy(
                    self.chip.at[block, self.rows],
                    self.near_q.at[2 + i],
                    self.q,
                    1 if i == 0 else -1,
                )
            )

    def total(self):
        self.collect(0)
        total = self.chip[self.index(0, 0), self.rows, :].astype(f32)
        for i in range(2):
            self.next_q_copies[i].wait_recv()
            total = total + self.near_q[2 + i].astype(f32)
        return total

    def drain(self):
        for copy in self.sent:
            copy.wait_send()


def return_kernel(
    part,
    misc_at,
    in_ref,
    out_ref,
    expert_ref,
    grads_out,
    misc_out,
    expert_out,
    near,
    near_p0,
    rest_p0,
    near_q0,
    near_p1,
    rest_p1,
    near_q1,
    pieces,
    landed,
    misc_landed,
    s_sem,
    r_sem,
    ps,
    pr,
    ms,
    mr,
    own,
):
    c, h, l = place()
    z = h * 2 + l
    me = c * 4 + z
    barrier = pltpu.get_barrier_semaphore()
    pl.semaphore_wait(barrier, greet_column(barrier) + greet_chips(barrier))
    lanes = Lanes(s_sem, r_sem)
    in_width = in_ref.shape[3]
    width = near.shape[2]
    half = near.shape[1] // 2
    other = column_peer(1, 0)
    x, y = lax.axis_index("x"), lax.axis_index("y")
    sums = [
        ChipSum(lanes, near, 0, half, "y", "x", near_p0, rest_p0, near_q0),
        ChipSum(lanes, near, half, half, "x", "y", near_p1, rest_p1, near_q1),
    ]
    order = [2, 1, 3, 0]
    arrive = {}
    for step in order:
        for which in range(2):
            for dq in range(4):
                block = sums[which].index(step, dq)
                rows = pl.ds(which * half, half)
                arrive[step, which, dq] = [
                    lanes.send(
                        in_ref.at[1 - c, block, rows],
                        near.at[block, rows, pl.ds(0, in_width)],
                        other,
                    ),
                    lanes.send(
                        out_ref.at[1 - c, block, rows],
                        near.at[block, rows, pl.ds(in_width, width - in_width)],
                        other,
                    ),
                ]
    own_copy = pltpu.make_async_copy(expert_ref.at[me], expert_out.at[me], own.at[0])
    own_copy.start()
    expert_copies = []
    for step in COLUMN:
        peer = column_peer(*step)
        to = (peer["c"] * 2 + peer["h"]) * 2 + peer["l"]
        expert_copies.append(lanes.send(expert_ref.at[to], expert_out.at[me], peer))

    def add_own(step, which):
        for dq in range(4):
            for copy in arrive[step, which, dq]:
                copy.wait_recv()
            block = sums[which].index(step, dq)
            rows = pl.ds(which * half, half)
            near[block, rows, pl.ds(0, in_width)] = (
                near[block, rows, pl.ds(0, in_width)] + in_ref[c, block, rows, :]
            )
            near[block, rows, pl.ds(in_width, width - in_width)] = (
                near[block, rows, pl.ds(in_width, width - in_width)] + out_ref[c, block, rows, :]
            )

    for which in range(2):
        add_own(2, which)
        sums[which].far()
    for step in (1, 3):
        for which in range(2):
            add_own(step, which)
    for each in sums:
        each.plain()
    for each in sums:
        each.joined()
    for which in range(2):
        add_own(0, which)
    for each in sums:
        each.far_q()
    for each in sums:
        each.next_q()
    for which in range(2):
        total = sums[which].total()
        for i in range(2):
            pieces[2 * which + i] = total[i * part : (i + 1) * part]

    def to_owner(target, owner, src, dst, send_sem, recv_sem, asked):
        is_me = (owner["c"] == c) & (owner["h"] == h) & (owner["l"] == l)
        there = pltpu.make_async_remote_copy(
            src_ref=src,
            dst_ref=dst,
            send_sem=send_sem,
            recv_sem=recv_sem,
            device_id=owner,
            device_id_type=MESH,
        )
        here = pltpu.make_async_copy(src, dst, recv_sem)
        pl.when(asked & jnp.logical_not(is_me))(there.start)
        pl.when(asked & is_me)(here.start)
        return asked & jnp.logical_not(is_me), there

    sent = []
    everyone = c < 2
    for target in range(4):
        owner = {"c": target // 2, "h": target % 2, "l": c}
        sent.append(
            to_owner(
                target, owner, pieces.at[target], landed.at[z], ps.at[target], pr.at[z], everyone
            )
        )
    misc = pl.ds(misc_at, MISC)
    for target in range(4):
        owner = {"c": target // 2, "h": target % 2, "l": 1}
        sent.append(
            to_owner(
                target,
                owner,
                pieces.at[target, :, misc],
                misc_landed.at[z],
                ms.at[target],
                mr.at[z],
                c == 0,
            )
        )
    for source in range(4):
        pltpu.make_async_copy(pieces.at[0], landed.at[source], pr.at[source]).wait()
    grads_out[...] = (landed[0] + landed[1]) + (landed[2] + landed[3])

    def from_core():
        for source in range(4):
            pltpu.make_async_copy(
                pieces.at[0, :, misc], misc_landed.at[source], mr.at[source]
            ).wait()
        misc_out[...] = (misc_landed[0] + misc_landed[1]) + (misc_landed[2] + misc_landed[3])

    def from_piece():
        misc_out[...] = (landed[0, :, misc] + landed[1, :, misc]) + (
            landed[2, :, misc] + landed[3, :, misc]
        )

    pl.when(l == 1)(from_core)
    pl.when(l == 0)(from_piece)
    for asked, there in sent:
        pl.when(asked)(there.wait_send)
    for copies in arrive.values():
        for copy in copies:
            copy.wait_send()
    for each in sums:
        each.drain()
    own_copy.wait()
    for copy in expert_copies:
        copy.wait()


def return_gradients(grad_in, grad_out, expert_pieces, part, misc_at):
    in_width, out_width = grad_in.shape[3], grad_out.shape[3]
    width, rows = in_width + out_width, grad_in.shape[2]
    half = rows // 2
    ring = [
        pltpu.VMEM((2, 2, half, width), bf16),
        pltpu.VMEM((2, 4, half, width), bf16),
        pltpu.VMEM((4, half, width), bf16),
    ]
    return pl.pallas_call(
        functools.partial(return_kernel, part, misc_at),
        name="return_gradients",
        out_shape=(
            jax.ShapeDtypeStruct((part, width), f32),
            jax.ShapeDtypeStruct((part, MISC), f32),
            jax.ShapeDtypeStruct(expert_pieces.shape, expert_pieces.dtype),
        ),
        in_specs=[VMEM, VMEM, ANY],
        out_specs=(VMEM, VMEM, ANY),
        scratch_shapes=[pltpu.VMEM((16, rows, width), bf16)]
        + ring
        + ring
        + [
            pltpu.VMEM((4, part, width), f32),
            pltpu.VMEM((4, part, width), f32),
            pltpu.VMEM((4, part, MISC), f32),
        ]
        + lanes_scratch(130)
        + [
            pltpu.SemaphoreType.DMA((4,)),
            pltpu.SemaphoreType.DMA((4,)),
            pltpu.SemaphoreType.DMA((4,)),
            pltpu.SemaphoreType.DMA((4,)),
            pltpu.SemaphoreType.DMA((1,)),
        ],
        compiler_params=pltpu.CompilerParams(
            collective_id=7, has_side_effects=True, vmem_limit_bytes=48 * 2**20
        ),
    )(grad_in, grad_out, expert_pieces)


def dot(a, b):
    return jnp.dot(a, b, preferred_element_type=f32)


def dot_nt(a, b):
    return lax.dot_general(a, b, (((1,), (1,)), ((), ())), preferred_element_type=f32)


def dot_tn(a, b):
    return lax.dot_general(a, b, (((0,), (0,)), ((), ())), preferred_element_type=f32)


def exchange_halves(own, l):
    other = lax.ppermute(own, "l", [(0, 1), (1, 0)])
    first = jnp.where(l == 0, own, other)
    second = jnp.where(l == 0, other, own)
    return jnp.concatenate([first, second], axis=0)


def body(
    tokens,
    segments,
    routes,
    attn_gain,
    w_query,
    key_matrix,
    value_matrix,
    w_output,
    mix_gain,
    w_router,
    w_gate,
    w_up,
    w_down,
    block_cotangent,
):
    c, h, l = place()
    model_width = tokens.shape[2]
    rows = tokens.shape[1] // 2
    seq_length = segments.shape[1]
    experts, part, ff_half = w_gate.shape
    q_half = w_query.shape[1]
    score_scale = HEAD_SIZE ** (-0.5)

    misc = jnp.concatenate([attn_gain[:, None], mix_gain[:, None], w_router], axis=1)
    misc = jnp.pad(misc, ((0, 0), (0, MISC - misc.shape[1])))
    attn_block = jnp.concatenate(
        [w_query, key_matrix, value_matrix, misc, w_output.T], axis=1
    )
    attn_block = jnp.pad(attn_block, ((0, PAD - part), (0, 0)))
    expert_pieces = jnp.pad(
        jnp.stack([w_gate, w_up, w_down], axis=1), ((0, 0), (0, 0), (0, PAD - part), (0, 0))
    )
    upstream_low = lax.dynamic_slice_in_dim(block_cotangent[0], l * rows, rows)
    hot_all = routes[0][:, :, None] == jnp.arange(experts, dtype=jnp.int32)[None, None, :]
    named = jnp.any(hot_all, axis=1)
    slot_of = jnp.cumsum(named.astype(jnp.int32), axis=0) - 1
    slot_of = jnp.where(named, slot_of, -1).astype(f32).T
    slot_of = lax.dynamic_slice_in_dim(slot_of, l * rows, rows, axis=1)[:, None, :]
    w_attn, expert_col, grads_all, slots = gather_weights(
        attn_block, expert_pieces, upstream_low, slot_of, part
    )
    kv_width = key_matrix.shape[1]
    in_width = q_half + 2 * kv_width + MISC
    w_attn = w_attn.reshape(2, model_width, attn_block.shape[1])
    w_out = w_attn[:, :, in_width:]
    expert_full = lax.all_gather(expert_col, ("x", "y"), axis=1, tiled=True)
    qkv_w = w_attn[:, :, : q_half + 2 * kv_width]
    misc_full = w_attn[0, :, q_half + 2 * kv_width : in_width]
    attn_scale = misc_full[:, 0].astype(f32)
    mix_scale = misc_full[:, 1].astype(f32)
    router_w = misc_full[:, 2 : 2 + experts]

    first = l * rows
    inputs = lax.dynamic_slice_in_dim(tokens[0], first, rows).astype(f32)
    upstream = upstream_low.astype(f32)
    route_rows = lax.dynamic_slice_in_dim(routes[0], first, rows)
    z = h * 2 + l
    positions = z * rows + jnp.arange(rows, dtype=jnp.int32)
    key_positions = jnp.arange(seq_length, dtype=jnp.int32)
    seg_all = segments[0]
    seg_local = lax.dynamic_slice_in_dim(seg_all, z * rows, rows)
    allowed = (seg_local[:, None] == seg_all[None, :]) & (
        positions[:, None] >= key_positions[None, :]
    )
    cosine_table, sine_table = rope_tables(positions)

    inv_attn = lax.rsqrt(jnp.mean(inputs * inputs, axis=1, keepdims=True) + EPS)
    scaled_in = inputs * inv_attn
    normalized_input = (scaled_in * attn_scale).astype(bf16)
    halves = [dot(normalized_input, qkv_w[i]) for i in range(2)]
    q_heads = [
        rotary_embed(p[:, :q_half].reshape(rows, GROUP, HEAD_SIZE), cosine_table, sine_table)
        .astype(bf16)
        .transpose(1, 0, 2)
        for p in halves
    ]
    k_own = [
        rotary_embed(
            p[:, None, q_half : q_half + kv_width], cosine_table, sine_table
        ).astype(bf16)[:, 0]
        for p in halves
    ]
    v_own = [p[:, q_half + kv_width :].astype(bf16) for p in halves]
    kv_all = gather_along_z(jnp.concatenate(k_own + v_own, axis=1)).reshape(
        seq_length, 4 * kv_width
    )
    keys = [kv_all[:, i * kv_width : (i + 1) * kv_width] for i in range(2)]
    values = [kv_all[:, (2 + i) * kv_width : (3 + i) * kv_width] for i in range(2)]

    def scores_of(i):
        scores = dot_nt(q_heads[i].reshape(GROUP * rows, HEAD_SIZE), keys[i]) * score_scale
        return jnp.where(
            allowed[None], scores.reshape(GROUP, rows, seq_length), NEG_FILL
        )

    attended, log_totals = [], []
    for i in range(2):
        masked = scores_of(i)
        row_peak = jnp.max(masked, axis=-1, keepdims=True)
        expo_vals = jnp.exp(masked - row_peak)
        row_total = jnp.sum(expo_vals, axis=-1, keepdims=True)
        weights_low = (expo_vals / row_total).astype(bf16)
        mixed = dot(weights_low.reshape(GROUP * rows, seq_length), values[i])
        attended.append(
            mixed.astype(bf16)
            .reshape(GROUP, rows, HEAD_SIZE)
            .transpose(1, 0, 2)
            .reshape(rows, q_half)
        )
        log_totals.append(row_peak + jnp.log(row_total))
    branch = dot_nt(attended[0], w_out[0]) + dot_nt(attended[1], w_out[1])
    residual = inputs + branch

    inv_mix = lax.rsqrt(jnp.mean(residual * residual, axis=1, keepdims=True) + EPS)
    scaled_mix = residual * inv_mix
    normed_mix = (scaled_mix * mix_scale).astype(bf16)
    logits = dot(normed_mix, router_w)
    hot_routes = (
        route_rows[:, :, None] == jnp.arange(experts, dtype=jnp.int32)[None, None, :]
    ).astype(f32)
    chosen = jnp.sum(hot_routes * logits[:, None, :], axis=-1)
    gate_expo = jnp.exp(chosen - jnp.max(chosen, axis=1, keepdims=True))
    gate_weights = gate_expo / jnp.sum(gate_expo, axis=1, keepdims=True)
    gate_rows = jnp.sum(gate_weights[:, :, None] * hot_routes, axis=1).T

    mix_parts, expert_grads, mix_back, gate_back = experts_of_column(
        normed_mix, gate_rows[:, None, :], grads_all, slots.reshape(4, 2 * rows), expert_full
    )
    mix_out, unused = column_sum(mix_parts, gate_back.reshape(8, 2, rows // 2), 6)
    expert_sum = lax.psum_scatter(expert_grads, ("x", "y"), scatter_dimension=1, tiled=True)
    block_out = exchange_halves((residual + mix_out).astype(bf16), l)

    gate_back = jnp.sum(hot_routes * gate_back.reshape(experts, rows).T[:, None, :], axis=-1)
    gate_mean = jnp.sum(gate_weights * gate_back, axis=1, keepdims=True)
    chosen_grad = gate_weights * (gate_back - gate_mean)
    logit_grad = jnp.sum(chosen_grad[:, :, None] * hot_routes, axis=1).astype(bf16)
    grad_router = dot_tn(normed_mix, logit_grad)
    normed_grad = mix_back + dot_nt(logit_grad, router_w)
    grad_mix_gain = jnp.sum(normed_grad * scaled_mix, axis=0)
    scaled_grad = normed_grad * mix_scale
    resid_grad = (
        upstream
        + inv_mix * scaled_grad
        - residual * inv_mix**3 * jnp.mean(scaled_grad * residual, axis=1, keepdims=True)
    )

    branch_low = resid_grad.astype(bf16)
    grad_out = jnp.stack([dot_tn(branch_low, attended[i]) for i in range(2)]).astype(bf16)
    query_low, key_parts, value_parts = [], [], []
    for i in range(2):
        back_low = (
            dot(branch_low, w_out[i])
            .astype(bf16)
            .reshape(rows, GROUP, HEAD_SIZE)
            .transpose(1, 0, 2)
            .reshape(GROUP * rows, HEAD_SIZE)
        )
        prob_vals = jnp.exp(scores_of(i) - log_totals[i]).reshape(GROUP * rows, seq_length)
        prob_low = prob_vals.astype(bf16)
        prob_grad = dot_nt(back_low, values[i])
        row_dot = jnp.sum(prob_vals * prob_grad, axis=-1, keepdims=True)
        score_grad = (prob_vals * (prob_grad - row_dot)).astype(bf16)
        query_grad = dot(score_grad, keys[i]) * score_scale
        key_parts.append(
            dot_tn(score_grad, q_heads[i].reshape(GROUP * rows, HEAD_SIZE)) * score_scale
        )
        value_parts.append(dot_tn(prob_low, back_low))
        query_low.append(
            rotate_back(
                query_grad.reshape(GROUP, rows, HEAD_SIZE).transpose(1, 0, 2),
                cosine_table,
                sine_table,
            )
            .astype(bf16)
            .reshape(rows, q_half)
        )
    kv_back = sum_along_z(
        jnp.concatenate(key_parts + value_parts, axis=1)
        .astype(bf16)
        .reshape(4, rows, 4 * kv_width)
    )
    grad_in, normed_back = [], 0.0
    for i in range(2):
        key_low = rotate_back(
            kv_back[:, None, i * kv_width : (i + 1) * kv_width], cosine_table, sine_table
        ).astype(bf16)[:, 0]
        value_low = kv_back[:, (2 + i) * kv_width : (3 + i) * kv_width].astype(bf16)
        back_rows = jnp.concatenate([query_low[i], key_low, value_low], axis=1)
        grad_in.append(dot_tn(normalized_input, back_rows))
        normed_back = normed_back + dot_nt(back_rows, qkv_w[i])
    grad_attn_gain = jnp.sum(normed_back * scaled_in, axis=0)
    scaled_back = normed_back * attn_scale
    input_grad = (
        resid_grad
        + inv_attn * scaled_back
        - inputs * inv_attn**3 * jnp.mean(scaled_back * inputs, axis=1, keepdims=True)
    )
    input_grad = exchange_halves(input_grad.astype(bf16), l).astype(f32)

    misc_grad = jnp.concatenate(
        [grad_attn_gain[:, None], grad_mix_gain[:, None], grad_router], axis=1
    )
    misc_grad = jnp.pad(misc_grad, ((0, 0), (0, MISC - misc_grad.shape[1])))
    misc_grad = jnp.stack([misc_grad, jnp.zeros_like(misc_grad)]).astype(bf16)
    attn_grads = jnp.concatenate([jnp.stack(grad_in).astype(bf16), misc_grad], axis=2)

    pieces = (
        jnp.pad(expert_sum.reshape(3, 4, part, 2, ff_half), ((0, 0), (0, 0), (0, PAD - part), (0, 0), (0, 0)))
        .transpose(1, 3, 0, 2, 4)
        .reshape(8, 3, PAD, ff_half)
    )
    returned, misc_back, expert_back = return_gradients(
        attn_grads.reshape(2, 16, 4 * part, in_width),
        grad_out.reshape(2, 16, 4 * part, q_half),
        pieces,
        part,
        in_width - MISC,
    )
    expert_back = expert_back[:, :, :part].astype(f32)
    return (
        block_out[None],
        input_grad[None],
        misc_back[:, 0],
        returned[:, :q_half],
        returned[:, q_half : q_half + kv_width],
        returned[:, q_half + kv_width : q_half + 2 * kv_width],
        returned[:, in_width:].T,
        misc_back[:, 1],
        misc_back[:, 2 : 2 + experts],
        expert_back[:, 0],
        expert_back[:, 1],
        expert_back[:, 2],
    )


def solution(mesh):
    split = Mesh(mesh.devices.reshape(4, 4, 2, 2, 2), ("x", "y", "c", "h", "l"))
    fsdp = ("x", "y", "c")
    owner = ("x", "y", "c", "h")
    return jax.shard_map(
        body,
        mesh=split,
        in_specs=(
            P(fsdp, "h", None),
            P(fsdp, None),
            P(fsdp, "h", None),
            P(owner),
            P(owner, "l"),
            P(owner, "l"),
            P(owner, "l"),
            P("l", owner),
            P(owner),
            P(owner, None),
            P(None, owner, "l"),
            P(None, owner, "l"),
            P(None, owner, "l"),
            P(fsdp, "h", None),
        ),
        out_specs=(
            P(fsdp, "h", None),
            P(fsdp, "h", None),
            P(owner),
            P(owner, "l"),
            P(owner, "l"),
            P(owner, "l"),
            P("l", owner),
            P(owner),
            P(owner, None),
            P(None, owner, "l"),
            P(None, owner, "l"),
            P(None, owner, "l"),
        ),
        check_vma=False,
    )
```

```python
import functools

import jax
import jax.numpy as jnp
from jax import lax
from jax.experimental import pallas as pl
from jax.experimental.pallas import tpu as pltpu
from jax.sharding import Mesh
from jax.sharding import PartitionSpec as P

QUERY_HEADS = 12
KEY_VALUE_HEADS = 2
HEAD_SIZE = 128
GROUP = QUERY_HEADS // KEY_VALUE_HEADS
EPS = 1e-06
ROPE_BASE = 1000000.0
NEG_FILL = -1e30
MISC = 128
SLOTS = 320
PAD = 32
MESH = pl.DeviceIdType.MESH
ANY = pl.BlockSpec(memory_space=pl.ANY)
VMEM = pl.BlockSpec(memory_space=pltpu.VMEM)
f32 = jnp.float32
bf16 = jnp.bfloat16


def rope_tables(positions):
    half_dim = HEAD_SIZE // 2
    frequency = ROPE_BASE ** (-jnp.arange(half_dim, dtype=f32) * (2.0 / HEAD_SIZE))
    angles = positions.astype(f32)[:, None] * frequency[None, :]
    cosine, sine = jnp.cos(angles), jnp.sin(angles)
    return jnp.concatenate([cosine, cosine], axis=1), jnp.concatenate([-sine, sine], axis=1)


def place():
    return lax.axis_index("c"), lax.axis_index("h"), lax.axis_index("l")


def column_peer(core_step, z_step):
    c, h, l = place()
    z = lax.rem(h * 2 + l + z_step, 4)
    return {"c": lax.rem(c + core_step, 2), "h": z // 2, "l": lax.rem(z, 2)}


def at_z(core, z):
    return {"c": core, "h": z // 2, "l": lax.rem(z, 2)}


def greet(steps):
    barrier = pltpu.get_barrier_semaphore()
    for core_step, z_step in steps:
        pl.semaphore_signal(
            barrier, inc=1, device_id=column_peer(core_step, (4 - z_step) % 4), device_id_type=MESH
        )
    pl.semaphore_wait(barrier, len(steps))


def send(src, dst, send_sem, recv_sem, peer):
    copy = pltpu.make_async_remote_copy(
        src_ref=src,
        dst_ref=dst,
        send_sem=send_sem,
        recv_sem=recv_sem,
        device_id=peer,
        device_id_type=MESH,
    )
    copy.start()
    return copy


COLUMN = [(0, 1), (0, 2), (0, 3), (1, 0), (1, 1), (1, 2), (1, 3)]
ALONG_Z = [(0, 1), (0, 2), (0, 3)]


class Lanes:
    def __init__(self, send_sem, recv_sem):
        self.send_sem, self.recv_sem, self.used = send_sem, recv_sem, 0

    def send(self, src, dst, peer):
        i = self.used
        self.used += 1
        return send(src, dst, self.send_sem.at[i], self.recv_sem.at[i], peer)


def lanes_scratch(count):
    return [pltpu.SemaphoreType.DMA((count,)), pltpu.SemaphoreType.DMA((count,))]


def chip_peer(axis, step):
    return {axis: lax.rem(lax.axis_index(axis) + step + 4, 4)}


def greet_chips(barrier):
    for axis in ("x", "y"):
        for step in (1, 3):
            pl.semaphore_signal(
                barrier, inc=1, device_id=chip_peer(axis, step), device_id_type=MESH
            )
    return 4


def greet_column(barrier):
    for step in COLUMN:
        pl.semaphore_signal(barrier, inc=1, device_id=column_peer(*step), device_id_type=MESH)
    return len(COLUMN)


def partner():
    return {"l": 1 - lax.axis_index("l")}


def cross():
    return {"h": 1 - lax.axis_index("h"), "l": 1 - lax.axis_index("l")}


def other_core():
    return {"c": 1 - lax.axis_index("c")}


class ColumnRing:
    def __init__(self, lanes, rows_ref, out_ref):
        c, h, l = place()
        self.lanes, self.rows, self.out = lanes, rows_ref, out_ref
        half = rows_ref.shape[0] // 2
        self.first, self.second = pl.ds(0, half), pl.ds(half, half)
        self.at = {
            "own": c * 4 + h * 2 + l,
            "partner": c * 4 + h * 2 + 1 - l,
            "cross": c * 4 + (1 - h) * 2 + 1 - l,
            "far": c * 4 + (1 - h) * 2 + l,
        }
        self.shared = {}

    def share(self, which):
        block = self.out.at[self.at[which]]
        self.shared[which] = self.lanes.send(block, block, other_core())

    def start(self):
        here = self.out.at[self.at["own"]]
        self.to_partner = self.lanes.send(self.rows, here, partner())
        self.to_cross = self.lanes.send(self.rows, here, cross())
        self.shared["own"] = self.lanes.send(self.rows, here, other_core())

    def relay(self):
        self.to_partner.wait_recv()
        block = self.out.at[self.at["partner"], self.first]
        self.far_cross = self.lanes.send(block, block, cross())
        self.to_cross.wait_recv()
        block = self.out.at[self.at["cross"], self.second]
        self.far_partner = self.lanes.send(block, block, partner())
        self.share("partner")
        self.share("cross")

    def far(self):
        self.far_cross.wait_recv()
        self.far_partner.wait_recv()
        self.share("far")

    def drain(self):
        for copy in (self.to_partner, self.to_cross, self.far_cross, self.far_partner):
            copy.wait_send()
        for copy in self.shared.values():
            copy.wait_send()

    def finish(self):
        self.far()
        for copy in self.shared.values():
            copy.wait_recv()
        self.drain()


class ChipRing:
    def __init__(self, lanes, w_out, block, low, rows, a, b):
        self.lanes, self.w_out, self.block = lanes, w_out, block
        self.rows, self.a, self.b = pl.ds(low, rows), a, b
        self.c = lax.axis_index("c")
        self.split = 1024
        self.sent, self.near = [], []

    def ref(self, da, db, columns=None):
        steps = {self.a: da, self.b: db}
        x = lax.rem(lax.axis_index("x") + steps["x"] + 4, 4)
        y = lax.rem(lax.axis_index("y") + steps["y"] + 4, 4)
        if columns is None:
            return self.w_out.at[self.c, x * 4 + y, self.rows]
        return self.w_out.at[self.c, x * 4 + y, self.rows, columns]

    def copy(self, src, dst, axis, step):
        made = self.lanes.send(src, dst, chip_peer(axis, step))
        self.sent.append(made)
        return made

    def share(self, da, db):
        block = self.ref(da, db)
        self.near.append(self.lanes.send(block, block, column_peer(1, 0)))

    def start(self):
        own = self.block.at[self.rows]
        here = self.ref(0, 0)
        self.first = [self.copy(own, here, self.a, step) for step in (1, -1)]
        self.turn = {0: [self.copy(own, here, self.b, step) for step in (1, -1)]}
        self.near.append(self.lanes.send(own, here, column_peer(1, 0)))

    def pass_on(self, da):
        block = self.ref(da, 0)
        self.turn[da] = [self.copy(block, block, self.b, step) for step in (1, -1)]
        self.share(da, 0)

    def relay_first(self):
        width = self.w_out.shape[3]
        low, high = pl.ds(0, self.split), pl.ds(self.split, width - self.split)
        for copy in self.first:
            copy.wait_recv()
        block = self.ref(-1, 0, low)
        one = self.copy(block, block, self.a, 1)
        block = self.ref(1, 0, high)
        self.second = [one, self.copy(block, block, self.a, -1)]
        self.pass_on(-1)
        self.pass_on(1)

    def relay_turn(self, da):
        for copy in self.turn[da]:
            copy.wait_recv()
        step = 1 if da in (0, -1) else -1
        block = self.ref(da, -step)
        self.last[da] = self.copy(block, block, self.b, step)
        self.share(da, 1)
        self.share(da, -1)

    def relay_second(self):
        for copy in self.second:
            copy.wait_recv()
        self.pass_on(2)

    def finish(self):
        for da in (0, -1, 1, 2):
            self.last[da].wait_recv()
            self.share(da, 2)

    def drain(self):
        for copy in self.sent:
            copy.wait_send()
        for copy in self.near:
            copy.wait()


def weights_kernel(
    part,
    attn_ref,
    expert_ref,
    rows_ref,
    slots_ref,
    w_out,
    expert_out,
    rows_out,
    slots_out,
    attn_in,
    expert_in,
    block,
    s_sem,
    r_sem,
    as_sem,
    ar_sem,
    own,
):
    c, h, l = place()
    me = (c * 2 + h) * 2 + l
    barrier = pltpu.get_barrier_semaphore()
    pl.semaphore_wait(barrier, greet_column(barrier) + greet_chips(barrier))
    lanes = Lanes(s_sem, r_sem)
    slot = c * 2 + h
    here = pltpu.make_async_copy(attn_ref, attn_in.at[slot], own.at[1])
    there = pltpu.make_async_remote_copy(
        src_ref=attn_ref,
        dst_ref=attn_in.at[slot],
        send_sem=as_sem.at[0],
        recv_sem=ar_sem.at[slot],
        device_id=column_peer(1, 0),
        device_id_type=MESH,
    )
    pl.when(c == l)(here.start)
    pl.when(c != l)(there.start)
    for z_step in range(1, 4):
        z = lax.rem(h * 2 + l + z_step, 4)
        send(attn_ref, attn_in.at[slot], as_sem.at[z_step], ar_sem.at[slot], at_z(l, z))
    own_copy = pltpu.make_async_copy(expert_ref.at[me], expert_in.at[me], own.at[0])
    own_copy.start()
    pieces = []
    for step in COLUMN:
        peer = column_peer(*step)
        to = (peer["c"] * 2 + peer["h"]) * 2 + peer["l"]
        pieces.append(lanes.send(expert_ref.at[to], expert_in.at[me], peer))
        pieces.append(lanes.send(slots_ref.at[to], slots_out.at[me], peer))
    own_rows = pltpu.make_async_copy(rows_ref, rows_out.at[me], own.at[2])
    own_rows.start()
    own_slots = pltpu.make_async_copy(slots_ref.at[me], slots_out.at[me], own.at[4])
    own_slots.start()
    ring = ColumnRing(lanes, rows_ref, rows_out)
    ring.start()

    for source in range(4):
        mine = (c == l) & (slot == source)

        def landed(source=source):
            pltpu.make_async_remote_copy(
                src_ref=attn_ref,
                dst_ref=attn_in.at[source],
                send_sem=as_sem.at[0],
                recv_sem=ar_sem.at[source],
                device_id=column_peer(1, 0),
                device_id_type=MESH,
            ).wait_recv()

        pl.when(jnp.logical_not(mine))(landed)
    pl.when(c == l)(here.wait)
    block[...] = jnp.concatenate(
        [attn_in[i].astype(f32)[:part] for i in range(4)], axis=0
    ).astype(block.dtype)
    x, y = lax.axis_index("x"), lax.axis_index("y")
    keep = pltpu.make_async_copy(block, w_out.at[c, x * 4 + y], own.at[3])
    keep.start()
    half = block.shape[0] // 2
    halves = [
        ChipRing(lanes, w_out, block, 0, half, "x", "y"),
        ChipRing(lanes, w_out, block, half, half, "y", "x"),
    ]
    for ring_half in halves:
        ring_half.last = {}
        ring_half.start()

    own_copy.wait()
    for copy in pieces:
        copy.wait()
    for i in range(3):
        for l_side in range(2):
            expert_out[i, :, l_side * 384 : (l_side + 1) * 384] = jnp.concatenate(
                [expert_in[2 * j + l_side, i].astype(f32)[:part] for j in range(4)], axis=0
            ).astype(expert_out.dtype)

    for ring_half in halves:
        ring_half.relay_first()
    for ring_half in halves:
        ring_half.relay_turn(0)
    for ring_half in halves:
        ring_half.relay_second()
    ring.relay()
    for da in (-1, 1, 2):
        for ring_half in halves:
            ring_half.relay_turn(da)
    ring.finish()
    for ring_half in halves:
        ring_half.finish()
    for ring_half in halves:
        ring_half.drain()
    keep.wait()
    own_rows.wait()
    own_slots.wait()
    pl.when(c != l)(there.wait_send)
    for z_step in range(1, 4):
        pltpu.make_async_remote_copy(
            src_ref=attn_ref,
            dst_ref=attn_in.at[slot],
            send_sem=as_sem.at[z_step],
            recv_sem=ar_sem.at[slot],
            device_id=column_peer(0, z_step),
            device_id_type=MESH,
        ).wait_send()


def gather_weights(attn_block, expert_pieces, rows, slots, part):
    width = attn_block.shape[1]
    ff_half = expert_pieces.shape[3]
    return pl.pallas_call(
        functools.partial(weights_kernel, part),
        name="gather_weights",
        out_shape=(
            jax.ShapeDtypeStruct((2, 16, 4 * part, width), bf16),
            jax.ShapeDtypeStruct((3, 4 * part, 2 * ff_half), bf16),
            jax.ShapeDtypeStruct((8,) + rows.shape, bf16),
            jax.ShapeDtypeStruct(slots.shape, f32),
        ),
        in_specs=[VMEM, ANY, ANY, ANY],
        out_specs=(ANY, VMEM, ANY, ANY),
        scratch_shapes=[
            pltpu.VMEM((4,) + attn_block.shape, bf16),
            pltpu.VMEM(expert_pieces.shape, bf16),
            pltpu.VMEM((4 * part, width), bf16),
        ]
        + lanes_scratch(100)
        + [
            pltpu.SemaphoreType.DMA((4,)),
            pltpu.SemaphoreType.DMA((4,)),
            pltpu.SemaphoreType.DMA((5,)),
        ],
        compiler_params=pltpu.CompilerParams(
            collective_id=1, has_side_effects=True, vmem_limit_bytes=32 * 2**20
        ),
    )(attn_block, expert_pieces, rows, slots)


def ref_dot(a, b):
    return jnp.dot(a, b, preferred_element_type=f32)


def ref_dot_nt(a, b):
    return lax.dot_general(a, b, (((1,), (1,)), ((), ())), preferred_element_type=f32)


def ref_dot_tn(a, b):
    return lax.dot_general(a, b, (((0,), (0,)), ((), ())), preferred_element_type=f32)


def at(i, size):
    return pl.ds(pl.multiple_of(i * size, size), size)


def gain_rows(misc):
    pick = lax.broadcasted_iota(jnp.int32, (16, MISC), 0)
    pick = (pick == lax.broadcasted_iota(jnp.int32, (16, MISC), 1)).astype(f32).astype(bf16)
    return ref_dot_nt(pick, misc)


def turn(values, cosine, sine):
    return values * cosine + pltpu.roll(values, HEAD_SIZE // 2, 1) * sine


def turn_back(values, cosine, sine):
    return values * cosine - pltpu.roll(values, HEAD_SIZE // 2, 1) * sine


def fill_bias(bias, seg_column, seg_row, first):
    keys, queries = bias.shape
    chunk = 256

    def fill(i, carry):
        here = at(i, chunk)
        key = lax.broadcasted_iota(jnp.int32, (chunk, queries), 0) + i * chunk
        query = lax.broadcasted_iota(jnp.int32, (chunk, queries), 1) + first
        seen = (seg_column[here, :] == seg_row[...]) & (key <= query)
        bias[here, :] = jnp.where(seen, 0.0, NEG_FILL)
        return carry

    lax.fori_loop(0, keys // chunk, fill, 0)


def attention_kernel(
    x_ref,
    w_ref,
    cos_ref,
    sin_ref,
    seg_column,
    seg_row,
    named_ref,
    a_out,
    q_out,
    kv_out,
    o_out,
    lse_out,
    h1_out,
    b_out,
    gates_out,
    w,
    bias,
    value_turned,
    s_sem,
    r_sem,
    w_sem,
):
    c, h, l = place()
    z = h * 2 + l
    rows, width = x_ref.shape
    q_half = w.shape[2] // 2 - (HEAD_SIZE * 2 + MISC) // 2
    kv_at, misc_at, out_at = q_half, q_half + 2 * HEAD_SIZE, q_half + 2 * HEAD_SIZE + MISC
    pieces = [(kv_at, out_at - kv_at), (0, q_half), (out_at, q_half)]
    loads = []
    for i, (start, size) in enumerate(pieces):
        columns = pl.ds(start, size)
        copy = pltpu.make_async_copy(
            w_ref.at[:, :, columns], w.at[:, :, columns], w_sem.at[i]
        )
        copy.start()
        loads.append(copy)
    barrier = pltpu.get_barrier_semaphore()
    for step in ALONG_Z:
        pl.semaphore_signal(barrier, inc=1, device_id=column_peer(*step), device_id_type=MESH)
    pl.semaphore_wait(barrier, len(ALONG_Z))
    lanes = Lanes(s_sem, r_sem)
    scale = HEAD_SIZE ** (-0.5)
    fill_bias(bias, seg_column, seg_row, z * rows)
    loads[0].wait()
    gains = gain_rows(w[0, :, misc_at:out_at])
    chunk = 32

    def norm(i, carry):
        here = at(i, chunk)
        x = x_ref[here, :].astype(f32)
        inverse = lax.rsqrt(jnp.mean(x * x, axis=1, keepdims=True) + EPS)
        a_out[here, :] = (x * inverse * gains[8:9, :]).astype(bf16)
        return carry

    lax.fori_loop(0, rows // chunk, norm, 0)
    cosine, sine = cos_ref[...], sin_ref[...]
    head = pl.ds(0, HEAD_SIZE)
    sends = []
    for i in range(2):
        kv = ref_dot(a_out[...], w[i, :, kv_at:misc_at])
        kv_out[z, :, i * 128 : (i + 1) * 128] = turn(kv[:, :128], cosine, sine).astype(bf16)
        kv_out[z, :, (2 + i) * 128 : (3 + i) * 128] = kv[:, 128:].astype(bf16)
    for step in ALONG_Z:
        sends.append(lanes.send(kv_out.at[z], kv_out.at[z], column_peer(*step)))
    loads[1].wait()
    for i in range(2):

        def project(j, carry, i=i):
            columns = at(j, 256)
            q = ref_dot(a_out[...], w[i, :, columns])
            q_out[i * GROUP + 2 * j] = turn(q[:, :128], cosine, sine).astype(bf16)
            q_out[i * GROUP + 2 * j + 1] = turn(q[:, 128:], cosine, sine).astype(bf16)
            return carry

        lax.fori_loop(0, q_half // 256, project, 0)
    for copy in sends:
        copy.wait_recv()
    keys_count = 4 * rows
    for i in range(2):
        values = kv_out[:, :, (2 + i) * 128 : (3 + i) * 128].reshape(keys_count, HEAD_SIZE)
        value_turned[...] = values.T

        def attend(j, carry, i=i):
            keys = kv_out[:, :, i * 128 : (i + 1) * 128].reshape(keys_count, HEAD_SIZE)
            scores = ref_dot_nt(keys, q_out[i * GROUP + j]) * scale + bias[...]
            peak = jnp.max(scores, axis=0, keepdims=True)
            expo = jnp.exp(scores - peak)
            total = jnp.sum(expo, axis=0, keepdims=True)
            weights = (expo * (1.0 / total)).astype(bf16)
            mixed = ref_dot(value_turned[...], weights)
            o_out[:, at(i * GROUP + j, HEAD_SIZE)] = mixed.T.astype(bf16)
            lse_out[i * GROUP + j] = peak + jnp.log(total)
            return carry

        lax.fori_loop(0, GROUP, attend, 0)
    loads[2].wait()

    def leave(j, carry):
        here = at(j, 512)
        u = ref_dot_nt(o_out[:, :q_half], w[0, here, out_at:])
        u = u + ref_dot_nt(o_out[:, q_half:], w[1, here, out_at:])
        h1_out[:, here] = x_ref[:, here].astype(f32) + u
        return carry

    lax.fori_loop(0, width // 512, leave, 0)

    def second(i, carry):
        here = at(i, chunk)
        h1 = h1_out[here, :]
        inverse = lax.rsqrt(jnp.mean(h1 * h1, axis=1, keepdims=True) + EPS)
        b_out[here, :] = (h1 * inverse * gains[9:10, :]).astype(bf16)
        return carry

    lax.fori_loop(0, rows // chunk, second, 0)
    logits = ref_dot(b_out[...], w[0, :, misc_at:out_at]).T[:8]
    named = named_ref[...] > 0
    masked = jnp.where(named, logits, NEG_FILL)
    expo = jnp.where(named, jnp.exp(masked - jnp.max(masked, axis=0, keepdims=True)), 0.0)
    gates = expo / jnp.sum(expo, axis=0, keepdims=True)
    for e in range(8):
        gates_out[e] = gates[e : e + 1]
    for copy in sends:
        copy.wait_send()


def attention(x, w_attn, cosine, sine, seg_column, seg_row, named):
    rows, width = x.shape
    keys = 4 * rows
    sds = jax.ShapeDtypeStruct
    return pl.pallas_call(
        attention_kernel,
        name="attention",
        out_shape=(
            sds((rows, width), bf16),
            sds((QUERY_HEADS, rows, HEAD_SIZE), bf16),
            sds((4, rows, 4 * HEAD_SIZE), bf16),
            sds((rows, QUERY_HEADS * HEAD_SIZE), bf16),
            sds((QUERY_HEADS, 1, rows), f32),
            sds((rows, width), f32),
            sds((rows, width), bf16),
            sds((8, 1, rows), f32),
        ),
        in_specs=[VMEM, ANY] + [VMEM] * 5,
        out_specs=(VMEM,) * 8,
        scratch_shapes=[
            pltpu.VMEM(w_attn.shape, bf16),
            pltpu.VMEM((keys, rows), f32),
            pltpu.VMEM((HEAD_SIZE, keys), bf16),
            pltpu.SemaphoreType.DMA((3,)),
            pltpu.SemaphoreType.DMA((3,)),
            pltpu.SemaphoreType.DMA((3,)),
        ],
        compiler_params=pltpu.CompilerParams(
            collective_id=2, has_side_effects=True, vmem_limit_bytes=56 * 2**20
        ),
    )(x, w_attn, cosine, sine, seg_column, seg_row, named)


def attention_back_kernel(
    back_ref,
    gate_back_ref,
    gates_ref,
    b_ref,
    h1_ref,
    x_ref,
    g_ref,
    a_ref,
    o_ref,
    q_ref,
    kv_ref,
    lse_ref,
    cos_ref,
    sin_ref,
    seg_column,
    seg_row,
    w_ref,
    parts_ref,
    grad_in,
    grad_out,
    tokens_out,
    block_out,
    w,
    bias,
    key_turned,
    dh1,
    da,
    du,
    do,
    back_rows,
    key_sum,
    value_sum,
    kv_send,
    kv_held,
    stage_in,
    stage_out,
    misc_grad,
    parts,
    near,
    far,
    nearest,
    s_sem,
    r_sem,
    w_sem,
    stage_in_sem,
    stage_out_sem,
    own,
):
    c, h, l = place()
    z = h * 2 + l
    rows, width = x_ref.shape
    q_half = w.shape[2] // 2 - (HEAD_SIZE * 2 + MISC) // 2
    kv_at, misc_at, out_at = q_half, q_half + 2 * HEAD_SIZE, q_half + 2 * HEAD_SIZE + MISC
    pieces = [(misc_at, w.shape[2] - misc_at), (0, misc_at)]
    loads = []
    for i, (start, size) in enumerate(pieces):
        columns = pl.ds(start, size)
        copy = pltpu.make_async_copy(
            w_ref.at[:, :, columns], w.at[:, :, columns], w_sem.at[i]
        )
        copy.start()
        loads.append(copy)
    parts_load = pltpu.make_async_copy(parts_ref.at[pl.ds(c * 4, 4)], parts, own.at[0])
    parts_load.start()
    barrier = pltpu.get_barrier_semaphore()
    pl.semaphore_wait(barrier, greet_column(barrier))
    lanes = Lanes(s_sem, r_sem)
    places = {
        "own": z,
        "partner": h * 2 + 1 - l,
        "cross": (1 - h) * 2 + 1 - l,
        "far": (1 - h) * 2 + l,
    }
    near_copies = {
        which: lanes.send(
            parts_ref.at[(1 - c) * 4 + places[which]], near.at[places[which]], other_core()
        )
        for which in ("far", "cross", "partner", "own")
    }
    scale = HEAD_SIZE ** (-0.5)
    fill_bias(bias, seg_column, seg_row, z * rows)

    def add_near(which):
        near_copies[which].wait_recv()
        k = places[which]

        def add(i, carry):
            here = at(i, 64)
            parts[k, here] = parts[k, here] + near[k, here]
            return carry

        lax.fori_loop(0, rows // 64, add, 0)

    half = rows // 2
    first, second = pl.ds(0, half), pl.ds(half, half)

    def part_at(which, some):
        return parts.at[places[which], some]

    parts_load.wait()
    add_near("far")
    far_partner = lanes.send(part_at("far", first), far.at[0], partner())
    far_cross = lanes.send(part_at("far", second), far.at[1], cross())
    add_near("cross")
    add_near("partner")
    early_cross = lanes.send(part_at("cross", second), nearest.at[1, second], cross())
    early_partner = lanes.send(part_at("partner", first), nearest.at[0, first], partner())
    add_near("own")

    loads[0].wait()
    misc = w[0, :, misc_at:out_at]
    gains = gain_rows(misc)
    gates = jnp.concatenate([gates_ref[e] for e in range(8)], axis=0)
    gate_back = jnp.concatenate([gate_back_ref[e] for e in range(8)], axis=0)
    mean = jnp.sum(gates * gate_back, axis=0, keepdims=True)
    logit_grad = gates * (gate_back - mean)
    logit_grad = jnp.concatenate(
        [logit_grad, jnp.zeros((MISC - 8, rows), f32)], axis=0
    ).T.astype(bf16)
    chunk = 32

    def norm_back(i, carry):
        mix_sum = carry
        here = at(i, chunk)
        h1 = h1_ref[here, :]
        inverse = lax.rsqrt(jnp.mean(h1 * h1, axis=1, keepdims=True) + EPS)
        db = back_ref[here, :] + dh1[here, :]
        mix_sum = mix_sum + jnp.sum(db * h1 * inverse, axis=0, keepdims=True)
        dz = db * gains[9:10, :]
        mean = jnp.mean(dz * h1, axis=1, keepdims=True)
        value = g_ref[here, :].astype(f32) + inverse * dz - h1 * (inverse * inverse * inverse * mean)
        dh1[here, :] = value
        du[here, :] = value.astype(bf16)
        return mix_sum

    dh1[...] = ref_dot_nt(logit_grad, misc)
    mix_sum = lax.fori_loop(0, rows // chunk, norm_back, jnp.zeros((1, width), f32))
    misc_grad[...] = ref_dot_tn(b_ref[...], logit_grad)

    def project(i, carry):
        columns = at(i, 256)
        for g in range(2):
            do[g, :, columns] = ref_dot(
                du[...], w[g, :, pl.ds(pl.multiple_of(out_at + i * 256, 128), 256)]
            ).astype(bf16)
        return carry

    lax.fori_loop(0, q_half // 256, project, 0)

    def stage_out_copy(g, i, slot):
        return pltpu.make_async_copy(
            stage_out.at[slot], grad_out.at[g, at(i, 256)], stage_out_sem.at[slot]
        )

    for g in range(2):

        def out_grad(i, carry, g=g):
            slot = lax.rem(i, 2)

            @pl.when(i >= 2)
            def _():
                stage_out_copy(g, i - 2, slot).wait()

            stage_out[slot] = ref_dot_tn(
                du[:, at(i, 256)], o_ref[:, g * q_half : (g + 1) * q_half]
            ).astype(bf16)
            stage_out_copy(g, i, slot).start()
            return carry

        lax.fori_loop(0, width // 256, out_grad, 0)
        for i in range(2):
            stage_out_copy(g, width // 256 - 2 + i, i).wait()

    far_partner.wait_recv()
    mine = part_at("cross", first)
    mine[...] = mine[...] + far[0]
    late_cross = lanes.send(mine, nearest.at[1, first], cross())
    far_cross.wait_recv()
    mine = part_at("partner", second)
    mine[...] = mine[...] + far[1]
    late_partner = lanes.send(mine, nearest.at[0, second], partner())

    keys_count = 4 * rows
    kv_sends = []
    cosine, sine = cos_ref[...], sin_ref[...]
    for g in range(2):
        key_turned[...] = (
            kv_ref[:, :, g * 128 : (g + 1) * 128].reshape(keys_count, HEAD_SIZE).T
        )
        key_sum[...] = jnp.zeros_like(key_sum)
        value_sum[...] = jnp.zeros_like(value_sum)

        def head_back(j, carry, g=g):
            columns = at(j, HEAD_SIZE)
            keys = kv_ref[:, :, g * 128 : (g + 1) * 128].reshape(keys_count, HEAD_SIZE)
            values = kv_ref[:, :, (2 + g) * 128 : (3 + g) * 128].reshape(keys_count, HEAD_SIZE)
            query = q_ref[g * GROUP + j]
            out_back = do[g, :, columns]
            scores = ref_dot_nt(keys, query) * scale + bias[...]
            prob = jnp.exp(scores - lse_ref[g * GROUP + j])
            prob_back = ref_dot_nt(values, out_back)
            value_sum[...] += ref_dot(prob.astype(bf16), out_back)
            row_dot = jnp.sum(prob * prob_back, axis=0, keepdims=True)
            score_back = (prob * (prob_back - row_dot)).astype(bf16)
            key_sum[...] += ref_dot(score_back, query)
            query_back = (ref_dot(key_turned[...], score_back) * scale).T
            back_rows[g, :, columns] = turn_back(query_back, cosine, sine).astype(bf16)
            return carry

        lax.fori_loop(0, GROUP, head_back, 0)
        kv_send[g, :, :, :128] = (key_sum[...] * scale).astype(bf16).reshape(4, rows, 128)
        kv_send[g, :, :, 128:] = value_sum[...].astype(bf16).reshape(4, rows, 128)
        for i, step in enumerate(ALONG_Z):
            to = lax.rem(z + step[1], 4)
            kv_sends.append(lanes.send(kv_send.at[g, to], kv_held.at[g, i], column_peer(*step)))

    for copy in (early_partner, early_cross, late_cross, late_partner):
        copy.wait_recv()

    def total(i, carry):
        here = at(i, 64)
        value = parts[z, here].astype(f32)
        value = value + nearest[0, here].astype(f32) + nearest[1, here].astype(f32)
        block_out[l, here] = (h1_ref[here, :] + value).astype(bf16)
        return carry

    lax.fori_loop(0, rows // 64, total, 0)
    block_send = lanes.send(block_out.at[l], block_out.at[l], partner())
    loads[1].wait()
    for copy in kv_sends:
        copy.wait_recv()
    for g in range(2):
        own_part = kv_send[g, z].astype(f32)
        for i in range(3):
            own_part = own_part + kv_held[g, i].astype(f32)
        back_rows[g, :, q_half : q_half + 128] = turn_back(
            own_part[:, :128], cosine, sine
        ).astype(bf16)
        back_rows[g, :, q_half + 128 :] = own_part[:, 128:].astype(bf16)

    def input_back(i, carry):
        here = at(i, 512)
        value = ref_dot_nt(back_rows[0], w[0, here, :misc_at])
        da[:, here] = value + ref_dot_nt(back_rows[1], w[1, here, :misc_at])
        return carry

    lax.fori_loop(0, width // 512, input_back, 0)

    def first_back(i, carry):
        here = at(i, chunk)
        x = x_ref[here, :].astype(f32)
        inverse = lax.rsqrt(jnp.mean(x * x, axis=1, keepdims=True) + EPS)
        back = da[here, :]
        carry = carry + jnp.sum(back * x * inverse, axis=0, keepdims=True)
        dz = back * gains[8:9, :]
        mean = jnp.mean(dz * x, axis=1, keepdims=True)
        value = dh1[here, :] + inverse * dz - x * (inverse * inverse * inverse * mean)
        tokens_out[here, :] = value.astype(bf16)
        return carry

    attn_sum = lax.fori_loop(0, rows // chunk, first_back, jnp.zeros((1, width), f32))
    number = lax.broadcasted_iota(jnp.int32, (MISC, width), 0)
    gain_grads = jnp.where(number == 8, attn_sum, jnp.where(number == 9, mix_sum, 0.0))
    misc_grad[...] += gain_grads.T

    def stage_in_copy(g, i, slot):
        return pltpu.make_async_copy(
            stage_in.at[slot], grad_in.at[g, at(i, 256)], stage_in_sem.at[slot]
        )

    for g in range(2):

        def in_grad(i, carry, g=g):
            slot = lax.rem(i, 2)
            here = at(i, 256)

            @pl.when(i >= 2)
            def _():
                stage_in_copy(g, i - 2, slot).wait()

            stage_in[slot, :, :misc_at] = ref_dot_tn(a_ref[:, here], back_rows[g]).astype(bf16)
            if g == 0:
                stage_in[slot, :, misc_at:] = misc_grad[here, :].astype(bf16)
            else:
                stage_in[slot, :, misc_at:] = jnp.zeros((256, MISC), bf16)
            stage_in_copy(g, i, slot).start()
            return carry

        lax.fori_loop(0, width // 256, in_grad, 0)
        for i in range(2):
            stage_in_copy(g, width // 256 - 2 + i, i).wait()
    block_send.wait()
    for copy in kv_sends:
        copy.wait_send()
    for copy in near_copies.values():
        copy.wait_send()
    for copy in (early_partner, early_cross, late_cross, late_partner, far_partner, far_cross):
        copy.wait_send()


def attention_back(
    back, gate_back, gates, b, h1, x, g, a, o, q, kv, lse, cosine, sine, seg_column, seg_row, w_attn, parts
):
    rows, width = x.shape
    keys = 4 * rows
    q_half = o.shape[1] // 2
    qkv = q_half + 2 * HEAD_SIZE
    sds = jax.ShapeDtypeStruct
    return pl.pallas_call(
        attention_back_kernel,
        name="attention_back",
        out_shape=(
            sds((2, width, qkv + MISC), bf16),
            sds((2, width, q_half), bf16),
            sds((rows, width), bf16),
            sds((2, rows, width), bf16),
        ),
        in_specs=[VMEM] * 16 + [ANY, ANY],
        out_specs=(ANY, ANY, VMEM, VMEM),
        scratch_shapes=[
            pltpu.VMEM(w_attn.shape, bf16),
            pltpu.VMEM((keys, rows), f32),
            pltpu.VMEM((HEAD_SIZE, keys), bf16),
            pltpu.VMEM((rows, width), f32),
            pltpu.VMEM((rows, width), f32),
            pltpu.VMEM((rows, width), bf16),
            pltpu.VMEM((2, rows, q_half), bf16),
            pltpu.VMEM((2, rows, qkv), bf16),
            pltpu.VMEM((keys, HEAD_SIZE), f32),
            pltpu.VMEM((keys, HEAD_SIZE), f32),
            pltpu.VMEM((2, 4, rows, 2 * HEAD_SIZE), bf16),
            pltpu.VMEM((2, 3, rows, 2 * HEAD_SIZE), bf16),
            pltpu.VMEM((2, 256, qkv + MISC), bf16),
            pltpu.VMEM((2, 256, q_half), bf16),
            pltpu.VMEM((width, MISC), f32),
            pltpu.VMEM((4, rows, width), bf16),
            pltpu.VMEM((4, rows, width), bf16),
            pltpu.VMEM((2, rows // 2, width), bf16),
            pltpu.VMEM((2, rows, width), bf16),
        ]
        + lanes_scratch(24)
        + [
            pltpu.SemaphoreType.DMA((2,)),
            pltpu.SemaphoreType.DMA((2,)),
            pltpu.SemaphoreType.DMA((2,)),
            pltpu.SemaphoreType.DMA((1,)),
        ],
        compiler_params=pltpu.CompilerParams(
            collective_id=3, has_side_effects=True, vmem_limit_bytes=56 * 2**20
        ),
    )(
        back, gate_back, gates, b, h1, x, g, a, o, q, kv, lse, cosine, sine, seg_column, seg_row, w_attn, parts
    )


def experts_kernel(
    rows_ref,
    gate_ref,
    grads_ref,
    slot_rows,
    slot_columns,
    weights_ref,
    mix_out,
    weight_grads,
    back_out,
    gate_back_out,
    rows_all,
    held,
    w_gate,
    w_up,
    w_down,
    picked,
    picked_grads,
    hidden_back,
    hidden_gated,
    gate_low,
    up_low,
    mix_stage,
    near,
    far,
    nearest,
    gates_in,
    gate_back,
    s_sem,
    r_sem,
    own,
    stage_sem,
    near_send,
    near_recv,
):
    c, h, l = place()
    me = (c * 2 + h) * 2 + l
    barrier = pltpu.get_barrier_semaphore()
    pl.semaphore_wait(barrier, greet_column(barrier))
    lanes = Lanes(s_sem, r_sem)
    rows, width = rows_ref.shape
    slots = picked.shape[1]
    ff = w_gate.shape[1]
    block = 2 * rows

    ring = ColumnRing(lanes, rows_ref, rows_all)
    ring.start()
    local = [
        pltpu.make_async_copy(grads_ref, held, own.at[0]),
        pltpu.make_async_copy(weights_ref.at[2], w_down, own.at[1]),
        pltpu.make_async_copy(weights_ref.at[0], w_gate, own.at[2]),
        pltpu.make_async_copy(weights_ref.at[1], w_up, own.at[3]),
        pltpu.make_async_copy(rows_ref, rows_all.at[me], own.at[4]),
        pltpu.make_async_copy(gate_ref.at[me], gates_in.at[me], own.at[5]),
    ]
    for copy in local:
        copy.start()
    gate_copies = []
    for step in COLUMN:
        peer = column_peer(*step)
        to = (peer["c"] * 2 + peer["h"]) * 2 + peer["l"]
        gate_copies.append(lanes.send(gate_ref.at[to], gates_in.at[me], peer))

    def pick_of(k):
        number = lax.broadcasted_iota(jnp.int32, (slots, block), 0).astype(f32)
        return slot_rows[k] == number

    def spread_of(k):
        number = lax.broadcasted_iota(jnp.int32, (block, slots), 1).astype(f32)
        return (slot_columns[k] == number).astype(f32).astype(bf16)

    def low(mask):
        return mask.astype(f32).astype(bf16)

    def both(ref, k, columns=None):
        if columns is None:
            return ref[pl.ds(2 * k, 2)].reshape(block, width)
        return ref[pl.ds(2 * k, 2), :, columns].reshape(block, -1)

    wide = 512
    narrow = 256

    local[0].wait()
    local[1].wait()

    def prepare(k, carry):
        pick = low(pick_of(k))

        def gather(i, carry):
            columns = at(i, wide)
            values = ref_dot(pick, held[pl.ds(2 * k, 2), :, columns].reshape(block, wide))
            picked_grads[k, :, columns] = values.astype(bf16)
            return carry

        lax.fori_loop(0, width // wide, gather, 0)

        def down(i, carry):
            columns = at(i, narrow)
            hidden_back[k, :, columns] = ref_dot(picked_grads[k], w_down[:, columns])
            return carry

        lax.fori_loop(0, ff // narrow, down, 0)
        return carry

    lax.fori_loop(0, 4, prepare, 0)
    ring.relay()
    for copy in local[2:]:
        copy.wait()
    for copy in gate_copies:
        copy.wait()
    ring.shared["own"].wait_recv()
    ring.shared["partner"].wait_recv()

    def expert(k, stage):
        pick = pick_of(k)
        pick_low = low(pick)
        spread = spread_of(k)
        gates = gates_in[pl.ds(2 * k, 2)]
        gate_row = jnp.concatenate([gates[0], gates[1]], axis=1)
        gate = jnp.sum(jnp.where(pick, gate_row, 0.0), axis=1, keepdims=True)

        def gather(i, carry):
            columns = at(i, wide)
            values = ref_dot(pick_low, rows_all[pl.ds(2 * k, 2), :, columns].reshape(block, wide))
            picked[k, :, columns] = values.astype(bf16)
            return carry

        lax.fori_loop(0, width // wide, gather, 0)

        def hide(i, total):
            columns = at(i, narrow)
            gate_act = ref_dot(picked[k], w_gate[:, columns])
            up_act = ref_dot(picked[k], w_up[:, columns])
            back = hidden_back[k, :, columns]
            sigmoid_act = 1.0 / (1.0 + jnp.exp(-gate_act))
            silu_act = gate_act * sigmoid_act
            hidden = silu_act * up_act
            hidden_gated[k, :, columns] = (hidden * gate).astype(bf16)
            total = total + jnp.sum(hidden * back, axis=1, keepdims=True)
            back = back * gate
            slope = sigmoid_act * (1.0 + gate_act * (1.0 - sigmoid_act))
            gate_low[k, :, columns] = (back * up_act * slope).astype(bf16)
            up_low[k, :, columns] = (back * silu_act).astype(bf16)
            return total

        gate_slots = lax.fori_loop(0, ff // narrow, hide, jnp.zeros((slots, 1), f32))
        back_row = jnp.sum(jnp.where(pick, gate_slots, 0.0), axis=0, keepdims=True)
        gate_back[2 * k] = back_row[:, :rows]
        gate_back[2 * k + 1] = back_row[:, rows:]

        def leave(i, carry):
            columns = at(i, wide)
            out = ref_dot_nt(hidden_gated[k], w_down[columns, :]).astype(bf16)
            mix_stage[stage, :, :, columns] = (
                ref_dot(spread, out).astype(bf16).reshape(2, rows, wide)
            )
            back = ref_dot_nt(gate_low[k], w_gate[columns, :])
            back = (back + ref_dot_nt(up_low[k], w_up[columns, :])).astype(bf16)
            held[pl.ds(2 * k, 2), :, columns] = (
                ref_dot(spread, back).astype(bf16).reshape(2, rows, wide)
            )
            return carry

        lax.fori_loop(0, width // wide, leave, 0)

    def stage_copy(k, stage):
        return pltpu.make_async_copy(
            mix_stage.at[stage], mix_out.at[pl.ds(2 * k, 2)], stage_sem.at[stage]
        )

    def near_copy(side, i):
        return pltpu.make_async_remote_copy(
            src_ref=held.at[pl.ds(((1 - c) * 2 + side) * 2, 2)],
            dst_ref=near.at[pl.ds(side * 2, 2)],
            send_sem=near_send.at[i],
            recv_sem=near_recv.at[i],
            device_id=other_core(),
            device_id_type=MESH,
        )

    expert((1 - c) * 2 + h, 0)
    near_copy(h, 0).start()
    stage_copy((1 - c) * 2 + h, 0).start()
    ring.far()
    expert(c * 2 + h, 1)
    stage_copy(c * 2 + h, 1).start()

    def add_near(z):
        mine = held.at[c * 4 + z]

        def add(i, carry):
            here = at(i, 64)
            mine[here] = mine[here] + near[z, here]
            return carry

        lax.fori_loop(0, rows // 64, add, 0)

    half = rows // 2
    first, second = pl.ds(0, half), pl.ds(half, half)
    z = {
        "own": h * 2 + l,
        "partner": h * 2 + 1 - l,
        "cross": (1 - h) * 2 + 1 - l,
        "far": (1 - h) * 2 + l,
    }

    def block_at(which, part):
        return held.at[c * 4 + z[which], part]

    near_copy(h, 0).wait_recv()
    add_near(z["partner"])
    sends = []
    early_partner = lanes.send(
        block_at("partner", first), nearest.at[0, first], partner()
    )
    add_near(z["own"])
    ring.shared["cross"].wait_recv()
    ring.shared["far"].wait_recv()

    for stage, k in ((0, (1 - c) * 2 + 1 - h), (1, c * 2 + 1 - h)):
        stage_copy(k, stage).wait()
        expert(k, stage)
        stage_copy(k, stage).start()
        if stage == 0:
            near_copy(1 - h, 1).start()
    gate_own = pltpu.make_async_copy(gate_back.at[me], gate_back_out.at[me], own.at[6])
    gate_own.start()
    for step in COLUMN:
        peer = column_peer(*step)
        to = (peer["c"] * 2 + peer["h"]) * 2 + peer["l"]
        sends.append(lanes.send(gate_back.at[to], gate_back_out.at[me], peer))
    near_copy(1 - h, 1).wait_recv()
    add_near(z["far"])
    far_partner = lanes.send(block_at("far", first), far.at[0], partner())
    far_cross = lanes.send(block_at("far", second), far.at[1], cross())
    add_near(z["cross"])
    early_cross = lanes.send(block_at("cross", second), nearest.at[1, second], cross())

    def weight_grad(values, others, target, number):
        def rows_of(i, carry):
            columns = at(i, narrow)
            left = values[:, :, columns].reshape(4 * slots, narrow)
            target[columns, :] = ref_dot_tn(left, others[...].reshape(4 * slots, ff)).astype(bf16)
            return carry

        lax.fori_loop(0, width // narrow, rows_of, 0)
        copy = pltpu.make_async_copy(target, weight_grads.at[number], own.at[1 + number])
        copy.start()
        return copy

    grad_copies = [weight_grad(picked_grads, hidden_gated, w_down, 2)]
    far_partner.wait_recv()
    mine = block_at("cross", first)
    mine[...] = mine[...] + far[0]
    late_cross = lanes.send(mine, nearest.at[1, first], cross())
    far_cross.wait_recv()
    mine = block_at("partner", second)
    mine[...] = mine[...] + far[1]
    late_partner = lanes.send(mine, nearest.at[0, second], partner())
    grad_copies.append(weight_grad(picked, gate_low, w_gate, 0))
    grad_copies.append(weight_grad(picked, up_low, w_up, 1))
    for copy in (early_partner, early_cross, late_cross, late_partner):
        copy.wait_recv()

    def finish(i, carry):
        here = at(i, 64)
        total = held[c * 4 + z["own"], here].astype(f32)
        back_out[here, :] = (
            total + nearest[0, here].astype(f32) + nearest[1, here].astype(f32)
        )
        return carry

    lax.fori_loop(0, rows // 64, finish, 0)
    for copy in (early_partner, early_cross, late_cross, late_partner, far_partner, far_cross):
        copy.wait_send()
    for i, side in ((0, h), (1, 1 - h)):
        near_copy(side, i).wait_send()
    for copy in sends + grad_copies + [gate_own]:
        copy.wait()
    for stage, k in ((0, (1 - c) * 2 + 1 - h), (1, c * 2 + 1 - h)):
        stage_copy(k, stage).wait()
    ring.drain()


def experts_of_column(rows, gates, grads_all, slots, weights):
    count, width = rows.shape
    ff = weights.shape[2]
    return pl.pallas_call(
        experts_kernel,
        name="experts",
        out_shape=(
            jax.ShapeDtypeStruct((8, count, width), bf16),
            jax.ShapeDtypeStruct(weights.shape, bf16),
            jax.ShapeDtypeStruct((count, width), f32),
            jax.ShapeDtypeStruct(gates.shape, f32),
        ),
        in_specs=[VMEM, VMEM, ANY, VMEM, VMEM, ANY],
        out_specs=(ANY, ANY, VMEM, VMEM),
        scratch_shapes=[
            pltpu.VMEM((8, count, width), bf16),
            pltpu.VMEM((8, count, width), bf16),
            pltpu.VMEM((width, ff), bf16),
            pltpu.VMEM((width, ff), bf16),
            pltpu.VMEM((width, ff), bf16),
            pltpu.VMEM((4, SLOTS, width), bf16),
            pltpu.VMEM((4, SLOTS, width), bf16),
            pltpu.VMEM((4, SLOTS, ff), f32),
            pltpu.VMEM((4, SLOTS, ff), bf16),
            pltpu.VMEM((4, SLOTS, ff), bf16),
            pltpu.VMEM((4, SLOTS, ff), bf16),
            pltpu.VMEM((2, 2, count, width), bf16),
            pltpu.VMEM((4, count, width), bf16),
            pltpu.VMEM((2, count // 2, width), bf16),
            pltpu.VMEM((2, count, width), bf16),
            pltpu.VMEM(gates.shape, f32),
            pltpu.VMEM(gates.shape, f32),
        ]
        + lanes_scratch(32)
        + [
            pltpu.SemaphoreType.DMA((7,)),
            pltpu.SemaphoreType.DMA((2,)),
            pltpu.SemaphoreType.DMA((2,)),
            pltpu.SemaphoreType.DMA((2,)),
        ],
        compiler_params=pltpu.CompilerParams(
            collective_id=4, has_side_effects=True, vmem_limit_bytes=60 * 2**20
        ),
    )(rows, gates, grads_all, slots[:, None, :], slots[:, :, None], weights)


class ChipSum:
    def __init__(self, lanes, chip, low, rows, p, q, near_p, rest_p, near_q):
        self.lanes, self.chip = lanes, chip
        self.rows, self.p, self.q = pl.ds(low, rows), p, q
        self.near_p, self.rest_p, self.near_q = near_p, rest_p, near_q
        self.sent = []

    def index(self, dp, dq):
        steps = {self.p: dp, self.q: dq}
        x = lax.rem(lax.axis_index("x") + steps["x"] + 4, 4)
        y = lax.rem(lax.axis_index("y") + steps["y"] + 4, 4)
        return x * 4 + y

    def copy(self, src, dst, axis, step):
        made = self.lanes.send(src, dst, chip_peer(axis, step))
        self.sent.append(made)
        return made

    def own(self, dp, dq):
        return self.chip.at[self.index(dp, dq), self.rows]

    def far(self):
        self.far_copies = {}
        for dq, step, i in ((2, 1, 0), (3, -1, 0), (1, 1, 1), (0, -1, 1)):
            direction = 0 if step == 1 else 1
            self.far_copies[direction, i] = self.copy(
                self.own(2, dq), self.near_p.at[direction, i], self.p, step
            )

    def plain(self):
        self.next_copies = {}
        for dq, step in ((2, -1), (3, 1), (1, -1), (0, 1)):
            self.next_to(dq, step)

    def next_to(self, dq, step):
        direction = 0 if step == 1 else 1
        self.next_copies[direction, dq] = self.copy(
            self.own(step, dq), self.rest_p.at[direction, dq], self.p, step
        )

    def joined(self):
        for dq, step, i in ((2, 1, 0), (3, -1, 0), (1, 1, 1), (0, -1, 1)):
            direction = 0 if step == 1 else 1
            self.far_copies[direction, i].wait_recv()
            mine = self.own(step, dq)
            mine[...] = mine[...] + self.near_p[direction, i]
            self.next_to(dq, step)

    def collect(self, dq):
        for direction in range(2):
            self.next_copies[direction, dq].wait_recv()
        mine = self.own(0, dq)
        total = mine[...].astype(f32)
        for direction in range(2):
            total = total + self.rest_p[direction, dq].astype(f32)
        mine[...] = total.astype(mine.dtype)

    def far_q(self):
        width = self.chip.shape[2]
        self.low, self.high = pl.ds(0, 1024), pl.ds(1024, width - 1024)
        self.collect(2)
        block = self.index(0, 2)
        self.far_q_copies = [
            self.copy(
                self.chip.at[block, self.rows, self.low], self.near_q.at[0, :, self.low], self.q, 1
            ),
            self.copy(
                self.chip.at[block, self.rows, self.high], self.near_q.at[1, :, self.high], self.q, -1
            ),
        ]

    def next_q(self):
        self.next_q_copies = []
        for i, (dq, columns) in enumerate(((1, self.low), (3, self.high))):
            self.collect(dq)
            self.far_q_copies[i].wait_recv()
            block = self.index(0, dq)
            self.chip[block, self.rows, columns] = (
                self.chip[block, self.rows, columns] + self.near_q[i, :, columns]
            )
            self.next_q_copies.append(
                self.copy(
                    self.chip.at[block, self.rows],
                    self.near_q.at[2 + i],
                    self.q,
                    1 if i == 0 else -1,
                )
            )

    def total(self):
        self.collect(0)
        total = self.chip[self.index(0, 0), self.rows, :].astype(f32)
        for i in range(2):
            self.next_q_copies[i].wait_recv()
            total = total + self.near_q[2 + i].astype(f32)
        return total

    def drain(self):
        for copy in self.sent:
            copy.wait_send()


def return_kernel(
    part,
    misc_at,
    in_ref,
    out_ref,
    expert_ref,
    tokens_ref,
    grads_out,
    misc_out,
    expert_out,
    tokens_out,
    near,
    near_p0,
    rest_p0,
    near_q0,
    near_p1,
    rest_p1,
    near_q1,
    pieces,
    landed,
    misc_landed,
    s_sem,
    r_sem,
    ps,
    pr,
    ms,
    mr,
    own,
):
    c, h, l = place()
    z = h * 2 + l
    me = c * 4 + z
    barrier = pltpu.get_barrier_semaphore()
    pl.semaphore_wait(barrier, greet_column(barrier) + greet_chips(barrier))
    lanes = Lanes(s_sem, r_sem)
    in_width = in_ref.shape[3]
    width = near.shape[2]
    half = near.shape[1] // 2
    other = column_peer(1, 0)
    x, y = lax.axis_index("x"), lax.axis_index("y")
    sums = [
        ChipSum(lanes, near, 0, half, "y", "x", near_p0, rest_p0, near_q0),
        ChipSum(lanes, near, half, half, "x", "y", near_p1, rest_p1, near_q1),
    ]
    order = [2, 1, 3, 0]
    arrive = {}
    for step in order:
        for which in range(2):
            for dq in range(4):
                block = sums[which].index(step, dq)
                rows = pl.ds(which * half, half)
                arrive[step, which, dq] = [
                    lanes.send(
                        in_ref.at[1 - c, block, rows],
                        near.at[block, rows, pl.ds(0, in_width)],
                        other,
                    ),
                    lanes.send(
                        out_ref.at[1 - c, block, rows],
                        near.at[block, rows, pl.ds(in_width, width - in_width)],
                        other,
                    ),
                ]
    own_copy = pltpu.make_async_copy(expert_ref.at[me], expert_out.at[me], own.at[0])
    own_copy.start()
    own_tokens = pltpu.make_async_copy(tokens_ref, tokens_out.at[l], own.at[1])
    own_tokens.start()
    expert_copies = [lanes.send(tokens_ref, tokens_out.at[l], partner())]
    for step in COLUMN:
        peer = column_peer(*step)
        to = (peer["c"] * 2 + peer["h"]) * 2 + peer["l"]
        expert_copies.append(lanes.send(expert_ref.at[to], expert_out.at[me], peer))

    def add_own(step, which):
        for dq in range(4):
            for copy in arrive[step, which, dq]:
                copy.wait_recv()
            block = sums[which].index(step, dq)
            rows = pl.ds(which * half, half)
            near[block, rows, pl.ds(0, in_width)] = (
                near[block, rows, pl.ds(0, in_width)] + in_ref[c, block, rows, :]
            )
            near[block, rows, pl.ds(in_width, width - in_width)] = (
                near[block, rows, pl.ds(in_width, width - in_width)] + out_ref[c, block, rows, :]
            )

    for which in range(2):
        add_own(2, which)
        sums[which].far()
    for step in (1, 3):
        for which in range(2):
            add_own(step, which)
    for each in sums:
        each.plain()
    for each in sums:
        each.joined()
    for which in range(2):
        add_own(0, which)
    for each in sums:
        each.far_q()
    for each in sums:
        each.next_q()
    for which in range(2):
        total = sums[which].total()
        for i in range(2):
            pieces[2 * which + i] = total[i * part : (i + 1) * part]

    def to_owner(target, owner, src, dst, send_sem, recv_sem, asked):
        is_me = (owner["c"] == c) & (owner["h"] == h) & (owner["l"] == l)
        there = pltpu.make_async_remote_copy(
            src_ref=src,
            dst_ref=dst,
            send_sem=send_sem,
            recv_sem=recv_sem,
            device_id=owner,
            device_id_type=MESH,
        )
        here = pltpu.make_async_copy(src, dst, recv_sem)
        pl.when(asked & jnp.logical_not(is_me))(there.start)
        pl.when(asked & is_me)(here.start)
        return asked & jnp.logical_not(is_me), there

    sent = []
    everyone = c < 2
    for target in range(4):
        owner = {"c": target // 2, "h": target % 2, "l": c}
        sent.append(
            to_owner(
                target, owner, pieces.at[target], landed.at[z], ps.at[target], pr.at[z], everyone
            )
        )
    misc = pl.ds(misc_at, MISC)
    for target in range(4):
        owner = {"c": target // 2, "h": target % 2, "l": 1}
        sent.append(
            to_owner(
                target,
                owner,
                pieces.at[target, :, misc],
                misc_landed.at[z],
                ms.at[target],
                mr.at[z],
                c == 0,
            )
        )
    for source in range(4):
        pltpu.make_async_copy(pieces.at[0], landed.at[source], pr.at[source]).wait()
    grads_out[...] = (landed[0] + landed[1]) + (landed[2] + landed[3])

    def from_core():
        for source in range(4):
            pltpu.make_async_copy(
                pieces.at[0, :, misc], misc_landed.at[source], mr.at[source]
            ).wait()
        misc_out[...] = (misc_landed[0] + misc_landed[1]) + (misc_landed[2] + misc_landed[3])

    def from_piece():
        misc_out[...] = (landed[0, :, misc] + landed[1, :, misc]) + (
            landed[2, :, misc] + landed[3, :, misc]
        )

    pl.when(l == 1)(from_core)
    pl.when(l == 0)(from_piece)
    for asked, there in sent:
        pl.when(asked)(there.wait_send)
    for copies in arrive.values():
        for copy in copies:
            copy.wait_send()
    for each in sums:
        each.drain()
    own_copy.wait()
    own_tokens.wait()
    for copy in expert_copies:
        copy.wait()


def return_gradients(grad_in, grad_out, expert_pieces, tokens, part, misc_at):
    in_width, out_width = grad_in.shape[3], grad_out.shape[3]
    width, rows = in_width + out_width, grad_in.shape[2]
    half = rows // 2
    ring = [
        pltpu.VMEM((2, 2, half, width), bf16),
        pltpu.VMEM((2, 4, half, width), bf16),
        pltpu.VMEM((4, half, width), bf16),
    ]
    return pl.pallas_call(
        functools.partial(return_kernel, part, misc_at),
        name="return_gradients",
        out_shape=(
            jax.ShapeDtypeStruct((part, width), f32),
            jax.ShapeDtypeStruct((part, MISC), f32),
            jax.ShapeDtypeStruct(expert_pieces.shape, expert_pieces.dtype),
            jax.ShapeDtypeStruct((2,) + tokens.shape, tokens.dtype),
        ),
        in_specs=[VMEM, VMEM, ANY, ANY],
        out_specs=(VMEM, VMEM, ANY, ANY),
        scratch_shapes=[pltpu.VMEM((16, rows, width), bf16)]
        + ring
        + ring
        + [
            pltpu.VMEM((4, part, width), f32),
            pltpu.VMEM((4, part, width), f32),
            pltpu.VMEM((4, part, MISC), f32),
        ]
        + lanes_scratch(130)
        + [
            pltpu.SemaphoreType.DMA((4,)),
            pltpu.SemaphoreType.DMA((4,)),
            pltpu.SemaphoreType.DMA((4,)),
            pltpu.SemaphoreType.DMA((4,)),
            pltpu.SemaphoreType.DMA((2,)),
        ],
        compiler_params=pltpu.CompilerParams(
            collective_id=7, has_side_effects=True, vmem_limit_bytes=48 * 2**20
        ),
    )(grad_in, grad_out, expert_pieces, tokens)


def body(
    tokens,
    segments,
    routes,
    attn_gain,
    w_query,
    key_matrix,
    value_matrix,
    w_output,
    mix_gain,
    w_router,
    w_gate,
    w_up,
    w_down,
    block_cotangent,
):
    c, h, l = place()
    model_width = tokens.shape[2]
    rows = tokens.shape[1] // 2
    experts, part, ff_half = w_gate.shape
    q_half = w_query.shape[1]

    misc = jnp.concatenate([w_router, attn_gain[:, None], mix_gain[:, None]], axis=1)
    misc = jnp.pad(misc, ((0, 0), (0, MISC - misc.shape[1])))
    attn_block = jnp.concatenate(
        [w_query, key_matrix, value_matrix, misc, w_output.T], axis=1
    )
    attn_block = jnp.pad(attn_block, ((0, PAD - part), (0, 0)))
    expert_pieces = jnp.pad(
        jnp.stack([w_gate, w_up, w_down], axis=1), ((0, 0), (0, 0), (0, PAD - part), (0, 0))
    )
    kv_width = key_matrix.shape[1]
    in_width = q_half + 2 * kv_width + MISC

    z = h * 2 + l
    inputs = lax.dynamic_slice_in_dim(tokens[0], l * rows, rows)
    upstream = lax.dynamic_slice_in_dim(block_cotangent[0], l * rows, rows)
    named = jnp.any(
        routes[0][:, :, None] == jnp.arange(experts, dtype=jnp.int32)[None, None, :], axis=1
    )
    slot_of = jnp.cumsum(named.astype(jnp.int32), axis=0) - 1
    slot_of = jnp.where(named, slot_of, -1).astype(f32).T
    slot_of = lax.dynamic_slice_in_dim(slot_of, l * rows, rows, axis=1)
    named = (slot_of >= 0).astype(f32)
    positions = z * rows + jnp.arange(rows, dtype=jnp.int32)
    cosine, sine = rope_tables(positions)
    seg_column = segments[0][:, None]
    seg_row = lax.dynamic_slice_in_dim(segments[0], z * rows, rows)[None, :]

    w_attn, expert_col, grads_all, slots = gather_weights(
        attn_block, expert_pieces, upstream, slot_of[:, None, :], part
    )
    w_attn = w_attn.reshape(2, model_width, attn_block.shape[1])
    expert_full = lax.all_gather(expert_col, ("x", "y"), axis=1, tiled=True)
    normed_in, q, kv, attended, lse, residual, normed_mix, gates = attention(
        inputs, w_attn, cosine, sine, seg_column, seg_row, named
    )
    mix_parts, expert_grads, mix_back, gate_back = experts_of_column(
        normed_mix, gates, grads_all, slots.reshape(4, 2 * rows), expert_full
    )
    expert_sum = lax.psum_scatter(expert_grads, ("x", "y"), scatter_dimension=1, tiled=True)
    grad_in, grad_out, tokens_back, block_out = attention_back(
        mix_back,
        gate_back,
        gates,
        normed_mix,
        residual,
        inputs,
        upstream,
        normed_in,
        attended,
        q,
        kv,
        lse,
        cosine,
        sine,
        seg_column,
        seg_row,
        w_attn,
        mix_parts,
    )

    pieces = (
        jnp.pad(
            expert_sum.reshape(3, 4, part, 2, ff_half),
            ((0, 0), (0, 0), (0, PAD - part), (0, 0), (0, 0)),
        )
        .transpose(1, 3, 0, 2, 4)
        .reshape(8, 3, PAD, ff_half)
    )
    returned, misc_back, expert_back, tokens_back = return_gradients(
        grad_in.reshape(2, 16, 4 * part, in_width),
        grad_out.reshape(2, 16, 4 * part, q_half),
        pieces,
        tokens_back,
        part,
        in_width - MISC,
    )
    expert_back = expert_back[:, :, :part].astype(f32)
    return (
        block_out.reshape(1, 2 * rows, model_width),
        tokens_back.reshape(1, 2 * rows, model_width).astype(f32),
        misc_back[:, experts],
        returned[:, :q_half],
        returned[:, q_half : q_half + kv_width],
        returned[:, q_half + kv_width : q_half + 2 * kv_width],
        returned[:, in_width:].T,
        misc_back[:, experts + 1],
        misc_back[:, :experts],
        expert_back[:, 0],
        expert_back[:, 1],
        expert_back[:, 2],
    )


def solution(mesh):
    split = Mesh(mesh.devices.reshape(4, 4, 2, 2, 2), ("x", "y", "c", "h", "l"))
    fsdp = ("x", "y", "c")
    owner = ("x", "y", "c", "h")
    return jax.shard_map(
        body,
        mesh=split,
        in_specs=(
            P(fsdp, "h", None),
            P(fsdp, None),
            P(fsdp, "h", None),
            P(owner),
            P(owner, "l"),
            P(owner, "l"),
            P(owner, "l"),
            P("l", owner),
            P(owner),
            P(owner, None),
            P(None, owner, "l"),
            P(None, owner, "l"),
            P(None, owner, "l"),
            P(fsdp, "h", None),
        ),
        out_specs=(
            P(fsdp, "h", None),
            P(fsdp, "h", None),
            P(owner),
            P(owner, "l"),
            P(owner, "l"),
            P(owner, "l"),
            P("l", owner),
            P(owner),
            P(owner, None),
            P(None, owner, "l"),
            P(None, owner, "l"),
            P(None, owner, "l"),
        ),
        check_vma=False,
    )
```

```python
import functools

import jax
import jax.numpy as jnp
from jax import lax
from jax.experimental import pallas as pl
from jax.experimental.pallas import tpu as pltpu
from jax.sharding import Mesh
from jax.sharding import PartitionSpec as P

QUERY_HEADS = 12
KEY_VALUE_HEADS = 2
HEAD_SIZE = 128
GROUP = QUERY_HEADS // KEY_VALUE_HEADS
EPS = 1e-06
ROPE_BASE = 1000000.0
NEG_FILL = -1e30
MISC = 128
SLOTS = 320
PAD = 32
MESH = pl.DeviceIdType.MESH
ANY = pl.BlockSpec(memory_space=pl.ANY)
HBM = pl.BlockSpec(memory_space=pltpu.HBM)
VMEM = pl.BlockSpec(memory_space=pltpu.VMEM)
f32 = jnp.float32
bf16 = jnp.bfloat16


def rope_tables(positions):
    half_dim = HEAD_SIZE // 2
    frequency = ROPE_BASE ** (-jnp.arange(half_dim, dtype=f32) * (2.0 / HEAD_SIZE))
    angles = positions.astype(f32)[:, None] * frequency[None, :]
    cosine, sine = jnp.cos(angles), jnp.sin(angles)
    return jnp.concatenate([cosine, cosine], axis=1), jnp.concatenate([-sine, sine], axis=1)


def place():
    return lax.axis_index("c"), lax.axis_index("h"), lax.axis_index("l")


def column_peer(core_step, z_step):
    c, h, l = place()
    z = lax.rem(h * 2 + l + z_step, 4)
    return {"c": lax.rem(c + core_step, 2), "h": z // 2, "l": lax.rem(z, 2)}


def at_z(core, z):
    return {"c": core, "h": z // 2, "l": lax.rem(z, 2)}


def greet(steps):
    barrier = pltpu.get_barrier_semaphore()
    for core_step, z_step in steps:
        pl.semaphore_signal(
            barrier, inc=1, device_id=column_peer(core_step, (4 - z_step) % 4), device_id_type=MESH
        )
    pl.semaphore_wait(barrier, len(steps))


def send(src, dst, send_sem, recv_sem, peer):
    copy = pltpu.make_async_remote_copy(
        src_ref=src,
        dst_ref=dst,
        send_sem=send_sem,
        recv_sem=recv_sem,
        device_id=peer,
        device_id_type=MESH,
    )
    copy.start()
    return copy


COLUMN = [(0, 1), (0, 2), (0, 3), (1, 0), (1, 1), (1, 2), (1, 3)]
ALONG_Z = [(0, 1), (0, 2), (0, 3)]


class Lanes:
    def __init__(self, send_sem, recv_sem):
        self.send_sem, self.recv_sem, self.used = send_sem, recv_sem, 0

    def send(self, src, dst, peer):
        i = self.used
        self.used += 1
        return send(src, dst, self.send_sem.at[i], self.recv_sem.at[i], peer)


def lanes_scratch(count):
    return [pltpu.SemaphoreType.DMA((count,)), pltpu.SemaphoreType.DMA((count,))]


def chip_peer(axis, step):
    return {axis: lax.rem(lax.axis_index(axis) + step + 4, 4)}


def greet_chips(barrier):
    for axis in ("x", "y"):
        for step in (1, 3):
            pl.semaphore_signal(
                barrier, inc=1, device_id=chip_peer(axis, step), device_id_type=MESH
            )
    return 4


def greet_column(barrier):
    for step in COLUMN:
        pl.semaphore_signal(barrier, inc=1, device_id=column_peer(*step), device_id_type=MESH)
    return len(COLUMN)


def partner():
    return {"l": 1 - lax.axis_index("l")}


def cross():
    return {"h": 1 - lax.axis_index("h"), "l": 1 - lax.axis_index("l")}


def other_core():
    return {"c": 1 - lax.axis_index("c")}


class ColumnRing:
    def __init__(self, lanes, rows_ref, out_ref):
        c, h, l = place()
        self.lanes, self.rows, self.out = lanes, rows_ref, out_ref
        half = rows_ref.shape[0] // 2
        self.first, self.second = pl.ds(0, half), pl.ds(half, half)
        self.at = {
            "own": c * 4 + h * 2 + l,
            "partner": c * 4 + h * 2 + 1 - l,
            "cross": c * 4 + (1 - h) * 2 + 1 - l,
            "far": c * 4 + (1 - h) * 2 + l,
        }
        self.shared = {}

    def share(self, which):
        block = self.out.at[self.at[which]]
        self.shared[which] = self.lanes.send(block, block, other_core())

    def half_to(self, part, peer):
        return self.lanes.send(self.rows.at[part], self.out.at[self.at["own"], part], peer)

    def start(self):
        self.partner_first = self.half_to(self.first, partner())
        self.cross_second = self.half_to(self.second, cross())
        self.partner_second = self.half_to(self.second, partner())
        self.cross_first = self.half_to(self.first, cross())
        here = self.out.at[self.at["own"]]
        self.shared["own"] = self.lanes.send(self.rows, here, other_core())

    def relay(self):
        self.partner_first.wait_recv()
        block = self.out.at[self.at["partner"], self.first]
        self.far_cross = self.lanes.send(block, block, cross())
        self.cross_second.wait_recv()
        block = self.out.at[self.at["cross"], self.second]
        self.far_partner = self.lanes.send(block, block, partner())

    def nearest(self):
        self.partner_second.wait_recv()
        self.share("partner")
        self.cross_first.wait_recv()
        self.share("cross")

    def far(self):
        self.far_cross.wait_recv()
        self.far_partner.wait_recv()
        self.share("far")

    def drain(self):
        for copy in (self.partner_first, self.partner_second, self.cross_first, self.cross_second):
            copy.wait_send()
        for copy in (self.far_cross, self.far_partner):
            copy.wait_send()
        for copy in self.shared.values():
            copy.wait_send()

    def finish(self):
        self.far()
        for copy in self.shared.values():
            copy.wait_recv()
        self.drain()


def chip_index(steps):
    x = lax.rem(lax.axis_index("x") + steps["x"] + 4, 4)
    y = lax.rem(lax.axis_index("y") + steps["y"] + 4, 4)
    return x * 4 + y


def shifted(columns, start, size):
    if columns == slice(None):
        return pl.ds(start, size)
    return pl.ds(start + columns.start, columns.size)


class ChipRing:
    def __init__(self, lanes, own, view, cut, width, a, b, hand_on):
        self.lanes, self.own, self.view = lanes, own, view
        self.low, self.high = pl.ds(0, cut), pl.ds(cut, width - cut)
        self.a, self.b, self.hand_on = a, b, hand_on
        self.sent, self.near, self.last = [], [], {}

    def ref(self, da, db, columns=slice(None)):
        return self.view(chip_index({self.a: da, self.b: db}), columns)

    def copy(self, src, dst, axis, step):
        made = self.lanes.send(src, dst, chip_peer(axis, step))
        self.sent.append(made)
        return made

    def share(self, da, db):
        if self.hand_on:
            block = self.ref(da, db)
            self.near.append(self.lanes.send(block, block, other_core()))

    def start(self):
        here = self.ref(0, 0)
        self.first = [self.copy(self.own, here, self.a, step) for step in (1, -1)]
        self.turn = {0: [self.copy(self.own, here, self.b, step) for step in (1, -1)]}
        if self.hand_on:
            self.near.append(self.lanes.send(self.own, here, other_core()))

    def pass_on(self, da):
        block = self.ref(da, 0)
        self.turn[da] = [self.copy(block, block, self.b, step) for step in (1, -1)]
        self.share(da, 0)

    def relay_first(self):
        for copy in self.first:
            copy.wait_recv()
        block = self.ref(-1, 0, self.low)
        one = self.copy(block, block, self.a, 1)
        block = self.ref(1, 0, self.high)
        self.second = [one, self.copy(block, block, self.a, -1)]
        self.pass_on(-1)
        self.pass_on(1)

    def relay_turn(self, da):
        for copy in self.turn[da]:
            copy.wait_recv()
        step = 1 if da in (0, -1) else -1
        block = self.ref(da, -step)
        self.last[da] = self.copy(block, block, self.b, step)
        self.share(da, 1)
        self.share(da, -1)

    def relay_second(self):
        for copy in self.second:
            copy.wait_recv()
        self.pass_on(2)

    def finish(self):
        for da in (0, -1, 1, 2):
            self.last[da].wait_recv()
            self.share(da, 2)

    def drain(self):
        for copy in self.sent:
            copy.wait_send()
        for copy in self.near:
            copy.wait()


class ChipSum:
    def __init__(self, lanes, view, cut, width, p, q, near_p, rest_p, near_q):
        self.lanes, self.view = lanes, view
        self.low, self.high = pl.ds(0, cut), pl.ds(cut, width - cut)
        self.p, self.q = p, q
        self.near_p, self.rest_p, self.near_q = near_p, rest_p, near_q
        self.sent = []

    def index(self, dp, dq):
        return chip_index({self.p: dp, self.q: dq})

    def copy(self, src, dst, axis, step):
        made = self.lanes.send(src, dst, chip_peer(axis, step))
        self.sent.append(made)
        return made

    def own(self, dp, dq, columns=slice(None)):
        return self.view(self.index(dp, dq), columns)

    def side(self, i, columns):
        return self.near_q.at[i, :, columns]

    def far(self):
        self.far_copies = {}
        for dq, step, i in ((2, 1, 0), (3, -1, 0), (1, 1, 1), (0, -1, 1)):
            direction = 0 if step == 1 else 1
            self.far_copies[direction, i] = self.copy(
                self.own(2, dq), self.near_p.at[direction, i], self.p, step
            )

    def plain(self):
        for dq, step in ((2, -1), (3, 1), (1, -1), (0, 1)):
            self.next_to(dq, step)

    def next_to(self, dq, step):
        direction = 0 if step == 1 else 1
        self.next_copies[direction, dq] = self.copy(
            self.own(step, dq), self.rest_p.at[direction, dq], self.p, step
        )

    def joined(self):
        self.next_copies = {}
        for dq, step, i in ((2, 1, 0), (3, -1, 0), (1, 1, 1), (0, -1, 1)):
            direction = 0 if step == 1 else 1
            self.far_copies[direction, i].wait_recv()
            mine = self.own(step, dq)
            mine[...] = mine[...] + self.near_p[direction, i]
            self.next_to(dq, step)

    def collect(self, dq):
        for direction in range(2):
            self.next_copies[direction, dq].wait_recv()
        mine = self.own(0, dq)
        total = mine[...].astype(f32)
        for direction in range(2):
            total = total + self.rest_p[direction, dq].astype(f32)
        mine[...] = total.astype(mine.dtype)

    def far_q(self):
        self.collect(2)
        self.far_q_copies = [
            self.copy(self.own(0, 2, self.low), self.side(0, self.low), self.q, 1),
            self.copy(self.own(0, 2, self.high), self.side(1, self.high), self.q, -1),
        ]

    def next_q(self):
        self.next_q_copies = []
        for i, (dq, columns) in enumerate(((1, self.low), (3, self.high))):
            self.collect(dq)
            self.far_q_copies[i].wait_recv()
            mine = self.own(0, dq, columns)
            mine[...] = mine[...] + self.side(i, columns)[...]
            self.next_q_copies.append(
                self.copy(self.own(0, dq), self.near_q.at[2 + i], self.q, 1 if i == 0 else -1)
            )

    def total(self):
        self.collect(0)
        total = self.own(0, 0)[...].astype(f32)
        for i in range(2):
            self.next_q_copies[i].wait_recv()
            total = total + self.near_q[2 + i].astype(f32)
        return total

    def drain(self):
        for copy in self.sent:
            copy.wait_send()


def ref_dot(a, b):
    return jnp.dot(a, b, preferred_element_type=f32)


def ref_dot_nt(a, b):
    return lax.dot_general(a, b, (((1,), (1,)), ((), ())), preferred_element_type=f32)


def ref_dot_tn(a, b):
    return lax.dot_general(a, b, (((0,), (0,)), ((), ())), preferred_element_type=f32)


def at(i, size):
    return pl.ds(pl.multiple_of(i * size, size), size)


def gain_rows(misc):
    pick = lax.broadcasted_iota(jnp.int32, (16, MISC), 0)
    pick = (pick == lax.broadcasted_iota(jnp.int32, (16, MISC), 1)).astype(f32).astype(bf16)
    return ref_dot_nt(pick, misc)


def turn(values, cosine, sine):
    return values * cosine + pltpu.roll(values, HEAD_SIZE // 2, 1) * sine


def turn_back(values, cosine, sine):
    return values * cosine - pltpu.roll(values, HEAD_SIZE // 2, 1) * sine


def fill_bias(bias, seg_column, seg_row, first):
    keys, queries = bias.shape
    chunk = 256

    def fill(i, carry):
        here = at(i, chunk)
        key = lax.broadcasted_iota(jnp.int32, (chunk, queries), 0) + i * chunk
        query = lax.broadcasted_iota(jnp.int32, (chunk, queries), 1) + first
        seen = (seg_column[here, :] == seg_row[...]) & (key <= query)
        bias[here, :] = jnp.where(seen, 0.0, NEG_FILL)
        return carry

    lax.fori_loop(0, keys // chunk, fill, 0)


KEYS = 128


def key_block(kv, i, k):
    per_block = kv.shape[1] // KEYS
    start = (k % per_block) * KEYS
    return kv[k // per_block, start : start + KEYS, i * HEAD_SIZE : (i + 1) * HEAD_SIZE]


class RowsRing:
    def __init__(self, lanes, rows_ref, out_ref):
        c, h, l = place()
        self.lanes, self.out, self.l = lanes, out_ref, l
        self.rows = rows_ref
        self.own = pl.ds((c * 2 + h) * 2, 2)
        self.here = c * 4 + h * 2 + l
        self.cross_at = c * 4 + (1 - h) * 2 + 1 - l
        self.far_at = c * 4 + (1 - h) * 2 + l
        self.shared = []

    def share(self, index):
        block = self.out.at[index]
        self.shared.append(self.lanes.send(block, block, other_core()))

    def start(self):
        size = self.rows.shape[1] // 4
        self.parts = [pl.ds(i * size, size) for i in range(4)]
        self.to_cross = [
            self.lanes.send(self.rows.at[self.l, some], self.out.at[self.here, some], cross())
            for some in self.parts
        ]
        self.shared.append(self.lanes.send(self.rows, self.out.at[self.own], other_core()))
        self.to_partner = []

    def relay(self, i):
        self.to_cross[i].wait_recv()
        block = self.out.at[self.cross_at, self.parts[i]]
        self.to_partner.append(self.lanes.send(block, block, partner()))

    def finish(self):
        self.share(self.cross_at)
        for copy in self.to_partner:
            copy.wait_recv()
        self.share(self.far_at)

    def drain(self):
        for copy in self.to_cross + self.to_partner:
            copy.wait_send()
        for copy in self.shared:
            copy.wait()


def attention_kernel(
    part,
    attn_ref,
    expert_ref,
    rows_ref,
    slots_ref,
    x_ref,
    cos_ref,
    sin_ref,
    seg_column,
    seg_row,
    named_ref,
    w_out,
    rows_out,
    slots_out,
    expert_out,
    expert_block,
    a_out,
    q_out,
    kv_out,
    o_out,
    lse_out,
    h1_out,
    b_out,
    gates_out,
    w,
    attn_in,
    expert_in,
    block,
    bias,
    value_turned,
    s_sem,
    r_sem,
    as_sem,
    ar_sem,
    own,
):
    c, h, l = place()
    z = h * 2 + l
    me = (c * 2 + h) * 2 + l
    rows, width = x_ref.shape
    q_half = w.shape[3] // 2 - (HEAD_SIZE * 2 + MISC) // 2
    kv_at, misc_at, out_at = q_half, q_half + 2 * HEAD_SIZE, q_half + 2 * HEAD_SIZE + MISC
    ff = expert_block.shape[2]
    barrier = pltpu.get_barrier_semaphore()
    pl.semaphore_wait(barrier, greet_column(barrier) + greet_chips(barrier))
    lanes = Lanes(s_sem, r_sem)

    slot = c * 2 + h
    here = pltpu.make_async_copy(attn_ref, attn_in.at[slot], own.at[1])
    there = pltpu.make_async_remote_copy(
        src_ref=attn_ref,
        dst_ref=attn_in.at[slot],
        send_sem=as_sem.at[0],
        recv_sem=ar_sem.at[slot],
        device_id=column_peer(1, 0),
        device_id_type=MESH,
    )
    pl.when(c == l)(here.start)
    pl.when(c != l)(there.start)
    for z_step in range(1, 4):
        to_z = lax.rem(z + z_step, 4)
        send(attn_ref, attn_in.at[slot], as_sem.at[z_step], ar_sem.at[slot], at_z(l, to_z))
    local = [
        pltpu.make_async_copy(expert_ref.at[me], expert_in.at[me], own.at[0]),
        pltpu.make_async_copy(slots_ref.at[me], slots_out.at[me], own.at[2]),
        pltpu.make_async_copy(rows_ref, rows_out.at[pl.ds((c * 2 + h) * 2, 2)], own.at[3]),
    ]
    for copy in local:
        copy.start()
    pieces = []
    for step in COLUMN:
        peer = column_peer(*step)
        to = (peer["c"] * 2 + peer["h"]) * 2 + peer["l"]
        pieces.append(lanes.send(expert_ref.at[to], expert_in.at[me], peer))
        pieces.append(lanes.send(slots_ref.at[to], slots_out.at[me], peer))
    fill_bias(bias, seg_column, seg_row, z * rows)

    for source in range(4):
        mine = (c == l) & (slot == source)

        def landed(source=source):
            pltpu.make_async_remote_copy(
                src_ref=attn_ref,
                dst_ref=attn_in.at[source],
                send_sem=as_sem.at[0],
                recv_sem=ar_sem.at[source],
                device_id=column_peer(1, 0),
                device_id_type=MESH,
            ).wait_recv()

        pl.when(jnp.logical_not(mine))(landed)
    pl.when(c == l)(here.wait)
    block[...] = jnp.concatenate(
        [attn_in[i].astype(f32)[:part] for i in range(4)], axis=0
    ).astype(block.dtype)
    index = chip_index({"x": 0, "y": 0})
    keep = [pltpu.make_async_copy(block, w.at[c, index], own.at[4])]
    keep[0].start()
    half = block.shape[0] // 2
    rings = {}
    for name, start, size, cut in (("in", 0, out_at, 640), ("out", out_at, q_half, 384)):
        rings[name] = []
        for low, a, b in ((0, "x", "y"), (half, "y", "x")):
            mine = pl.ds(low, half)

            def view(index, columns, mine=mine, start=start, size=size):
                return w.at[c, index, mine, shifted(columns, start, size)]

            own_part = block.at[mine, pl.ds(start, size)]
            rings[name].append(ChipRing(lanes, own_part, view, cut, size, a, b, True))
    rings["expert"] = []
    for low, a, b in ((0, "x", "y"), (half, "y", "x")):
        mine = pl.ds(low, half)

        def expert_view(index, columns, mine=mine):
            return expert_out.at[index, mine, columns]

        own_part = expert_block.at[2, mine]
        rings["expert"].append(
            ChipRing(lanes, own_part, expert_view, ff // 2, ff, a, b, False)
        )

    def go(name, step, *args):
        for ring in rings[name]:
            getattr(ring, step)(*args)

    go("in", "start")
    rows_ring = RowsRing(lanes, rows_ref, rows_out)
    rows_ring.start()

    local[0].wait()
    for copy in pieces:
        copy.wait()
    for i in range(3):
        for l_side in range(2):
            expert_block[i, :, l_side * 384 : (l_side + 1) * 384] = jnp.concatenate(
                [expert_in[2 * j + l_side, i].astype(f32)[:part] for j in range(4)], axis=0
            ).astype(bf16)
    keep.append(pltpu.make_async_copy(expert_block.at[2], expert_out.at[index], own.at[0]))
    keep[1].start()

    go("in", "relay_first")
    go("in", "relay_turn", 0)
    go("in", "relay_second")
    rows_ring.relay(0)
    go("out", "start")
    go("in", "relay_turn", -1)
    rows_ring.relay(1)
    go("in", "relay_turn", 1)
    rows_ring.relay(2)
    go("in", "relay_turn", 2)
    go("out", "relay_first")
    rows_ring.relay(3)
    go("in", "finish")
    go("expert", "start")
    go("out", "relay_turn", 0)
    go("out", "relay_second")
    for ring in rings["in"]:
        for copy in ring.near:
            copy.wait_recv()

    keep[0].wait()

    def projection(i, columns):
        return w[i, :, :, columns].reshape(width, -1)

    scale = HEAD_SIZE ** (-0.5)
    misc = projection(0, slice(misc_at, out_at))
    gains = gain_rows(misc)
    chunk = 32

    def norm(i, carry):
        here = at(i, chunk)
        x = x_ref[here, :].astype(f32)
        inverse = lax.rsqrt(jnp.mean(x * x, axis=1, keepdims=True) + EPS)
        a_out[here, :] = (x * inverse * gains[8:9, :]).astype(bf16)
        return carry

    lax.fori_loop(0, rows // chunk, norm, 0)
    cosine, sine = cos_ref[...], sin_ref[...]
    sends = []
    for i in range(2):
        kv = ref_dot(a_out[...], projection(i, slice(kv_at, misc_at)))
        kv_out[z, :, i * 128 : (i + 1) * 128] = turn(kv[:, :128], cosine, sine).astype(bf16)
        kv_out[z, :, (2 + i) * 128 : (3 + i) * 128] = kv[:, 128:].astype(bf16)
    for step in ALONG_Z:
        sends.append(lanes.send(kv_out.at[z], kv_out.at[z], column_peer(*step)))
    go("out", "relay_turn", -1)
    go("out", "relay_turn", 1)
    for i in range(2):

        def project(j, carry, i=i):
            q = ref_dot(a_out[...], w[i, :, :, at(j, 256)].reshape(width, 256))
            q_out[i * GROUP + 2 * j] = turn(q[:, :128], cosine, sine).astype(bf16)
            q_out[i * GROUP + 2 * j + 1] = turn(q[:, 128:], cosine, sine).astype(bf16)
            return carry

        lax.fori_loop(0, q_half // 256, project, 0)
    go("out", "relay_turn", 2)
    go("expert", "relay_first")
    for copy in sends:
        copy.wait_recv()
    rows_ring.finish()
    keys_count = 4 * rows
    for i in range(2):
        values = kv_out[:, :, (2 + i) * 128 : (3 + i) * 128].reshape(keys_count, HEAD_SIZE)
        value_turned[...] = values.T

        def attend(j, carry, i=i):
            keys = kv_out[:, :, i * 128 : (i + 1) * 128].reshape(keys_count, HEAD_SIZE)
            scores = ref_dot_nt(keys, q_out[i * GROUP + j]) * scale + bias[...]
            peak = jnp.max(scores, axis=0, keepdims=True)
            expo = jnp.exp(scores - peak)
            total = jnp.sum(expo, axis=0, keepdims=True)
            weights = (expo * (1.0 / total)).astype(bf16)
            mixed = ref_dot(value_turned[...], weights)
            o_out[:, at(i * GROUP + j, HEAD_SIZE)] = mixed.T.astype(bf16)
            lse_out[i * GROUP + j] = peak + jnp.log(total)
            return carry

        for some in range(2):
            lax.fori_loop(some * GROUP // 2, (some + 1) * GROUP // 2, attend, 0)
            if (i, some) == (0, 0):
                go("out", "finish")
                go("expert", "relay_turn", 0)
            elif (i, some) == (0, 1):
                go("expert", "relay_second")
            elif (i, some) == (1, 0):
                go("expert", "relay_turn", -1)
    for ring in rings["out"]:
        for copy in ring.near:
            copy.wait_recv()
    keep.append(pltpu.make_async_copy(w, w_out, own.at[1]))
    keep[2].start()

    def leave(j, carry):
        here = at(j, 384)
        u = ref_dot_nt(
            o_out[:, :q_half], w[0, pl.ds(4 * j, 4), :, out_at:].reshape(384, q_half)
        )
        u = u + ref_dot_nt(
            o_out[:, q_half:], w[1, pl.ds(4 * j, 4), :, out_at:].reshape(384, q_half)
        )
        h1_out[:, here] = x_ref[:, here].astype(f32) + u
        return carry

    lax.fori_loop(0, width // 384, leave, 0)
    go("expert", "relay_turn", 1)

    def second(i, carry):
        here = at(i, chunk)
        h1 = h1_out[here, :]
        inverse = lax.rsqrt(jnp.mean(h1 * h1, axis=1, keepdims=True) + EPS)
        b_out[here, :] = (h1 * inverse * gains[9:10, :]).astype(bf16)
        return carry

    lax.fori_loop(0, rows // chunk, second, 0)
    logits = ref_dot(b_out[...], misc).T[:8]
    named = named_ref[...] > 0
    masked = jnp.where(named, logits, NEG_FILL)
    expo = jnp.where(named, jnp.exp(masked - jnp.max(masked, axis=0, keepdims=True)), 0.0)
    gates = expo / jnp.sum(expo, axis=0, keepdims=True)
    for e in range(8):
        gates_out[e] = gates[e : e + 1]
    go("expert", "relay_turn", 2)
    go("expert", "finish")
    for copy in sends:
        copy.wait_send()
    rows_ring.drain()
    for copy in local[1:]:
        copy.wait()
    pl.when(c != l)(there.wait_send)
    for z_step in range(1, 4):
        pltpu.make_async_remote_copy(
            src_ref=attn_ref,
            dst_ref=attn_in.at[slot],
            send_sem=as_sem.at[z_step],
            recv_sem=ar_sem.at[slot],
            device_id=column_peer(0, z_step),
            device_id_type=MESH,
        ).wait_send()
    for name in ("in", "out"):
        for ring in rings[name]:
            for copy in ring.near:
                copy.wait_send()
            for copy in ring.sent:
                copy.wait_send()
    go("expert", "drain")
    for copy in keep[1:]:
        copy.wait()


def attention(attn_block, expert_pieces, upstream, slots, x, cosine, sine, seg_column, seg_row, named, part):
    rows, width = x.shape
    keys = 4 * rows
    w_width = attn_block.shape[1]
    ff = 2 * expert_pieces.shape[3]
    sds = jax.ShapeDtypeStruct
    return pl.pallas_call(
        functools.partial(attention_kernel, part),
        name="attention",
        out_shape=(
            sds((2, 16, 4 * part, w_width), bf16),
            sds((8, rows, width), bf16),
            sds(slots.shape, f32),
            sds((16, 4 * part, ff), bf16),
            sds((3, 4 * part, ff), bf16),
            sds((rows, width), bf16),
            sds((QUERY_HEADS, rows, HEAD_SIZE), bf16),
            sds((4, rows, 4 * HEAD_SIZE), bf16),
            sds((rows, QUERY_HEADS * HEAD_SIZE), bf16),
            sds((QUERY_HEADS, 1, rows), f32),
            sds((rows, width), f32),
            sds((rows, width), bf16),
            sds((8, 1, rows), f32),
        ),
        in_specs=[VMEM] * 10,
        out_specs=(HBM,) * 4 + (VMEM,) * 9,
        scratch_shapes=[
            pltpu.VMEM((2, 16, 4 * part, w_width), bf16),
            pltpu.VMEM((4,) + attn_block.shape, bf16),
            pltpu.VMEM(expert_pieces.shape, bf16),
            pltpu.VMEM((4 * part, w_width), bf16),
            pltpu.VMEM((keys, rows), f32),
            pltpu.VMEM((HEAD_SIZE, keys), bf16),
        ]
        + lanes_scratch(250)
        + [
            pltpu.SemaphoreType.DMA((4,)),
            pltpu.SemaphoreType.DMA((4,)),
            pltpu.SemaphoreType.DMA((5,)),
        ],
        compiler_params=pltpu.CompilerParams(
            collective_id=2, has_side_effects=True, vmem_limit_bytes=60 * 2**20
        ),
    )(attn_block, expert_pieces, upstream, slots, x, cosine, sine, seg_column, seg_row, named)


def attention_back_kernel(
    back_ref,
    gate_back_ref,
    gates_ref,
    b_ref,
    h1_ref,
    x_ref,
    g_ref,
    a_ref,
    o_ref,
    q_ref,
    kv_ref,
    lse_ref,
    cos_ref,
    sin_ref,
    seg_column,
    seg_row,
    w_ref,
    parts_ref,
    expert_ref,
    grad_in,
    out_sum,
    tokens_out,
    block_out,
    block_half,
    pieces_out,
    w,
    bias,
    key_turned,
    dh1,
    da,
    du,
    do,
    back_rows,
    key_sum,
    value_sum,
    probs,
    probs_back,
    probs_low,
    scores_back,
    kv_send,
    kv_held,
    stage_in,
    stage_out,
    misc_grad,
    parts,
    near,
    far,
    nearest,
    terms,
    near_p0,
    rest_p0,
    near_q0,
    near_p1,
    rest_p1,
    near_q1,
    out_terms,
    out_near_p0,
    out_rest_p0,
    out_near_q0,
    out_near_p1,
    out_rest_p1,
    out_near_q1,
    s_sem,
    r_sem,
    w_sem,
    stage_in_sem,
    own,
):
    c, h, l = place()
    z = h * 2 + l
    rows, width = x_ref.shape
    q_half = o_ref.shape[1] // 2
    misc_at, out_at = q_half + 2 * HEAD_SIZE, q_half + 2 * HEAD_SIZE + MISC

    def load(start, size, to, i):
        return pltpu.make_async_copy(
            w_ref.at[:, :, pl.ds(start, size)], w.at[:, :, pl.ds(to, size)], w_sem.at[i]
        )

    loads = [load(misc_at, MISC, misc_at, 0), load(out_at, q_half, 0, 1), load(0, misc_at, 0, 2)]
    loads[0].start()
    loads[1].start()
    terms_load = pltpu.make_async_copy(expert_ref, terms, own.at[1])
    terms_load.start()
    parts_load = pltpu.make_async_copy(parts_ref.at[pl.ds(c * 4, 4)], parts, own.at[0])
    parts_load.start()
    back_load = pltpu.make_async_copy(back_ref, da, own.at[2])
    back_load.start()
    barrier = pltpu.get_barrier_semaphore()
    pl.semaphore_wait(barrier, greet_column(barrier) + greet_chips(barrier))
    lanes = Lanes(s_sem, r_sem)
    part, ff = terms.shape[2] // 4, terms.shape[3]
    sums = []
    for weight in range(3):
        for low, p, q, held in (
            (0, "y", "x", (near_p0, rest_p0, near_q0)),
            (2 * part, "x", "y", (near_p1, rest_p1, near_q1)),
        ):

            def view(index, columns, mine=pl.ds(low, 2 * part), weight=weight):
                return terms.at[index, weight, mine, columns]

            held = [buffer.at[weight] for buffer in held]
            sums.append(ChipSum(lanes, view, ff // 2, ff, p, q, *held))
    out_sums = []
    for low, p, q, held in (
        (0, "y", "x", (out_near_p0, out_rest_p0, out_near_q0)),
        (2 * part, "x", "y", (out_near_p1, out_rest_p1, out_near_q1)),
    ):

        def out_view(index, columns, mine=pl.ds(low, 2 * part)):
            return out_terms.at[index, mine, columns]

        out_sums.append(ChipSum(lanes, out_view, q_half // 2, q_half, p, q, *held))
    places = {
        "own": z,
        "partner": h * 2 + 1 - l,
        "cross": (1 - h) * 2 + 1 - l,
        "far": (1 - h) * 2 + l,
    }
    near_copies = {
        which: lanes.send(
            parts_ref.at[(1 - c) * 4 + places[which]], near.at[places[which]], other_core()
        )
        for which in ("far", "cross", "partner", "own")
    }
    scale = HEAD_SIZE ** (-0.5)
    fill_bias(bias, seg_column, seg_row, z * rows)

    def add_near(which):
        near_copies[which].wait_recv()
        k = places[which]

        def add(i, carry):
            here = at(i, 64)
            parts[k, here] = parts[k, here] + near[k, here]
            return carry

        lax.fori_loop(0, rows // 64, add, 0)

    half = rows // 2
    first, second = pl.ds(0, half), pl.ds(half, half)

    def part_at(which, some):
        return parts.at[places[which], some]

    terms_load.wait()
    for each in sums:
        each.far()
    parts_load.wait()
    add_near("far")
    far_partner = lanes.send(part_at("far", first), far.at[0], partner())
    far_cross = lanes.send(part_at("far", second), far.at[1], cross())
    add_near("cross")
    add_near("partner")
    early_cross = lanes.send(part_at("cross", second), nearest.at[1, second], cross())
    early_partner = lanes.send(part_at("partner", first), nearest.at[0, first], partner())
    add_near("own")

    loads[0].wait()
    loads[1].wait()
    misc = w[0, :, misc_at:out_at]
    gains = gain_rows(misc)
    gates = jnp.concatenate([gates_ref[e] for e in range(8)], axis=0)
    gate_back = jnp.concatenate([gate_back_ref[e] for e in range(8)], axis=0)
    mean = jnp.sum(gates * gate_back, axis=0, keepdims=True)
    logit_grad = gates * (gate_back - mean)
    logit_grad = jnp.concatenate(
        [logit_grad, jnp.zeros((MISC - 8, rows), f32)], axis=0
    ).T.astype(bf16)
    chunk = 32

    def norm_back(i, carry):
        mix_sum = carry
        here = at(i, chunk)
        h1 = h1_ref[here, :]
        inverse = lax.rsqrt(jnp.mean(h1 * h1, axis=1, keepdims=True) + EPS)
        db = da[here, :] + dh1[here, :]
        mix_sum = mix_sum + jnp.sum(db * h1 * inverse, axis=0, keepdims=True)
        dz = db * gains[9:10, :]
        mean = jnp.mean(dz * h1, axis=1, keepdims=True)
        value = g_ref[here, :].astype(f32) + inverse * dz - h1 * (inverse * inverse * inverse * mean)
        dh1[here, :] = value
        du[here, :] = value.astype(bf16)
        return mix_sum

    dh1[...] = ref_dot_nt(logit_grad, misc)
    back_load.wait()
    mix_sum = lax.fori_loop(0, rows // chunk, norm_back, jnp.zeros((1, width), f32))
    misc_grad[...] = ref_dot_tn(b_ref[...], logit_grad)

    def project(i, carry):
        columns = at(i, 256)
        for g in range(2):
            do[g, :, columns] = ref_dot(du[...], w[g, :, columns]).astype(bf16)
        return carry

    lax.fori_loop(0, q_half // 256, project, 0)
    loads[2].start()

    far_partner.wait_recv()
    mine = part_at("cross", first)
    mine[...] = mine[...] + far[0]
    late_cross = lanes.send(mine, nearest.at[1, first], cross())
    far_cross.wait_recv()
    mine = part_at("partner", second)
    mine[...] = mine[...] + far[1]
    late_partner = lanes.send(mine, nearest.at[0, second], partner())

    def add_block():
        for copy in (early_partner, early_cross, late_cross, late_partner):
            copy.wait_recv()

        def add_up(i, carry):
            here = at(i, 64)
            value = parts[z, here].astype(f32)
            value = value + nearest[0, here].astype(f32) + nearest[1, here].astype(f32)
            block_out[here, :] = (h1_ref[here, :] + value).astype(bf16)
            return carry

        lax.fori_loop(0, rows // 64, add_up, 0)
        return lanes.send(block_out.at[first], block_half, partner())

    for each in sums:
        each.joined()
    for each in sums:
        each.plain()

    size = 4 * 4 * part

    def out_grad(g, i):
        columns = pl.ds(pl.multiple_of(g * q_half, q_half), q_half)
        grad = ref_dot_tn(du[:, i * size : (i + 1) * size], o_ref[:, columns])
        return grad.astype(bf16).reshape(4, 4 * part, q_half)

    out_sends = []
    for i in range(4):
        if i >= 2:
            out_sends[i - 2].wait_send()
        stage_out[i % 2] = out_grad(1 - c, i)
        out_sends.append(
            lanes.send(stage_out.at[i % 2], out_terms.at[pl.ds(4 * i, 4)], other_core())
        )
    for i in range(4):
        mine = out_grad(c, i)
        out_sends[i].wait_recv()
        out_terms[4 * i : 4 * i + 4] = out_terms[4 * i : 4 * i + 4] + mine
    for each in out_sums:
        each.far()

    keys_count = 4 * rows
    kv_sends = []

    def returned(each):
        total = each.total()
        weight, first_block = sums.index(each) // 2, 2 * (sums.index(each) % 2)
        for i in range(2):
            for side in range(2):
                to = 2 * (first_block + i) + side
                pieces_out[to, weight, :part] = total[
                    i * part : (i + 1) * part, side * ff // 2 : (side + 1) * ff // 2
                ].astype(bf16)
                pieces_out[to, weight, part:] = jnp.zeros((PAD - part, ff // 2), bf16)

    cosine, sine = cos_ref[...], sin_ref[...]
    for g in range(2):
        key_turned[...] = (
            kv_ref[:, :, g * 128 : (g + 1) * 128].reshape(keys_count, HEAD_SIZE).T
        )
        key_sum[...] = jnp.zeros_like(key_sum)
        value_sum[...] = jnp.zeros_like(value_sum)

        def head_back(j, carry, g=g):
            columns = at(j, HEAD_SIZE)
            query = q_ref[g * GROUP + j]
            out_back = do[g, :, columns]
            shift = lse_ref[g * GROUP + j]
            row_dot = jnp.zeros((8, rows), f32)
            for k in range(keys_count // KEYS):
                here = slice(k * KEYS, (k + 1) * KEYS)
                value = ref_dot_nt(key_block(kv_ref, g, k), query) * scale + bias[here, :]
                prob = jnp.exp(value - shift)
                prob_back = ref_dot_nt(key_block(kv_ref, 2 + g, k), out_back)
                probs[here, :] = prob
                probs_back[here, :] = prob_back
                probs_low[here, :] = prob.astype(bf16)
                product = (prob * prob_back).reshape(KEYS // 8, 8, rows)
                row_dot = row_dot + jnp.sum(product, axis=0)
            row_dot = jnp.sum(row_dot, axis=0, keepdims=True)
            for k in range(keys_count // KEYS):
                here = slice(k * KEYS, (k + 1) * KEYS)
                value = probs[here, :] * (probs_back[here, :] - row_dot)
                scores_back[here, :] = value.astype(bf16)
            value_sum[...] += ref_dot(probs_low[...], out_back)
            key_sum[...] += ref_dot(scores_back[...], query)
            query_back = (ref_dot(key_turned[...], scores_back[...]) * scale).T
            back_rows[g, :, columns] = turn_back(query_back, cosine, sine).astype(bf16)
            return carry

        lax.fori_loop(0, GROUP // 2, head_back, 0)
        if g == 0:
            for each in sums:
                each.far_q()
            for each in out_sums:
                each.joined()
            for each in out_sums:
                each.plain()
        else:
            for each in out_sums:
                each.next_q()
            for each in sums:
                returned(each)
        lax.fori_loop(GROUP // 2, GROUP, head_back, 0)
        if g == 0:
            for each in sums:
                each.next_q()
            for each in out_sums:
                each.far_q()
        kv_send[g, :, :, :128] = (key_sum[...] * scale).astype(bf16).reshape(4, rows, 128)
        kv_send[g, :, :, 128:] = value_sum[...].astype(bf16).reshape(4, rows, 128)
        for i, step in enumerate(ALONG_Z):
            to = lax.rem(z + step[1], 4)
            kv_sends.append(lanes.send(kv_send.at[g, to], kv_held.at[g, i], column_peer(*step)))

    block_send = add_block()
    for i in range(2):
        out_sum[2 * part * i : 2 * part * (i + 1)] = out_sums[i].total()
    loads[2].wait()
    for copy in kv_sends:
        copy.wait_recv()
    for g in range(2):
        own_part = kv_send[g, z].astype(f32)
        for i in range(3):
            own_part = own_part + kv_held[g, i].astype(f32)
        back_rows[g, :, q_half : q_half + 128] = turn_back(
            own_part[:, :128], cosine, sine
        ).astype(bf16)
        back_rows[g, :, q_half + 128 :] = own_part[:, 128:].astype(bf16)

    def input_back(i, carry):
        here = at(i, 512)
        value = ref_dot_nt(back_rows[0], w[0, here, :misc_at])
        da[:, here] = value + ref_dot_nt(back_rows[1], w[1, here, :misc_at])
        return carry

    lax.fori_loop(0, width // 512, input_back, 0)

    def first_back(i, carry):
        here = at(i, chunk)
        x = x_ref[here, :].astype(f32)
        inverse = lax.rsqrt(jnp.mean(x * x, axis=1, keepdims=True) + EPS)
        back = da[here, :]
        carry = carry + jnp.sum(back * x * inverse, axis=0, keepdims=True)
        dz = back * gains[8:9, :]
        mean = jnp.mean(dz * x, axis=1, keepdims=True)
        value = dh1[here, :] + inverse * dz - x * (inverse * inverse * inverse * mean)
        tokens_out[here, :] = value.astype(bf16)
        return carry

    attn_sum = lax.fori_loop(0, rows // chunk, first_back, jnp.zeros((1, width), f32))
    number = lax.broadcasted_iota(jnp.int32, (MISC, width), 0)
    gain_grads = jnp.where(number == 8, attn_sum, jnp.where(number == 9, mix_sum, 0.0))
    misc_grad[...] += gain_grads.T

    def stage_in_copy(g, i, slot):
        return pltpu.make_async_copy(
            stage_in.at[slot], grad_in.at[g, at(i, 256)], stage_in_sem.at[slot]
        )

    for g in range(2):

        def in_grad(i, carry, g=g):
            slot = lax.rem(i, 2)
            here = at(i, 256)

            @pl.when(i >= 2)
            def _():
                stage_in_copy(g, i - 2, slot).wait()

            stage_in[slot, :, :misc_at] = ref_dot_tn(a_ref[:, here], back_rows[g]).astype(bf16)
            if g == 0:
                stage_in[slot, :, misc_at:] = misc_grad[here, :].astype(bf16)
            else:
                stage_in[slot, :, misc_at:] = jnp.zeros((256, MISC), bf16)
            stage_in_copy(g, i, slot).start()
            return carry

        lax.fori_loop(0, width // 256, in_grad, 0)
        for i in range(2):
            stage_in_copy(g, width // 256 - 2 + i, i).wait()
    block_send.wait()
    for each in sums + out_sums:
        each.drain()
    for copy in out_sends[2:]:
        copy.wait_send()
    for copy in kv_sends:
        copy.wait_send()
    for copy in near_copies.values():
        copy.wait_send()
    for copy in (early_partner, early_cross, late_cross, late_partner, far_partner, far_cross):
        copy.wait_send()


def attention_back(
    back, gate_back, gates, b, h1, x, g, a, o, q, kv, lse, cosine, sine, seg_column, seg_row, w_attn, parts, expert_grads
):
    rows, width = x.shape
    keys = 4 * rows
    q_half = o.shape[1] // 2
    qkv = q_half + 2 * HEAD_SIZE
    sds = jax.ShapeDtypeStruct
    count, block_rows, ff = expert_grads.shape[1:]
    half_block = (block_rows // 2, ff)
    ring = [
        pltpu.VMEM((count, 2, 2) + half_block, bf16),
        pltpu.VMEM((count, 2, 4) + half_block, bf16),
        pltpu.VMEM((count, 4) + half_block, bf16),
    ]
    out_half = (block_rows // 2, q_half)
    out_ring = [
        pltpu.VMEM((2, 2) + out_half, bf16),
        pltpu.VMEM((2, 4) + out_half, bf16),
        pltpu.VMEM((4,) + out_half, bf16),
    ]
    return pl.pallas_call(
        attention_back_kernel,
        name="attention_back",
        out_shape=(
            sds((2, width, qkv + MISC), bf16),
            sds((block_rows, q_half), f32),
            sds((rows, width), bf16),
            sds((rows, width), bf16),
            sds((rows // 2, width), bf16),
            sds((8, count, PAD, ff // 2), bf16),
        ),
        in_specs=[ANY] + [VMEM] * 15 + [ANY, ANY, ANY],
        out_specs=(HBM, VMEM, VMEM, VMEM, VMEM, VMEM),
        scratch_shapes=[
            pltpu.VMEM((2, width, qkv + MISC), bf16),
            pltpu.VMEM((keys, rows), f32),
            pltpu.VMEM((HEAD_SIZE, keys), bf16),
            pltpu.VMEM((rows, width), f32),
            pltpu.VMEM((rows, width), f32),
            pltpu.VMEM((rows, width), bf16),
            pltpu.VMEM((2, rows, q_half), bf16),
            pltpu.VMEM((2, rows, qkv), bf16),
            pltpu.VMEM((keys, HEAD_SIZE), f32),
            pltpu.VMEM((keys, HEAD_SIZE), f32),
            pltpu.VMEM((keys, rows), f32),
            pltpu.VMEM((keys, rows), f32),
            pltpu.VMEM((keys, rows), bf16),
            pltpu.VMEM((keys, rows), bf16),
            pltpu.VMEM((2, 4, rows, 2 * HEAD_SIZE), bf16),
            pltpu.VMEM((2, 3, rows, 2 * HEAD_SIZE), bf16),
            pltpu.VMEM((2, 256, qkv + MISC), bf16),
            pltpu.VMEM((2, 4, block_rows, q_half), bf16),
            pltpu.VMEM((width, MISC), f32),
            pltpu.VMEM((4, rows, width), bf16),
            pltpu.VMEM((4, rows, width), bf16),
            pltpu.VMEM((2, rows // 2, width), bf16),
            pltpu.VMEM((2, rows, width), bf16),
            pltpu.VMEM(expert_grads.shape, bf16),
        ]
        + ring
        + ring
        + [pltpu.VMEM((16, block_rows, q_half), bf16)]
        + out_ring
        + out_ring
        + lanes_scratch(180)
        + [
            pltpu.SemaphoreType.DMA((3,)),
            pltpu.SemaphoreType.DMA((2,)),
            pltpu.SemaphoreType.DMA((3,)),
        ],
        compiler_params=pltpu.CompilerParams(
            collective_id=3, has_side_effects=True, vmem_limit_bytes=62 * 2**20
        ),
    )(
        back, gate_back, gates, b, h1, x, g, a, o, q, kv, lse, cosine, sine, seg_column, seg_row, w_attn, parts, expert_grads
    )


def experts_kernel(
    rows_ref,
    gate_ref,
    grads_ref,
    slot_rows,
    slot_columns,
    down_ref,
    block_ref,
    mix_out,
    weight_grads,
    back_out,
    gate_back_out,
    rows_all,
    held,
    w_gate,
    w_up,
    w_down,
    picked,
    picked_grads,
    hidden_back,
    hidden_gated,
    gate_low,
    up_low,
    mix_stage,
    near,
    far,
    nearest,
    gates_in,
    gate_back,
    s_sem,
    r_sem,
    own,
    stage_sem,
    near_send,
    near_recv,
):
    c, h, l = place()
    me = (c * 2 + h) * 2 + l
    barrier = pltpu.get_barrier_semaphore()
    pl.semaphore_wait(barrier, greet_column(barrier) + greet_chips(barrier))
    lanes = Lanes(s_sem, r_sem)
    rows, width = rows_ref.shape
    slots = picked.shape[1]
    ff = w_gate.shape[2]
    block = 2 * rows

    ring = ColumnRing(lanes, rows_ref, rows_all)
    ring.start()
    index = chip_index({"x": 0, "y": 0})
    half = block_ref.shape[1] // 2
    weight_rings = []
    for weight, target in ((0, w_gate), (1, w_up)):
        for low, a, b in ((0, "x", "y"), (half, "y", "x")):
            mine = pl.ds(low, half)

            def view(index, columns, mine=mine, target=target):
                return target.at[index, mine, columns]

            own_part = block_ref.at[weight, mine]
            weight_rings.append(ChipRing(lanes, own_part, view, ff // 2, ff, a, b, False))

    def go(step, *args):
        for each in weight_rings:
            getattr(each, step)(*args)

    go("start")
    local = [
        pltpu.make_async_copy(grads_ref, held, own.at[0]),
        pltpu.make_async_copy(down_ref, w_down, own.at[1]),
        pltpu.make_async_copy(block_ref.at[0], w_gate.at[index], own.at[2]),
        pltpu.make_async_copy(block_ref.at[1], w_up.at[index], own.at[3]),
        pltpu.make_async_copy(rows_ref, rows_all.at[me], own.at[4]),
        pltpu.make_async_copy(gate_ref.at[me], gates_in.at[me], own.at[5]),
    ]
    for copy in local:
        copy.start()
    gate_copies = []
    for step in COLUMN:
        peer = column_peer(*step)
        to = (peer["c"] * 2 + peer["h"]) * 2 + peer["l"]
        gate_copies.append(lanes.send(gate_ref.at[to], gates_in.at[me], peer))

    def pick_of(k):
        number = lax.broadcasted_iota(jnp.int32, (slots, block), 0).astype(f32)
        return slot_rows[k] == number

    def spread_of(k):
        number = lax.broadcasted_iota(jnp.int32, (block, slots), 1).astype(f32)
        return (slot_columns[k] == number).astype(f32).astype(bf16)

    def low(mask):
        return mask.astype(f32).astype(bf16)

    def columns_of(weight, columns):
        return weight[:, :, columns].reshape(width, narrow)

    def rows_of(weight, i):
        return weight[pl.ds(8 * i, 8)].reshape(ff, ff)

    wide = 512
    narrow = 256

    local[0].wait()
    local[1].wait()

    def prepare(k, carry):
        pick = low(pick_of(k))

        def gather(i, carry):
            columns = at(i, wide)
            values = ref_dot(pick, held[pl.ds(2 * k, 2), :, columns].reshape(block, wide))
            picked_grads[k, :, columns] = values.astype(bf16)
            return carry

        lax.fori_loop(0, width // wide, gather, 0)

        def down(i, carry):
            columns = at(i, narrow)
            hidden_back[k, :, columns] = ref_dot(picked_grads[k], columns_of(w_down, columns))
            return carry

        lax.fori_loop(0, ff // narrow, down, 0)
        return carry

    lax.fori_loop(0, 2, prepare, 0)
    go("relay_first")
    go("relay_turn", 0)
    ring.relay()
    go("relay_second")
    lax.fori_loop(2, 4, prepare, 0)
    go("relay_turn", -1)
    go("relay_turn", 1)
    ring.nearest()
    go("relay_turn", 2)
    go("finish")
    for copy in local[2:]:
        copy.wait()
    for copy in gate_copies:
        copy.wait()
    ring.shared["own"].wait_recv()
    ring.shared["partner"].wait_recv()

    def expert(k, stage):
        pick = pick_of(k)
        pick_low = low(pick)
        spread = spread_of(k)
        gates = gates_in[pl.ds(2 * k, 2)]
        gate_row = jnp.concatenate([gates[0], gates[1]], axis=1)
        gate = jnp.sum(jnp.where(pick, gate_row, 0.0), axis=1, keepdims=True)

        def gather(i, carry):
            columns = at(i, wide)
            values = ref_dot(pick_low, rows_all[pl.ds(2 * k, 2), :, columns].reshape(block, wide))
            picked[k, :, columns] = values.astype(bf16)
            return carry

        lax.fori_loop(0, width // wide, gather, 0)

        def hide(i, total):
            columns = at(i, narrow)
            gate_act = ref_dot(picked[k], columns_of(w_gate, columns))
            up_act = ref_dot(picked[k], columns_of(w_up, columns))
            back = hidden_back[k, :, columns]
            sigmoid_act = 1.0 / (1.0 + jnp.exp(-gate_act))
            silu_act = gate_act * sigmoid_act
            hidden = silu_act * up_act
            hidden_gated[k, :, columns] = (hidden * gate).astype(bf16)
            total = total + jnp.sum(hidden * back, axis=1, keepdims=True)
            back = back * gate
            slope = sigmoid_act * (1.0 + gate_act * (1.0 - sigmoid_act))
            gate_low[k, :, columns] = (back * up_act * slope).astype(bf16)
            up_low[k, :, columns] = (back * silu_act).astype(bf16)
            return total

        gate_slots = lax.fori_loop(0, ff // narrow, hide, jnp.zeros((slots, 1), f32))
        back_row = jnp.sum(jnp.where(pick, gate_slots, 0.0), axis=0, keepdims=True)
        gate_back[2 * k] = back_row[:, :rows]
        gate_back[2 * k + 1] = back_row[:, rows:]

        def leave(i, carry):
            columns = at(i, ff)
            out = ref_dot_nt(hidden_gated[k], rows_of(w_down, i)).astype(bf16)
            mix_stage[stage, :, :, columns] = (
                ref_dot(spread, out).astype(bf16).reshape(2, rows, ff)
            )
            back = ref_dot_nt(gate_low[k], rows_of(w_gate, i))
            back = (back + ref_dot_nt(up_low[k], rows_of(w_up, i))).astype(bf16)
            held[pl.ds(2 * k, 2), :, columns] = (
                ref_dot(spread, back).astype(bf16).reshape(2, rows, ff)
            )
            return carry

        lax.fori_loop(0, width // ff, leave, 0)

    def stage_copy(k, stage):
        return pltpu.make_async_copy(
            mix_stage.at[stage], mix_out.at[pl.ds(2 * k, 2)], stage_sem.at[stage]
        )

    def near_copy(side, i):
        return pltpu.make_async_remote_copy(
            src_ref=held.at[pl.ds(((1 - c) * 2 + side) * 2, 2)],
            dst_ref=near.at[pl.ds(side * 2, 2)],
            send_sem=near_send.at[i],
            recv_sem=near_recv.at[i],
            device_id=other_core(),
            device_id_type=MESH,
        )

    def add_near(z):
        mine = held.at[c * 4 + z]

        def add(i, carry):
            here = at(i, 64)
            mine[here] = mine[here] + near[z, here]
            return carry

        lax.fori_loop(0, rows // 64, add, 0)

    half = rows // 2
    first, second = pl.ds(0, half), pl.ds(half, half)
    z = {
        "own": h * 2 + l,
        "partner": h * 2 + 1 - l,
        "cross": (1 - h) * 2 + 1 - l,
        "far": (1 - h) * 2 + l,
    }

    def block_at(which, part):
        return held.at[c * 4 + z[which], part]

    order = [(1 - c) * 2 + h, (1 - c) * 2 + 1 - h, c * 2 + 1 - h, c * 2 + h]
    expert(order[0], 0)
    near_copy(h, 0).start()
    stage_copy(order[0], 0).start()
    ring.far()
    ring.shared["cross"].wait_recv()
    ring.shared["far"].wait_recv()
    expert(order[1], 1)
    near_copy(1 - h, 1).start()
    stage_copy(order[1], 1).start()
    stage_copy(order[0], 0).wait()
    expert(order[2], 0)
    stage_copy(order[2], 0).start()
    near_copy(1 - h, 1).wait_recv()
    add_near(z["far"])
    far_partner = lanes.send(block_at("far", first), far.at[0], partner())
    far_cross = lanes.send(block_at("far", second), far.at[1], cross())
    add_near(z["cross"])
    early_cross = lanes.send(block_at("cross", second), nearest.at[1, second], cross())
    stage_copy(order[1], 1).wait()
    expert(order[3], 1)
    stage_copy(order[3], 1).start()
    near_copy(h, 0).wait_recv()
    add_near(z["partner"])
    early_partner = lanes.send(block_at("partner", first), nearest.at[0, first], partner())
    add_near(z["own"])
    sends = []
    gate_own = pltpu.make_async_copy(gate_back.at[me], gate_back_out.at[me], own.at[6])
    gate_own.start()
    for step in COLUMN:
        peer = column_peer(*step)
        to = (peer["c"] * 2 + peer["h"]) * 2 + peer["l"]
        sends.append(lanes.send(gate_back.at[to], gate_back_out.at[me], peer))

    def weight_grad(values, others, target, number):
        part = 384

        def make(i, carry):
            left = values[:, :, at(i, part)].reshape(4 * slots, part)
            grad = ref_dot_tn(left, others[...].reshape(4 * slots, ff)).astype(bf16)
            target[pl.ds(4 * i, 4)] = grad.reshape(4, part // 4, ff)
            return carry

        lax.fori_loop(0, width // part, make, 0)
        copy = pltpu.make_async_copy(target, weight_grads.at[:, number], own.at[1 + number])
        copy.start()
        return copy

    far_partner.wait_recv()
    mine = block_at("cross", first)
    mine[...] = mine[...] + far[0]
    late_cross = lanes.send(mine, nearest.at[1, first], cross())
    far_cross.wait_recv()
    mine = block_at("partner", second)
    mine[...] = mine[...] + far[1]
    late_partner = lanes.send(mine, nearest.at[0, second], partner())
    go("drain")
    grad_copies = [
        weight_grad(picked_grads, hidden_gated, w_down, 2),
        weight_grad(picked, gate_low, w_gate, 0),
        weight_grad(picked, up_low, w_up, 1),
    ]
    for copy in (early_partner, early_cross, late_cross, late_partner):
        copy.wait_recv()

    def finish(i, carry):
        here = at(i, 64)
        total = held[c * 4 + z["own"], here].astype(f32)
        back_out[here, :] = (
            total + nearest[0, here].astype(f32) + nearest[1, here].astype(f32)
        )
        return carry

    lax.fori_loop(0, rows // 64, finish, 0)
    for copy in (early_partner, early_cross, late_cross, late_partner, far_partner, far_cross):
        copy.wait_send()
    for i, side in ((0, h), (1, 1 - h)):
        near_copy(side, i).wait_send()
    for copy in sends + grad_copies + [gate_own]:
        copy.wait()
    stage_copy(order[2], 0).wait()
    stage_copy(order[3], 1).wait()
    ring.drain()


def experts_of_column(rows, gates, grads_all, slots, down, block):
    count, width = rows.shape
    ff = down.shape[2]
    return pl.pallas_call(
        experts_kernel,
        name="experts",
        out_shape=(
            jax.ShapeDtypeStruct((8, count, width), bf16),
            jax.ShapeDtypeStruct((16, 3) + down.shape[1:], bf16),
            jax.ShapeDtypeStruct((count, width), f32),
            jax.ShapeDtypeStruct(gates.shape, f32),
        ),
        in_specs=[VMEM, VMEM, ANY, VMEM, VMEM, ANY, VMEM],
        out_specs=(HBM, HBM, VMEM, VMEM),
        scratch_shapes=[
            pltpu.VMEM((8, count, width), bf16),
            pltpu.VMEM((8, count, width), bf16),
            pltpu.VMEM((16, width // 16, ff), bf16),
            pltpu.VMEM((16, width // 16, ff), bf16),
            pltpu.VMEM((16, width // 16, ff), bf16),
            pltpu.VMEM((4, SLOTS, width), bf16),
            pltpu.VMEM((4, SLOTS, width), bf16),
            pltpu.VMEM((4, SLOTS, ff), f32),
            pltpu.VMEM((4, SLOTS, ff), bf16),
            pltpu.VMEM((4, SLOTS, ff), bf16),
            pltpu.VMEM((4, SLOTS, ff), bf16),
            pltpu.VMEM((2, 2, count, width), bf16),
            pltpu.VMEM((4, count, width), bf16),
            pltpu.VMEM((2, count // 2, width), bf16),
            pltpu.VMEM((2, count, width), bf16),
            pltpu.VMEM(gates.shape, f32),
            pltpu.VMEM(gates.shape, f32),
        ]
        + lanes_scratch(96)
        + [
            pltpu.SemaphoreType.DMA((7,)),
            pltpu.SemaphoreType.DMA((2,)),
            pltpu.SemaphoreType.DMA((2,)),
            pltpu.SemaphoreType.DMA((2,)),
        ],
        compiler_params=pltpu.CompilerParams(
            collective_id=4, has_side_effects=True, vmem_limit_bytes=60 * 2**20
        ),
    )(rows, gates, grads_all, slots[:, None, :], slots[:, :, None], down, block)


def return_kernel(
    part,
    misc_at,
    in_ref,
    out_ref,
    expert_ref,
    tokens_ref,
    block_ref,
    block_half,
    grads_out,
    misc_out,
    expert_out,
    tokens_out,
    block_out,
    near,
    near_p0,
    rest_p0,
    near_q0,
    near_p1,
    rest_p1,
    near_q1,
    pieces,
    landed,
    misc_landed,
    s_sem,
    r_sem,
    ps,
    pr,
    ms,
    mr,
    own,
):
    c, h, l = place()
    z = h * 2 + l
    me = c * 4 + z
    barrier = pltpu.get_barrier_semaphore()
    pl.semaphore_wait(barrier, greet_column(barrier) + greet_chips(barrier))
    lanes = Lanes(s_sem, r_sem)
    width = near.shape[2]
    half = near.shape[1] // 2
    other = column_peer(1, 0)
    x, y = lax.axis_index("x"), lax.axis_index("y")
    sums = []
    group = width // 3
    for k in range(3):
        for low, p, q, held in (
            (0, "y", "x", (near_p0, rest_p0, near_q0)),
            (half, "x", "y", (near_p1, rest_p1, near_q1)),
        ):

            def view(index, columns, mine=pl.ds(low, half), start=k * group):
                return near.at[index, mine, shifted(columns, start, group)]

            held = [buffer.at[k] for buffer in held]
            sums.append(ChipSum(lanes, view, 256, group, p, q, *held))
    order = [2, 1, 3, 0]
    arrive = {}
    for step in order:
        for which in range(2):
            for dq in range(4):
                block = sums[which].index(step, dq)
                rows = pl.ds(which * half, half)
                arrive[step, which, dq] = lanes.send(
                    in_ref.at[1 - c, block, rows], near.at[block, rows], other
                )
    own_copy = pltpu.make_async_copy(expert_ref.at[me], expert_out.at[me], own.at[0])
    own_copy.start()
    own_tokens = pltpu.make_async_copy(tokens_ref, tokens_out.at[l], own.at[1])
    own_tokens.start()
    own_block = pltpu.make_async_copy(block_ref, block_out.at[l], own.at[2])
    own_block.start()
    count = block_half.shape[0]
    rest = pl.ds(count, count)
    had = pltpu.make_async_copy(block_half, block_out.at[1 - l, pl.ds(0, count)], own.at[3])
    had.start()
    expert_copies = [
        lanes.send(tokens_ref, tokens_out.at[l], partner()),
        lanes.send(block_ref.at[rest], block_out.at[l, rest], partner()),
    ]
    for step in COLUMN:
        peer = column_peer(*step)
        to = (peer["c"] * 2 + peer["h"]) * 2 + peer["l"]
        expert_copies.append(lanes.send(expert_ref.at[to], expert_out.at[me], peer))

    def add_own(step, which):
        for dq in range(4):
            arrive[step, which, dq].wait_recv()
            block = sums[which].index(step, dq)
            rows = pl.ds(which * half, half)
            near[block, rows] = near[block, rows] + in_ref[c, block, rows, :]

    for which in range(2):
        add_own(2, which)
        for each in sums[which::2]:
            each.far()
    for step in (1, 3):
        for which in range(2):
            add_own(step, which)
    for each in sums:
        each.joined()
    for each in sums:
        each.plain()
    for which in range(2):
        add_own(0, which)
    for each in sums:
        each.far_q()
    for each in sums:
        each.next_q()
    for number, each in enumerate(sums):
        total = each.total()
        columns = slice(number // 2 * group, (number // 2 + 1) * group)
        for i in range(2):
            pieces[2 * (number % 2) + i, :, columns] = total[i * part : (i + 1) * part]
    for k in range(4):
        pieces[k, :, width:] = out_ref[k * part : (k + 1) * part, :]

    def to_owner(target, owner, src, dst, send_sem, recv_sem, asked):
        is_me = (owner["c"] == c) & (owner["h"] == h) & (owner["l"] == l)
        there = pltpu.make_async_remote_copy(
            src_ref=src,
            dst_ref=dst,
            send_sem=send_sem,
            recv_sem=recv_sem,
            device_id=owner,
            device_id_type=MESH,
        )
        here = pltpu.make_async_copy(src, dst, recv_sem)
        pl.when(asked & jnp.logical_not(is_me))(there.start)
        pl.when(asked & is_me)(here.start)
        return asked & jnp.logical_not(is_me), there

    sent = []
    everyone = c < 2
    for target in range(4):
        owner = {"c": target // 2, "h": target % 2, "l": c}
        sent.append(
            to_owner(
                target, owner, pieces.at[target], landed.at[z], ps.at[target], pr.at[z], everyone
            )
        )
    misc = pl.ds(misc_at, MISC)
    for target in range(4):
        owner = {"c": target // 2, "h": target % 2, "l": 1}
        sent.append(
            to_owner(
                target,
                owner,
                pieces.at[target, :, misc],
                misc_landed.at[z],
                ms.at[target],
                mr.at[z],
                c == 0,
            )
        )
    for source in range(4):
        pltpu.make_async_copy(pieces.at[0], landed.at[source], pr.at[source]).wait()
    grads_out[...] = (landed[0] + landed[1]) + (landed[2] + landed[3])

    def from_core():
        for source in range(4):
            pltpu.make_async_copy(
                pieces.at[0, :, misc], misc_landed.at[source], mr.at[source]
            ).wait()
        misc_out[...] = (misc_landed[0] + misc_landed[1]) + (misc_landed[2] + misc_landed[3])

    def from_piece():
        misc_out[...] = (landed[0, :, misc] + landed[1, :, misc]) + (
            landed[2, :, misc] + landed[3, :, misc]
        )

    pl.when(l == 1)(from_core)
    pl.when(l == 0)(from_piece)
    for asked, there in sent:
        pl.when(asked)(there.wait_send)
    for copy in arrive.values():
        copy.wait_send()
    for each in sums:
        each.drain()
    own_copy.wait()
    own_tokens.wait()
    own_block.wait()
    had.wait()
    for copy in expert_copies:
        copy.wait()


def return_gradients(grad_in, out_sum, expert_pieces, tokens, block, block_half, part, misc_at):
    width, rows = grad_in.shape[3], grad_in.shape[2]
    full = width + out_sum.shape[1]
    half = rows // 2
    ring = [
        pltpu.VMEM((3, 2, 2, half, width // 3), bf16),
        pltpu.VMEM((3, 2, 4, half, width // 3), bf16),
        pltpu.VMEM((3, 4, half, width // 3), bf16),
    ]
    return pl.pallas_call(
        functools.partial(return_kernel, part, misc_at),
        name="return_gradients",
        out_shape=(
            jax.ShapeDtypeStruct((part, full), f32),
            jax.ShapeDtypeStruct((part, MISC), f32),
            jax.ShapeDtypeStruct(expert_pieces.shape, expert_pieces.dtype),
            jax.ShapeDtypeStruct((2,) + tokens.shape, tokens.dtype),
            jax.ShapeDtypeStruct((2,) + block.shape, block.dtype),
        ),
        in_specs=[VMEM] * 6,
        out_specs=(VMEM, VMEM, HBM, HBM, HBM),
        scratch_shapes=[pltpu.VMEM((16, rows, width), bf16)]
        + ring
        + ring
        + [
            pltpu.VMEM((4, part, full), f32),
            pltpu.VMEM((4, part, full), f32),
            pltpu.VMEM((4, part, MISC), f32),
        ]
        + lanes_scratch(150)
        + [
            pltpu.SemaphoreType.DMA((4,)),
            pltpu.SemaphoreType.DMA((4,)),
            pltpu.SemaphoreType.DMA((4,)),
            pltpu.SemaphoreType.DMA((4,)),
            pltpu.SemaphoreType.DMA((4,)),
        ],
        compiler_params=pltpu.CompilerParams(
            collective_id=7, has_side_effects=True, vmem_limit_bytes=62 * 2**20
        ),
    )(grad_in, out_sum, expert_pieces, tokens, block, block_half)


def body(
    tokens,
    segments,
    routes,
    attn_gain,
    w_query,
    key_matrix,
    value_matrix,
    w_output,
    mix_gain,
    w_router,
    w_gate,
    w_up,
    w_down,
    block_cotangent,
):
    c, h, l = place()
    model_width = tokens.shape[2]
    rows = tokens.shape[1] // 2
    experts, part, ff_half = w_gate.shape
    q_half = w_query.shape[1]

    misc = jnp.concatenate([w_router, attn_gain[:, None], mix_gain[:, None]], axis=1)
    misc = jnp.pad(misc, ((0, 0), (0, MISC - misc.shape[1])))
    attn_block = jnp.concatenate(
        [w_query, key_matrix, value_matrix, misc, w_output.T], axis=1
    )
    attn_block = jnp.pad(attn_block, ((0, PAD - part), (0, 0)))
    expert_pieces = jnp.pad(
        jnp.stack([w_gate, w_up, w_down], axis=1), ((0, 0), (0, 0), (0, PAD - part), (0, 0))
    )
    kv_width = key_matrix.shape[1]
    in_width = q_half + 2 * kv_width + MISC

    z = h * 2 + l
    inputs = lax.dynamic_slice_in_dim(tokens[0], l * rows, rows)
    upstream = lax.dynamic_slice_in_dim(block_cotangent[0], l * rows, rows)
    named = jnp.any(
        routes[0][:, :, None] == jnp.arange(experts, dtype=jnp.int32)[None, None, :], axis=1
    )
    slot_of = jnp.cumsum(named.astype(jnp.int32), axis=0) - 1
    slot_of = jnp.where(named, slot_of, -1).astype(f32).T
    slot_of = lax.dynamic_slice_in_dim(slot_of, l * rows, rows, axis=1)
    named = (slot_of >= 0).astype(f32)
    positions = z * rows + jnp.arange(rows, dtype=jnp.int32)
    cosine, sine = rope_tables(positions)
    seg_column = segments[0][:, None]
    seg_row = lax.dynamic_slice_in_dim(segments[0], z * rows, rows)[None, :]

    (
        w_attn,
        grads_all,
        slots,
        down_full,
        expert_block,
        normed_in,
        q,
        kv,
        attended,
        lse,
        residual,
        normed_mix,
        gates,
    ) = attention(
        attn_block,
        expert_pieces,
        block_cotangent.reshape(2, rows, model_width),
        slot_of[:, None, :],
        inputs,
        cosine,
        sine,
        seg_column,
        seg_row,
        named,
        part,
    )
    w_attn = w_attn.reshape(2, model_width, attn_block.shape[1])
    mix_parts, expert_grads, mix_back, gate_back = experts_of_column(
        normed_mix, gates, grads_all, slots.reshape(4, 2 * rows), down_full, expert_block
    )
    grad_in, out_sum, tokens_back, block_out, block_half, pieces = attention_back(
        mix_back,
        gate_back,
        gates,
        normed_mix,
        residual,
        inputs,
        upstream,
        normed_in,
        attended,
        q,
        kv,
        lse,
        cosine,
        sine,
        seg_column,
        seg_row,
        w_attn,
        mix_parts,
        expert_grads,
    )

    returned, misc_back, expert_back, tokens_back, block_out = return_gradients(
        grad_in.reshape(2, 16, 4 * part, in_width),
        out_sum,
        pieces,
        tokens_back,
        block_out,
        block_half,
        part,
        in_width - MISC,
    )
    expert_back = expert_back[:, :, :part].astype(f32)
    return (
        block_out.reshape(1, 2 * rows, model_width),
        tokens_back.reshape(1, 2 * rows, model_width).astype(f32),
        misc_back[:, experts],
        returned[:, :q_half],
        returned[:, q_half : q_half + kv_width],
        returned[:, q_half + kv_width : q_half + 2 * kv_width],
        returned[:, in_width:].T,
        misc_back[:, experts + 1],
        misc_back[:, :experts],
        expert_back[:, 0],
        expert_back[:, 1],
        expert_back[:, 2],
    )


def solution(mesh):
    split = Mesh(mesh.devices.reshape(4, 4, 2, 2, 2), ("x", "y", "c", "h", "l"))
    fsdp = ("x", "y", "c")
    owner = ("x", "y", "c", "h")
    return jax.shard_map(
        body,
        mesh=split,
        in_specs=(
            P(fsdp, "h", None),
            P(fsdp, None),
            P(fsdp, "h", None),
            P(owner),
            P(owner, "l"),
            P(owner, "l"),
            P(owner, "l"),
            P("l", owner),
            P(owner),
            P(owner, None),
            P(None, owner, "l"),
            P(None, owner, "l"),
            P(None, owner, "l"),
            P(fsdp, "h", None),
        ),
        out_specs=(
            P(fsdp, "h", None),
            P(fsdp, "h", None),
            P(owner),
            P(owner, "l"),
            P(owner, "l"),
            P(owner, "l"),
            P("l", owner),
            P(owner),
            P(owner, None),
            P(None, owner, "l"),
            P(None, owner, "l"),
            P(None, owner, "l"),
        ),
        check_vma=False,
    )
```

```python
import functools

import jax
import jax.numpy as jnp
import numpy as np
from jax import lax
from jax.experimental import pallas as pl
from jax.experimental.pallas import tpu as pltpu
from jax.sharding import Mesh
from jax.sharding import PartitionSpec as P

QUERY_HEADS = 12
KEY_VALUE_HEADS = 2
HEAD_SIZE = 128
GROUP = QUERY_HEADS // KEY_VALUE_HEADS
EPS = 1e-06
ROPE_BASE = 1000000.0
NEG_FILL = -1e30
MISC = 128
SLOTS = 320
PAD = 32
MESH = pl.DeviceIdType.MESH
ANY = pl.BlockSpec(memory_space=pl.ANY)
HBM = pl.BlockSpec(memory_space=pltpu.HBM)
VMEM = pl.BlockSpec(memory_space=pltpu.VMEM)
f32 = jnp.float32
bf16 = jnp.bfloat16


def rope_tables(count):
    exponents = -np.arange(HEAD_SIZE // 2, dtype=np.float64) * (2.0 / HEAD_SIZE)
    frequency = (ROPE_BASE**exponents).astype(np.float32)
    angles = np.arange(count, dtype=np.float32)[:, None] * frequency[None, :]
    angles = angles.astype(np.float64)
    cosine, sine = np.cos(angles).astype(np.float32), np.sin(angles).astype(np.float32)
    return np.concatenate([cosine, cosine], axis=1), np.concatenate([-sine, sine], axis=1)


def place():
    return lax.axis_index("c"), lax.axis_index("h"), lax.axis_index("l")


def column_peer(core_step, z_step):
    c, h, l = place()
    z = lax.rem(h * 2 + l + z_step, 4)
    return {"c": lax.rem(c + core_step, 2), "h": z // 2, "l": lax.rem(z, 2)}


def at_z(core, z):
    return {"c": core, "h": z // 2, "l": lax.rem(z, 2)}


def greet(steps):
    barrier = pltpu.get_barrier_semaphore()
    for core_step, z_step in steps:
        pl.semaphore_signal(
            barrier, inc=1, device_id=column_peer(core_step, (4 - z_step) % 4), device_id_type=MESH
        )
    pl.semaphore_wait(barrier, len(steps))


def send(src, dst, send_sem, recv_sem, peer):
    copy = pltpu.make_async_remote_copy(
        src_ref=src,
        dst_ref=dst,
        send_sem=send_sem,
        recv_sem=recv_sem,
        device_id=peer,
        device_id_type=MESH,
    )
    copy.start()
    return copy


COLUMN = [(0, 1), (0, 2), (0, 3), (1, 0), (1, 1), (1, 2), (1, 3)]
ALONG_Z = [(0, 1), (0, 2), (0, 3)]


class Lanes:
    def __init__(self, send_sem, recv_sem):
        self.send_sem, self.recv_sem, self.used = send_sem, recv_sem, 0

    def send(self, src, dst, peer):
        i = self.used
        self.used += 1
        return send(src, dst, self.send_sem.at[i], self.recv_sem.at[i], peer)


def lanes_scratch(count):
    return [pltpu.SemaphoreType.DMA((count,)), pltpu.SemaphoreType.DMA((count,))]


def chip_peer(axis, step):
    return {axis: lax.rem(lax.axis_index(axis) + step + 4, 4)}


def greet_chips(barrier):
    for axis in ("x", "y"):
        for step in (1, 3):
            pl.semaphore_signal(
                barrier, inc=1, device_id=chip_peer(axis, step), device_id_type=MESH
            )
    return 4


def greet_column(barrier):
    for step in COLUMN:
        pl.semaphore_signal(barrier, inc=1, device_id=column_peer(*step), device_id_type=MESH)
    return len(COLUMN)


def partner():
    return {"l": 1 - lax.axis_index("l")}


def cross():
    return {"h": 1 - lax.axis_index("h"), "l": 1 - lax.axis_index("l")}


def other_core():
    return {"c": 1 - lax.axis_index("c")}


class ColumnRing:
    def __init__(self, lanes, rows_ref, out_ref):
        c, h, l = place()
        self.lanes, self.rows, self.out = lanes, rows_ref, out_ref
        half = rows_ref.shape[0] // 2
        self.first, self.second = pl.ds(0, half), pl.ds(half, half)
        self.at = {
            "own": c * 4 + h * 2 + l,
            "partner": c * 4 + h * 2 + 1 - l,
            "cross": c * 4 + (1 - h) * 2 + 1 - l,
            "far": c * 4 + (1 - h) * 2 + l,
        }
        self.shared = {}

    def share(self, which):
        block = self.out.at[self.at[which]]
        self.shared[which] = self.lanes.send(block, block, other_core())

    def half_to(self, part, peer):
        return self.lanes.send(self.rows.at[part], self.out.at[self.at["own"], part], peer)

    def start(self):
        self.partner_first = self.half_to(self.first, partner())
        self.cross_second = self.half_to(self.second, cross())
        self.partner_second = self.half_to(self.second, partner())
        self.cross_first = self.half_to(self.first, cross())
        here = self.out.at[self.at["own"]]
        self.shared["own"] = self.lanes.send(self.rows, here, other_core())

    def relay(self):
        self.partner_first.wait_recv()
        block = self.out.at[self.at["partner"], self.first]
        self.far_cross = self.lanes.send(block, block, cross())
        self.cross_second.wait_recv()
        block = self.out.at[self.at["cross"], self.second]
        self.far_partner = self.lanes.send(block, block, partner())

    def nearest(self):
        self.partner_second.wait_recv()
        self.share("partner")
        self.cross_first.wait_recv()
        self.share("cross")

    def far(self):
        self.far_cross.wait_recv()
        self.far_partner.wait_recv()
        self.share("far")

    def drain(self):
        for copy in (self.partner_first, self.partner_second, self.cross_first, self.cross_second):
            copy.wait_send()
        for copy in (self.far_cross, self.far_partner):
            copy.wait_send()
        for copy in self.shared.values():
            copy.wait_send()

    def finish(self):
        self.far()
        for copy in self.shared.values():
            copy.wait_recv()
        self.drain()


def chip_index(steps):
    x = lax.rem(lax.axis_index("x") + steps["x"] + 4, 4)
    y = lax.rem(lax.axis_index("y") + steps["y"] + 4, 4)
    return x * 4 + y


def shifted(columns, start, size):
    if columns == slice(None):
        return pl.ds(start, size)
    return pl.ds(start + columns.start, columns.size)


class ChipRing:
    def __init__(self, lanes, own, view, cut, width, a, b, line=None):
        self.lanes, self.own, self.view = lanes, own, view
        self.low, self.high = pl.ds(0, cut), pl.ds(cut, width - cut)
        self.a, self.b, self.line = a, b, line
        self.sent, self.near, self.last = [], [], {}

    def ref(self, da, db, columns=slice(None)):
        return self.view(chip_index({self.a: da, self.b: db}), columns)

    def copy(self, src, dst, axis, step):
        made = self.lanes.send(src, dst, chip_peer(axis, step))
        self.sent.append(made)
        return made

    def start(self):
        here = self.ref(0, 0)
        self.first = [self.copy(self.own, here, self.a, step) for step in (1, -1)]
        self.turn = {0: [self.copy(self.own, here, self.b, step) for step in (1, -1)]}

    def pass_on(self, da):
        block = self.ref(da, 0)
        self.turn[da] = [self.copy(block, block, self.b, step) for step in (1, -1)]

    def relay_first(self):
        for copy in self.first:
            copy.wait_recv()
        block = self.ref(-1, 0, self.low)
        one = self.copy(block, block, self.a, 1)
        block = self.ref(1, 0, self.high)
        self.second = [one, self.copy(block, block, self.a, -1)]
        self.pass_on(-1)
        self.pass_on(1)

    def relay_turn(self, da):
        for copy in self.turn[da]:
            copy.wait_recv()
        step = 1 if da in (0, -1) else -1
        block = self.ref(da, -step)
        self.last[da] = self.copy(block, block, self.b, step)

    def relay_second(self):
        for copy in self.second:
            copy.wait_recv()
        self.pass_on(2)

    def finish(self):
        for da in (0, -1, 1, 2):
            self.last[da].wait_recv()
            if self.line is not None:
                block = self.line(lax.rem(lax.axis_index(self.a) + da + 4, 4))
                self.near.append(self.lanes.send(block, block, other_core()))

    def drain(self):
        for copy in self.sent:
            copy.wait_send()
        for copy in self.near:
            copy.wait()


class ChipSum:
    def __init__(self, lanes, view, cut, width, p, q, near_p, rest_p, near_q):
        self.lanes, self.view = lanes, view
        self.low, self.high = pl.ds(0, cut), pl.ds(cut, width - cut)
        self.p, self.q = p, q
        self.near_p, self.rest_p, self.near_q = near_p, rest_p, near_q
        self.sent = []

    def index(self, dp, dq):
        return chip_index({self.p: dp, self.q: dq})

    def copy(self, src, dst, axis, step):
        made = self.lanes.send(src, dst, chip_peer(axis, step))
        self.sent.append(made)
        return made

    def own(self, dp, dq, columns=slice(None)):
        return self.view(self.index(dp, dq), columns)

    def side(self, i, columns):
        lead = (slice(None),) * (len(self.near_q.shape) - 2)
        return self.near_q.at[(i,) + lead + (columns,)]

    def far(self):
        self.far_copies = {}
        for dq, step, i in ((2, 1, 0), (3, -1, 0), (1, 1, 1), (0, -1, 1)):
            direction = 0 if step == 1 else 1
            self.far_copies[direction, i] = self.copy(
                self.own(2, dq), self.near_p.at[direction, i], self.p, step
            )

    def plain(self):
        for dq, step in ((2, -1), (3, 1), (1, -1), (0, 1)):
            self.next_to(dq, step)

    def next_to(self, dq, step):
        direction = 0 if step == 1 else 1
        self.next_copies[direction, dq] = self.copy(
            self.own(step, dq), self.rest_p.at[direction, dq], self.p, step
        )

    def joined(self):
        self.next_copies = {}
        for dq, step, i in ((2, 1, 0), (3, -1, 0), (1, 1, 1), (0, -1, 1)):
            direction = 0 if step == 1 else 1
            self.far_copies[direction, i].wait_recv()
            mine = self.own(step, dq)
            mine[...] = mine[...] + self.near_p[direction, i]
            self.next_to(dq, step)

    def collect(self, dq):
        for direction in range(2):
            self.next_copies[direction, dq].wait_recv()
        mine = self.own(0, dq)
        total = mine[...].astype(f32)
        for direction in range(2):
            total = total + self.rest_p[direction, dq].astype(f32)
        mine[...] = total.astype(mine.dtype)

    def far_q(self):
        self.collect(2)
        self.far_q_copies = [
            self.copy(self.own(0, 2, self.low), self.side(0, self.low), self.q, 1),
            self.copy(self.own(0, 2, self.high), self.side(1, self.high), self.q, -1),
        ]

    def next_q(self):
        self.next_q_copies = []
        for i, (dq, columns) in enumerate(((1, self.low), (3, self.high))):
            self.collect(dq)
            self.far_q_copies[i].wait_recv()
            mine = self.own(0, dq, columns)
            mine[...] = mine[...] + self.side(i, columns)[...]
            self.next_q_copies.append(
                self.copy(self.own(0, dq), self.near_q.at[2 + i], self.q, 1 if i == 0 else -1)
            )

    def total(self):
        self.collect(0)
        total = self.own(0, 0)[...].astype(f32)
        for i in range(2):
            self.next_q_copies[i].wait_recv()
            total = total + self.near_q[2 + i].astype(f32)
        return total

    def drain(self):
        for copy in self.sent:
            copy.wait_send()


def ref_dot(a, b):
    return jnp.dot(a, b, preferred_element_type=f32)


def ref_dot_nt(a, b):
    return lax.dot_general(a, b, (((1,), (1,)), ((), ())), preferred_element_type=f32)


def ref_dot_tn(a, b):
    return lax.dot_general(a, b, (((0,), (0,)), ((), ())), preferred_element_type=f32)


def at(i, size):
    return pl.ds(pl.multiple_of(i * size, size), size)


def gain_rows(misc):
    pick = lax.broadcasted_iota(jnp.int32, (16, MISC), 0)
    pick = (pick == lax.broadcasted_iota(jnp.int32, (16, MISC), 1)).astype(f32).astype(bf16)
    return ref_dot_nt(pick, misc)


def turn(values, cosine, sine):
    return values * cosine + pltpu.roll(values, HEAD_SIZE // 2, 1) * sine


def turn_back(values, cosine, sine):
    return values * cosine - pltpu.roll(values, HEAD_SIZE // 2, 1) * sine


def as_column(row):
    count = row.shape[1]
    same = lax.broadcasted_iota(jnp.int32, (count, count), 0) == lax.broadcasted_iota(
        jnp.int32, (count, count), 1
    )
    return jnp.sum(jnp.where(same, row.astype(f32), 0.0), axis=1, keepdims=True)


def fill_bias(bias, seg_ref, z):
    keys, queries = bias.shape
    seg_row = seg_ref[:, at(z, queries)].astype(f32)

    def fill(i, carry):
        seg_column = as_column(seg_ref[:, at(i, queries)])
        key = lax.broadcasted_iota(jnp.int32, (queries, queries), 0) + i * queries
        query = lax.broadcasted_iota(jnp.int32, (queries, queries), 1) + z * queries
        seen = (seg_column == seg_row) & (key <= query)
        bias[at(i, queries), :] = jnp.where(seen, 0.0, NEG_FILL)
        return carry

    lax.fori_loop(0, keys // queries, fill, 0)


KEYS = 128


def key_block(kv, i, k):
    per_block = kv.shape[1] // KEYS
    start = (k % per_block) * KEYS
    return kv[k // per_block, start : start + KEYS, i * HEAD_SIZE : (i + 1) * HEAD_SIZE]


class RowsRing:
    def __init__(self, lanes, rows_ref, out_ref):
        c, h, l = place()
        self.lanes, self.out, self.l = lanes, out_ref, l
        self.rows = rows_ref
        self.own = pl.ds((c * 2 + h) * 2, 2)
        self.here = c * 4 + h * 2 + l
        self.cross_at = c * 4 + (1 - h) * 2 + 1 - l
        self.far_at = c * 4 + (1 - h) * 2 + l
        self.shared = []

    def share(self, index):
        block = self.out.at[index]
        self.shared.append(self.lanes.send(block, block, other_core()))

    def start(self):
        size = self.rows.shape[1] // 4
        self.parts = [pl.ds(i * size, size) for i in range(4)]
        self.to_cross = [
            self.lanes.send(self.rows.at[self.l, some], self.out.at[self.here, some], cross())
            for some in self.parts
        ]
        self.shared.append(self.lanes.send(self.rows, self.out.at[self.own], other_core()))
        self.to_partner = []

    def relay(self, i):
        self.to_cross[i].wait_recv()
        block = self.out.at[self.cross_at, self.parts[i]]
        self.to_partner.append(self.lanes.send(block, block, partner()))

    def finish(self):
        self.share(self.cross_at)
        for copy in self.to_partner:
            copy.wait_recv()
        self.share(self.far_at)

    def drain(self):
        for copy in self.to_cross + self.to_partner:
            copy.wait_send()
        for copy in self.shared:
            copy.wait()


def attention_kernel(
    part,
    wq_ref,
    wk_ref,
    wv_ref,
    wo_ref,
    router_ref,
    attn_gain_ref,
    mix_gain_ref,
    wg_ref,
    wu_ref,
    wd_ref,
    rows_ref,
    tokens_ref,
    routes_ref,
    seg_ref,
    cos_table,
    sin_table,
    w_out,
    rows_out,
    slots_out,
    expert_out,
    expert_block,
    a_out,
    q_out,
    kv_out,
    o_out,
    lse_out,
    h1_out,
    b_out,
    gates_out,
    w,
    attn_in,
    expert_in,
    block,
    bias,
    value_turned,
    attn_ref,
    expert_ref,
    slots_ref,
    slots_own,
    cos_ref,
    sin_ref,
    s_sem,
    r_sem,
    as_sem,
    ar_sem,
    own,
):
    c, h, l = place()
    z = h * 2 + l
    me = (c * 2 + h) * 2 + l
    x_ref = tokens_ref.at[l]
    rows, width = rows_ref.shape[1:]
    q_half = w.shape[4] // 2 - (HEAD_SIZE * 2 + MISC) // 2
    kv_at, misc_at, out_at = q_half, q_half + 2 * HEAD_SIZE, q_half + 2 * HEAD_SIZE + MISC
    ff = expert_block.shape[2]
    tables = [
        pltpu.make_async_copy(cos_table.at[pl.ds(z * rows, rows)], cos_ref, own.at[5]),
        pltpu.make_async_copy(sin_table.at[pl.ds(z * rows, rows)], sin_ref, own.at[6]),
    ]
    for copy in tables:
        copy.start()

    place_of = lax.broadcasted_iota(jnp.int32, (8, MISC), 0)
    place_of = (place_of == lax.broadcasted_iota(jnp.int32, (8, MISC), 1)).astype(f32)
    misc = ref_dot(router_ref[...], place_of.astype(bf16))
    column = lax.broadcasted_iota(jnp.int32, (part, MISC), 1)
    misc = jnp.where(column == 8, as_column(attn_gain_ref[...]), misc)
    misc = jnp.where(column == 9, as_column(mix_gain_ref[...]), misc)
    attn_ref[...] = jnp.zeros_like(attn_ref)
    attn_ref[:part, :q_half] = wq_ref[...]
    attn_ref[:part, kv_at : kv_at + HEAD_SIZE] = wk_ref[...]
    attn_ref[:part, kv_at + HEAD_SIZE : misc_at] = wv_ref[...]
    attn_ref[:part, misc_at:out_at] = misc.astype(bf16)
    attn_ref[:part, out_at:] = wo_ref[...]
    for i, ref in enumerate((wg_ref, wu_ref, wd_ref)):
        expert_ref[:, i, :part, :] = ref[...]
        expert_ref[:, i, part:, :] = jnp.zeros((8, PAD - part, ff // 2), bf16)

    block_rows = 2 * rows
    expert = lax.broadcasted_iota(jnp.int32, (8, block_rows), 0)
    taken = routes_ref[0:1, :] == expert
    for j in range(1, routes_ref.shape[0]):
        taken = taken | (routes_ref[j : j + 1, :] == expert)
    earlier = lax.broadcasted_iota(jnp.int32, (block_rows, block_rows), 0)
    earlier = (earlier < lax.broadcasted_iota(jnp.int32, (block_rows, block_rows), 1)).astype(f32)
    count = ref_dot(taken.astype(f32).astype(bf16), earlier.astype(bf16))
    count = jnp.where(taken, count, -1.0)
    slots_own[...] = jnp.where(l == 0, count[:, :rows], count[:, rows:])
    for e in range(8):
        slots_ref[e] = slots_own[e : e + 1, :]

    barrier = pltpu.get_barrier_semaphore()
    pl.semaphore_wait(barrier, greet_column(barrier) + greet_chips(barrier))
    lanes = Lanes(s_sem, r_sem)

    slot = c * 2 + h
    here = pltpu.make_async_copy(attn_ref, attn_in.at[slot], own.at[1])
    there = pltpu.make_async_remote_copy(
        src_ref=attn_ref,
        dst_ref=attn_in.at[slot],
        send_sem=as_sem.at[0],
        recv_sem=ar_sem.at[slot],
        device_id=column_peer(1, 0),
        device_id_type=MESH,
    )
    pl.when(c == l)(here.start)
    pl.when(c != l)(there.start)
    for z_step in range(1, 4):
        to_z = lax.rem(z + z_step, 4)
        send(attn_ref, attn_in.at[slot], as_sem.at[z_step], ar_sem.at[slot], at_z(l, to_z))
    local = [
        pltpu.make_async_copy(expert_ref.at[me], expert_in.at[me], own.at[0]),
        pltpu.make_async_copy(slots_ref.at[me], slots_out.at[me], own.at[2]),
        pltpu.make_async_copy(rows_ref, rows_out.at[pl.ds((c * 2 + h) * 2, 2)], own.at[3]),
    ]
    for copy in local:
        copy.start()
    pieces = []
    for step in COLUMN:
        peer = column_peer(*step)
        to = (peer["c"] * 2 + peer["h"]) * 2 + peer["l"]
        pieces.append(lanes.send(expert_ref.at[to], expert_in.at[me], peer))
        pieces.append(lanes.send(slots_ref.at[to], slots_out.at[me], peer))
    fill_bias(bias, seg_ref, z)

    for source in range(4):
        mine = (c == l) & (slot == source)

        def landed(source=source):
            pltpu.make_async_remote_copy(
                src_ref=attn_ref,
                dst_ref=attn_in.at[source],
                send_sem=as_sem.at[0],
                recv_sem=ar_sem.at[source],
                device_id=column_peer(1, 0),
                device_id_type=MESH,
            ).wait_recv()

        pl.when(jnp.logical_not(mine))(landed)
    pl.when(c == l)(here.wait)
    block[...] = jnp.concatenate(
        [attn_in[i].astype(f32)[:part] for i in range(4)], axis=0
    ).astype(block.dtype)
    index = chip_index({"x": 0, "y": 0})
    x_at, y_at = lax.axis_index("x"), lax.axis_index("y")
    keep = [pltpu.make_async_copy(block, w.at[c, x_at, y_at], own.at[4])]
    keep[0].start()
    half = block.shape[0] // 2
    rings = {}
    for name, start, size, cut in (("in", 0, out_at, 640), ("out", out_at, q_half, 384)):
        rings[name] = []
        for low, a, b in ((0, "x", "y"), (half, "y", "x")):
            mine = pl.ds(low, half)

            def view(index, columns, mine=mine, start=start, size=size):
                return w.at[c, index // 4, lax.rem(index, 4), mine, shifted(columns, start, size)]

            def line(i, a=a, mine=mine, columns=pl.ds(start, size)):
                return w.at[c, i, :, mine, columns] if a == "x" else w.at[c, :, i, mine, columns]

            own_part = block.at[mine, pl.ds(start, size)]
            rings[name].append(ChipRing(lanes, own_part, view, cut, size, a, b, line))
    rings["expert"] = []
    for low, a, b in ((0, "x", "y"), (half, "y", "x")):
        mine = pl.ds(low, half)

        def expert_view(index, columns, mine=mine):
            return expert_out.at[:, index, mine, columns]

        own_part = expert_block.at[pl.ds(1, 2), mine]
        rings["expert"].append(ChipRing(lanes, own_part, expert_view, ff // 2, ff, a, b))

    def go(name, step, *args):
        for ring in rings[name]:
            getattr(ring, step)(*args)

    go("in", "start")
    rows_ring = RowsRing(lanes, rows_ref, rows_out)
    rows_ring.start()

    local[0].wait()
    for copy in pieces:
        copy.wait()
    for i in range(3):
        for l_side in range(2):
            expert_block[i, :, l_side * 384 : (l_side + 1) * 384] = jnp.concatenate(
                [expert_in[2 * j + l_side, i].astype(f32)[:part] for j in range(4)], axis=0
            ).astype(bf16)
    keep.append(
        pltpu.make_async_copy(expert_block.at[pl.ds(1, 2)], expert_out.at[:, index], own.at[0])
    )
    keep[1].start()

    keep[0].wait()
    go("in", "relay_first")
    go("in", "relay_turn", 0)
    go("in", "relay_second")
    go("out", "start")
    for da in (-1, 1, 2):
        go("in", "relay_turn", da)
    go("out", "relay_first")
    go("in", "finish")
    go("expert", "start")
    go("out", "relay_turn", 0)
    go("out", "relay_second")
    for ring in rings["in"]:
        for copy in ring.near:
            copy.wait_recv()


    def projection(i, columns):
        return w[i, :, :, :, columns].reshape(width, -1)

    scale = HEAD_SIZE ** (-0.5)
    misc = projection(0, slice(misc_at, out_at))
    gains = gain_rows(misc)
    chunk = 32

    def norm(i, carry):
        here = at(i, chunk)
        x = x_ref[here, :].astype(f32)
        inverse = lax.rsqrt(jnp.mean(x * x, axis=1, keepdims=True) + EPS)
        a_out[here, :] = (x * inverse * gains[8:9, :]).astype(bf16)
        return carry

    lax.fori_loop(0, rows // chunk, norm, 0)
    for copy in tables:
        copy.wait()
    cosine, sine = cos_ref[...], sin_ref[...]
    sends = []
    for i in range(2):
        kv = ref_dot(a_out[...], projection(i, slice(kv_at, misc_at)))
        kv_out[z, :, i * 128 : (i + 1) * 128] = turn(kv[:, :128], cosine, sine).astype(bf16)
        kv_out[z, :, (2 + i) * 128 : (3 + i) * 128] = kv[:, 128:].astype(bf16)
    for step in ALONG_Z:
        sends.append(lanes.send(kv_out.at[z], kv_out.at[z], column_peer(*step)))
    go("out", "relay_turn", -1)
    go("out", "relay_turn", 1)
    for i in range(2):

        def project(j, carry, i=i):
            q = ref_dot(a_out[...], w[i, :, :, :, at(j, 256)].reshape(width, 256))
            q_out[i * GROUP + 2 * j] = turn(q[:, :128], cosine, sine).astype(bf16)
            q_out[i * GROUP + 2 * j + 1] = turn(q[:, 128:], cosine, sine).astype(bf16)
            return carry

        lax.fori_loop(0, q_half // 256, project, 0)
    go("out", "relay_turn", 2)
    go("expert", "relay_first")
    for copy in sends:
        copy.wait_recv()
    for i in range(4):
        rows_ring.relay(i)
    keys_count = 4 * rows
    for i in range(2):
        values = kv_out[:, :, (2 + i) * 128 : (3 + i) * 128].reshape(keys_count, HEAD_SIZE)
        value_turned[...] = values.T

        def attend(j, carry, i=i):
            keys = kv_out[:, :, i * 128 : (i + 1) * 128].reshape(keys_count, HEAD_SIZE)
            scores = ref_dot_nt(keys, q_out[i * GROUP + j]) * scale + bias[...]
            peak = jnp.max(scores, axis=0, keepdims=True)
            expo = jnp.exp(scores - peak)
            total = jnp.sum(expo, axis=0, keepdims=True)
            weights = (expo * (1.0 / total)).astype(bf16)
            mixed = ref_dot(value_turned[...], weights)
            o_out[:, at(i * GROUP + j, HEAD_SIZE)] = mixed.T.astype(bf16)
            lse_out[i * GROUP + j] = peak + jnp.log(total)
            return carry

        for some in range(2):
            lax.fori_loop(some * GROUP // 2, (some + 1) * GROUP // 2, attend, 0)
            if (i, some) == (0, 0):
                go("out", "finish")
                go("expert", "relay_turn", 0)
            elif (i, some) == (0, 1):
                go("expert", "relay_second")
            elif (i, some) == (1, 0):
                go("expert", "relay_turn", -1)
    for ring in rings["out"]:
        for copy in ring.near:
            copy.wait_recv()
    keep.append(pltpu.make_async_copy(w, w_out, own.at[1]))
    keep[2].start()

    def leave(j, carry):
        here = at(j, 384)
        u = ref_dot_nt(
            o_out[:, :q_half], w[0, j, :, :, out_at:].reshape(384, q_half)
        )
        u = u + ref_dot_nt(
            o_out[:, q_half:], w[1, j, :, :, out_at:].reshape(384, q_half)
        )
        h1_out[:, here] = x_ref[:, here].astype(f32) + u
        return carry

    lax.fori_loop(0, width // 384, leave, 0)
    go("expert", "relay_turn", 1)

    def second(i, carry):
        here = at(i, chunk)
        h1 = h1_out[here, :]
        inverse = lax.rsqrt(jnp.mean(h1 * h1, axis=1, keepdims=True) + EPS)
        b_out[here, :] = (h1 * inverse * gains[9:10, :]).astype(bf16)
        return carry

    lax.fori_loop(0, rows // chunk, second, 0)
    logits = ref_dot(b_out[...], misc).T[:8]
    named = slots_own[...] >= 0
    masked = jnp.where(named, logits, NEG_FILL)
    expo = jnp.where(named, jnp.exp(masked - jnp.max(masked, axis=0, keepdims=True)), 0.0)
    gates = expo / jnp.sum(expo, axis=0, keepdims=True)
    for e in range(8):
        gates_out[e] = gates[e : e + 1]
    go("expert", "relay_turn", 2)
    rows_ring.finish()
    go("expert", "finish")
    for copy in sends:
        copy.wait_send()
    rows_ring.drain()
    for copy in local[1:]:
        copy.wait()
    pl.when(c != l)(there.wait_send)
    for z_step in range(1, 4):
        pltpu.make_async_remote_copy(
            src_ref=attn_ref,
            dst_ref=attn_in.at[slot],
            send_sem=as_sem.at[z_step],
            recv_sem=ar_sem.at[slot],
            device_id=column_peer(0, z_step),
            device_id_type=MESH,
        ).wait_send()
    for name in ("in", "out"):
        for ring in rings[name]:
            for copy in ring.near:
                copy.wait_send()
            for copy in ring.sent:
                copy.wait_send()
    go("expert", "drain")
    for copy in keep[1:]:
        copy.wait()


def attention(projections, gains, experts, upstream, tokens, routes, segments, tables, part):
    rows, width = upstream.shape[1:]
    keys = 4 * rows
    w_width = 2 * projections[0].shape[1] + 2 * HEAD_SIZE + MISC
    ff = 2 * experts[0].shape[2]
    pieces = (8, 3, PAD, ff // 2)
    sds = jax.ShapeDtypeStruct
    return pl.pallas_call(
        functools.partial(attention_kernel, part),
        name="attention",
        out_shape=(
            sds((2, 4, 4, 4 * part, w_width), bf16),
            sds((8, rows, width), bf16),
            sds((8, 1, rows), f32),
            sds((2, 16, 4 * part, ff), bf16),
            sds((3, 4 * part, ff), bf16),
            sds((rows, width), bf16),
            sds((QUERY_HEADS, rows, HEAD_SIZE), bf16),
            sds((4, rows, 4 * HEAD_SIZE), bf16),
            sds((rows, QUERY_HEADS * HEAD_SIZE), bf16),
            sds((QUERY_HEADS, 1, rows), f32),
            sds((rows, width), f32),
            sds((rows, width), bf16),
            sds((8, 1, rows), f32),
        ),
        in_specs=[VMEM] * 14 + [ANY] * 2,
        out_specs=(HBM,) * 4 + (VMEM,) * 9,
        scratch_shapes=[
            pltpu.VMEM((2, 4, 4, 4 * part, w_width), bf16),
            pltpu.VMEM((4, PAD, w_width), bf16),
            pltpu.VMEM(pieces, bf16),
            pltpu.VMEM((4 * part, w_width), bf16),
            pltpu.VMEM((keys, rows), f32),
            pltpu.VMEM((HEAD_SIZE, keys), bf16),
            pltpu.VMEM((PAD, w_width), bf16),
            pltpu.VMEM(pieces, bf16),
            pltpu.VMEM((8, 1, rows), f32),
            pltpu.VMEM((8, rows), f32),
            pltpu.VMEM((rows, HEAD_SIZE), f32),
            pltpu.VMEM((rows, HEAD_SIZE), f32),
        ]
        + lanes_scratch(150)
        + [
            pltpu.SemaphoreType.DMA((4,)),
            pltpu.SemaphoreType.DMA((4,)),
            pltpu.SemaphoreType.DMA((7,)),
        ],
        compiler_params=pltpu.CompilerParams(
            collective_id=2, has_side_effects=True, vmem_limit_bytes=60 * 2**20
        ),
    )(*projections, *gains, *experts, upstream, tokens, routes, segments, *tables)


def attention_back_kernel(
    back_ref,
    gate_back_ref,
    gates_ref,
    b_ref,
    h1_ref,
    tokens_ref,
    rows_ref,
    a_ref,
    o_ref,
    q_ref,
    kv_ref,
    lse_ref,
    cos_table,
    sin_table,
    seg_ref,
    w_ref,
    parts_ref,
    expert_ref,
    grad_in,
    out_sum,
    tokens_out,
    block_out,
    block_half,
    pieces_out,
    w,
    bias,
    key_turned,
    dh1,
    da,
    du,
    do,
    back_rows,
    key_sum,
    value_sum,
    probs,
    probs_back,
    probs_low,
    scores_back,
    kv_send,
    kv_held,
    stage_in,
    misc_held,
    parts,
    near,
    far,
    nearest,
    terms,
    near_p0,
    rest_p0,
    near_q0,
    near_p1,
    rest_p1,
    near_q1,
    out_terms,
    out_near_p0,
    out_rest_p0,
    out_near_q0,
    out_near_p1,
    out_rest_p1,
    out_near_q1,
    x_ref,
    g_ref,
    cos_ref,
    sin_ref,
    s_sem,
    r_sem,
    w_sem,
    own,
):
    c, h, l = place()
    z = h * 2 + l
    rows, width = x_ref.shape
    q_half = o_ref.shape[1] // 2
    misc_at, out_at = q_half + 2 * HEAD_SIZE, q_half + 2 * HEAD_SIZE + MISC

    def load(start, size, to, i):
        return pltpu.make_async_copy(
            w_ref.at[:, :, pl.ds(start, size)], w.at[:, :, pl.ds(to, size)], w_sem.at[i]
        )

    loads = [load(misc_at, MISC, misc_at, 0), load(out_at, q_half, 0, 1), load(0, misc_at, 0, 2)]
    loads[0].start()
    loads[1].start()
    terms_load = pltpu.make_async_copy(expert_ref, terms, own.at[1])
    terms_load.start()
    own_loads = [
        pltpu.make_async_copy(tokens_ref.at[l], x_ref, own.at[4]),
        pltpu.make_async_copy(rows_ref.at[l], g_ref, own.at[5]),
        pltpu.make_async_copy(cos_table.at[pl.ds(z * rows, rows)], cos_ref, own.at[6]),
        pltpu.make_async_copy(sin_table.at[pl.ds(z * rows, rows)], sin_ref, own.at[7]),
    ]
    for copy in own_loads:
        copy.start()
    back_load = pltpu.make_async_copy(back_ref, da, own.at[2])
    back_load.start()
    barrier = pltpu.get_barrier_semaphore()
    pl.semaphore_wait(barrier, greet_column(barrier) + greet_chips(barrier))
    lanes = Lanes(s_sem, r_sem)
    part, ff = terms.shape[2] // 4, terms.shape[3]
    sums = []
    for low, p, q, held in (
        (0, "y", "x", (near_p0, rest_p0, near_q0)),
        (2 * part, "x", "y", (near_p1, rest_p1, near_q1)),
    ):

        def view(index, columns, mine=pl.ds(low, 2 * part)):
            return terms.at[index, :, mine, columns]

        sums.append(ChipSum(lanes, view, ff // 2, ff, p, q, *held))
    out_sums = []
    for low, p, q, held in (
        (0, "y", "x", (out_near_p0, out_rest_p0, out_near_q0)),
        (2 * part, "x", "y", (out_near_p1, out_rest_p1, out_near_q1)),
    ):

        def out_view(index, columns, mine=pl.ds(low, 2 * part)):
            return out_terms.at[index, mine, columns]

        out_sums.append(ChipSum(lanes, out_view, q_half // 2, q_half, p, q, *held))
    places = {
        "own": z,
        "partner": h * 2 + 1 - l,
        "cross": (1 - h) * 2 + 1 - l,
        "far": (1 - h) * 2 + l,
    }
    queue = ("far", "cross", "partner", "own")

    def parts_load(i):
        return pltpu.make_async_copy(
            parts_ref.at[c * 4 + places[queue[i]]], parts.at[i % 2], own.at[(0, 3)[i % 2]]
        )

    parts_load(0).start()
    parts_load(1).start()
    near_copies = {
        which: lanes.send(
            parts_ref.at[(1 - c) * 4 + places[which]], near.at[places[which]], other_core()
        )
        for which in ("far", "cross", "partner", "own")
    }
    scale = HEAD_SIZE ** (-0.5)
    fill_bias(bias, seg_ref, z)
    for copy in own_loads:
        copy.wait()

    def add_near(which):
        near_copies[which].wait_recv()
        k, number = places[which], queue.index(which)
        parts_load(number).wait()

        def add(i, carry):
            here = at(i, 64)
            near[k, here] = near[k, here] + parts[number % 2, here]
            return carry

        lax.fori_loop(0, rows // 64, add, 0)
        if number < 2:
            parts_load(number + 2).start()

    half = rows // 2
    first, second = pl.ds(0, half), pl.ds(half, half)

    def part_at(which, some):
        return near.at[places[which], some]

    terms_load.wait()
    for each in sums:
        each.far()
    add_near("far")
    far_partner = lanes.send(part_at("far", first), far.at[0], partner())
    far_cross = lanes.send(part_at("far", second), far.at[1], cross())
    add_near("cross")
    add_near("partner")
    early_cross = lanes.send(part_at("cross", second), nearest.at[1, second], cross())
    early_partner = lanes.send(part_at("partner", first), nearest.at[0, first], partner())
    add_near("own")

    loads[0].wait()
    loads[1].wait()
    misc = w[0, :, misc_at:out_at]
    gains = gain_rows(misc)
    gates = jnp.concatenate([gates_ref[e] for e in range(8)], axis=0)
    gate_back = jnp.concatenate([gate_back_ref[e] for e in range(8)], axis=0)
    mean = jnp.sum(gates * gate_back, axis=0, keepdims=True)
    logit_grad = gates * (gate_back - mean)
    logit_grad = jnp.concatenate(
        [logit_grad, jnp.zeros((MISC - 8, rows), f32)], axis=0
    ).T.astype(bf16)
    chunk = 32

    def norm_back(i, carry):
        mix_sum = carry
        here = at(i, chunk)
        h1 = h1_ref[here, :]
        inverse = lax.rsqrt(jnp.mean(h1 * h1, axis=1, keepdims=True) + EPS)
        db = da[here, :] + dh1[here, :]
        mix_sum = mix_sum + jnp.sum(db * h1 * inverse, axis=0, keepdims=True)
        dz = db * gains[9:10, :]
        mean = jnp.mean(dz * h1, axis=1, keepdims=True)
        value = g_ref[here, :].astype(f32) + inverse * dz - h1 * (inverse * inverse * inverse * mean)
        dh1[here, :] = value
        du[here, :] = value.astype(bf16)
        return mix_sum

    dh1[...] = ref_dot_nt(logit_grad, misc)
    back_load.wait()
    mix_sum = lax.fori_loop(0, rows // chunk, norm_back, jnp.zeros((1, width), f32))
    tail = pl.ds(misc_at, MISC)
    router_grad = ref_dot_tn(b_ref[...], logit_grad).astype(bf16)
    grad_in[:, :, tail] = router_grad.reshape(16, 4 * part, MISC)

    def project(i, carry):
        columns = at(i, 256)
        for g in range(2):
            do[g, :, columns] = ref_dot(du[...], w[g, :, columns]).astype(bf16)
        return carry

    lax.fori_loop(0, q_half // 256, project, 0)
    loads[2].start()

    far_partner.wait_recv()
    mine = part_at("cross", first)
    mine[...] = mine[...] + far[0]
    late_cross = lanes.send(mine, nearest.at[1, first], cross())
    far_cross.wait_recv()
    mine = part_at("partner", second)
    mine[...] = mine[...] + far[1]
    late_partner = lanes.send(mine, nearest.at[0, second], partner())

    def add_block():
        for copy in (early_partner, early_cross, late_cross, late_partner):
            copy.wait_recv()

        def add_up(i, carry):
            here = at(i, 64)
            value = near[z, here].astype(f32)
            value = value + nearest[0, here].astype(f32) + nearest[1, here].astype(f32)
            block_out[here, :] = (h1_ref[here, :] + value).astype(bf16)
            return carry

        lax.fori_loop(0, rows // 64, add_up, 0)
        return lanes.send(block_out.at[first], block_half, partner())

    for each in sums:
        each.joined()
    for each in sums:
        each.plain()

    size = 4 * 4 * part

    def out_grad(g, i):
        columns = pl.ds(pl.multiple_of(g * q_half, q_half), q_half)
        grad = ref_dot_tn(du[:, i * size : (i + 1) * size], o_ref[:, columns])
        return grad.astype(bf16).reshape(4, 4 * part, q_half)

    out_sends = []
    for i in range(4):
        if i >= 2:
            out_sends[i - 2].wait_send()
        stage = stage_in.at[i % 2, :, :, pl.ds(0, q_half)]
        stage[...] = out_grad(1 - c, i)
        out_sends.append(lanes.send(stage, out_terms.at[pl.ds(4 * i, 4)], other_core()))
    for i in range(4):
        mine = out_grad(c, i)
        out_sends[i].wait_recv()
        out_terms[4 * i : 4 * i + 4] = out_terms[4 * i : 4 * i + 4] + mine
    for each in out_sums:
        each.far()

    keys_count = 4 * rows
    kv_sends = []

    def returned(each):
        total = each.total()
        first_block = 2 * sums.index(each)
        for i in range(2):
            for side in range(2):
                to = 2 * (first_block + i) + side
                pieces_out[to, :, :part] = total[
                    :, i * part : (i + 1) * part, side * ff // 2 : (side + 1) * ff // 2
                ].astype(bf16)
                pieces_out[to, :, part:] = jnp.zeros((3, PAD - part, ff // 2), bf16)

    cosine, sine = cos_ref[...], sin_ref[...]
    for g in range(2):
        key_turned[...] = (
            kv_ref[:, :, g * 128 : (g + 1) * 128].reshape(keys_count, HEAD_SIZE).T
        )
        key_sum[...] = jnp.zeros_like(key_sum)
        value_sum[...] = jnp.zeros_like(value_sum)

        def head_back(j, carry, g=g):
            columns = at(j, HEAD_SIZE)
            query = q_ref[g * GROUP + j]
            out_back = do[g, :, columns]
            shift = lse_ref[g * GROUP + j]
            row_dot = jnp.zeros((8, rows), f32)
            for k in range(keys_count // KEYS):
                here = slice(k * KEYS, (k + 1) * KEYS)
                value = ref_dot_nt(key_block(kv_ref, g, k), query) * scale + bias[here, :]
                prob = jnp.exp(value - shift)
                prob_back = ref_dot_nt(key_block(kv_ref, 2 + g, k), out_back)
                probs[here, :] = prob
                probs_back[here, :] = prob_back
                probs_low[here, :] = prob.astype(bf16)
                product = (prob * prob_back).reshape(KEYS // 8, 8, rows)
                row_dot = row_dot + jnp.sum(product, axis=0)
            row_dot = jnp.sum(row_dot, axis=0, keepdims=True)
            for k in range(keys_count // KEYS):
                here = slice(k * KEYS, (k + 1) * KEYS)
                value = probs[here, :] * (probs_back[here, :] - row_dot)
                scores_back[here, :] = value.astype(bf16)
            value_sum[...] += ref_dot(probs_low[...], out_back)
            key_sum[...] += ref_dot(scores_back[...], query)
            query_back = (ref_dot(key_turned[...], scores_back[...]) * scale).T
            back_rows[g, :, columns] = turn_back(query_back, cosine, sine).astype(bf16)
            return carry

        lax.fori_loop(0, GROUP // 2, head_back, 0)
        if g == 0:
            for each in sums:
                each.far_q()
            for each in out_sums:
                each.joined()
            for each in out_sums:
                each.plain()
        else:
            for each in out_sums:
                each.next_q()
            for each in sums:
                returned(each)
        lax.fori_loop(GROUP // 2, GROUP, head_back, 0)
        if g == 0:
            for each in sums:
                each.next_q()
            for each in out_sums:
                each.far_q()
        kv_send[g, :, :, :128] = (key_sum[...] * scale).astype(bf16).reshape(4, rows, 128)
        kv_send[g, :, :, 128:] = value_sum[...].astype(bf16).reshape(4, rows, 128)
        for i, step in enumerate(ALONG_Z):
            to = lax.rem(z + step[1], 4)
            kv_sends.append(lanes.send(kv_send.at[g, to], kv_held.at[g, i], column_peer(*step)))

    block_send = add_block()
    for i in range(2):
        out_sum[2 * part * i : 2 * part * (i + 1)] = out_sums[i].total()
    loads[2].wait()
    every = pl.ds(0, q_half)
    kv = pl.ds(q_half, 2 * HEAD_SIZE)

    def input_back(columns, add):
        def step(i, carry):
            here = at(i, 512)
            value = ref_dot_nt(back_rows[0, :, columns], w[0, here, columns])
            value = value + ref_dot_nt(back_rows[1, :, columns], w[1, here, columns])
            da[:, here] = da[:, here] + value if add else value
            return carry

        lax.fori_loop(0, width // 512, step, 0)

    in_sends = {}

    def in_grad(g, i, columns):
        grad = ref_dot_tn(a_ref[:, i * size : (i + 1) * size], back_rows[g, :, columns])
        return grad.astype(bf16).reshape(4, 4 * part, columns.size)

    def leave(i, columns, before):
        slot = i % 2
        if before is not None:
            in_sends[before].wait_send()
        stage_in[slot, :, :, columns] = in_grad(1 - c, i, columns)
        block = pl.ds(4 * i, 4)
        in_sends[i, columns.start] = lanes.send(
            stage_in.at[slot, :, :, columns], grad_in.at[block, :, columns], other_core()
        )

    input_back(every, False)
    for copy in out_sends[2:]:
        copy.wait_send()
    for i in range(4):
        leave(i, every, (i - 2, every.start) if i >= 2 else None)
    for copy in kv_sends:
        copy.wait_recv()
    for g in range(2):
        own_part = kv_send[g, z].astype(f32)
        for i in range(3):
            own_part = own_part + kv_held[g, i].astype(f32)
        back_rows[g, :, q_half : q_half + 128] = turn_back(
            own_part[:, :128], cosine, sine
        ).astype(bf16)
        back_rows[g, :, q_half + 128 :] = own_part[:, 128:].astype(bf16)
    for i in range(4):
        leave(i, kv, (i - 2, kv.start) if i >= 2 else None)
    input_back(kv, True)
    for i in range(4):
        for columns in (every, kv):
            mine = in_grad(c, i, columns)
            in_sends[i, columns.start].wait_recv()
            block = pl.ds(4 * i, 4)
            grad_in[block, :, columns] = grad_in[block, :, columns] + mine

    def first_back(i, carry):
        here = at(i, chunk)
        x = x_ref[here, :].astype(f32)
        inverse = lax.rsqrt(jnp.mean(x * x, axis=1, keepdims=True) + EPS)
        back = da[here, :]
        carry = carry + jnp.sum(back * x * inverse, axis=0, keepdims=True)
        dz = back * gains[8:9, :]
        mean = jnp.mean(dz * x, axis=1, keepdims=True)
        value = dh1[here, :] + inverse * dz - x * (inverse * inverse * inverse * mean)
        tokens_out[here, :] = value.astype(bf16)
        return carry

    attn_sum = lax.fori_loop(0, rows // chunk, first_back, jnp.zeros((1, width), f32))
    number = lax.broadcasted_iota(jnp.int32, (MISC, width), 0)
    gain_grads = jnp.where(number == 8, attn_sum, jnp.where(number == 9, mix_sum, 0.0))
    gain_grads = gain_grads.T.astype(bf16).reshape(16, 4 * part, MISC)
    grad_in[:, :, tail] = grad_in[:, :, tail] + gain_grads
    crossing = lanes.send(grad_in.at[:, :, tail], misc_held, other_core())
    crossing.wait()
    grad_in[:, :, tail] = grad_in[:, :, tail] + misc_held[...]
    for i in range(2, 4):
        for columns in (every, kv):
            in_sends[i, columns.start].wait_send()
    block_send.wait()
    for each in sums + out_sums:
        each.drain()
    for copy in kv_sends:
        copy.wait_send()
    for copy in near_copies.values():
        copy.wait_send()
    for copy in (early_partner, early_cross, late_cross, late_partner, far_partner, far_cross):
        copy.wait_send()


def attention_back(
    back, gate_back, gates, b, h1, tokens, rows_in, a, o, q, kv, lse, cosine, sine, segments, w_attn, parts, expert_grads
):
    rows, width = h1.shape
    keys = 4 * rows
    q_half = o.shape[1] // 2
    qkv = q_half + 2 * HEAD_SIZE
    sds = jax.ShapeDtypeStruct
    count, block_rows, ff = expert_grads.shape[1:]
    half_block = (count, block_rows // 2, ff)
    ring = [
        pltpu.VMEM((2, 2) + half_block, bf16),
        pltpu.VMEM((2, 4) + half_block, bf16),
        pltpu.VMEM((4,) + half_block, bf16),
    ]
    out_half = (block_rows // 2, q_half)
    out_ring = [
        pltpu.VMEM((2, 2) + out_half, bf16),
        pltpu.VMEM((2, 4) + out_half, bf16),
        pltpu.VMEM((4,) + out_half, bf16),
    ]
    return pl.pallas_call(
        attention_back_kernel,
        name="attention_back",
        out_shape=(
            sds((16, block_rows, qkv + MISC), bf16),
            sds((block_rows, q_half), f32),
            sds((rows, width), bf16),
            sds((rows, width), bf16),
            sds((rows // 2, width), bf16),
            sds((8, count, PAD, ff // 2), bf16),
        ),
        in_specs=[ANY] + [VMEM] * 4 + [ANY] * 2 + [VMEM] * 5 + [ANY] * 2 + [VMEM] + [ANY] * 3,
        out_specs=(VMEM,) * 6,
        scratch_shapes=[
            pltpu.VMEM((2, width, qkv + MISC), bf16),
            pltpu.VMEM((keys, rows), f32),
            pltpu.VMEM((HEAD_SIZE, keys), bf16),
            pltpu.VMEM((rows, width), f32),
            pltpu.VMEM((rows, width), f32),
            pltpu.VMEM((rows, width), bf16),
            pltpu.VMEM((2, rows, q_half), bf16),
            pltpu.VMEM((2, rows, qkv), bf16),
            pltpu.VMEM((keys, HEAD_SIZE), f32),
            pltpu.VMEM((keys, HEAD_SIZE), f32),
            pltpu.VMEM((keys, rows), f32),
            pltpu.VMEM((keys, rows), f32),
            pltpu.VMEM((keys, rows), bf16),
            pltpu.VMEM((keys, rows), bf16),
            pltpu.VMEM((2, 4, rows, 2 * HEAD_SIZE), bf16),
            pltpu.VMEM((2, 3, rows, 2 * HEAD_SIZE), bf16),
            pltpu.VMEM((2, 4, block_rows, qkv), bf16),
            pltpu.VMEM((16, block_rows, MISC), bf16),
            pltpu.VMEM((2, rows, width), bf16),
            pltpu.VMEM((4, rows, width), bf16),
            pltpu.VMEM((2, rows // 2, width), bf16),
            pltpu.VMEM((2, rows, width), bf16),
            pltpu.VMEM(expert_grads.shape, bf16),
        ]
        + ring
        + ring
        + [pltpu.VMEM((16, block_rows, q_half), bf16)]
        + out_ring
        + out_ring
        + [
            pltpu.VMEM((rows, width), bf16),
            pltpu.VMEM((rows, width), bf16),
            pltpu.VMEM((rows, HEAD_SIZE), f32),
            pltpu.VMEM((rows, HEAD_SIZE), f32),
        ]
        + lanes_scratch(100)
        + [
            pltpu.SemaphoreType.DMA((3,)),
            pltpu.SemaphoreType.DMA((8,)),
        ],
        compiler_params=pltpu.CompilerParams(
            collective_id=3, has_side_effects=True, vmem_limit_bytes=62 * 2**20
        ),
    )(
        back, gate_back, gates, b, h1, tokens, rows_in, a, o, q, kv, lse, cosine, sine, segments, w_attn, parts, expert_grads
    )


def experts_kernel(
    rows_ref,
    gate_ref,
    grads_ref,
    slot_rows,
    others_ref,
    block_ref,
    mix_out,
    weight_grads,
    back_out,
    gate_back_out,
    rows_all,
    held,
    w_gate,
    w_up,
    w_down,
    picked,
    picked_grads,
    hidden_back,
    hidden_gated,
    gate_low,
    up_low,
    mix_stage,
    near,
    far,
    nearest,
    gates_in,
    gate_back,
    s_sem,
    r_sem,
    own,
    stage_sem,
    near_send,
    near_recv,
):
    c, h, l = place()
    me = (c * 2 + h) * 2 + l
    barrier = pltpu.get_barrier_semaphore()
    pl.semaphore_wait(barrier, greet_column(barrier) + greet_chips(barrier))
    lanes = Lanes(s_sem, r_sem)
    rows, width = rows_ref.shape
    slots = picked.shape[1]
    ff = w_gate.shape[2]
    block = 2 * rows

    ring = ColumnRing(lanes, rows_ref, rows_all)
    ring.start()
    index = chip_index({"x": 0, "y": 0})
    half = block_ref.shape[1] // 2
    weight_rings = []
    for weight, target in ((0, w_gate),):
        for low, a, b in ((0, "x", "y"), (half, "y", "x")):
            mine = pl.ds(low, half)

            def view(index, columns, mine=mine, target=target):
                return target.at[index, mine, columns]

            own_part = block_ref.at[weight, mine]
            weight_rings.append(ChipRing(lanes, own_part, view, ff // 2, ff, a, b))

    def go(step, *args):
        for each in weight_rings:
            getattr(each, step)(*args)

    go("start")
    local = [
        pltpu.make_async_copy(grads_ref, held, own.at[0]),
        pltpu.make_async_copy(others_ref.at[1], w_down, own.at[1]),
        pltpu.make_async_copy(block_ref.at[0], w_gate.at[index], own.at[2]),
        pltpu.make_async_copy(others_ref.at[0], w_up, own.at[3]),
        pltpu.make_async_copy(rows_ref, rows_all.at[me], own.at[4]),
        pltpu.make_async_copy(gate_ref.at[me], gates_in.at[me], own.at[5]),
    ]
    for copy in local:
        copy.start()
    gate_copies = []
    for step in COLUMN:
        peer = column_peer(*step)
        to = (peer["c"] * 2 + peer["h"]) * 2 + peer["l"]
        gate_copies.append(lanes.send(gate_ref.at[to], gates_in.at[me], peer))

    def pick_of(k):
        number = lax.broadcasted_iota(jnp.int32, (slots, block), 0).astype(f32)
        return slot_rows[k] == number

    def low(mask):
        return mask.astype(f32).astype(bf16)

    def columns_of(weight, columns):
        return weight[:, :, columns].reshape(width, narrow)

    def rows_of(weight, i):
        return weight[pl.ds(8 * i, 8)].reshape(ff, ff)

    wide = 512
    narrow = 256

    local[0].wait()
    local[1].wait()

    def prepare(k, carry):
        pick = low(pick_of(k))

        def gather(i, carry):
            columns = at(i, wide)
            values = ref_dot(pick, held[pl.ds(2 * k, 2), :, columns].reshape(block, wide))
            picked_grads[k, :, columns] = values.astype(bf16)
            return carry

        lax.fori_loop(0, width // wide, gather, 0)

        def down(i, carry):
            columns = at(i, narrow)
            hidden_back[k, :, columns] = ref_dot(picked_grads[k], columns_of(w_down, columns))
            return carry

        lax.fori_loop(0, ff // narrow, down, 0)
        return carry

    lax.fori_loop(0, 2, prepare, 0)
    go("relay_first")
    go("relay_turn", 0)
    ring.relay()
    go("relay_second")
    lax.fori_loop(2, 4, prepare, 0)
    go("relay_turn", -1)
    go("relay_turn", 1)
    ring.nearest()
    go("relay_turn", 2)
    go("finish")
    for copy in local[2:]:
        copy.wait()
    for copy in gate_copies:
        copy.wait()
    ring.shared["own"].wait_recv()
    ring.shared["partner"].wait_recv()

    def expert(k, stage):
        pick = pick_of(k)
        pick_low = low(pick)
        spread = pick.astype(f32).T.astype(bf16)
        gates = gates_in[pl.ds(2 * k, 2)]
        gate_row = jnp.concatenate([gates[0], gates[1]], axis=1)
        gate = jnp.sum(jnp.where(pick, gate_row, 0.0), axis=1, keepdims=True)

        def gather(i, carry):
            columns = at(i, wide)
            values = ref_dot(pick_low, rows_all[pl.ds(2 * k, 2), :, columns].reshape(block, wide))
            picked[k, :, columns] = values.astype(bf16)
            return carry

        lax.fori_loop(0, width // wide, gather, 0)

        def hide(i, total):
            columns = at(i, narrow)
            gate_act = ref_dot(picked[k], columns_of(w_gate, columns))
            up_act = ref_dot(picked[k], columns_of(w_up, columns))
            back = hidden_back[k, :, columns]
            sigmoid_act = 0.5 + 0.5 * jnp.tanh(0.5 * gate_act)
            silu_act = gate_act * sigmoid_act
            hidden = silu_act * up_act
            hidden_gated[k, :, columns] = (hidden * gate).astype(bf16)
            total = total + jnp.sum(hidden * back, axis=1, keepdims=True)
            back = back * gate
            slope = sigmoid_act * (1.0 + gate_act * (1.0 - sigmoid_act))
            gate_low[k, :, columns] = (back * up_act * slope).astype(bf16)
            up_low[k, :, columns] = (back * silu_act).astype(bf16)
            return total

        gate_slots = lax.fori_loop(0, ff // narrow, hide, jnp.zeros((slots, 1), f32))
        back_row = jnp.sum(jnp.where(pick, gate_slots, 0.0), axis=0, keepdims=True)
        gate_back[2 * k] = back_row[:, :rows]
        gate_back[2 * k + 1] = back_row[:, rows:]

        def leave(i, carry):
            columns = at(i, ff)
            out = ref_dot_nt(hidden_gated[k], rows_of(w_down, i)).astype(bf16)
            mix_stage[stage, :, :, columns] = (
                ref_dot(spread, out).astype(bf16).reshape(2, rows, ff)
            )
            back = ref_dot_nt(gate_low[k], rows_of(w_gate, i))
            back = (back + ref_dot_nt(up_low[k], rows_of(w_up, i))).astype(bf16)
            held[pl.ds(2 * k, 2), :, columns] = (
                ref_dot(spread, back).astype(bf16).reshape(2, rows, ff)
            )
            return carry

        lax.fori_loop(0, width // ff, leave, 0)

    def stage_copy(k, stage):
        return pltpu.make_async_copy(
            mix_stage.at[stage], mix_out.at[pl.ds(2 * k, 2)], stage_sem.at[stage]
        )

    def near_copy(side, i):
        return pltpu.make_async_remote_copy(
            src_ref=held.at[pl.ds(((1 - c) * 2 + side) * 2, 2)],
            dst_ref=near.at[pl.ds(side * 2, 2)],
            send_sem=near_send.at[i],
            recv_sem=near_recv.at[i],
            device_id=other_core(),
            device_id_type=MESH,
        )

    def add_near(z):
        mine = held.at[c * 4 + z]

        def add(i, carry):
            here = at(i, 64)
            mine[here] = mine[here] + near[z, here]
            return carry

        lax.fori_loop(0, rows // 64, add, 0)

    half = rows // 2
    first, second = pl.ds(0, half), pl.ds(half, half)
    z = {
        "own": h * 2 + l,
        "partner": h * 2 + 1 - l,
        "cross": (1 - h) * 2 + 1 - l,
        "far": (1 - h) * 2 + l,
    }

    def block_at(which, part):
        return held.at[c * 4 + z[which], part]

    order = [(1 - c) * 2 + h, (1 - c) * 2 + 1 - h, c * 2 + 1 - h, c * 2 + h]
    expert(order[0], 0)
    near_copy(h, 0).start()
    stage_copy(order[0], 0).start()
    ring.far()
    ring.shared["cross"].wait_recv()
    ring.shared["far"].wait_recv()
    expert(order[1], 1)
    near_copy(1 - h, 1).start()
    stage_copy(order[1], 1).start()
    stage_copy(order[0], 0).wait()
    expert(order[2], 0)
    stage_copy(order[2], 0).start()
    near_copy(1 - h, 1).wait_recv()
    add_near(z["far"])
    far_partner = lanes.send(block_at("far", first), far.at[0], partner())
    far_cross = lanes.send(block_at("far", second), far.at[1], cross())
    add_near(z["cross"])
    early_cross = lanes.send(block_at("cross", second), nearest.at[1, second], cross())
    stage_copy(order[1], 1).wait()
    expert(order[3], 1)
    stage_copy(order[3], 1).start()
    near_copy(h, 0).wait_recv()
    add_near(z["partner"])
    early_partner = lanes.send(block_at("partner", first), nearest.at[0, first], partner())
    add_near(z["own"])
    sends = []
    gate_own = pltpu.make_async_copy(gate_back.at[me], gate_back_out.at[me], own.at[6])
    gate_own.start()
    for step in COLUMN:
        peer = column_peer(*step)
        to = (peer["c"] * 2 + peer["h"]) * 2 + peer["l"]
        sends.append(lanes.send(gate_back.at[to], gate_back_out.at[me], peer))

    def weight_grad(values, others, target, number):
        part = 384

        def make(i, carry):
            left = values[:, :, at(i, part)].reshape(4 * slots, part)
            grad = ref_dot_tn(left, others[...].reshape(4 * slots, ff)).astype(bf16)
            target[pl.ds(4 * i, 4)] = grad.reshape(4, part // 4, ff)
            return carry

        lax.fori_loop(0, width // part, make, 0)
        copy = pltpu.make_async_copy(target, weight_grads.at[:, number], own.at[1 + number])
        copy.start()
        return copy

    far_partner.wait_recv()
    mine = block_at("cross", first)
    mine[...] = mine[...] + far[0]
    late_cross = lanes.send(mine, nearest.at[1, first], cross())
    far_cross.wait_recv()
    mine = block_at("partner", second)
    mine[...] = mine[...] + far[1]
    late_partner = lanes.send(mine, nearest.at[0, second], partner())
    go("drain")
    grad_copies = [
        weight_grad(picked_grads, hidden_gated, w_down, 2),
        weight_grad(picked, gate_low, w_gate, 0),
        weight_grad(picked, up_low, w_up, 1),
    ]
    for copy in (early_partner, early_cross, late_cross, late_partner):
        copy.wait_recv()

    def finish(i, carry):
        here = at(i, 64)
        total = held[c * 4 + z["own"], here].astype(f32)
        back_out[here, :] = (
            total + nearest[0, here].astype(f32) + nearest[1, here].astype(f32)
        )
        return carry

    lax.fori_loop(0, rows // 64, finish, 0)
    for copy in (early_partner, early_cross, late_cross, late_partner, far_partner, far_cross):
        copy.wait_send()
    for i, side in ((0, h), (1, 1 - h)):
        near_copy(side, i).wait_send()
    for copy in sends + grad_copies + [gate_own]:
        copy.wait()
    stage_copy(order[2], 0).wait()
    stage_copy(order[3], 1).wait()
    ring.drain()


def experts_of_column(rows, gates, grads_all, slots, others, block):
    count, width = rows.shape
    ff = others.shape[3]
    return pl.pallas_call(
        experts_kernel,
        name="experts",
        out_shape=(
            jax.ShapeDtypeStruct((8, count, width), bf16),
            jax.ShapeDtypeStruct((16, 3) + others.shape[2:], bf16),
            jax.ShapeDtypeStruct((count, width), f32),
            jax.ShapeDtypeStruct(gates.shape, f32),
        ),
        in_specs=[VMEM, VMEM, ANY, VMEM, ANY, VMEM],
        out_specs=(HBM, HBM, VMEM, VMEM),
        scratch_shapes=[
            pltpu.VMEM((8, count, width), bf16),
            pltpu.VMEM((8, count, width), bf16),
            pltpu.VMEM((16, width // 16, ff), bf16),
            pltpu.VMEM((16, width // 16, ff), bf16),
            pltpu.VMEM((16, width // 16, ff), bf16),
            pltpu.VMEM((4, SLOTS, width), bf16),
            pltpu.VMEM((4, SLOTS, width), bf16),
            pltpu.VMEM((4, SLOTS, ff), f32),
            pltpu.VMEM((4, SLOTS, ff), bf16),
            pltpu.VMEM((4, SLOTS, ff), bf16),
            pltpu.VMEM((4, SLOTS, ff), bf16),
            pltpu.VMEM((2, 2, count, width), bf16),
            pltpu.VMEM((4, count, width), bf16),
            pltpu.VMEM((2, count // 2, width), bf16),
            pltpu.VMEM((2, count, width), bf16),
            pltpu.VMEM(gates.shape, f32),
            pltpu.VMEM(gates.shape, f32),
        ]
        + lanes_scratch(64)
        + [
            pltpu.SemaphoreType.DMA((7,)),
            pltpu.SemaphoreType.DMA((2,)),
            pltpu.SemaphoreType.DMA((2,)),
            pltpu.SemaphoreType.DMA((2,)),
        ],
        compiler_params=pltpu.CompilerParams(
            collective_id=4, has_side_effects=True, vmem_limit_bytes=60 * 2**20
        ),
    )(rows, gates, grads_all, slots[:, None, :], others, block)


def return_kernel(
    part,
    misc_at,
    in_ref,
    out_ref,
    expert_ref,
    tokens_ref,
    block_ref,
    block_half,
    grads_out,
    misc_out,
    expert_out,
    tokens_out,
    block_out,
    near,
    near_p0,
    rest_p0,
    near_q0,
    near_p1,
    rest_p1,
    near_q1,
    pieces,
    landed,
    misc_landed,
    s_sem,
    r_sem,
    ps,
    pr,
    ms,
    mr,
    own,
):
    c, h, l = place()
    z = h * 2 + l
    me = c * 4 + z
    barrier = pltpu.get_barrier_semaphore()
    pl.semaphore_wait(barrier, greet_column(barrier) + greet_chips(barrier))
    lanes = Lanes(s_sem, r_sem)
    width = near.shape[2]
    half = near.shape[1] // 2
    load = pltpu.make_async_copy(in_ref, near, own.at[4])
    load.start()
    sums = []
    for low, p, q, held in (
        (0, "y", "x", (near_p0, rest_p0, near_q0)),
        (half, "x", "y", (near_p1, rest_p1, near_q1)),
    ):

        def view(index, columns, mine=pl.ds(low, half)):
            return near.at[index, mine, columns]

        sums.append(ChipSum(lanes, view, 640, width, p, q, *held))
    load.wait()
    for each in sums:
        each.far()
    own_copy = pltpu.make_async_copy(expert_ref.at[me], expert_out.at[me], own.at[0])
    own_copy.start()
    own_tokens = pltpu.make_async_copy(tokens_ref, tokens_out.at[l], own.at[1])
    own_tokens.start()
    own_block = pltpu.make_async_copy(block_ref, block_out.at[l], own.at[2])
    own_block.start()
    count = block_half.shape[0]
    rest = pl.ds(count, count)
    had = pltpu.make_async_copy(block_half, block_out.at[1 - l, pl.ds(0, count)], own.at[3])
    had.start()
    expert_copies = [
        lanes.send(tokens_ref, tokens_out.at[l], partner()),
        lanes.send(block_ref.at[rest], block_out.at[l, rest], partner()),
    ]
    for step in COLUMN:
        peer = column_peer(*step)
        to = (peer["c"] * 2 + peer["h"]) * 2 + peer["l"]
        expert_copies.append(lanes.send(expert_ref.at[to], expert_out.at[me], peer))

    for each in sums:
        each.joined()
    for each in sums:
        each.plain()
    for each in sums:
        each.far_q()
    for each in sums:
        each.next_q()
    for number, each in enumerate(sums):
        total = each.total()
        for i in range(2):
            pieces[2 * number + i, :, :width] = total[i * part : (i + 1) * part]
    for k in range(4):
        pieces[k, :, width:] = out_ref[k * part : (k + 1) * part, :]

    def to_owner(target, owner, src, dst, send_sem, recv_sem, asked):
        is_me = (owner["c"] == c) & (owner["h"] == h) & (owner["l"] == l)
        there = pltpu.make_async_remote_copy(
            src_ref=src,
            dst_ref=dst,
            send_sem=send_sem,
            recv_sem=recv_sem,
            device_id=owner,
            device_id_type=MESH,
        )
        here = pltpu.make_async_copy(src, dst, recv_sem)
        pl.when(asked & jnp.logical_not(is_me))(there.start)
        pl.when(asked & is_me)(here.start)
        return asked & jnp.logical_not(is_me), there

    sent = []
    everyone = c < 2
    for target in range(4):
        owner = {"c": target // 2, "h": target % 2, "l": c}
        sent.append(
            to_owner(
                target, owner, pieces.at[target], landed.at[z], ps.at[target], pr.at[z], everyone
            )
        )
    misc = pl.ds(misc_at, MISC)
    for target in range(4):
        owner = {"c": target // 2, "h": target % 2, "l": 1}
        sent.append(
            to_owner(
                target,
                owner,
                pieces.at[target, :, misc],
                misc_landed.at[z],
                ms.at[target],
                mr.at[z],
                c == 0,
            )
        )
    for source in range(4):
        pltpu.make_async_copy(pieces.at[0], landed.at[source], pr.at[source]).wait()
    grads_out[...] = (landed[0] + landed[1]) + (landed[2] + landed[3])

    def from_core():
        for source in range(4):
            pltpu.make_async_copy(
                pieces.at[0, :, misc], misc_landed.at[source], mr.at[source]
            ).wait()
        misc_out[...] = (misc_landed[0] + misc_landed[1]) + (misc_landed[2] + misc_landed[3])

    def from_piece():
        misc_out[...] = (landed[0, :, misc] + landed[1, :, misc]) + (
            landed[2, :, misc] + landed[3, :, misc]
        )

    pl.when(l == 1)(from_core)
    pl.when(l == 0)(from_piece)
    for asked, there in sent:
        pl.when(asked)(there.wait_send)
    for each in sums:
        each.drain()
    own_copy.wait()
    own_tokens.wait()
    own_block.wait()
    had.wait()
    for copy in expert_copies:
        copy.wait()


def return_gradients(grad_in, out_sum, expert_pieces, tokens, block, block_half, part, misc_at):
    width, rows = grad_in.shape[2], grad_in.shape[1]
    full = width + out_sum.shape[1]
    half = rows // 2
    ring = [
        pltpu.VMEM((2, 2, half, width), bf16),
        pltpu.VMEM((2, 4, half, width), bf16),
        pltpu.VMEM((4, half, width), bf16),
    ]
    return pl.pallas_call(
        functools.partial(return_kernel, part, misc_at),
        name="return_gradients",
        out_shape=(
            jax.ShapeDtypeStruct((part, full), f32),
            jax.ShapeDtypeStruct((part, MISC), f32),
            jax.ShapeDtypeStruct(expert_pieces.shape, expert_pieces.dtype),
            jax.ShapeDtypeStruct((2,) + tokens.shape, tokens.dtype),
            jax.ShapeDtypeStruct((2,) + block.shape, block.dtype),
        ),
        in_specs=[ANY] + [VMEM] * 5,
        out_specs=(VMEM, VMEM, HBM, HBM, HBM),
        scratch_shapes=[pltpu.VMEM((16, rows, width), bf16)]
        + ring
        + ring
        + [
            pltpu.VMEM((4, part, full), f32),
            pltpu.VMEM((4, part, full), f32),
            pltpu.VMEM((4, part, MISC), f32),
        ]
        + lanes_scratch(50)
        + [
            pltpu.SemaphoreType.DMA((4,)),
            pltpu.SemaphoreType.DMA((4,)),
            pltpu.SemaphoreType.DMA((4,)),
            pltpu.SemaphoreType.DMA((4,)),
            pltpu.SemaphoreType.DMA((5,)),
        ],
        compiler_params=pltpu.CompilerParams(
            collective_id=7, has_side_effects=True, vmem_limit_bytes=62 * 2**20
        ),
    )(grad_in, out_sum, expert_pieces, tokens, block, block_half)


def body(
    tokens,
    segments,
    routes,
    attn_gain,
    w_query,
    key_matrix,
    value_matrix,
    w_output,
    mix_gain,
    w_router,
    w_gate,
    w_up,
    w_down,
    block_cotangent,
):
    c, h, l = place()
    model_width = tokens.shape[2]
    rows = tokens.shape[1] // 2
    experts, part, ff_half = w_gate.shape
    q_half = w_query.shape[1]

    kv_width = key_matrix.shape[1]
    in_width = q_half + 2 * kv_width + MISC
    halves = (2, rows, model_width)
    tables = [jnp.asarray(table) for table in rope_tables(segments.shape[1])]
    (
        w_attn,
        grads_all,
        slots,
        others_full,
        expert_block,
        normed_in,
        q,
        kv,
        attended,
        lse,
        residual,
        normed_mix,
        gates,
    ) = attention(
        (w_query, key_matrix, value_matrix, w_output.T, w_router),
        (attn_gain[None], mix_gain[None]),
        (w_gate, w_up, w_down),
        block_cotangent.reshape(halves),
        tokens.reshape(halves),
        routes[0].T,
        segments,
        tables,
        part,
    )
    w_attn = w_attn.reshape(2, model_width, in_width + q_half)
    mix_parts, expert_grads, mix_back, gate_back = experts_of_column(
        normed_mix, gates, grads_all, slots.reshape(4, 2 * rows), others_full, expert_block
    )
    grad_in, out_sum, tokens_back, block_out, block_half, pieces = attention_back(
        mix_back,
        gate_back,
        gates,
        normed_mix,
        residual,
        tokens.reshape(halves),
        block_cotangent.reshape(halves),
        normed_in,
        attended,
        q,
        kv,
        lse,
        *tables,
        segments,
        w_attn,
        mix_parts,
        expert_grads,
    )

    returned, misc_back, expert_back, tokens_back, block_out = return_gradients(
        grad_in,
        out_sum,
        pieces,
        tokens_back,
        block_out,
        block_half,
        part,
        in_width - MISC,
    )
    expert_back = expert_back[:, :, :part].astype(f32)
    return (
        block_out.reshape(1, 2 * rows, model_width),
        tokens_back.reshape(1, 2 * rows, model_width).astype(f32),
        misc_back[:, experts],
        returned[:, :q_half],
        returned[:, q_half : q_half + kv_width],
        returned[:, q_half + kv_width : q_half + 2 * kv_width],
        returned[:, in_width:].T,
        misc_back[:, experts + 1],
        misc_back[:, :experts],
        expert_back[:, 0],
        expert_back[:, 1],
        expert_back[:, 2],
    )


def solution(mesh):
    split = Mesh(mesh.devices.reshape(4, 4, 2, 2, 2), ("x", "y", "c", "h", "l"))
    fsdp = ("x", "y", "c")
    owner = ("x", "y", "c", "h")
    return jax.shard_map(
        body,
        mesh=split,
        in_specs=(
            P(fsdp, "h", None),
            P(fsdp, None),
            P(fsdp, "h", None),
            P(owner),
            P(owner, "l"),
            P(owner, "l"),
            P(owner, "l"),
            P("l", owner),
            P(owner),
            P(owner, None),
            P(None, owner, "l"),
            P(None, owner, "l"),
            P(None, owner, "l"),
            P(fsdp, "h", None),
        ),
        out_specs=(
            P(fsdp, "h", None),
            P(fsdp, "h", None),
            P(owner),
            P(owner, "l"),
            P(owner, "l"),
            P(owner, "l"),
            P("l", owner),
            P(owner),
            P(owner, None),
            P(None, owner, "l"),
            P(None, owner, "l"),
            P(None, owner, "l"),
        ),
        check_vma=False,
    )
```

```python
import functools

import jax
import jax.numpy as jnp
import numpy as np
from jax import lax
from jax.experimental import pallas as pl
from jax.experimental.pallas import tpu as pltpu
from jax.sharding import Mesh
from jax.sharding import PartitionSpec as P

QUERY_HEADS = 12
KEY_VALUE_HEADS = 2
HEAD_SIZE = 128
GROUP = QUERY_HEADS // KEY_VALUE_HEADS
EPS = 1e-06
ROPE_BASE = 1000000.0
NEG_FILL = -1e30
MISC = 128
SLOTS = 320
PAD = 32
MESH = pl.DeviceIdType.MESH
ANY = pl.BlockSpec(memory_space=pl.ANY)
HBM = pl.BlockSpec(memory_space=pltpu.HBM)
VMEM = pl.BlockSpec(memory_space=pltpu.VMEM)
f32 = jnp.float32
bf16 = jnp.bfloat16


def rope_tables(count):
    exponents = -np.arange(HEAD_SIZE // 2, dtype=np.float64) * (2.0 / HEAD_SIZE)
    frequency = (ROPE_BASE**exponents).astype(np.float32)
    angles = np.arange(count, dtype=np.float32)[:, None] * frequency[None, :]
    angles = angles.astype(np.float64)
    cosine, sine = np.cos(angles).astype(np.float32), np.sin(angles).astype(np.float32)
    return np.concatenate([cosine, cosine], axis=1), np.concatenate([-sine, sine], axis=1)


def place():
    return lax.axis_index("c"), lax.axis_index("h"), lax.axis_index("l")


def column_peer(core_step, z_step):
    c, h, l = place()
    z = lax.rem(h * 2 + l + z_step, 4)
    return {"c": lax.rem(c + core_step, 2), "h": z // 2, "l": lax.rem(z, 2)}


def at_z(core, z):
    return {"c": core, "h": z // 2, "l": lax.rem(z, 2)}


def greet(steps):
    barrier = pltpu.get_barrier_semaphore()
    for core_step, z_step in steps:
        pl.semaphore_signal(
            barrier, inc=1, device_id=column_peer(core_step, (4 - z_step) % 4), device_id_type=MESH
        )
    pl.semaphore_wait(barrier, len(steps))


def send(src, dst, send_sem, recv_sem, peer):
    copy = pltpu.make_async_remote_copy(
        src_ref=src,
        dst_ref=dst,
        send_sem=send_sem,
        recv_sem=recv_sem,
        device_id=peer,
        device_id_type=MESH,
    )
    copy.start()
    return copy


COLUMN = [(0, 1), (0, 2), (0, 3), (1, 0), (1, 1), (1, 2), (1, 3)]
ALONG_Z = [(0, 1), (0, 2), (0, 3)]


class Lanes:
    def __init__(self, send_sem, recv_sem):
        self.send_sem, self.recv_sem, self.used = send_sem, recv_sem, 0

    def send(self, src, dst, peer):
        i = self.used
        self.used += 1
        return send(src, dst, self.send_sem.at[i], self.recv_sem.at[i], peer)


def lanes_scratch(count):
    return [pltpu.SemaphoreType.DMA((count,)), pltpu.SemaphoreType.DMA((count,))]


def chip_peer(axis, step):
    return {axis: lax.rem(lax.axis_index(axis) + step + 4, 4)}


def greet_chips(barrier):
    for axis in ("x", "y"):
        for step in (1, 3):
            pl.semaphore_signal(
                barrier, inc=1, device_id=chip_peer(axis, step), device_id_type=MESH
            )
    return 4


def greet_column(barrier):
    for step in COLUMN:
        pl.semaphore_signal(barrier, inc=1, device_id=column_peer(*step), device_id_type=MESH)
    return len(COLUMN)


def partner():
    return {"l": 1 - lax.axis_index("l")}


def cross():
    return {"h": 1 - lax.axis_index("h"), "l": 1 - lax.axis_index("l")}


def other_core():
    return {"c": 1 - lax.axis_index("c")}


class ColumnRing:
    def __init__(self, lanes, rows_ref, out_ref):
        c, h, l = place()
        self.lanes, self.rows, self.out = lanes, rows_ref, out_ref
        half = rows_ref.shape[0] // 2
        self.first, self.second = pl.ds(0, half), pl.ds(half, half)
        self.at = {
            "own": c * 4 + h * 2 + l,
            "partner": c * 4 + h * 2 + 1 - l,
            "cross": c * 4 + (1 - h) * 2 + 1 - l,
            "far": c * 4 + (1 - h) * 2 + l,
        }
        self.shared = {}

    def share(self, which):
        block = self.out.at[self.at[which]]
        self.shared[which] = self.lanes.send(block, block, other_core())

    def half_to(self, part, peer):
        return self.lanes.send(self.rows.at[part], self.out.at[self.at["own"], part], peer)

    def start(self):
        self.partner_first = self.half_to(self.first, partner())
        self.cross_second = self.half_to(self.second, cross())
        self.partner_second = self.half_to(self.second, partner())
        self.cross_first = self.half_to(self.first, cross())
        here = self.out.at[self.at["own"]]
        self.shared["own"] = self.lanes.send(self.rows, here, other_core())

    def relay(self):
        self.partner_first.wait_recv()
        block = self.out.at[self.at["partner"], self.first]
        self.far_cross = self.lanes.send(block, block, cross())
        self.cross_second.wait_recv()
        block = self.out.at[self.at["cross"], self.second]
        self.far_partner = self.lanes.send(block, block, partner())

    def nearest(self):
        self.partner_second.wait_recv()
        self.share("partner")
        self.cross_first.wait_recv()
        self.share("cross")

    def far(self):
        self.far_cross.wait_recv()
        self.far_partner.wait_recv()
        self.share("far")

    def drain(self):
        for copy in (self.partner_first, self.partner_second, self.cross_first, self.cross_second):
            copy.wait_send()
        for copy in (self.far_cross, self.far_partner):
            copy.wait_send()
        for copy in self.shared.values():
            copy.wait_send()

    def finish(self):
        self.far()
        for copy in self.shared.values():
            copy.wait_recv()
        self.drain()


def chip_index(steps):
    x = lax.rem(lax.axis_index("x") + steps["x"] + 4, 4)
    y = lax.rem(lax.axis_index("y") + steps["y"] + 4, 4)
    return x * 4 + y


def shifted(columns, start, size):
    if columns == slice(None):
        return pl.ds(start, size)
    return pl.ds(start + columns.start, columns.size)


class ChipRing:
    def __init__(self, lanes, own, view, cut, width, a, b, line=None):
        self.lanes, self.own, self.view = lanes, own, view
        self.low, self.high = pl.ds(0, cut), pl.ds(cut, width - cut)
        self.a, self.b, self.line = a, b, line
        self.sent, self.near, self.last = [], [], {}

    def ref(self, da, db, columns=slice(None)):
        return self.view(chip_index({self.a: da, self.b: db}), columns)

    def copy(self, src, dst, axis, step):
        made = self.lanes.send(src, dst, chip_peer(axis, step))
        self.sent.append(made)
        return made

    def start(self):
        here = self.ref(0, 0)
        self.first = [self.copy(self.own, here, self.a, step) for step in (1, -1)]
        self.turn = {0: [self.copy(self.own, here, self.b, step) for step in (1, -1)]}

    def pass_on(self, da):
        block = self.ref(da, 0)
        self.turn[da] = [self.copy(block, block, self.b, step) for step in (1, -1)]

    def relay_first(self):
        for copy in self.first:
            copy.wait_recv()
        block = self.ref(-1, 0, self.low)
        one = self.copy(block, block, self.a, 1)
        block = self.ref(1, 0, self.high)
        self.second = [one, self.copy(block, block, self.a, -1)]
        self.pass_on(-1)
        self.pass_on(1)

    def relay_turn(self, da):
        for copy in self.turn[da]:
            copy.wait_recv()
        step = 1 if da in (0, -1) else -1
        block = self.ref(da, -step)
        self.last[da] = self.copy(block, block, self.b, step)

    def relay_second(self):
        for copy in self.second:
            copy.wait_recv()
        self.pass_on(2)

    def end(self, da):
        self.last[da].wait_recv()
        if self.line is not None:
            block = self.line(lax.rem(lax.axis_index(self.a) + da + 4, 4))
            self.near.append(self.lanes.send(block, block, other_core()))

    def finish(self):
        for da in (0, -1, 1, 2):
            self.end(da)

    def drain(self):
        for copy in self.sent:
            copy.wait_send()
        for copy in self.near:
            copy.wait()


class ChipSum:
    def __init__(self, lanes, view, source, cut, width, p, q, near_p, rest_p, near_q):
        self.lanes, self.view, self.source = lanes, view, source
        self.low, self.high = pl.ds(0, cut), pl.ds(cut, width - cut)
        self.p, self.q = p, q
        self.near_p, self.rest_p, self.near_q = near_p, rest_p, near_q
        self.sent, self.next_copies = [], {}

    def index(self, dp, dq):
        return chip_index({self.p: dp, self.q: dq})

    def copy(self, src, dst, axis, step):
        made = self.lanes.send(src, dst, chip_peer(axis, step))
        self.sent.append(made)
        return made

    def own(self, dp, dq, columns=slice(None)):
        return self.view(self.index(dp, dq), columns)

    def side(self, i, columns):
        lead = (slice(None),) * (len(self.near_q.shape) - 2)
        return self.near_q.at[(i,) + lead + (columns,)]

    def far(self):
        self.far_copies = {}
        for dq, step, i in ((2, 1, 0), (3, -1, 0), (1, 1, 1), (0, -1, 1)):
            direction = 0 if step == 1 else 1
            self.far_copies[direction, i] = self.copy(
                self.source(self.index(2, dq)), self.near_p.at[direction, i], self.p, step
            )

    def plain(self):
        for dq, step in ((2, -1), (3, 1), (1, -1), (0, 1)):
            self.next_to(dq, step, self.source(self.index(step, dq)))

    def next_to(self, dq, step, block):
        direction = 0 if step == 1 else 1
        self.next_copies[direction, dq] = self.copy(
            block, self.rest_p.at[direction, dq], self.p, step
        )

    def joined(self):
        for dq, step, i in ((2, 1, 0), (3, -1, 0), (1, 1, 1), (0, -1, 1)):
            direction = 0 if step == 1 else 1
            self.far_copies[direction, i].wait_recv()
            mine = self.own(step, dq)
            mine[...] = mine[...] + self.near_p[direction, i]
            self.next_to(dq, step, mine)

    def collect(self, dq):
        for direction in range(2):
            self.next_copies[direction, dq].wait_recv()
        mine = self.own(0, dq)
        total = mine[...].astype(f32)
        for direction in range(2):
            total = total + self.rest_p[direction, dq].astype(f32)
        mine[...] = total.astype(mine.dtype)

    def far_q(self):
        self.collect(2)
        self.far_q_copies = [
            self.copy(self.own(0, 2, self.low), self.side(0, self.low), self.q, 1),
            self.copy(self.own(0, 2, self.high), self.side(1, self.high), self.q, -1),
        ]

    def next_q(self):
        self.next_q_copies = []
        for i, (dq, columns) in enumerate(((1, self.low), (3, self.high))):
            self.collect(dq)
            self.far_q_copies[i].wait_recv()
            mine = self.own(0, dq, columns)
            mine[...] = mine[...] + self.side(i, columns)[...]
            self.next_q_copies.append(
                self.copy(self.own(0, dq), self.near_q.at[2 + i], self.q, 1 if i == 0 else -1)
            )

    def total(self):
        self.collect(0)
        total = self.own(0, 0)[...].astype(f32)
        for i in range(2):
            self.next_q_copies[i].wait_recv()
            total = total + self.near_q[2 + i].astype(f32)
        return total

    def drain(self):
        for copy in self.sent:
            copy.wait_send()


def ref_dot(a, b):
    return jnp.dot(a, b, preferred_element_type=f32)


def ref_dot_nt(a, b):
    return lax.dot_general(a, b, (((1,), (1,)), ((), ())), preferred_element_type=f32)


def ref_dot_tn(a, b):
    return lax.dot_general(a, b, (((0,), (0,)), ((), ())), preferred_element_type=f32)


def at(i, size):
    return pl.ds(pl.multiple_of(i * size, size), size)


def gain_rows(misc):
    pick = lax.broadcasted_iota(jnp.int32, (16, MISC), 0)
    pick = (pick == lax.broadcasted_iota(jnp.int32, (16, MISC), 1)).astype(f32).astype(bf16)
    return ref_dot_nt(pick, misc)


def turn(values, cosine, sine):
    return values * cosine + pltpu.roll(values, HEAD_SIZE // 2, 1) * sine


def turn_back(values, cosine, sine):
    return values * cosine - pltpu.roll(values, HEAD_SIZE // 2, 1) * sine


def as_column(row):
    count = row.shape[1]
    same = lax.broadcasted_iota(jnp.int32, (count, count), 0) == lax.broadcasted_iota(
        jnp.int32, (count, count), 1
    )
    return jnp.sum(jnp.where(same, row.astype(f32), 0.0), axis=1, keepdims=True)


def fill_bias(bias, seg_ref, z):
    keys, queries = bias.shape
    seg_row = seg_ref[:, at(z, queries)].astype(f32)

    def fill(i, carry):
        seg_column = as_column(seg_ref[:, at(i, queries)])
        key = lax.broadcasted_iota(jnp.int32, (queries, queries), 0) + i * queries
        query = lax.broadcasted_iota(jnp.int32, (queries, queries), 1) + z * queries
        seen = (seg_column == seg_row) & (key <= query)
        bias[at(i, queries), :] = jnp.where(seen, 0.0, NEG_FILL)
        return carry

    lax.fori_loop(0, keys // queries, fill, 0)


KEYS = 128


def key_block(kv, i, k):
    per_block = kv.shape[1] // KEYS
    start = (k % per_block) * KEYS
    return kv[k // per_block, start : start + KEYS, i * HEAD_SIZE : (i + 1) * HEAD_SIZE]


class RowsRing:
    def __init__(self, lanes, rows_ref, out_ref):
        c, h, l = place()
        self.lanes, self.out, self.l = lanes, out_ref, l
        self.rows = rows_ref
        self.own = pl.ds((c * 2 + h) * 2, 2)
        self.here = c * 4 + h * 2 + l
        self.cross_at = c * 4 + (1 - h) * 2 + 1 - l
        self.far_at = c * 4 + (1 - h) * 2 + l
        self.shared = []

    def share(self, index):
        block = self.out.at[index]
        self.shared.append(self.lanes.send(block, block, other_core()))

    def start(self):
        size = self.rows.shape[1] // 4
        self.parts = [pl.ds(i * size, size) for i in range(4)]
        self.to_cross = [
            self.lanes.send(self.rows.at[self.l, some], self.out.at[self.here, some], cross())
            for some in self.parts
        ]
        self.shared.append(self.lanes.send(self.rows, self.out.at[self.own], other_core()))
        self.to_partner = []

    def relay(self, i):
        self.to_cross[i].wait_recv()
        block = self.out.at[self.cross_at, self.parts[i]]
        self.to_partner.append(self.lanes.send(block, block, partner()))

    def finish(self):
        self.share(self.cross_at)
        for copy in self.to_partner:
            copy.wait_recv()
        self.share(self.far_at)

    def drain(self):
        for copy in self.to_cross + self.to_partner:
            copy.wait_send()
        for copy in self.shared:
            copy.wait()


def attention_kernel(
    part,
    wq_ref,
    wk_ref,
    wv_ref,
    wo_ref,
    router_ref,
    attn_gain_ref,
    mix_gain_ref,
    wg_ref,
    wu_ref,
    wd_ref,
    rows_ref,
    tokens_ref,
    routes_ref,
    seg_ref,
    cos_table,
    sin_table,
    w_out,
    rows_out,
    slots_out,
    expert_out,
    expert_block,
    a_out,
    q_out,
    kv_out,
    o_out,
    lse_out,
    h1_out,
    b_out,
    gates_out,
    w,
    attn_in,
    expert_in,
    block,
    bias,
    value_turned,
    attn_ref,
    expert_ref,
    slots_ref,
    slots_own,
    cos_ref,
    sin_ref,
    s_sem,
    r_sem,
    as_sem,
    ar_sem,
    own,
):
    c, h, l = place()
    z = h * 2 + l
    me = (c * 2 + h) * 2 + l
    x_ref = tokens_ref.at[l]
    rows, width = rows_ref.shape[1:]
    q_half = w.shape[4] // 2 - (HEAD_SIZE * 2 + MISC) // 2
    kv_at, misc_at, out_at = q_half, q_half + 2 * HEAD_SIZE, q_half + 2 * HEAD_SIZE + MISC
    ff = expert_block.shape[2]
    tables = [
        pltpu.make_async_copy(cos_table.at[pl.ds(z * rows, rows)], cos_ref, own.at[5]),
        pltpu.make_async_copy(sin_table.at[pl.ds(z * rows, rows)], sin_ref, own.at[6]),
    ]
    for copy in tables:
        copy.start()

    place_of = lax.broadcasted_iota(jnp.int32, (8, MISC), 0)
    place_of = (place_of == lax.broadcasted_iota(jnp.int32, (8, MISC), 1)).astype(f32)
    misc = ref_dot(router_ref[...], place_of.astype(bf16))
    column = lax.broadcasted_iota(jnp.int32, (part, MISC), 1)
    misc = jnp.where(column == 8, as_column(attn_gain_ref[...]), misc)
    misc = jnp.where(column == 9, as_column(mix_gain_ref[...]), misc)
    attn_ref[...] = jnp.zeros_like(attn_ref)
    attn_ref[:part, :q_half] = wq_ref[...]
    attn_ref[:part, kv_at : kv_at + HEAD_SIZE] = wk_ref[...]
    attn_ref[:part, kv_at + HEAD_SIZE : misc_at] = wv_ref[...]
    attn_ref[:part, misc_at:out_at] = misc.astype(bf16)
    attn_ref[:part, out_at:] = wo_ref[...]
    for i, ref in enumerate((wg_ref, wu_ref, wd_ref)):
        expert_ref[:, i, :part, :] = ref[...]
        expert_ref[:, i, part:, :] = jnp.zeros((8, PAD - part, ff // 2), bf16)

    block_rows = 2 * rows
    expert = lax.broadcasted_iota(jnp.int32, (8, block_rows), 0)
    taken = routes_ref[0:1, :] == expert
    for j in range(1, routes_ref.shape[0]):
        taken = taken | (routes_ref[j : j + 1, :] == expert)
    earlier = lax.broadcasted_iota(jnp.int32, (block_rows, block_rows), 0)
    earlier = (earlier < lax.broadcasted_iota(jnp.int32, (block_rows, block_rows), 1)).astype(f32)
    count = ref_dot(taken.astype(f32).astype(bf16), earlier.astype(bf16))
    count = jnp.where(taken, count, -1.0)
    slots_own[...] = jnp.where(l == 0, count[:, :rows], count[:, rows:])
    for e in range(8):
        slots_ref[e] = slots_own[e : e + 1, :]

    barrier = pltpu.get_barrier_semaphore()
    pl.semaphore_wait(barrier, greet_column(barrier) + greet_chips(barrier))
    lanes = Lanes(s_sem, r_sem)

    slot = c * 2 + h
    here = pltpu.make_async_copy(attn_ref, attn_in.at[slot], own.at[1])
    there = pltpu.make_async_remote_copy(
        src_ref=attn_ref,
        dst_ref=attn_in.at[slot],
        send_sem=as_sem.at[0],
        recv_sem=ar_sem.at[slot],
        device_id=column_peer(1, 0),
        device_id_type=MESH,
    )
    pl.when(c == l)(here.start)
    pl.when(c != l)(there.start)
    for z_step in range(1, 4):
        to_z = lax.rem(z + z_step, 4)
        send(attn_ref, attn_in.at[slot], as_sem.at[z_step], ar_sem.at[slot], at_z(l, to_z))
    local = [
        pltpu.make_async_copy(expert_ref.at[me], expert_in.at[me], own.at[0]),
        pltpu.make_async_copy(slots_ref.at[me], slots_out.at[me], own.at[2]),
        pltpu.make_async_copy(rows_ref, rows_out.at[pl.ds((c * 2 + h) * 2, 2)], own.at[3]),
    ]
    for copy in local:
        copy.start()
    pieces = []
    for step in COLUMN:
        peer = column_peer(*step)
        to = (peer["c"] * 2 + peer["h"]) * 2 + peer["l"]
        pieces.append(lanes.send(expert_ref.at[to], expert_in.at[me], peer))
        pieces.append(lanes.send(slots_ref.at[to], slots_out.at[me], peer))
    fill_bias(bias, seg_ref, z)

    for source in range(4):
        mine = (c == l) & (slot == source)

        def landed(source=source):
            pltpu.make_async_remote_copy(
                src_ref=attn_ref,
                dst_ref=attn_in.at[source],
                send_sem=as_sem.at[0],
                recv_sem=ar_sem.at[source],
                device_id=column_peer(1, 0),
                device_id_type=MESH,
            ).wait_recv()

        pl.when(jnp.logical_not(mine))(landed)
    pl.when(c == l)(here.wait)
    block[...] = jnp.concatenate(
        [attn_in[i].astype(f32)[:part] for i in range(4)], axis=0
    ).astype(block.dtype)
    index = chip_index({"x": 0, "y": 0})
    x_at, y_at = lax.axis_index("x"), lax.axis_index("y")
    keep = [pltpu.make_async_copy(block, w.at[c, x_at, y_at], own.at[4])]
    keep[0].start()
    half = block.shape[0] // 2
    rings = {}
    for name, start, size, cut in (("in", 0, out_at, 640), ("out", out_at, q_half, 384)):
        rings[name] = []
        for low, a, b in ((0, "x", "y"), (half, "y", "x")):
            mine = pl.ds(low, half)

            def view(index, columns, mine=mine, start=start, size=size):
                return w.at[c, index // 4, lax.rem(index, 4), mine, shifted(columns, start, size)]

            def line(i, a=a, mine=mine, columns=pl.ds(start, size)):
                return w.at[c, i, :, mine, columns] if a == "x" else w.at[c, :, i, mine, columns]

            own_part = block.at[mine, pl.ds(start, size)]
            rings[name].append(ChipRing(lanes, own_part, view, cut, size, a, b, line))
    rings["expert"] = []
    for low, a, b in ((0, "x", "y"), (half, "y", "x")):
        mine = pl.ds(low, half)

        def expert_view(index, columns, mine=mine):
            return expert_out.at[:, index, mine, columns]

        own_part = expert_block.at[pl.ds(1, 2), mine]
        rings["expert"].append(ChipRing(lanes, own_part, expert_view, ff // 2, ff, a, b))

    def go(name, step, *args):
        for ring in rings[name]:
            getattr(ring, step)(*args)

    go("in", "start")
    rows_ring = RowsRing(lanes, rows_ref, rows_out)
    rows_ring.start()

    local[0].wait()
    for copy in pieces:
        copy.wait()
    for i in range(3):
        for l_side in range(2):
            expert_block[i, :, l_side * 384 : (l_side + 1) * 384] = jnp.concatenate(
                [expert_in[2 * j + l_side, i].astype(f32)[:part] for j in range(4)], axis=0
            ).astype(bf16)
    keep.append(
        pltpu.make_async_copy(expert_block.at[pl.ds(1, 2)], expert_out.at[:, index], own.at[0])
    )
    keep[1].start()

    keep[0].wait()
    go("in", "relay_first")
    go("in", "relay_turn", 0)
    go("in", "relay_second")
    go("out", "start")
    go("in", "relay_turn", -1)
    go("in", "end", 0)
    go("in", "relay_turn", 1)
    go("in", "end", -1)
    go("in", "relay_turn", 2)
    go("in", "end", 1)
    go("out", "relay_first")
    go("in", "end", 2)
    go("expert", "start")
    go("out", "relay_turn", 0)
    go("out", "relay_second")
    for ring in rings["in"]:
        for copy in ring.near:
            copy.wait_recv()


    def projection(i, columns):
        return w[i, :, :, :, columns].reshape(width, -1)

    scale = HEAD_SIZE ** (-0.5)
    misc = projection(0, slice(misc_at, out_at))
    gains = gain_rows(misc)
    chunk = 32

    def norm(i, carry):
        here = at(i, chunk)
        x = x_ref[here, :].astype(f32)
        inverse = lax.rsqrt(jnp.mean(x * x, axis=1, keepdims=True) + EPS)
        a_out[here, :] = (x * inverse * gains[8:9, :]).astype(bf16)
        return carry

    lax.fori_loop(0, rows // chunk, norm, 0)
    for copy in tables:
        copy.wait()
    cosine, sine = cos_ref[...], sin_ref[...]
    sends = []
    for i in range(2):
        kv = ref_dot(a_out[...], projection(i, slice(kv_at, misc_at)))
        kv_out[z, :, 2 * i * 128 : (2 * i + 1) * 128] = turn(kv[:, :128], cosine, sine).astype(
            bf16
        )
        kv_out[z, :, (2 * i + 1) * 128 : (2 * i + 2) * 128] = kv[:, 128:].astype(bf16)
        pair = kv_out.at[z, :, pl.ds(2 * i * 128, 256)]
        sends.append([lanes.send(pair, pair, column_peer(*step)) for step in ALONG_Z])
    go("out", "relay_turn", -1)
    go("out", "relay_turn", 1)
    for i in range(2):

        def project(j, carry, i=i):
            q = ref_dot(a_out[...], w[i, :, :, :, at(j, 256)].reshape(width, 256))
            q_out[i * GROUP + 2 * j] = turn(q[:, :128], cosine, sine).astype(bf16)
            q_out[i * GROUP + 2 * j + 1] = turn(q[:, 128:], cosine, sine).astype(bf16)
            return carry

        lax.fori_loop(0, q_half // 256, project, 0)
    go("out", "relay_turn", 2)
    go("expert", "relay_first")
    for i in range(4):
        rows_ring.relay(i)
    keys_count = 4 * rows
    for i in range(2):
        for copy in sends[i]:
            copy.wait_recv()
        values = kv_out[:, :, (2 * i + 1) * 128 : (2 * i + 2) * 128]
        value_turned[...] = values.reshape(keys_count, HEAD_SIZE).T

        def attend(j, carry, i=i):
            keys = kv_out[:, :, 2 * i * 128 : (2 * i + 1) * 128]
            keys = keys.reshape(keys_count, HEAD_SIZE)
            scores = ref_dot_nt(keys, q_out[i * GROUP + j]) * scale + bias[...]
            peak = jnp.max(scores, axis=0, keepdims=True)
            expo = jnp.exp(scores - peak)
            total = jnp.sum(expo, axis=0, keepdims=True)
            weights = (expo * (1.0 / total)).astype(bf16)
            mixed = ref_dot(value_turned[...], weights)
            o_out[:, at(i * GROUP + j, HEAD_SIZE)] = mixed.T.astype(bf16)
            lse_out[i * GROUP + j] = peak + jnp.log(total)
            return carry

        for some in range(2):
            lax.fori_loop(some * GROUP // 2, (some + 1) * GROUP // 2, attend, 0)
            if (i, some) == (0, 0):
                go("out", "finish")
                go("expert", "relay_turn", 0)
            elif (i, some) == (0, 1):
                go("expert", "relay_second")
            elif (i, some) == (1, 0):
                go("expert", "relay_turn", -1)
    for ring in rings["out"]:
        for copy in ring.near:
            copy.wait_recv()
    keep.append(pltpu.make_async_copy(w, w_out, own.at[1]))
    keep[2].start()

    def leave(j, carry):
        here = at(j, 384)
        u = ref_dot_nt(
            o_out[:, :q_half], w[0, j, :, :, out_at:].reshape(384, q_half)
        )
        u = u + ref_dot_nt(
            o_out[:, q_half:], w[1, j, :, :, out_at:].reshape(384, q_half)
        )
        h1_out[:, here] = x_ref[:, here].astype(f32) + u
        return carry

    lax.fori_loop(0, width // 384, leave, 0)
    go("expert", "relay_turn", 1)

    def second(i, carry):
        here = at(i, chunk)
        h1 = h1_out[here, :]
        inverse = lax.rsqrt(jnp.mean(h1 * h1, axis=1, keepdims=True) + EPS)
        b_out[here, :] = (h1 * inverse * gains[9:10, :]).astype(bf16)
        return carry

    lax.fori_loop(0, rows // chunk, second, 0)
    logits = ref_dot(b_out[...], misc).T[:8]
    named = slots_own[...] >= 0
    masked = jnp.where(named, logits, NEG_FILL)
    expo = jnp.where(named, jnp.exp(masked - jnp.max(masked, axis=0, keepdims=True)), 0.0)
    gates = expo / jnp.sum(expo, axis=0, keepdims=True)
    for e in range(8):
        gates_out[e] = gates[e : e + 1]
    go("expert", "relay_turn", 2)
    rows_ring.finish()
    go("expert", "finish")
    for copy in sends[0] + sends[1]:
        copy.wait_send()
    rows_ring.drain()
    for copy in local[1:]:
        copy.wait()
    pl.when(c != l)(there.wait_send)
    for z_step in range(1, 4):
        pltpu.make_async_remote_copy(
            src_ref=attn_ref,
            dst_ref=attn_in.at[slot],
            send_sem=as_sem.at[z_step],
            recv_sem=ar_sem.at[slot],
            device_id=column_peer(0, z_step),
            device_id_type=MESH,
        ).wait_send()
    for name in ("in", "out"):
        for ring in rings[name]:
            for copy in ring.near:
                copy.wait_send()
            for copy in ring.sent:
                copy.wait_send()
    go("expert", "drain")
    for copy in keep[1:]:
        copy.wait()


def attention(projections, gains, experts, upstream, tokens, routes, segments, tables, part):
    rows, width = upstream.shape[1:]
    keys = 4 * rows
    w_width = 2 * projections[0].shape[1] + 2 * HEAD_SIZE + MISC
    ff = 2 * experts[0].shape[2]
    pieces = (8, 3, PAD, ff // 2)
    sds = jax.ShapeDtypeStruct
    return pl.pallas_call(
        functools.partial(attention_kernel, part),
        name="attention",
        out_shape=(
            sds((2, 4, 4, 4 * part, w_width), bf16),
            sds((8, rows, width), bf16),
            sds((8, 1, rows), f32),
            sds((2, 16, 4 * part, ff), bf16),
            sds((3, 4 * part, ff), bf16),
            sds((rows, width), bf16),
            sds((QUERY_HEADS, rows, HEAD_SIZE), bf16),
            sds((4, rows, 4 * HEAD_SIZE), bf16),
            sds((rows, QUERY_HEADS * HEAD_SIZE), bf16),
            sds((QUERY_HEADS, 1, rows), f32),
            sds((rows, width), f32),
            sds((rows, width), bf16),
            sds((8, 1, rows), f32),
        ),
        in_specs=[VMEM] * 14 + [ANY] * 2,
        out_specs=(HBM,) * 4 + (VMEM,) * 9,
        scratch_shapes=[
            pltpu.VMEM((2, 4, 4, 4 * part, w_width), bf16),
            pltpu.VMEM((4, PAD, w_width), bf16),
            pltpu.VMEM(pieces, bf16),
            pltpu.VMEM((4 * part, w_width), bf16),
            pltpu.VMEM((keys, rows), f32),
            pltpu.VMEM((HEAD_SIZE, keys), bf16),
            pltpu.VMEM((PAD, w_width), bf16),
            pltpu.VMEM(pieces, bf16),
            pltpu.VMEM((8, 1, rows), f32),
            pltpu.VMEM((8, rows), f32),
            pltpu.VMEM((rows, HEAD_SIZE), f32),
            pltpu.VMEM((rows, HEAD_SIZE), f32),
        ]
        + lanes_scratch(150)
        + [
            pltpu.SemaphoreType.DMA((4,)),
            pltpu.SemaphoreType.DMA((4,)),
            pltpu.SemaphoreType.DMA((7,)),
        ],
        compiler_params=pltpu.CompilerParams(
            collective_id=2, has_side_effects=True, vmem_limit_bytes=60 * 2**20
        ),
    )(*projections, *gains, *experts, upstream, tokens, routes, segments, *tables)


def attention_back_kernel(
    back_ref,
    gate_back_ref,
    gates_ref,
    b_ref,
    h1_ref,
    tokens_ref,
    rows_ref,
    a_ref,
    o_ref,
    q_ref,
    kv_ref,
    lse_ref,
    cos_table,
    sin_table,
    seg_ref,
    w_ref,
    parts_ref,
    expert_ref,
    grad_in,
    out_sum,
    tokens_out,
    block_out,
    block_half,
    pieces_out,
    w,
    bias,
    key_turned,
    dh1,
    da,
    du,
    do,
    back_rows,
    key_sum,
    value_sum,
    probs,
    probs_back,
    probs_low,
    scores_back,
    kv_send,
    kv_held,
    stage_in,
    misc_held,
    parts,
    near,
    far,
    nearest,
    terms,
    near_p0,
    rest_p0,
    near_q0,
    near_p1,
    rest_p1,
    near_q1,
    out_terms,
    out_near_p0,
    out_rest_p0,
    out_near_q0,
    out_near_p1,
    out_rest_p1,
    out_near_q1,
    x_ref,
    g_ref,
    cos_ref,
    sin_ref,
    s_sem,
    r_sem,
    w_sem,
    own,
):
    c, h, l = place()
    z = h * 2 + l
    rows, width = x_ref.shape
    q_half = o_ref.shape[1] // 2
    misc_at, out_at = q_half + 2 * HEAD_SIZE, q_half + 2 * HEAD_SIZE + MISC

    def load(start, size, to, i):
        return pltpu.make_async_copy(
            w_ref.at[:, :, pl.ds(start, size)], w.at[:, :, pl.ds(to, size)], w_sem.at[i]
        )

    loads = [load(misc_at, MISC, misc_at, 0), load(out_at, q_half, 0, 1), load(0, misc_at, 0, 2)]
    loads[0].start()
    loads[1].start()
    terms_load = pltpu.make_async_copy(expert_ref, terms, own.at[1])
    terms_load.start()
    own_loads = [
        pltpu.make_async_copy(tokens_ref.at[l], x_ref, own.at[4]),
        pltpu.make_async_copy(rows_ref.at[l], g_ref, own.at[5]),
        pltpu.make_async_copy(cos_table.at[pl.ds(z * rows, rows)], cos_ref, own.at[6]),
        pltpu.make_async_copy(sin_table.at[pl.ds(z * rows, rows)], sin_ref, own.at[7]),
    ]
    for copy in own_loads:
        copy.start()
    back_load = pltpu.make_async_copy(back_ref, da, own.at[2])
    back_load.start()
    barrier = pltpu.get_barrier_semaphore()
    pl.semaphore_wait(barrier, greet_column(barrier) + greet_chips(barrier))
    lanes = Lanes(s_sem, r_sem)
    part, ff = terms.shape[2] // 4, terms.shape[3]
    sums = []
    for low, p, q, held in (
        (0, "y", "x", (near_p0, rest_p0, near_q0)),
        (2 * part, "x", "y", (near_p1, rest_p1, near_q1)),
    ):

        def view(index, columns, mine=pl.ds(low, 2 * part)):
            return terms.at[index, :, mine, columns]

        def source(index, mine=pl.ds(low, 2 * part)):
            return expert_ref.at[index, :, mine]

        sums.append(ChipSum(lanes, view, source, ff // 2, ff, p, q, *held))
    out_sums = []
    for low, p, q, held in (
        (0, "y", "x", (out_near_p0, out_rest_p0, out_near_q0)),
        (2 * part, "x", "y", (out_near_p1, out_rest_p1, out_near_q1)),
    ):

        def out_view(index, columns=slice(None), mine=pl.ds(low, 2 * part)):
            return out_terms.at[index, mine, columns]

        out_sums.append(ChipSum(lanes, out_view, out_view, q_half // 2, q_half, p, q, *held))
    places = {
        "own": z,
        "partner": h * 2 + 1 - l,
        "cross": (1 - h) * 2 + 1 - l,
        "far": (1 - h) * 2 + l,
    }
    for each in sums:
        each.far()
    for each in sums:
        each.plain()
    queue = ("far", "cross", "partner", "own")

    def parts_load(i):
        return pltpu.make_async_copy(
            parts_ref.at[c * 4 + places[queue[i]]], parts.at[i % 2], own.at[(0, 3)[i % 2]]
        )

    parts_load(0).start()
    parts_load(1).start()
    near_copies = {
        which: lanes.send(
            parts_ref.at[(1 - c) * 4 + places[which]], near.at[places[which]], other_core()
        )
        for which in ("far", "cross", "partner", "own")
    }
    scale = HEAD_SIZE ** (-0.5)
    fill_bias(bias, seg_ref, z)
    for copy in own_loads:
        copy.wait()

    def add_near(which):
        near_copies[which].wait_recv()
        k, number = places[which], queue.index(which)
        parts_load(number).wait()

        def add(i, carry):
            here = at(i, 64)
            near[k, here] = near[k, here] + parts[number % 2, here]
            return carry

        lax.fori_loop(0, rows // 64, add, 0)
        if number < 2:
            parts_load(number + 2).start()

    half = rows // 2
    first, second = pl.ds(0, half), pl.ds(half, half)

    def part_at(which, some):
        return near.at[places[which], some]

    add_near("far")
    far_partner = lanes.send(part_at("far", first), far.at[0], partner())
    far_cross = lanes.send(part_at("far", second), far.at[1], cross())
    add_near("cross")
    add_near("partner")
    early_cross = lanes.send(part_at("cross", second), nearest.at[1, second], cross())
    early_partner = lanes.send(part_at("partner", first), nearest.at[0, first], partner())
    add_near("own")

    loads[0].wait()
    loads[1].wait()
    misc = w[0, :, misc_at:out_at]
    gains = gain_rows(misc)
    gates = jnp.concatenate([gates_ref[e] for e in range(8)], axis=0)
    gate_back = jnp.concatenate([gate_back_ref[e] for e in range(8)], axis=0)
    mean = jnp.sum(gates * gate_back, axis=0, keepdims=True)
    logit_grad = gates * (gate_back - mean)
    logit_grad = jnp.concatenate(
        [logit_grad, jnp.zeros((MISC - 8, rows), f32)], axis=0
    ).T.astype(bf16)
    chunk = 32

    def norm_back(i, carry):
        mix_sum = carry
        here = at(i, chunk)
        h1 = h1_ref[here, :]
        inverse = lax.rsqrt(jnp.mean(h1 * h1, axis=1, keepdims=True) + EPS)
        db = da[here, :] + dh1[here, :]
        mix_sum = mix_sum + jnp.sum(db * h1 * inverse, axis=0, keepdims=True)
        dz = db * gains[9:10, :]
        mean = jnp.mean(dz * h1, axis=1, keepdims=True)
        value = g_ref[here, :].astype(f32) + inverse * dz - h1 * (inverse * inverse * inverse * mean)
        dh1[here, :] = value
        du[here, :] = value.astype(bf16)
        return mix_sum

    dh1[...] = ref_dot_nt(logit_grad, misc)
    back_load.wait()
    mix_sum = lax.fori_loop(0, rows // chunk, norm_back, jnp.zeros((1, width), f32))
    tail = pl.ds(misc_at, MISC)
    router_grad = ref_dot_tn(b_ref[...], logit_grad).astype(bf16)
    grad_in[:, :, tail] = router_grad.reshape(16, 4 * part, MISC)

    far_partner.wait_recv()
    mine = part_at("cross", first)
    mine[...] = mine[...] + far[0]
    late_cross = lanes.send(mine, nearest.at[1, first], cross())
    far_cross.wait_recv()
    mine = part_at("partner", second)
    mine[...] = mine[...] + far[1]
    late_partner = lanes.send(mine, nearest.at[0, second], partner())

    def add_block():
        for copy in (early_partner, early_cross, late_cross, late_partner):
            copy.wait_recv()

        def add_up(i, carry):
            here = at(i, 64)
            value = near[z, here].astype(f32)
            value = value + nearest[0, here].astype(f32) + nearest[1, here].astype(f32)
            block_out[here, :] = (h1_ref[here, :] + value).astype(bf16)
            return carry

        lax.fori_loop(0, rows // 64, add_up, 0)
        return lanes.send(block_out.at[first], block_half, partner())

    terms_load.wait()
    for each in sums:
        each.joined()

    def project(i, carry):
        columns = at(i, 256)
        for g in range(2):
            do[g, :, columns] = ref_dot(du[...], w[g, :, columns]).astype(bf16)
        return carry

    lax.fori_loop(0, q_half // 256, project, 0)
    loads[2].start()

    size = 4 * 4 * part

    def out_grad(g, i):
        columns = pl.ds(pl.multiple_of(g * q_half, q_half), q_half)
        grad = ref_dot_tn(du[:, i * size : (i + 1) * size], o_ref[:, columns])
        return grad.astype(bf16).reshape(4, 4 * part, q_half)

    out_sends = []
    for i in range(4):
        if i >= 2:
            out_sends[i - 2].wait_send()
        stage = stage_in.at[i % 2, :, :, pl.ds(0, q_half)]
        stage[...] = out_grad(1 - c, i)
        out_sends.append(lanes.send(stage, out_terms.at[pl.ds(4 * i, 4)], other_core()))
    for i in range(4):
        mine = out_grad(c, i)
        out_sends[i].wait_recv()
        out_terms[4 * i : 4 * i + 4] = out_terms[4 * i : 4 * i + 4] + mine
    for each in out_sums:
        each.far()
    for each in out_sums:
        each.plain()

    keys_count = 4 * rows
    kv_sends = []

    def returned(each):
        total = each.total()
        first_block = 2 * sums.index(each)
        for i in range(2):
            for side in range(2):
                to = 2 * (first_block + i) + side
                pieces_out[to, :, :part] = total[
                    :, i * part : (i + 1) * part, side * ff // 2 : (side + 1) * ff // 2
                ].astype(bf16)
                pieces_out[to, :, part:] = jnp.zeros((3, PAD - part, ff // 2), bf16)

    cosine, sine = cos_ref[...], sin_ref[...]
    for g in range(2):
        key_turned[...] = (
            kv_ref[:, :, 2 * g * 128 : (2 * g + 1) * 128].reshape(keys_count, HEAD_SIZE).T
        )
        key_sum[...] = jnp.zeros_like(key_sum)
        value_sum[...] = jnp.zeros_like(value_sum)

        def head_back(j, carry, g=g):
            columns = at(j, HEAD_SIZE)
            query = q_ref[g * GROUP + j]
            out_back = do[g, :, columns]
            shift = lse_ref[g * GROUP + j]
            row_dot = jnp.zeros((8, rows), f32)
            for k in range(keys_count // KEYS):
                here = slice(k * KEYS, (k + 1) * KEYS)
                value = ref_dot_nt(key_block(kv_ref, 2 * g, k), query) * scale + bias[here, :]
                prob = jnp.exp(value - shift)
                prob_back = ref_dot_nt(key_block(kv_ref, 2 * g + 1, k), out_back)
                probs[here, :] = prob
                probs_back[here, :] = prob_back
                probs_low[here, :] = prob.astype(bf16)
                product = (prob * prob_back).reshape(KEYS // 8, 8, rows)
                row_dot = row_dot + jnp.sum(product, axis=0)
            row_dot = jnp.sum(row_dot, axis=0, keepdims=True)
            for k in range(keys_count // KEYS):
                here = slice(k * KEYS, (k + 1) * KEYS)
                value = probs[here, :] * (probs_back[here, :] - row_dot)
                scores_back[here, :] = value.astype(bf16)
            value_sum[...] += ref_dot(probs_low[...], out_back)
            key_sum[...] += ref_dot(scores_back[...], query)
            query_back = (ref_dot(key_turned[...], scores_back[...]) * scale).T
            back_rows[g, :, columns] = turn_back(query_back, cosine, sine).astype(bf16)
            return carry

        lax.fori_loop(0, GROUP // 2, head_back, 0)
        if g == 0:
            for each in sums:
                each.far_q()
            for each in out_sums:
                each.joined()
        else:
            for each in out_sums:
                each.next_q()
            for each in sums:
                returned(each)
        lax.fori_loop(GROUP // 2, GROUP, head_back, 0)
        if g == 0:
            for each in sums:
                each.next_q()
            for each in out_sums:
                each.far_q()
        kv_send[g, :, :, :128] = (key_sum[...] * scale).astype(bf16).reshape(4, rows, 128)
        kv_send[g, :, :, 128:] = value_sum[...].astype(bf16).reshape(4, rows, 128)
        for i, step in enumerate(ALONG_Z):
            to = lax.rem(z + step[1], 4)
            kv_sends.append(lanes.send(kv_send.at[g, to], kv_held.at[g, i], column_peer(*step)))

    block_send = add_block()
    for i in range(2):
        out_sum[2 * part * i : 2 * part * (i + 1)] = out_sums[i].total()
    loads[2].wait()
    every = pl.ds(0, q_half)
    kv = pl.ds(q_half, 2 * HEAD_SIZE)

    def input_back(columns, add):
        def step(i, carry):
            here = at(i, 512)
            value = ref_dot_nt(back_rows[0, :, columns], w[0, here, columns])
            value = value + ref_dot_nt(back_rows[1, :, columns], w[1, here, columns])
            da[:, here] = da[:, here] + value if add else value
            return carry

        lax.fori_loop(0, width // 512, step, 0)

    in_sends = {}

    def in_grad(g, i, columns):
        grad = ref_dot_tn(a_ref[:, i * size : (i + 1) * size], back_rows[g, :, columns])
        return grad.astype(bf16).reshape(4, 4 * part, columns.size)

    def leave(i, columns, before):
        slot = i % 2
        if before is not None:
            in_sends[before].wait_send()
        stage_in[slot, :, :, columns] = in_grad(1 - c, i, columns)
        block = pl.ds(4 * i, 4)
        in_sends[i, columns.start] = lanes.send(
            stage_in.at[slot, :, :, columns], grad_in.at[block, :, columns], other_core()
        )

    input_back(every, False)
    for copy in out_sends[2:]:
        copy.wait_send()
    for i in range(4):
        leave(i, every, (i - 2, every.start) if i >= 2 else None)
    for copy in kv_sends:
        copy.wait_recv()
    for g in range(2):
        own_part = kv_send[g, z].astype(f32)
        for i in range(3):
            own_part = own_part + kv_held[g, i].astype(f32)
        back_rows[g, :, q_half : q_half + 128] = turn_back(
            own_part[:, :128], cosine, sine
        ).astype(bf16)
        back_rows[g, :, q_half + 128 :] = own_part[:, 128:].astype(bf16)
    for i in range(4):
        leave(i, kv, (i - 2, kv.start) if i >= 2 else None)
    input_back(kv, True)
    for i in range(4):
        for columns in (every, kv):
            mine = in_grad(c, i, columns)
            in_sends[i, columns.start].wait_recv()
            block = pl.ds(4 * i, 4)
            grad_in[block, :, columns] = grad_in[block, :, columns] + mine

    def first_back(i, carry):
        here = at(i, chunk)
        x = x_ref[here, :].astype(f32)
        inverse = lax.rsqrt(jnp.mean(x * x, axis=1, keepdims=True) + EPS)
        back = da[here, :]
        carry = carry + jnp.sum(back * x * inverse, axis=0, keepdims=True)
        dz = back * gains[8:9, :]
        mean = jnp.mean(dz * x, axis=1, keepdims=True)
        value = dh1[here, :] + inverse * dz - x * (inverse * inverse * inverse * mean)
        tokens_out[here, :] = value.astype(bf16)
        return carry

    attn_sum = lax.fori_loop(0, rows // chunk, first_back, jnp.zeros((1, width), f32))
    number = lax.broadcasted_iota(jnp.int32, (MISC, width), 0)
    gain_grads = jnp.where(number == 8, attn_sum, jnp.where(number == 9, mix_sum, 0.0))
    gain_grads = gain_grads.T.astype(bf16).reshape(16, 4 * part, MISC)
    grad_in[:, :, tail] = grad_in[:, :, tail] + gain_grads
    crossing = lanes.send(grad_in.at[:, :, tail], misc_held, other_core())
    crossing.wait()
    grad_in[:, :, tail] = grad_in[:, :, tail] + misc_held[...]
    for i in range(2, 4):
        for columns in (every, kv):
            in_sends[i, columns.start].wait_send()
    block_send.wait()
    for each in sums + out_sums:
        each.drain()
    for copy in kv_sends:
        copy.wait_send()
    for copy in near_copies.values():
        copy.wait_send()
    for copy in (early_partner, early_cross, late_cross, late_partner, far_partner, far_cross):
        copy.wait_send()


def attention_back(
    back, gate_back, gates, b, h1, tokens, rows_in, a, o, q, kv, lse, cosine, sine, segments, w_attn, parts, expert_grads
):
    rows, width = h1.shape
    keys = 4 * rows
    q_half = o.shape[1] // 2
    qkv = q_half + 2 * HEAD_SIZE
    sds = jax.ShapeDtypeStruct
    count, block_rows, ff = expert_grads.shape[1:]
    half_block = (count, block_rows // 2, ff)
    ring = [
        pltpu.VMEM((2, 2) + half_block, bf16),
        pltpu.VMEM((2, 4) + half_block, bf16),
        pltpu.VMEM((4,) + half_block, bf16),
    ]
    out_half = (block_rows // 2, q_half)
    out_ring = [
        pltpu.VMEM((2, 2) + out_half, bf16),
        pltpu.VMEM((2, 4) + out_half, bf16),
        pltpu.VMEM((4,) + out_half, bf16),
    ]
    return pl.pallas_call(
        attention_back_kernel,
        name="attention_back",
        out_shape=(
            sds((16, block_rows, qkv + MISC), bf16),
            sds((block_rows, q_half), f32),
            sds((rows, width), bf16),
            sds((rows, width), bf16),
            sds((rows // 2, width), bf16),
            sds((8, count, PAD, ff // 2), bf16),
        ),
        in_specs=[ANY] + [VMEM] * 4 + [ANY] * 2 + [VMEM] * 5 + [ANY] * 2 + [VMEM] + [ANY] * 3,
        out_specs=(VMEM,) * 6,
        scratch_shapes=[
            pltpu.VMEM((2, width, qkv + MISC), bf16),
            pltpu.VMEM((keys, rows), f32),
            pltpu.VMEM((HEAD_SIZE, keys), bf16),
            pltpu.VMEM((rows, width), f32),
            pltpu.VMEM((rows, width), f32),
            pltpu.VMEM((rows, width), bf16),
            pltpu.VMEM((2, rows, q_half), bf16),
            pltpu.VMEM((2, rows, qkv), bf16),
            pltpu.VMEM((keys, HEAD_SIZE), f32),
            pltpu.VMEM((keys, HEAD_SIZE), f32),
            pltpu.VMEM((keys, rows), f32),
            pltpu.VMEM((keys, rows), f32),
            pltpu.VMEM((keys, rows), bf16),
            pltpu.VMEM((keys, rows), bf16),
            pltpu.VMEM((2, 4, rows, 2 * HEAD_SIZE), bf16),
            pltpu.VMEM((2, 3, rows, 2 * HEAD_SIZE), bf16),
            pltpu.VMEM((2, 4, block_rows, qkv), bf16),
            pltpu.VMEM((16, block_rows, MISC), bf16),
            pltpu.VMEM((2, rows, width), bf16),
            pltpu.VMEM((4, rows, width), bf16),
            pltpu.VMEM((2, rows // 2, width), bf16),
            pltpu.VMEM((2, rows, width), bf16),
            pltpu.VMEM(expert_grads.shape, bf16),
        ]
        + ring
        + ring
        + [pltpu.VMEM((16, block_rows, q_half), bf16)]
        + out_ring
        + out_ring
        + [
            pltpu.VMEM((rows, width), bf16),
            pltpu.VMEM((rows, width), bf16),
            pltpu.VMEM((rows, HEAD_SIZE), f32),
            pltpu.VMEM((rows, HEAD_SIZE), f32),
        ]
        + lanes_scratch(100)
        + [
            pltpu.SemaphoreType.DMA((3,)),
            pltpu.SemaphoreType.DMA((8,)),
        ],
        compiler_params=pltpu.CompilerParams(
            collective_id=3, has_side_effects=True, vmem_limit_bytes=62 * 2**20
        ),
    )(
        back, gate_back, gates, b, h1, tokens, rows_in, a, o, q, kv, lse, cosine, sine, segments, w_attn, parts, expert_grads
    )


def experts_kernel(
    rows_ref,
    gate_ref,
    grads_ref,
    slot_rows,
    others_ref,
    block_ref,
    mix_out,
    weight_grads,
    back_out,
    gate_back_out,
    rows_all,
    held,
    w_gate,
    w_up,
    w_down,
    picked,
    picked_grads,
    hidden_back,
    hidden_gated,
    gate_low,
    up_low,
    mix_stage,
    near,
    far,
    nearest,
    gates_in,
    gate_back,
    s_sem,
    r_sem,
    own,
    stage_sem,
    near_send,
    near_recv,
):
    c, h, l = place()
    me = (c * 2 + h) * 2 + l
    barrier = pltpu.get_barrier_semaphore()
    pl.semaphore_wait(barrier, greet_column(barrier) + greet_chips(barrier))
    lanes = Lanes(s_sem, r_sem)
    rows, width = rows_ref.shape
    slots = picked.shape[1]
    ff = w_gate.shape[2]
    block = 2 * rows

    ring = ColumnRing(lanes, rows_ref, rows_all)
    ring.start()
    index = chip_index({"x": 0, "y": 0})
    half = block_ref.shape[1] // 2
    weight_rings = []
    for weight, target in ((0, w_gate),):
        for low, a, b in ((0, "x", "y"), (half, "y", "x")):
            mine = pl.ds(low, half)

            def view(index, columns, mine=mine, target=target):
                return target.at[index, mine, columns]

            own_part = block_ref.at[weight, mine]
            weight_rings.append(ChipRing(lanes, own_part, view, ff // 2, ff, a, b))

    def go(step, *args):
        for each in weight_rings:
            getattr(each, step)(*args)

    go("start")
    local = [
        pltpu.make_async_copy(grads_ref, held, own.at[0]),
        pltpu.make_async_copy(others_ref.at[1], w_down, own.at[1]),
        pltpu.make_async_copy(block_ref.at[0], w_gate.at[index], own.at[2]),
        pltpu.make_async_copy(others_ref.at[0], w_up, own.at[3]),
        pltpu.make_async_copy(rows_ref, rows_all.at[me], own.at[4]),
        pltpu.make_async_copy(gate_ref.at[me], gates_in.at[me], own.at[5]),
    ]
    for copy in local:
        copy.start()
    gate_copies = []
    for step in COLUMN:
        peer = column_peer(*step)
        to = (peer["c"] * 2 + peer["h"]) * 2 + peer["l"]
        gate_copies.append(lanes.send(gate_ref.at[to], gates_in.at[me], peer))

    def pick_of(k):
        number = lax.broadcasted_iota(jnp.int32, (slots, block), 0).astype(f32)
        return slot_rows[k] == number

    def low(mask):
        return mask.astype(f32).astype(bf16)

    def columns_of(weight, columns):
        return weight[:, :, columns].reshape(width, narrow)

    def rows_of(weight, i):
        return weight[pl.ds(8 * i, 8)].reshape(ff, ff)

    wide = 512
    narrow = 256

    local[0].wait()
    local[1].wait()

    def prepare(k, carry):
        pick = low(pick_of(k))

        def gather(i, carry):
            columns = at(i, wide)
            values = ref_dot(pick, held[pl.ds(2 * k, 2), :, columns].reshape(block, wide))
            picked_grads[k, :, columns] = values.astype(bf16)
            return carry

        lax.fori_loop(0, width // wide, gather, 0)

        def down(i, carry):
            columns = at(i, narrow)
            hidden_back[k, :, columns] = ref_dot(picked_grads[k], columns_of(w_down, columns))
            return carry

        lax.fori_loop(0, ff // narrow, down, 0)
        return carry

    lax.fori_loop(0, 2, prepare, 0)
    go("relay_first")
    go("relay_turn", 0)
    ring.relay()
    go("relay_second")
    lax.fori_loop(2, 4, prepare, 0)
    go("relay_turn", -1)
    go("relay_turn", 1)
    ring.nearest()
    go("relay_turn", 2)
    go("finish")
    for copy in local[2:]:
        copy.wait()
    for copy in gate_copies:
        copy.wait()
    ring.shared["own"].wait_recv()
    ring.shared["partner"].wait_recv()

    def expert(k, stage):
        pick = pick_of(k)
        pick_low = low(pick)
        spread = pick.astype(f32).T.astype(bf16)
        gates = gates_in[pl.ds(2 * k, 2)]
        gate_row = jnp.concatenate([gates[0], gates[1]], axis=1)
        gate = jnp.sum(jnp.where(pick, gate_row, 0.0), axis=1, keepdims=True)

        def gather(i, carry):
            columns = at(i, wide)
            values = ref_dot(pick_low, rows_all[pl.ds(2 * k, 2), :, columns].reshape(block, wide))
            picked[k, :, columns] = values.astype(bf16)
            return carry

        lax.fori_loop(0, width // wide, gather, 0)

        def hide(i, total):
            columns = at(i, narrow)
            gate_act = ref_dot(picked[k], columns_of(w_gate, columns))
            up_act = ref_dot(picked[k], columns_of(w_up, columns))
            back = hidden_back[k, :, columns]
            sigmoid_act = 0.5 + 0.5 * jnp.tanh(0.5 * gate_act)
            silu_act = gate_act * sigmoid_act
            hidden = silu_act * up_act
            hidden_gated[k, :, columns] = (hidden * gate).astype(bf16)
            total = total + jnp.sum(hidden * back, axis=1, keepdims=True)
            back = back * gate
            slope = sigmoid_act * (1.0 + gate_act * (1.0 - sigmoid_act))
            gate_low[k, :, columns] = (back * up_act * slope).astype(bf16)
            up_low[k, :, columns] = (back * silu_act).astype(bf16)
            return total

        gate_slots = lax.fori_loop(0, ff // narrow, hide, jnp.zeros((slots, 1), f32))
        back_row = jnp.sum(jnp.where(pick, gate_slots, 0.0), axis=0, keepdims=True)
        gate_back[2 * k] = back_row[:, :rows]
        gate_back[2 * k + 1] = back_row[:, rows:]

        def leave(i, carry):
            columns = at(i, ff)
            out = ref_dot_nt(hidden_gated[k], rows_of(w_down, i)).astype(bf16)
            mix_stage[stage, :, :, columns] = (
                ref_dot(spread, out).astype(bf16).reshape(2, rows, ff)
            )
            back = ref_dot_nt(gate_low[k], rows_of(w_gate, i))
            back = (back + ref_dot_nt(up_low[k], rows_of(w_up, i))).astype(bf16)
            held[pl.ds(2 * k, 2), :, columns] = (
                ref_dot(spread, back).astype(bf16).reshape(2, rows, ff)
            )
            return carry

        lax.fori_loop(0, width // ff, leave, 0)

    def stage_copy(k, stage):
        return pltpu.make_async_copy(
            mix_stage.at[stage], mix_out.at[pl.ds(2 * k, 2)], stage_sem.at[stage]
        )

    def near_copy(side, i):
        return pltpu.make_async_remote_copy(
            src_ref=held.at[pl.ds(((1 - c) * 2 + side) * 2, 2)],
            dst_ref=near.at[pl.ds(side * 2, 2)],
            send_sem=near_send.at[i],
            recv_sem=near_recv.at[i],
            device_id=other_core(),
            device_id_type=MESH,
        )

    def add_near(z):
        mine = held.at[c * 4 + z]

        def add(i, carry):
            here = at(i, 64)
            mine[here] = mine[here] + near[z, here]
            return carry

        lax.fori_loop(0, rows // 64, add, 0)

    half = rows // 2
    first, second = pl.ds(0, half), pl.ds(half, half)
    z = {
        "own": h * 2 + l,
        "partner": h * 2 + 1 - l,
        "cross": (1 - h) * 2 + 1 - l,
        "far": (1 - h) * 2 + l,
    }

    def block_at(which, part):
        return held.at[c * 4 + z[which], part]

    order = [(1 - c) * 2 + h, (1 - c) * 2 + 1 - h, c * 2 + 1 - h, c * 2 + h]
    expert(order[0], 0)
    near_copy(h, 0).start()
    stage_copy(order[0], 0).start()
    ring.far()
    ring.shared["cross"].wait_recv()
    ring.shared["far"].wait_recv()
    expert(order[1], 1)
    near_copy(1 - h, 1).start()
    stage_copy(order[1], 1).start()
    stage_copy(order[0], 0).wait()
    expert(order[2], 0)
    stage_copy(order[2], 0).start()
    near_copy(1 - h, 1).wait_recv()
    add_near(z["far"])
    far_partner = lanes.send(block_at("far", first), far.at[0], partner())
    far_cross = lanes.send(block_at("far", second), far.at[1], cross())
    add_near(z["cross"])
    early_cross = lanes.send(block_at("cross", second), nearest.at[1, second], cross())
    stage_copy(order[1], 1).wait()
    expert(order[3], 1)
    stage_copy(order[3], 1).start()
    near_copy(h, 0).wait_recv()
    add_near(z["partner"])
    early_partner = lanes.send(block_at("partner", first), nearest.at[0, first], partner())
    add_near(z["own"])
    sends = []
    gate_own = pltpu.make_async_copy(gate_back.at[me], gate_back_out.at[me], own.at[6])
    gate_own.start()
    for step in COLUMN:
        peer = column_peer(*step)
        to = (peer["c"] * 2 + peer["h"]) * 2 + peer["l"]
        sends.append(lanes.send(gate_back.at[to], gate_back_out.at[me], peer))

    def weight_grad(values, others, target, number):
        part = 384

        def make(i, carry):
            left = values[:, :, at(i, part)].reshape(4 * slots, part)
            grad = ref_dot_tn(left, others[...].reshape(4 * slots, ff)).astype(bf16)
            target[pl.ds(4 * i, 4)] = grad.reshape(4, part // 4, ff)
            return carry

        lax.fori_loop(0, width // part, make, 0)
        copy = pltpu.make_async_copy(target, weight_grads.at[:, number], own.at[1 + number])
        copy.start()
        return copy

    far_partner.wait_recv()
    mine = block_at("cross", first)
    mine[...] = mine[...] + far[0]
    late_cross = lanes.send(mine, nearest.at[1, first], cross())
    far_cross.wait_recv()
    mine = block_at("partner", second)
    mine[...] = mine[...] + far[1]
    late_partner = lanes.send(mine, nearest.at[0, second], partner())
    go("drain")
    grad_copies = [
        weight_grad(picked_grads, hidden_gated, w_down, 2),
        weight_grad(picked, gate_low, w_gate, 0),
        weight_grad(picked, up_low, w_up, 1),
    ]
    for copy in (early_partner, early_cross, late_cross, late_partner):
        copy.wait_recv()

    def finish(i, carry):
        here = at(i, 64)
        total = held[c * 4 + z["own"], here].astype(f32)
        back_out[here, :] = (
            total + nearest[0, here].astype(f32) + nearest[1, here].astype(f32)
        )
        return carry

    lax.fori_loop(0, rows // 64, finish, 0)
    for copy in (early_partner, early_cross, late_cross, late_partner, far_partner, far_cross):
        copy.wait_send()
    for i, side in ((0, h), (1, 1 - h)):
        near_copy(side, i).wait_send()
    for copy in sends + grad_copies + [gate_own]:
        copy.wait()
    stage_copy(order[2], 0).wait()
    stage_copy(order[3], 1).wait()
    ring.drain()


def experts_of_column(rows, gates, grads_all, slots, others, block):
    count, width = rows.shape
    ff = others.shape[3]
    return pl.pallas_call(
        experts_kernel,
        name="experts",
        out_shape=(
            jax.ShapeDtypeStruct((8, count, width), bf16),
            jax.ShapeDtypeStruct((16, 3) + others.shape[2:], bf16),
            jax.ShapeDtypeStruct((count, width), f32),
            jax.ShapeDtypeStruct(gates.shape, f32),
        ),
        in_specs=[VMEM, VMEM, ANY, VMEM, ANY, VMEM],
        out_specs=(HBM, HBM, VMEM, VMEM),
        scratch_shapes=[
            pltpu.VMEM((8, count, width), bf16),
            pltpu.VMEM((8, count, width), bf16),
            pltpu.VMEM((16, width // 16, ff), bf16),
            pltpu.VMEM((16, width // 16, ff), bf16),
            pltpu.VMEM((16, width // 16, ff), bf16),
            pltpu.VMEM((4, SLOTS, width), bf16),
            pltpu.VMEM((4, SLOTS, width), bf16),
            pltpu.VMEM((4, SLOTS, ff), f32),
            pltpu.VMEM((4, SLOTS, ff), bf16),
            pltpu.VMEM((4, SLOTS, ff), bf16),
            pltpu.VMEM((4, SLOTS, ff), bf16),
            pltpu.VMEM((2, 2, count, width), bf16),
            pltpu.VMEM((4, count, width), bf16),
            pltpu.VMEM((2, count // 2, width), bf16),
            pltpu.VMEM((2, count, width), bf16),
            pltpu.VMEM(gates.shape, f32),
            pltpu.VMEM(gates.shape, f32),
        ]
        + lanes_scratch(64)
        + [
            pltpu.SemaphoreType.DMA((7,)),
            pltpu.SemaphoreType.DMA((2,)),
            pltpu.SemaphoreType.DMA((2,)),
            pltpu.SemaphoreType.DMA((2,)),
        ],
        compiler_params=pltpu.CompilerParams(
            collective_id=4, has_side_effects=True, vmem_limit_bytes=60 * 2**20
        ),
    )(rows, gates, grads_all, slots[:, None, :], others, block)


def return_kernel(
    part,
    misc_at,
    in_ref,
    out_ref,
    expert_ref,
    tokens_ref,
    block_ref,
    block_half,
    grads_out,
    misc_out,
    expert_out,
    tokens_out,
    block_out,
    near,
    near_p0,
    rest_p0,
    near_q0,
    near_p1,
    rest_p1,
    near_q1,
    pieces,
    landed,
    misc_landed,
    s_sem,
    r_sem,
    ps,
    pr,
    ms,
    mr,
    own,
):
    c, h, l = place()
    z = h * 2 + l
    me = c * 4 + z
    barrier = pltpu.get_barrier_semaphore()
    pl.semaphore_wait(barrier, greet_column(barrier) + greet_chips(barrier))
    lanes = Lanes(s_sem, r_sem)
    width = near.shape[2]
    half = near.shape[1] // 2
    load = pltpu.make_async_copy(in_ref, near, own.at[4])
    load.start()
    sums = []
    for low, p, q, held in (
        (0, "y", "x", (near_p0, rest_p0, near_q0)),
        (half, "x", "y", (near_p1, rest_p1, near_q1)),
    ):

        def view(index, columns, mine=pl.ds(low, half)):
            return near.at[index, mine, columns]

        def source(index, mine=pl.ds(low, half)):
            return in_ref.at[index, mine]

        sums.append(ChipSum(lanes, view, source, 640, width, p, q, *held))
    for each in sums:
        each.far()
    own_copy = pltpu.make_async_copy(expert_ref.at[me], expert_out.at[me], own.at[0])
    own_copy.start()
    own_tokens = pltpu.make_async_copy(tokens_ref, tokens_out.at[l], own.at[1])
    own_tokens.start()
    own_block = pltpu.make_async_copy(block_ref, block_out.at[l], own.at[2])
    own_block.start()
    count = block_half.shape[0]
    rest = pl.ds(count, count)
    had = pltpu.make_async_copy(block_half, block_out.at[1 - l, pl.ds(0, count)], own.at[3])
    had.start()
    expert_copies = [
        lanes.send(tokens_ref, tokens_out.at[l], partner()),
        lanes.send(block_ref.at[rest], block_out.at[l, rest], partner()),
    ]
    for step in COLUMN:
        peer = column_peer(*step)
        to = (peer["c"] * 2 + peer["h"]) * 2 + peer["l"]
        expert_copies.append(lanes.send(expert_ref.at[to], expert_out.at[me], peer))

    load.wait()
    for each in sums:
        each.joined()
    for each in sums:
        each.plain()
    for each in sums:
        each.far_q()
    for each in sums:
        each.next_q()
    for number, each in enumerate(sums):
        total = each.total()
        for i in range(2):
            pieces[2 * number + i, :part, :width] = total[i * part : (i + 1) * part].astype(bf16)
    for k in range(4):
        pieces[k, :part, width:] = out_ref[k * part : (k + 1) * part, :].astype(bf16)
        pieces[k, part:, :] = jnp.zeros((PAD - part, pieces.shape[2]), bf16)

    def to_owner(target, owner, src, dst, send_sem, recv_sem, asked):
        is_me = (owner["c"] == c) & (owner["h"] == h) & (owner["l"] == l)
        there = pltpu.make_async_remote_copy(
            src_ref=src,
            dst_ref=dst,
            send_sem=send_sem,
            recv_sem=recv_sem,
            device_id=owner,
            device_id_type=MESH,
        )
        here = pltpu.make_async_copy(src, dst, recv_sem)
        pl.when(asked & jnp.logical_not(is_me))(there.start)
        pl.when(asked & is_me)(here.start)
        return asked & jnp.logical_not(is_me), there

    sent = []
    everyone = c < 2
    for target in range(4):
        owner = {"c": target // 2, "h": target % 2, "l": c}
        sent.append(
            to_owner(
                target, owner, pieces.at[target], landed.at[z], ps.at[target], pr.at[z], everyone
            )
        )
    misc = pl.ds(misc_at, MISC)
    for target in range(4):
        owner = {"c": target // 2, "h": target % 2, "l": 1}
        sent.append(
            to_owner(
                target,
                owner,
                pieces.at[target, :, misc],
                misc_landed.at[z],
                ms.at[target],
                mr.at[z],
                c == 0,
            )
        )
    for source in range(4):
        pltpu.make_async_copy(pieces.at[0], landed.at[source], pr.at[source]).wait()

    def summed(ref, columns=slice(None)):
        parts = [ref[i, :, columns].astype(f32)[:part] for i in range(4)]
        return (parts[0] + parts[1]) + (parts[2] + parts[3])

    grads_out[...] = summed(landed)

    def from_core():
        for source in range(4):
            pltpu.make_async_copy(
                pieces.at[0, :, misc], misc_landed.at[source], mr.at[source]
            ).wait()
        misc_out[...] = summed(misc_landed)

    def from_piece():
        misc_out[...] = summed(landed, misc)

    pl.when(l == 1)(from_core)
    pl.when(l == 0)(from_piece)
    for asked, there in sent:
        pl.when(asked)(there.wait_send)
    for each in sums:
        each.drain()
    own_copy.wait()
    own_tokens.wait()
    own_block.wait()
    had.wait()
    for copy in expert_copies:
        copy.wait()


def return_gradients(grad_in, out_sum, expert_pieces, tokens, block, block_half, part, misc_at):
    width, rows = grad_in.shape[2], grad_in.shape[1]
    full = width + out_sum.shape[1]
    half = rows // 2
    ring = [
        pltpu.VMEM((2, 2, half, width), bf16),
        pltpu.VMEM((2, 4, half, width), bf16),
        pltpu.VMEM((4, half, width), bf16),
    ]
    return pl.pallas_call(
        functools.partial(return_kernel, part, misc_at),
        name="return_gradients",
        out_shape=(
            jax.ShapeDtypeStruct((part, full), f32),
            jax.ShapeDtypeStruct((part, MISC), f32),
            jax.ShapeDtypeStruct(expert_pieces.shape, expert_pieces.dtype),
            jax.ShapeDtypeStruct((2,) + tokens.shape, tokens.dtype),
            jax.ShapeDtypeStruct((2,) + block.shape, block.dtype),
        ),
        in_specs=[ANY] + [VMEM] * 5,
        out_specs=(VMEM, VMEM, HBM, HBM, HBM),
        scratch_shapes=[pltpu.VMEM((16, rows, width), bf16)]
        + ring
        + ring
        + [
            pltpu.VMEM((4, PAD, full), bf16),
            pltpu.VMEM((4, PAD, full), bf16),
            pltpu.VMEM((4, PAD, MISC), bf16),
        ]
        + lanes_scratch(50)
        + [
            pltpu.SemaphoreType.DMA((4,)),
            pltpu.SemaphoreType.DMA((4,)),
            pltpu.SemaphoreType.DMA((4,)),
            pltpu.SemaphoreType.DMA((4,)),
            pltpu.SemaphoreType.DMA((5,)),
        ],
        compiler_params=pltpu.CompilerParams(
            collective_id=7, has_side_effects=True, vmem_limit_bytes=62 * 2**20
        ),
    )(grad_in, out_sum, expert_pieces, tokens, block, block_half)


def body(
    tokens,
    segments,
    routes,
    attn_gain,
    w_query,
    key_matrix,
    value_matrix,
    w_output,
    mix_gain,
    w_router,
    w_gate,
    w_up,
    w_down,
    block_cotangent,
):
    c, h, l = place()
    model_width = tokens.shape[2]
    rows = tokens.shape[1] // 2
    experts, part, ff_half = w_gate.shape
    q_half = w_query.shape[1]

    kv_width = key_matrix.shape[1]
    in_width = q_half + 2 * kv_width + MISC
    halves = (2, rows, model_width)
    tables = [jnp.asarray(table) for table in rope_tables(segments.shape[1])]
    (
        w_attn,
        grads_all,
        slots,
        others_full,
        expert_block,
        normed_in,
        q,
        kv,
        attended,
        lse,
        residual,
        normed_mix,
        gates,
    ) = attention(
        (w_query, key_matrix, value_matrix, w_output.T, w_router),
        (attn_gain[None], mix_gain[None]),
        (w_gate, w_up, w_down),
        block_cotangent.reshape(halves),
        tokens.reshape(halves),
        routes[0].T,
        segments,
        tables,
        part,
    )
    w_attn = w_attn.reshape(2, model_width, in_width + q_half)
    mix_parts, expert_grads, mix_back, gate_back = experts_of_column(
        normed_mix, gates, grads_all, slots.reshape(4, 2 * rows), others_full, expert_block
    )
    grad_in, out_sum, tokens_back, block_out, block_half, pieces = attention_back(
        mix_back,
        gate_back,
        gates,
        normed_mix,
        residual,
        tokens.reshape(halves),
        block_cotangent.reshape(halves),
        normed_in,
        attended,
        q,
        kv,
        lse,
        *tables,
        segments,
        w_attn,
        mix_parts,
        expert_grads,
    )

    returned, misc_back, expert_back, tokens_back, block_out = return_gradients(
        grad_in,
        out_sum,
        pieces,
        tokens_back,
        block_out,
        block_half,
        part,
        in_width - MISC,
    )
    expert_back = expert_back[:, :, :part].astype(f32)
    return (
        block_out.reshape(1, 2 * rows, model_width),
        tokens_back.reshape(1, 2 * rows, model_width).astype(f32),
        misc_back[:, experts],
        returned[:, :q_half],
        returned[:, q_half : q_half + kv_width],
        returned[:, q_half + kv_width : q_half + 2 * kv_width],
        returned[:, in_width:].T,
        misc_back[:, experts + 1],
        misc_back[:, :experts],
        expert_back[:, 0],
        expert_back[:, 1],
        expert_back[:, 2],
    )


def solution(mesh):
    split = Mesh(mesh.devices.reshape(4, 4, 2, 2, 2), ("x", "y", "c", "h", "l"))
    fsdp = ("x", "y", "c")
    owner = ("x", "y", "c", "h")
    return jax.shard_map(
        body,
        mesh=split,
        in_specs=(
            P(fsdp, "h", None),
            P(fsdp, None),
            P(fsdp, "h", None),
            P(owner),
            P(owner, "l"),
            P(owner, "l"),
            P(owner, "l"),
            P("l", owner),
            P(owner),
            P(owner, None),
            P(None, owner, "l"),
            P(None, owner, "l"),
            P(None, owner, "l"),
            P(fsdp, "h", None),
        ),
        out_specs=(
            P(fsdp, "h", None),
            P(fsdp, "h", None),
            P(owner),
            P(owner, "l"),
            P(owner, "l"),
            P(owner, "l"),
            P("l", owner),
            P(owner),
            P(owner, None),
            P(None, owner, "l"),
            P(None, owner, "l"),
            P(None, owner, "l"),
        ),
        check_vma=False,
    )
```

```python
import functools

import jax
import jax.numpy as jnp
import numpy as np
from jax import lax
from jax.experimental import pallas as pl
from jax.experimental.pallas import tpu as pltpu
from jax.sharding import Mesh
from jax.sharding import PartitionSpec as P

QUERY_HEADS = 12
KEY_VALUE_HEADS = 2
HEAD_SIZE = 128
GROUP = QUERY_HEADS // KEY_VALUE_HEADS
EPS = 1e-06
ROPE_BASE = 1000000.0
NEG_FILL = -1e30
MISC = 128
SLOTS = 320
PAD = 32
MESH = pl.DeviceIdType.MESH
ANY = pl.BlockSpec(memory_space=pl.ANY)
HBM = pl.BlockSpec(memory_space=pltpu.HBM)
VMEM = pl.BlockSpec(memory_space=pltpu.VMEM)
f32 = jnp.float32
bf16 = jnp.bfloat16


def rope_tables(count):
    exponents = -np.arange(HEAD_SIZE // 2, dtype=np.float64) * (2.0 / HEAD_SIZE)
    frequency = (ROPE_BASE**exponents).astype(np.float32)
    angles = np.arange(count, dtype=np.float32)[:, None] * frequency[None, :]
    angles = angles.astype(np.float64)
    cosine, sine = np.cos(angles).astype(np.float32), np.sin(angles).astype(np.float32)
    return np.concatenate([cosine, cosine], axis=1), np.concatenate([-sine, sine], axis=1)


def place():
    return lax.axis_index("c"), lax.axis_index("h"), lax.axis_index("l")


def column_peer(core_step, z_step):
    c, h, l = place()
    z = lax.rem(h * 2 + l + z_step, 4)
    return {"c": lax.rem(c + core_step, 2), "h": z // 2, "l": lax.rem(z, 2)}


def at_z(core, z):
    return {"c": core, "h": z // 2, "l": lax.rem(z, 2)}


def greet(steps):
    barrier = pltpu.get_barrier_semaphore()
    for core_step, z_step in steps:
        pl.semaphore_signal(
            barrier, inc=1, device_id=column_peer(core_step, (4 - z_step) % 4), device_id_type=MESH
        )
    pl.semaphore_wait(barrier, len(steps))


def send(src, dst, send_sem, recv_sem, peer):
    copy = pltpu.make_async_remote_copy(
        src_ref=src,
        dst_ref=dst,
        send_sem=send_sem,
        recv_sem=recv_sem,
        device_id=peer,
        device_id_type=MESH,
    )
    copy.start()
    return copy


COLUMN = [(0, 1), (0, 2), (0, 3), (1, 0), (1, 1), (1, 2), (1, 3)]
ALONG_Z = [(0, 1), (0, 2), (0, 3)]


class Lanes:
    def __init__(self, send_sem, recv_sem):
        self.send_sem, self.recv_sem, self.used = send_sem, recv_sem, 0

    def send(self, src, dst, peer):
        i = self.used
        self.used += 1
        return send(src, dst, self.send_sem.at[i], self.recv_sem.at[i], peer)


def lanes_scratch(count):
    return [pltpu.SemaphoreType.DMA((count,)), pltpu.SemaphoreType.DMA((count,))]


def chip_peer(axis, step):
    return {axis: lax.rem(lax.axis_index(axis) + step + 4, 4)}


def greet_chips(barrier):
    for axis in ("x", "y"):
        for step in (1, 3):
            pl.semaphore_signal(
                barrier, inc=1, device_id=chip_peer(axis, step), device_id_type=MESH
            )
    return 4


def greet_column(barrier):
    for step in COLUMN:
        pl.semaphore_signal(barrier, inc=1, device_id=column_peer(*step), device_id_type=MESH)
    return len(COLUMN)


def partner():
    return {"l": 1 - lax.axis_index("l")}


def cross():
    return {"h": 1 - lax.axis_index("h"), "l": 1 - lax.axis_index("l")}


def other_core():
    return {"c": 1 - lax.axis_index("c")}


class ColumnRing:
    def __init__(self, lanes, rows_ref, out_ref):
        c, h, l = place()
        self.lanes, self.rows, self.out = lanes, rows_ref, out_ref
        half = rows_ref.shape[0] // 2
        self.first, self.second = pl.ds(0, half), pl.ds(half, half)
        self.at = {
            "own": c * 4 + h * 2 + l,
            "partner": c * 4 + h * 2 + 1 - l,
            "cross": c * 4 + (1 - h) * 2 + 1 - l,
            "far": c * 4 + (1 - h) * 2 + l,
        }
        self.shared = {}

    def share(self, which):
        block = self.out.at[self.at[which]]
        self.shared[which] = self.lanes.send(block, block, other_core())

    def half_to(self, part, peer):
        return self.lanes.send(self.rows.at[part], self.out.at[self.at["own"], part], peer)

    def start(self):
        self.partner_first = self.half_to(self.first, partner())
        self.cross_second = self.half_to(self.second, cross())
        self.partner_second = self.half_to(self.second, partner())
        self.cross_first = self.half_to(self.first, cross())
        here = self.out.at[self.at["own"]]
        self.shared["own"] = self.lanes.send(self.rows, here, other_core())

    def relay(self):
        self.partner_first.wait_recv()
        block = self.out.at[self.at["partner"], self.first]
        self.far_cross = self.lanes.send(block, block, cross())
        self.cross_second.wait_recv()
        block = self.out.at[self.at["cross"], self.second]
        self.far_partner = self.lanes.send(block, block, partner())

    def nearest(self):
        self.partner_second.wait_recv()
        self.share("partner")
        self.cross_first.wait_recv()
        self.share("cross")

    def far(self):
        self.far_cross.wait_recv()
        self.far_partner.wait_recv()
        self.share("far")

    def drain(self):
        for copy in (self.partner_first, self.partner_second, self.cross_first, self.cross_second):
            copy.wait_send()
        for copy in (self.far_cross, self.far_partner):
            copy.wait_send()
        for copy in self.shared.values():
            copy.wait_send()

    def finish(self):
        self.far()
        for copy in self.shared.values():
            copy.wait_recv()
        self.drain()


def chip_index(steps):
    x = lax.rem(lax.axis_index("x") + steps["x"] + 4, 4)
    y = lax.rem(lax.axis_index("y") + steps["y"] + 4, 4)
    return x * 4 + y


def shifted(columns, start, size):
    if columns == slice(None):
        return pl.ds(start, size)
    return pl.ds(start + columns.start, columns.size)


class ChipRing:
    def __init__(self, lanes, own, view, cut, width, a, b, line=None):
        self.lanes, self.own, self.view = lanes, own, view
        self.low, self.high = pl.ds(0, cut), pl.ds(cut, width - cut)
        self.a, self.b, self.line = a, b, line
        self.sent, self.near, self.last = [], [], {}

    def ref(self, da, db, columns=slice(None)):
        return self.view(chip_index({self.a: da, self.b: db}), columns)

    def copy(self, src, dst, axis, step):
        made = self.lanes.send(src, dst, chip_peer(axis, step))
        self.sent.append(made)
        return made

    def start(self):
        here = self.ref(0, 0)
        self.first = [self.copy(self.own, here, self.a, step) for step in (1, -1)]
        self.turn = {0: [self.copy(self.own, here, self.b, step) for step in (1, -1)]}

    def pass_on(self, da):
        block = self.ref(da, 0)
        self.turn[da] = [self.copy(block, block, self.b, step) for step in (1, -1)]

    def relay_first(self):
        for copy in self.first:
            copy.wait_recv()
        block = self.ref(-1, 0, self.low)
        one = self.copy(block, block, self.a, 1)
        block = self.ref(1, 0, self.high)
        self.second = [one, self.copy(block, block, self.a, -1)]
        self.pass_on(-1)
        self.pass_on(1)

    def relay_turn(self, da):
        for copy in self.turn[da]:
            copy.wait_recv()
        step = 1 if da in (0, -1) else -1
        block = self.ref(da, -step)
        self.last[da] = self.copy(block, block, self.b, step)

    def relay_second(self):
        for copy in self.second:
            copy.wait_recv()
        self.pass_on(2)

    def end(self, da):
        self.last[da].wait_recv()
        if self.line is not None:
            block = self.line(lax.rem(lax.axis_index(self.a) + da + 4, 4))
            self.near.append(self.lanes.send(block, block, other_core()))

    def finish(self):
        for da in (0, -1, 1, 2):
            self.end(da)

    def drain(self):
        for copy in self.sent:
            copy.wait_send()
        for copy in self.near:
            copy.wait()


class ChipSum:
    def __init__(self, lanes, view, source, cut, width, p, q, near_p, rest_p, near_q):
        self.lanes, self.view, self.source = lanes, view, source
        self.low, self.high = pl.ds(0, cut), pl.ds(cut, width - cut)
        self.p, self.q = p, q
        self.near_p, self.rest_p, self.near_q = near_p, rest_p, near_q
        self.sent, self.next_copies = [], {}

    def index(self, dp, dq):
        return chip_index({self.p: dp, self.q: dq})

    def copy(self, src, dst, axis, step):
        made = self.lanes.send(src, dst, chip_peer(axis, step))
        self.sent.append(made)
        return made

    def own(self, dp, dq, columns=slice(None)):
        return self.view(self.index(dp, dq), columns)

    def side(self, i, columns):
        lead = (slice(None),) * (len(self.near_q.shape) - 2)
        return self.near_q.at[(i,) + lead + (columns,)]

    def far(self):
        self.far_copies = {}
        for dq, step, i in ((2, 1, 0), (3, -1, 0), (1, 1, 1), (0, -1, 1)):
            direction = 0 if step == 1 else 1
            self.far_copies[direction, i] = self.copy(
                self.source(self.index(2, dq)), self.near_p.at[direction, i], self.p, step
            )

    def plain(self):
        for dq, step in ((2, -1), (3, 1), (1, -1), (0, 1)):
            self.next_to(dq, step, self.source(self.index(step, dq)))

    def next_to(self, dq, step, block):
        direction = 0 if step == 1 else 1
        self.next_copies[direction, dq] = self.copy(
            block, self.rest_p.at[direction, dq], self.p, step
        )

    def joined(self):
        for dq, step, i in ((2, 1, 0), (3, -1, 0), (1, 1, 1), (0, -1, 1)):
            direction = 0 if step == 1 else 1
            self.far_copies[direction, i].wait_recv()
            mine = self.own(step, dq)
            mine[...] = mine[...] + self.near_p[direction, i]
            self.next_to(dq, step, mine)

    def collect(self, dq):
        for direction in range(2):
            self.next_copies[direction, dq].wait_recv()
        mine = self.own(0, dq)
        total = mine[...].astype(f32)
        for direction in range(2):
            total = total + self.rest_p[direction, dq].astype(f32)
        mine[...] = total.astype(mine.dtype)

    def far_q(self):
        self.collect(2)
        self.far_q_copies = [
            self.copy(self.own(0, 2, self.low), self.side(0, self.low), self.q, 1),
            self.copy(self.own(0, 2, self.high), self.side(1, self.high), self.q, -1),
        ]

    def next_q(self):
        self.next_q_copies = []
        for i, (dq, columns) in enumerate(((1, self.low), (3, self.high))):
            self.collect(dq)
            self.far_q_copies[i].wait_recv()
            mine = self.own(0, dq, columns)
            mine[...] = mine[...] + self.side(i, columns)[...]
            self.next_q_copies.append(
                self.copy(self.own(0, dq), self.near_q.at[2 + i], self.q, 1 if i == 0 else -1)
            )

    def total(self):
        self.collect(0)
        total = self.own(0, 0)[...].astype(f32)
        for i in range(2):
            self.next_q_copies[i].wait_recv()
            total = total + self.near_q[2 + i].astype(f32)
        return total

    def drain(self):
        for copy in self.sent:
            copy.wait_send()


def ref_dot(a, b):
    return jnp.dot(a, b, preferred_element_type=f32)


def ref_dot_nt(a, b):
    return lax.dot_general(a, b, (((1,), (1,)), ((), ())), preferred_element_type=f32)


def ref_dot_tn(a, b):
    return lax.dot_general(a, b, (((0,), (0,)), ((), ())), preferred_element_type=f32)


def at(i, size):
    return pl.ds(pl.multiple_of(i * size, size), size)


def gain_rows(misc):
    pick = lax.broadcasted_iota(jnp.int32, (16, MISC), 0)
    pick = (pick == lax.broadcasted_iota(jnp.int32, (16, MISC), 1)).astype(f32).astype(bf16)
    return ref_dot_nt(pick, misc)


def turn(values, cosine, sine):
    return values * cosine + pltpu.roll(values, HEAD_SIZE // 2, 1) * sine


def turn_back(values, cosine, sine):
    return values * cosine - pltpu.roll(values, HEAD_SIZE // 2, 1) * sine


def as_column(row):
    count = row.shape[1]
    same = lax.broadcasted_iota(jnp.int32, (count, count), 0) == lax.broadcasted_iota(
        jnp.int32, (count, count), 1
    )
    return jnp.sum(jnp.where(same, row.astype(f32), 0.0), axis=1, keepdims=True)


def fill_bias(bias, seg_ref, z):
    keys, queries = bias.shape
    seg_row = seg_ref[:, at(z, queries)].astype(f32)

    def fill(i, carry):
        seg_column = as_column(seg_ref[:, at(i, queries)])
        key = lax.broadcasted_iota(jnp.int32, (queries, queries), 0) + i * queries
        query = lax.broadcasted_iota(jnp.int32, (queries, queries), 1) + z * queries
        seen = (seg_column == seg_row) & (key <= query)
        bias[at(i, queries), :] = jnp.where(seen, 0.0, NEG_FILL)
        return carry

    lax.fori_loop(0, keys // queries, fill, 0)


KEYS = 128


def key_block(kv, i, k):
    per_block = kv.shape[1] // KEYS
    start = (k % per_block) * KEYS
    return kv[k // per_block, start : start + KEYS, i * HEAD_SIZE : (i + 1) * HEAD_SIZE]


class RowsRing:
    def __init__(self, lanes, rows_ref, out_ref):
        c, h, l = place()
        self.lanes, self.out, self.l = lanes, out_ref, l
        self.rows = rows_ref
        self.own = pl.ds((c * 2 + h) * 2, 2)
        self.here = c * 4 + h * 2 + l
        self.cross_at = c * 4 + (1 - h) * 2 + 1 - l
        self.far_at = c * 4 + (1 - h) * 2 + l
        self.shared = []

    def share(self, index):
        block = self.out.at[index]
        self.shared.append(self.lanes.send(block, block, other_core()))

    def start(self):
        size = self.rows.shape[1] // 4
        self.parts = [pl.ds(i * size, size) for i in range(4)]
        self.to_cross = [
            self.lanes.send(self.rows.at[self.l, some], self.out.at[self.here, some], cross())
            for some in self.parts
        ]
        self.shared.append(self.lanes.send(self.rows, self.out.at[self.own], other_core()))
        self.to_partner = []

    def relay(self, i):
        self.to_cross[i].wait_recv()
        block = self.out.at[self.cross_at, self.parts[i]]
        self.to_partner.append(self.lanes.send(block, block, partner()))

    def finish(self):
        self.share(self.cross_at)
        for copy in self.to_partner:
            copy.wait_recv()
        self.share(self.far_at)

    def drain(self):
        for copy in self.to_cross + self.to_partner:
            copy.wait_send()
        for copy in self.shared:
            copy.wait()


def attention_kernel(
    part,
    wq_ref,
    wk_ref,
    wv_ref,
    wo_ref,
    router_ref,
    attn_gain_ref,
    mix_gain_ref,
    wg_ref,
    wu_ref,
    wd_ref,
    rows_ref,
    tokens_ref,
    routes_ref,
    seg_ref,
    cos_table,
    sin_table,
    w_out,
    rows_out,
    slots_out,
    expert_out,
    expert_block,
    a_out,
    q_out,
    kv_out,
    o_out,
    lse_out,
    h1_out,
    b_out,
    gates_out,
    w,
    attn_in,
    expert_in,
    block,
    bias,
    value_turned,
    attn_ref,
    expert_ref,
    slots_ref,
    slots_own,
    cos_ref,
    sin_ref,
    s_sem,
    r_sem,
    as_sem,
    ar_sem,
    own,
):
    c, h, l = place()
    z = h * 2 + l
    me = (c * 2 + h) * 2 + l
    x_ref = tokens_ref.at[l]
    rows, width = rows_ref.shape[1:]
    q_half = w.shape[4] // 2 - (HEAD_SIZE * 2 + MISC) // 2
    kv_at, misc_at, out_at = q_half, q_half + 2 * HEAD_SIZE, q_half + 2 * HEAD_SIZE + MISC
    ff = expert_block.shape[2]
    tables = [
        pltpu.make_async_copy(cos_table.at[pl.ds(z * rows, rows)], cos_ref, own.at[5]),
        pltpu.make_async_copy(sin_table.at[pl.ds(z * rows, rows)], sin_ref, own.at[6]),
    ]
    for copy in tables:
        copy.start()

    place_of = lax.broadcasted_iota(jnp.int32, (8, MISC), 0)
    place_of = (place_of == lax.broadcasted_iota(jnp.int32, (8, MISC), 1)).astype(f32)
    misc = ref_dot(router_ref[...], place_of.astype(bf16))
    column = lax.broadcasted_iota(jnp.int32, (part, MISC), 1)
    misc = jnp.where(column == 8, as_column(attn_gain_ref[...]), misc)
    misc = jnp.where(column == 9, as_column(mix_gain_ref[...]), misc)
    attn_ref[...] = jnp.zeros_like(attn_ref)
    attn_ref[:part, :q_half] = wq_ref[...]
    attn_ref[:part, kv_at : kv_at + HEAD_SIZE] = wk_ref[...]
    attn_ref[:part, kv_at + HEAD_SIZE : misc_at] = wv_ref[...]
    attn_ref[:part, misc_at:out_at] = misc.astype(bf16)
    attn_ref[:part, out_at:] = wo_ref[...]
    for i, ref in enumerate((wg_ref, wu_ref, wd_ref)):
        expert_ref[:, i, :part, :] = ref[...]
        expert_ref[:, i, part:, :] = jnp.zeros((8, PAD - part, ff // 2), bf16)

    block_rows = 2 * rows
    expert = lax.broadcasted_iota(jnp.int32, (8, block_rows), 0)
    taken = routes_ref[0:1, :] == expert
    for j in range(1, routes_ref.shape[0]):
        taken = taken | (routes_ref[j : j + 1, :] == expert)
    earlier = lax.broadcasted_iota(jnp.int32, (block_rows, block_rows), 0)
    earlier = (earlier < lax.broadcasted_iota(jnp.int32, (block_rows, block_rows), 1)).astype(f32)
    count = ref_dot(taken.astype(f32).astype(bf16), earlier.astype(bf16))
    count = jnp.where(taken, count, -1.0)
    slots_own[...] = jnp.where(l == 0, count[:, :rows], count[:, rows:])
    for e in range(8):
        slots_ref[e] = slots_own[e : e + 1, :]

    barrier = pltpu.get_barrier_semaphore()
    pl.semaphore_wait(barrier, greet_column(barrier) + greet_chips(barrier))
    lanes = Lanes(s_sem, r_sem)

    slot = c * 2 + h
    here = pltpu.make_async_copy(attn_ref, attn_in.at[slot], own.at[1])
    there = pltpu.make_async_remote_copy(
        src_ref=attn_ref,
        dst_ref=attn_in.at[slot],
        send_sem=as_sem.at[0],
        recv_sem=ar_sem.at[slot],
        device_id=column_peer(1, 0),
        device_id_type=MESH,
    )
    pl.when(c == l)(here.start)
    pl.when(c != l)(there.start)
    for z_step in range(1, 4):
        to_z = lax.rem(z + z_step, 4)
        send(attn_ref, attn_in.at[slot], as_sem.at[z_step], ar_sem.at[slot], at_z(l, to_z))
    local = [
        pltpu.make_async_copy(expert_ref.at[me], expert_in.at[me], own.at[0]),
        pltpu.make_async_copy(slots_ref.at[me], slots_out.at[me], own.at[2]),
        pltpu.make_async_copy(rows_ref, rows_out.at[pl.ds((c * 2 + h) * 2, 2)], own.at[3]),
    ]
    for copy in local:
        copy.start()
    pieces = []
    for step in COLUMN:
        peer = column_peer(*step)
        to = (peer["c"] * 2 + peer["h"]) * 2 + peer["l"]
        pieces.append(lanes.send(expert_ref.at[to], expert_in.at[me], peer))
        pieces.append(lanes.send(slots_ref.at[to], slots_out.at[me], peer))
    fill_bias(bias, seg_ref, z)

    for source in range(4):
        mine = (c == l) & (slot == source)

        def landed(source=source):
            pltpu.make_async_remote_copy(
                src_ref=attn_ref,
                dst_ref=attn_in.at[source],
                send_sem=as_sem.at[0],
                recv_sem=ar_sem.at[source],
                device_id=column_peer(1, 0),
                device_id_type=MESH,
            ).wait_recv()

        pl.when(jnp.logical_not(mine))(landed)
    pl.when(c == l)(here.wait)
    block[...] = jnp.concatenate(
        [attn_in[i].astype(f32)[:part] for i in range(4)], axis=0
    ).astype(block.dtype)
    index = chip_index({"x": 0, "y": 0})
    x_at, y_at = lax.axis_index("x"), lax.axis_index("y")
    keep = [pltpu.make_async_copy(block, w.at[c, x_at, y_at], own.at[4])]
    keep[0].start()
    half = block.shape[0] // 2
    rings = {}
    for name, start, size, cut in (("in", 0, out_at, 640), ("out", out_at, q_half, 384)):
        rings[name] = []
        for low, a, b in ((0, "x", "y"), (half, "y", "x")):
            mine = pl.ds(low, half)

            def view(index, columns, mine=mine, start=start, size=size):
                return w.at[c, index // 4, lax.rem(index, 4), mine, shifted(columns, start, size)]

            def line(i, a=a, mine=mine, columns=pl.ds(start, size)):
                return w.at[c, i, :, mine, columns] if a == "x" else w.at[c, :, i, mine, columns]

            own_part = block.at[mine, pl.ds(start, size)]
            rings[name].append(ChipRing(lanes, own_part, view, cut, size, a, b, line))
    rings["expert"] = []
    for low, a, b in ((0, "x", "y"), (half, "y", "x")):
        mine = pl.ds(low, half)

        def expert_view(index, columns, mine=mine):
            return expert_out.at[:, index, mine, columns]

        own_part = expert_block.at[pl.ds(1, 2), mine]
        rings["expert"].append(ChipRing(lanes, own_part, expert_view, ff // 2, ff, a, b))

    def go(name, step, *args):
        for ring in rings[name]:
            getattr(ring, step)(*args)

    go("in", "start")
    go("out", "start")
    rows_ring = RowsRing(lanes, rows_ref, rows_out)
    rows_ring.start()

    local[0].wait()
    for copy in pieces:
        copy.wait()
    for i in range(3):
        for l_side in range(2):
            expert_block[i, :, l_side * 384 : (l_side + 1) * 384] = jnp.concatenate(
                [expert_in[2 * j + l_side, i].astype(f32)[:part] for j in range(4)], axis=0
            ).astype(bf16)
    keep.append(
        pltpu.make_async_copy(expert_block.at[pl.ds(1, 2)], expert_out.at[:, index], own.at[0])
    )
    keep[1].start()

    keep[0].wait()
    go("in", "relay_first")
    go("in", "relay_turn", 0)
    go("in", "relay_second")
    go("in", "relay_turn", -1)
    go("in", "end", 0)
    rows_ring.relay(0)
    rows_ring.relay(1)
    go("in", "relay_turn", 1)
    go("in", "end", -1)
    go("in", "relay_turn", 2)
    go("in", "end", 1)
    rows_ring.relay(2)
    rows_ring.relay(3)
    go("out", "relay_first")
    go("in", "end", 2)
    go("expert", "start")
    go("out", "relay_turn", 0)
    go("out", "relay_second")
    for ring in rings["in"]:
        for copy in ring.near:
            copy.wait_recv()


    def projection(i, columns):
        return w[i, :, :, :, columns].reshape(width, -1)

    scale = HEAD_SIZE ** (-0.5)
    misc = projection(0, slice(misc_at, out_at))
    gains = gain_rows(misc)
    chunk = 32

    def norm(i, carry):
        here = at(i, chunk)
        x = x_ref[here, :].astype(f32)
        inverse = lax.rsqrt(jnp.mean(x * x, axis=1, keepdims=True) + EPS)
        a_out[here, :] = (x * inverse * gains[8:9, :]).astype(bf16)
        return carry

    lax.fori_loop(0, rows // chunk, norm, 0)
    for copy in tables:
        copy.wait()
    cosine, sine = cos_ref[...], sin_ref[...]
    sends = []
    for i in range(2):
        kv = ref_dot(a_out[...], projection(i, slice(kv_at, misc_at)))
        kv_out[z, :, 2 * i * 128 : (2 * i + 1) * 128] = turn(kv[:, :128], cosine, sine).astype(
            bf16
        )
        kv_out[z, :, (2 * i + 1) * 128 : (2 * i + 2) * 128] = kv[:, 128:].astype(bf16)
        pair = kv_out.at[z, :, pl.ds(2 * i * 128, 256)]
        sends.append([lanes.send(pair, pair, column_peer(*step)) for step in ALONG_Z])
    go("out", "relay_turn", -1)
    go("out", "relay_turn", 1)
    for i in range(2):

        def project(j, carry, i=i):
            q = ref_dot(a_out[...], w[i, :, :, :, at(j, 256)].reshape(width, 256))
            q_out[i * GROUP + 2 * j] = turn(q[:, :128], cosine, sine).astype(bf16)
            q_out[i * GROUP + 2 * j + 1] = turn(q[:, 128:], cosine, sine).astype(bf16)
            return carry

        lax.fori_loop(0, q_half // 256, project, 0)
    go("out", "relay_turn", 2)
    go("expert", "relay_first")
    keys_count = 4 * rows
    for i in range(2):
        for copy in sends[i]:
            copy.wait_recv()
        values = kv_out[:, :, (2 * i + 1) * 128 : (2 * i + 2) * 128]
        value_turned[...] = values.reshape(keys_count, HEAD_SIZE).T

        def attend(j, carry, i=i):
            keys = kv_out[:, :, 2 * i * 128 : (2 * i + 1) * 128]
            keys = keys.reshape(keys_count, HEAD_SIZE)
            scores = ref_dot_nt(keys, q_out[i * GROUP + j]) * scale + bias[...]
            peak = jnp.max(scores, axis=0, keepdims=True)
            expo = jnp.exp(scores - peak)
            total = jnp.sum(expo, axis=0, keepdims=True)
            weights = (expo * (1.0 / total)).astype(bf16)
            mixed = ref_dot(value_turned[...], weights)
            o_out[:, at(i * GROUP + j, HEAD_SIZE)] = mixed.T.astype(bf16)
            lse_out[i * GROUP + j] = peak + jnp.log(total)
            return carry

        for some in range(2):
            lax.fori_loop(some * GROUP // 2, (some + 1) * GROUP // 2, attend, 0)
            if (i, some) == (0, 0):
                go("out", "finish")
                go("expert", "relay_turn", 0)
            elif (i, some) == (0, 1):
                go("expert", "relay_second")
            elif (i, some) == (1, 0):
                go("expert", "relay_turn", -1)
    for ring in rings["out"]:
        for copy in ring.near:
            copy.wait_recv()
    keep.append(pltpu.make_async_copy(w, w_out, own.at[1]))
    keep[2].start()

    def leave(j, carry):
        here = at(j, 384)
        u = ref_dot_nt(
            o_out[:, :q_half], w[0, j, :, :, out_at:].reshape(384, q_half)
        )
        u = u + ref_dot_nt(
            o_out[:, q_half:], w[1, j, :, :, out_at:].reshape(384, q_half)
        )
        h1_out[:, here] = x_ref[:, here].astype(f32) + u
        return carry

    lax.fori_loop(0, width // 384, leave, 0)
    go("expert", "relay_turn", 1)

    def second(i, carry):
        here = at(i, chunk)
        h1 = h1_out[here, :]
        inverse = lax.rsqrt(jnp.mean(h1 * h1, axis=1, keepdims=True) + EPS)
        b_out[here, :] = (h1 * inverse * gains[9:10, :]).astype(bf16)
        return carry

    lax.fori_loop(0, rows // chunk, second, 0)
    logits = ref_dot(b_out[...], misc).T[:8]
    named = slots_own[...] >= 0
    masked = jnp.where(named, logits, NEG_FILL)
    expo = jnp.where(named, jnp.exp(masked - jnp.max(masked, axis=0, keepdims=True)), 0.0)
    gates = expo / jnp.sum(expo, axis=0, keepdims=True)
    for e in range(8):
        gates_out[e] = gates[e : e + 1]
    go("expert", "relay_turn", 2)
    rows_ring.finish()
    go("expert", "finish")
    for copy in sends[0] + sends[1]:
        copy.wait_send()
    rows_ring.drain()
    for copy in local[1:]:
        copy.wait()
    pl.when(c != l)(there.wait_send)
    for z_step in range(1, 4):
        pltpu.make_async_remote_copy(
            src_ref=attn_ref,
            dst_ref=attn_in.at[slot],
            send_sem=as_sem.at[z_step],
            recv_sem=ar_sem.at[slot],
            device_id=column_peer(0, z_step),
            device_id_type=MESH,
        ).wait_send()
    for name in ("in", "out"):
        for ring in rings[name]:
            for copy in ring.near:
                copy.wait_send()
            for copy in ring.sent:
                copy.wait_send()
    go("expert", "drain")
    for copy in keep[1:]:
        copy.wait()


def attention(projections, gains, experts, upstream, tokens, routes, segments, tables, part):
    rows, width = upstream.shape[1:]
    keys = 4 * rows
    w_width = 2 * projections[0].shape[1] + 2 * HEAD_SIZE + MISC
    ff = 2 * experts[0].shape[2]
    pieces = (8, 3, PAD, ff // 2)
    sds = jax.ShapeDtypeStruct
    return pl.pallas_call(
        functools.partial(attention_kernel, part),
        name="attention",
        out_shape=(
            sds((2, 4, 4, 4 * part, w_width), bf16),
            sds((8, rows, width), bf16),
            sds((8, 1, rows), f32),
            sds((2, 16, 4 * part, ff), bf16),
            sds((3, 4 * part, ff), bf16),
            sds((rows, width), bf16),
            sds((QUERY_HEADS, rows, HEAD_SIZE), bf16),
            sds((4, rows, 4 * HEAD_SIZE), bf16),
            sds((rows, QUERY_HEADS * HEAD_SIZE), bf16),
            sds((QUERY_HEADS, 1, rows), f32),
            sds((rows, width), f32),
            sds((rows, width), bf16),
            sds((8, 1, rows), f32),
        ),
        in_specs=[VMEM] * 14 + [ANY] * 2,
        out_specs=(HBM,) * 4 + (VMEM,) * 9,
        scratch_shapes=[
            pltpu.VMEM((2, 4, 4, 4 * part, w_width), bf16),
            pltpu.VMEM((4, PAD, w_width), bf16),
            pltpu.VMEM(pieces, bf16),
            pltpu.VMEM((4 * part, w_width), bf16),
            pltpu.VMEM((keys, rows), f32),
            pltpu.VMEM((HEAD_SIZE, keys), bf16),
            pltpu.VMEM((PAD, w_width), bf16),
            pltpu.VMEM(pieces, bf16),
            pltpu.VMEM((8, 1, rows), f32),
            pltpu.VMEM((8, rows), f32),
            pltpu.VMEM((rows, HEAD_SIZE), f32),
            pltpu.VMEM((rows, HEAD_SIZE), f32),
        ]
        + lanes_scratch(150)
        + [
            pltpu.SemaphoreType.DMA((4,)),
            pltpu.SemaphoreType.DMA((4,)),
            pltpu.SemaphoreType.DMA((7,)),
        ],
        compiler_params=pltpu.CompilerParams(
            collective_id=2, has_side_effects=True, vmem_limit_bytes=60 * 2**20
        ),
    )(*projections, *gains, *experts, upstream, tokens, routes, segments, *tables)


def attention_back_kernel(
    back_ref,
    gate_back_ref,
    gates_ref,
    b_ref,
    h1_ref,
    tokens_ref,
    rows_ref,
    a_ref,
    o_ref,
    q_ref,
    kv_ref,
    lse_ref,
    cos_table,
    sin_table,
    seg_ref,
    w_ref,
    parts_ref,
    expert_ref,
    grad_in,
    out_sum,
    tokens_out,
    block_out,
    block_half,
    pieces_out,
    w,
    bias,
    key_turned,
    dh1,
    da,
    du,
    do,
    back_rows,
    key_sum,
    value_sum,
    probs,
    probs_back,
    probs_low,
    scores_back,
    kv_send,
    kv_held,
    stage_in,
    misc_held,
    parts,
    near,
    far,
    nearest,
    terms,
    near_p0,
    rest_p0,
    near_q0,
    near_p1,
    rest_p1,
    near_q1,
    out_terms,
    out_near_p0,
    out_rest_p0,
    out_near_q0,
    out_near_p1,
    out_rest_p1,
    out_near_q1,
    x_ref,
    g_ref,
    cos_ref,
    sin_ref,
    s_sem,
    r_sem,
    w_sem,
    own,
):
    c, h, l = place()
    z = h * 2 + l
    rows, width = x_ref.shape
    q_half = o_ref.shape[1] // 2
    misc_at, out_at = q_half + 2 * HEAD_SIZE, q_half + 2 * HEAD_SIZE + MISC

    def load(start, size, to, i):
        return pltpu.make_async_copy(
            w_ref.at[:, :, pl.ds(start, size)], w.at[:, :, pl.ds(to, size)], w_sem.at[i]
        )

    loads = [load(misc_at, MISC, misc_at, 0), load(out_at, q_half, 0, 1), load(0, misc_at, 0, 2)]
    loads[0].start()
    loads[1].start()
    terms_load = pltpu.make_async_copy(expert_ref, terms, own.at[1])
    terms_load.start()
    own_loads = [
        pltpu.make_async_copy(tokens_ref.at[l], x_ref, own.at[4]),
        pltpu.make_async_copy(rows_ref.at[l], g_ref, own.at[5]),
        pltpu.make_async_copy(cos_table.at[pl.ds(z * rows, rows)], cos_ref, own.at[6]),
        pltpu.make_async_copy(sin_table.at[pl.ds(z * rows, rows)], sin_ref, own.at[7]),
    ]
    for copy in own_loads:
        copy.start()
    back_load = pltpu.make_async_copy(back_ref, da, own.at[2])
    back_load.start()
    barrier = pltpu.get_barrier_semaphore()
    pl.semaphore_wait(barrier, greet_column(barrier) + greet_chips(barrier))
    lanes = Lanes(s_sem, r_sem)
    part, ff = terms.shape[2] // 4, terms.shape[3]
    sums = []
    for low, p, q, held in (
        (0, "y", "x", (near_p0, rest_p0, near_q0)),
        (2 * part, "x", "y", (near_p1, rest_p1, near_q1)),
    ):

        def view(index, columns, mine=pl.ds(low, 2 * part)):
            return terms.at[index, :, mine, columns]

        def source(index, mine=pl.ds(low, 2 * part)):
            return expert_ref.at[index, :, mine]

        sums.append(ChipSum(lanes, view, source, ff // 2, ff, p, q, *held))
    out_sums = []
    for low, p, q, held in (
        (0, "y", "x", (out_near_p0, out_rest_p0, out_near_q0)),
        (2 * part, "x", "y", (out_near_p1, out_rest_p1, out_near_q1)),
    ):

        def out_view(index, columns=slice(None), mine=pl.ds(low, 2 * part)):
            return out_terms.at[index, mine, columns]

        out_sums.append(ChipSum(lanes, out_view, out_view, q_half // 2, q_half, p, q, *held))
    places = {
        "own": z,
        "partner": h * 2 + 1 - l,
        "cross": (1 - h) * 2 + 1 - l,
        "far": (1 - h) * 2 + l,
    }
    for each in sums:
        each.far()
    for each in sums:
        each.plain()
    queue = ("far", "cross", "partner", "own")

    def parts_load(i):
        return pltpu.make_async_copy(
            parts_ref.at[c * 4 + places[queue[i]]], parts.at[i % 2], own.at[(0, 3)[i % 2]]
        )

    parts_load(0).start()
    parts_load(1).start()
    near_copies = {
        which: lanes.send(
            parts_ref.at[(1 - c) * 4 + places[which]], near.at[places[which]], other_core()
        )
        for which in ("far", "cross", "partner", "own")
    }
    scale = HEAD_SIZE ** (-0.5)
    fill_bias(bias, seg_ref, z)
    for copy in own_loads:
        copy.wait()

    def add_near(which):
        near_copies[which].wait_recv()
        k, number = places[which], queue.index(which)
        parts_load(number).wait()

        def add(i, carry):
            here = at(i, 64)
            near[k, here] = near[k, here] + parts[number % 2, here]
            return carry

        lax.fori_loop(0, rows // 64, add, 0)
        if number < 2:
            parts_load(number + 2).start()

    half = rows // 2
    first, second = pl.ds(0, half), pl.ds(half, half)

    def part_at(which, some):
        return near.at[places[which], some]

    add_near("far")
    far_partner = lanes.send(part_at("far", first), far.at[0], partner())
    far_cross = lanes.send(part_at("far", second), far.at[1], cross())
    add_near("cross")
    add_near("partner")
    early_cross = lanes.send(part_at("cross", second), nearest.at[1, second], cross())
    early_partner = lanes.send(part_at("partner", first), nearest.at[0, first], partner())
    add_near("own")

    loads[0].wait()
    loads[1].wait()
    misc = w[0, :, misc_at:out_at]
    gains = gain_rows(misc)
    gates = jnp.concatenate([gates_ref[e] for e in range(8)], axis=0)
    gate_back = jnp.concatenate([gate_back_ref[e] for e in range(8)], axis=0)
    mean = jnp.sum(gates * gate_back, axis=0, keepdims=True)
    logit_grad = gates * (gate_back - mean)
    logit_grad = jnp.concatenate(
        [logit_grad, jnp.zeros((MISC - 8, rows), f32)], axis=0
    ).T.astype(bf16)
    chunk = 32

    def norm_back(i, carry):
        mix_sum = carry
        here = at(i, chunk)
        h1 = h1_ref[here, :]
        inverse = lax.rsqrt(jnp.mean(h1 * h1, axis=1, keepdims=True) + EPS)
        db = da[here, :] + dh1[here, :]
        mix_sum = mix_sum + jnp.sum(db * h1 * inverse, axis=0, keepdims=True)
        dz = db * gains[9:10, :]
        mean = jnp.mean(dz * h1, axis=1, keepdims=True)
        value = g_ref[here, :].astype(f32) + inverse * dz - h1 * (inverse * inverse * inverse * mean)
        dh1[here, :] = value
        du[here, :] = value.astype(bf16)
        return mix_sum

    dh1[...] = ref_dot_nt(logit_grad, misc)
    back_load.wait()
    mix_sum = lax.fori_loop(0, rows // chunk, norm_back, jnp.zeros((1, width), f32))
    tail = pl.ds(misc_at, MISC)
    router_grad = ref_dot_tn(b_ref[...], logit_grad).astype(bf16)
    grad_in[:, :, tail] = router_grad.reshape(16, 4 * part, MISC)

    far_partner.wait_recv()
    mine = part_at("cross", first)
    mine[...] = mine[...] + far[0]
    late_cross = lanes.send(mine, nearest.at[1, first], cross())
    far_cross.wait_recv()
    mine = part_at("partner", second)
    mine[...] = mine[...] + far[1]
    late_partner = lanes.send(mine, nearest.at[0, second], partner())

    def add_block():
        for copy in (early_partner, early_cross, late_cross, late_partner):
            copy.wait_recv()

        def add_up(i, carry):
            here = at(i, 64)
            value = near[z, here].astype(f32)
            value = value + nearest[0, here].astype(f32) + nearest[1, here].astype(f32)
            block_out[here, :] = (h1_ref[here, :] + value).astype(bf16)
            return carry

        lax.fori_loop(0, rows // 64, add_up, 0)
        return lanes.send(block_out.at[first], block_half, partner())

    terms_load.wait()
    for each in sums:
        each.joined()

    def project(i, carry):
        columns = at(i, 256)
        for g in range(2):
            do[g, :, columns] = ref_dot(du[...], w[g, :, columns]).astype(bf16)
        return carry

    lax.fori_loop(0, q_half // 256, project, 0)
    loads[2].start()

    size = 4 * 4 * part

    def out_grad(g, i):
        columns = pl.ds(pl.multiple_of(g * q_half, q_half), q_half)
        grad = ref_dot_tn(du[:, i * size : (i + 1) * size], o_ref[:, columns])
        return grad.astype(bf16).reshape(4, 4 * part, q_half)

    out_sends = []
    for i in range(4):
        if i >= 2:
            out_sends[i - 2].wait_send()
        stage = stage_in.at[i % 2, :, :, pl.ds(0, q_half)]
        stage[...] = out_grad(1 - c, i)
        out_sends.append(lanes.send(stage, out_terms.at[pl.ds(4 * i, 4)], other_core()))
    for i in range(4):
        mine = out_grad(c, i)
        out_sends[i].wait_recv()
        out_terms[4 * i : 4 * i + 4] = out_terms[4 * i : 4 * i + 4] + mine
    for each in out_sums:
        each.far()
    for each in out_sums:
        each.plain()

    keys_count = 4 * rows
    kv_sends = []

    def returned(each):
        total = each.total()
        first_block = 2 * sums.index(each)
        for i in range(2):
            for side in range(2):
                to = 2 * (first_block + i) + side
                pieces_out[to, :, :part] = total[
                    :, i * part : (i + 1) * part, side * ff // 2 : (side + 1) * ff // 2
                ].astype(bf16)
                pieces_out[to, :, part:] = jnp.zeros((3, PAD - part, ff // 2), bf16)

    cosine, sine = cos_ref[...], sin_ref[...]
    for g in range(2):
        key_turned[...] = (
            kv_ref[:, :, 2 * g * 128 : (2 * g + 1) * 128].reshape(keys_count, HEAD_SIZE).T
        )
        key_sum[...] = jnp.zeros_like(key_sum)
        value_sum[...] = jnp.zeros_like(value_sum)

        def head_back(j, carry, g=g):
            columns = at(j, HEAD_SIZE)
            query = q_ref[g * GROUP + j]
            out_back = do[g, :, columns]
            shift = lse_ref[g * GROUP + j]
            row_dot = jnp.zeros((8, rows), f32)
            for k in range(keys_count // KEYS):
                here = slice(k * KEYS, (k + 1) * KEYS)
                value = ref_dot_nt(key_block(kv_ref, 2 * g, k), query) * scale + bias[here, :]
                prob = jnp.exp(value - shift)
                prob_back = ref_dot_nt(key_block(kv_ref, 2 * g + 1, k), out_back)
                probs[here, :] = prob
                probs_back[here, :] = prob_back
                probs_low[here, :] = prob.astype(bf16)
                product = (prob * prob_back).reshape(KEYS // 8, 8, rows)
                row_dot = row_dot + jnp.sum(product, axis=0)
            row_dot = jnp.sum(row_dot, axis=0, keepdims=True)
            for k in range(keys_count // KEYS):
                here = slice(k * KEYS, (k + 1) * KEYS)
                value = probs[here, :] * (probs_back[here, :] - row_dot)
                scores_back[here, :] = value.astype(bf16)
            value_sum[...] += ref_dot(probs_low[...], out_back)
            key_sum[...] += ref_dot(scores_back[...], query)
            query_back = (ref_dot(key_turned[...], scores_back[...]) * scale).T
            back_rows[g, :, columns] = turn_back(query_back, cosine, sine).astype(bf16)
            return carry

        lax.fori_loop(0, GROUP // 2, head_back, 0)
        if g == 0:
            for each in sums:
                each.far_q()
            for each in out_sums:
                each.joined()
        else:
            for each in out_sums:
                each.next_q()
            for each in sums:
                returned(each)
        lax.fori_loop(GROUP // 2, GROUP, head_back, 0)
        if g == 0:
            for each in sums:
                each.next_q()
            for each in out_sums:
                each.far_q()
        kv_send[g, :, :, :128] = (key_sum[...] * scale).astype(bf16).reshape(4, rows, 128)
        kv_send[g, :, :, 128:] = value_sum[...].astype(bf16).reshape(4, rows, 128)
        for i, step in enumerate(ALONG_Z):
            to = lax.rem(z + step[1], 4)
            kv_sends.append(lanes.send(kv_send.at[g, to], kv_held.at[g, i], column_peer(*step)))

    block_send = add_block()
    for i in range(2):
        out_sum[2 * part * i : 2 * part * (i + 1)] = out_sums[i].total()
    loads[2].wait()
    every = pl.ds(0, q_half)
    kv = pl.ds(q_half, 2 * HEAD_SIZE)

    def input_back(columns, add):
        def step(i, carry):
            here = at(i, 512)
            value = ref_dot_nt(back_rows[0, :, columns], w[0, here, columns])
            value = value + ref_dot_nt(back_rows[1, :, columns], w[1, here, columns])
            da[:, here] = da[:, here] + value if add else value
            return carry

        lax.fori_loop(0, width // 512, step, 0)

    in_sends = {}

    def in_grad(g, i, columns):
        grad = ref_dot_tn(a_ref[:, i * size : (i + 1) * size], back_rows[g, :, columns])
        return grad.astype(bf16).reshape(4, 4 * part, columns.size)

    def leave(i, columns, before):
        slot = i % 2
        if before is not None:
            in_sends[before].wait_send()
        stage_in[slot, :, :, columns] = in_grad(1 - c, i, columns)
        block = pl.ds(4 * i, 4)
        in_sends[i, columns.start] = lanes.send(
            stage_in.at[slot, :, :, columns], grad_in.at[block, :, columns], other_core()
        )

    input_back(every, False)
    for copy in out_sends[2:]:
        copy.wait_send()
    for i in range(4):
        leave(i, every, (i - 2, every.start) if i >= 2 else None)
    for copy in kv_sends:
        copy.wait_recv()
    for g in range(2):
        own_part = kv_send[g, z].astype(f32)
        for i in range(3):
            own_part = own_part + kv_held[g, i].astype(f32)
        back_rows[g, :, q_half : q_half + 128] = turn_back(
            own_part[:, :128], cosine, sine
        ).astype(bf16)
        back_rows[g, :, q_half + 128 :] = own_part[:, 128:].astype(bf16)
    for i in range(4):
        leave(i, kv, (i - 2, kv.start) if i >= 2 else None)
    input_back(kv, True)
    for i in range(4):
        for columns in (every, kv):
            mine = in_grad(c, i, columns)
            in_sends[i, columns.start].wait_recv()
            block = pl.ds(4 * i, 4)
            grad_in[block, :, columns] = grad_in[block, :, columns] + mine

    def first_back(i, carry):
        here = at(i, chunk)
        x = x_ref[here, :].astype(f32)
        inverse = lax.rsqrt(jnp.mean(x * x, axis=1, keepdims=True) + EPS)
        back = da[here, :]
        carry = carry + jnp.sum(back * x * inverse, axis=0, keepdims=True)
        dz = back * gains[8:9, :]
        mean = jnp.mean(dz * x, axis=1, keepdims=True)
        value = dh1[here, :] + inverse * dz - x * (inverse * inverse * inverse * mean)
        tokens_out[here, :] = value.astype(bf16)
        return carry

    attn_sum = lax.fori_loop(0, rows // chunk, first_back, jnp.zeros((1, width), f32))
    number = lax.broadcasted_iota(jnp.int32, (MISC, width), 0)
    gain_grads = jnp.where(number == 8, attn_sum, jnp.where(number == 9, mix_sum, 0.0))
    gain_grads = gain_grads.T.astype(bf16).reshape(16, 4 * part, MISC)
    grad_in[:, :, tail] = grad_in[:, :, tail] + gain_grads
    crossing = lanes.send(grad_in.at[:, :, tail], misc_held, other_core())
    crossing.wait()
    grad_in[:, :, tail] = grad_in[:, :, tail] + misc_held[...]
    for i in range(2, 4):
        for columns in (every, kv):
            in_sends[i, columns.start].wait_send()
    block_send.wait()
    for each in sums + out_sums:
        each.drain()
    for copy in kv_sends:
        copy.wait_send()
    for copy in near_copies.values():
        copy.wait_send()
    for copy in (early_partner, early_cross, late_cross, late_partner, far_partner, far_cross):
        copy.wait_send()


def attention_back(
    back, gate_back, gates, b, h1, tokens, rows_in, a, o, q, kv, lse, cosine, sine, segments, w_attn, parts, expert_grads
):
    rows, width = h1.shape
    keys = 4 * rows
    q_half = o.shape[1] // 2
    qkv = q_half + 2 * HEAD_SIZE
    sds = jax.ShapeDtypeStruct
    count, block_rows, ff = expert_grads.shape[1:]
    half_block = (count, block_rows // 2, ff)
    ring = [
        pltpu.VMEM((2, 2) + half_block, bf16),
        pltpu.VMEM((2, 4) + half_block, bf16),
        pltpu.VMEM((4,) + half_block, bf16),
    ]
    out_half = (block_rows // 2, q_half)
    out_ring = [
        pltpu.VMEM((2, 2) + out_half, bf16),
        pltpu.VMEM((2, 4) + out_half, bf16),
        pltpu.VMEM((4,) + out_half, bf16),
    ]
    return pl.pallas_call(
        attention_back_kernel,
        name="attention_back",
        out_shape=(
            sds((16, block_rows, qkv + MISC), bf16),
            sds((block_rows, q_half), f32),
            sds((rows, width), bf16),
            sds((rows, width), bf16),
            sds((rows // 2, width), bf16),
            sds((8, count, PAD, ff // 2), bf16),
        ),
        in_specs=[ANY] + [VMEM] * 4 + [ANY] * 2 + [VMEM] * 5 + [ANY] * 2 + [VMEM] + [ANY] * 3,
        out_specs=(VMEM,) * 6,
        scratch_shapes=[
            pltpu.VMEM((2, width, qkv + MISC), bf16),
            pltpu.VMEM((keys, rows), f32),
            pltpu.VMEM((HEAD_SIZE, keys), bf16),
            pltpu.VMEM((rows, width), f32),
            pltpu.VMEM((rows, width), f32),
            pltpu.VMEM((rows, width), bf16),
            pltpu.VMEM((2, rows, q_half), bf16),
            pltpu.VMEM((2, rows, qkv), bf16),
            pltpu.VMEM((keys, HEAD_SIZE), f32),
            pltpu.VMEM((keys, HEAD_SIZE), f32),
            pltpu.VMEM((keys, rows), f32),
            pltpu.VMEM((keys, rows), f32),
            pltpu.VMEM((keys, rows), bf16),
            pltpu.VMEM((keys, rows), bf16),
            pltpu.VMEM((2, 4, rows, 2 * HEAD_SIZE), bf16),
            pltpu.VMEM((2, 3, rows, 2 * HEAD_SIZE), bf16),
            pltpu.VMEM((2, 4, block_rows, qkv), bf16),
            pltpu.VMEM((16, block_rows, MISC), bf16),
            pltpu.VMEM((2, rows, width), bf16),
            pltpu.VMEM((4, rows, width), bf16),
            pltpu.VMEM((2, rows // 2, width), bf16),
            pltpu.VMEM((2, rows, width), bf16),
            pltpu.VMEM(expert_grads.shape, bf16),
        ]
        + ring
        + ring
        + [pltpu.VMEM((16, block_rows, q_half), bf16)]
        + out_ring
        + out_ring
        + [
            pltpu.VMEM((rows, width), bf16),
            pltpu.VMEM((rows, width), bf16),
            pltpu.VMEM((rows, HEAD_SIZE), f32),
            pltpu.VMEM((rows, HEAD_SIZE), f32),
        ]
        + lanes_scratch(100)
        + [
            pltpu.SemaphoreType.DMA((3,)),
            pltpu.SemaphoreType.DMA((8,)),
        ],
        compiler_params=pltpu.CompilerParams(
            collective_id=3, has_side_effects=True, vmem_limit_bytes=62 * 2**20
        ),
    )(
        back, gate_back, gates, b, h1, tokens, rows_in, a, o, q, kv, lse, cosine, sine, segments, w_attn, parts, expert_grads
    )


def experts_kernel(
    rows_ref,
    gate_ref,
    grads_ref,
    slot_rows,
    others_ref,
    block_ref,
    mix_out,
    weight_grads,
    back_out,
    gate_back_out,
    rows_all,
    held,
    w_gate,
    w_up,
    w_down,
    picked,
    picked_grads,
    hidden_back,
    hidden_gated,
    gate_low,
    up_low,
    mix_stage,
    near,
    far,
    nearest,
    gates_in,
    gate_back,
    s_sem,
    r_sem,
    own,
    stage_sem,
    near_send,
    near_recv,
):
    c, h, l = place()
    me = (c * 2 + h) * 2 + l
    barrier = pltpu.get_barrier_semaphore()
    pl.semaphore_wait(barrier, greet_column(barrier) + greet_chips(barrier))
    lanes = Lanes(s_sem, r_sem)
    rows, width = rows_ref.shape
    slots = picked.shape[1]
    ff = w_gate.shape[2]
    block = 2 * rows

    ring = ColumnRing(lanes, rows_ref, rows_all)
    ring.start()
    index = chip_index({"x": 0, "y": 0})
    half = block_ref.shape[1] // 2
    weight_rings = []
    for weight, target in ((0, w_gate),):
        for low, a, b in ((0, "x", "y"), (half, "y", "x")):
            mine = pl.ds(low, half)

            def view(index, columns, mine=mine, target=target):
                return target.at[index, mine, columns]

            own_part = block_ref.at[weight, mine]
            weight_rings.append(ChipRing(lanes, own_part, view, ff // 2, ff, a, b))

    def go(step, *args):
        for each in weight_rings:
            getattr(each, step)(*args)

    go("start")
    local = [
        pltpu.make_async_copy(grads_ref, held, own.at[0]),
        pltpu.make_async_copy(others_ref.at[1], w_down, own.at[1]),
        pltpu.make_async_copy(block_ref.at[0], w_gate.at[index], own.at[2]),
        pltpu.make_async_copy(others_ref.at[0], w_up, own.at[3]),
        pltpu.make_async_copy(rows_ref, rows_all.at[me], own.at[4]),
        pltpu.make_async_copy(gate_ref.at[me], gates_in.at[me], own.at[5]),
    ]
    for copy in local:
        copy.start()
    gate_copies = []
    for step in COLUMN:
        peer = column_peer(*step)
        to = (peer["c"] * 2 + peer["h"]) * 2 + peer["l"]
        gate_copies.append(lanes.send(gate_ref.at[to], gates_in.at[me], peer))

    def pick_of(k):
        number = lax.broadcasted_iota(jnp.int32, (slots, block), 0).astype(f32)
        return slot_rows[k] == number

    def low(mask):
        return mask.astype(f32).astype(bf16)

    def columns_of(weight, columns):
        return weight[:, :, columns].reshape(width, narrow)

    def rows_of(weight, i):
        return weight[pl.ds(8 * i, 8)].reshape(ff, ff)

    wide = 512
    narrow = 256

    local[0].wait()
    local[1].wait()

    def prepare(k, carry):
        pick = low(pick_of(k))

        def gather(i, carry):
            columns = at(i, wide)
            values = ref_dot(pick, held[pl.ds(2 * k, 2), :, columns].reshape(block, wide))
            picked_grads[k, :, columns] = values.astype(bf16)
            return carry

        lax.fori_loop(0, width // wide, gather, 0)

        def down(i, carry):
            columns = at(i, narrow)
            hidden_back[k, :, columns] = ref_dot(picked_grads[k], columns_of(w_down, columns))
            return carry

        lax.fori_loop(0, ff // narrow, down, 0)
        return carry

    lax.fori_loop(0, 2, prepare, 0)
    go("relay_first")
    go("relay_turn", 0)
    ring.relay()
    go("relay_second")
    lax.fori_loop(2, 4, prepare, 0)
    go("relay_turn", -1)
    go("relay_turn", 1)
    ring.nearest()
    go("relay_turn", 2)
    go("finish")
    for copy in local[2:]:
        copy.wait()
    for copy in gate_copies:
        copy.wait()
    ring.shared["own"].wait_recv()
    ring.shared["partner"].wait_recv()

    def expert(k, stage):
        pick = pick_of(k)
        pick_low = low(pick)
        spread = pick.astype(f32).T.astype(bf16)
        gates = gates_in[pl.ds(2 * k, 2)]
        gate_row = jnp.concatenate([gates[0], gates[1]], axis=1)
        gate = jnp.sum(jnp.where(pick, gate_row, 0.0), axis=1, keepdims=True)

        def gather(i, carry):
            columns = at(i, wide)
            values = ref_dot(pick_low, rows_all[pl.ds(2 * k, 2), :, columns].reshape(block, wide))
            picked[k, :, columns] = values.astype(bf16)
            return carry

        lax.fori_loop(0, width // wide, gather, 0)

        def hide(i, total):
            columns = at(i, narrow)
            gate_act = ref_dot(picked[k], columns_of(w_gate, columns))
            up_act = ref_dot(picked[k], columns_of(w_up, columns))
            back = hidden_back[k, :, columns]
            sigmoid_act = 0.5 + 0.5 * jnp.tanh(0.5 * gate_act)
            silu_act = gate_act * sigmoid_act
            hidden = silu_act * up_act
            hidden_gated[k, :, columns] = (hidden * gate).astype(bf16)
            total = total + jnp.sum(hidden * back, axis=1, keepdims=True)
            back = back * gate
            slope = sigmoid_act * (1.0 + gate_act * (1.0 - sigmoid_act))
            gate_low[k, :, columns] = (back * up_act * slope).astype(bf16)
            up_low[k, :, columns] = (back * silu_act).astype(bf16)
            return total

        gate_slots = lax.fori_loop(0, ff // narrow, hide, jnp.zeros((slots, 1), f32))
        back_row = jnp.sum(jnp.where(pick, gate_slots, 0.0), axis=0, keepdims=True)
        gate_back[2 * k] = back_row[:, :rows]
        gate_back[2 * k + 1] = back_row[:, rows:]

        def leave(i, carry):
            columns = at(i, ff)
            out = ref_dot_nt(hidden_gated[k], rows_of(w_down, i)).astype(bf16)
            mix_stage[stage, :, :, columns] = (
                ref_dot(spread, out).astype(bf16).reshape(2, rows, ff)
            )
            back = ref_dot_nt(gate_low[k], rows_of(w_gate, i))
            back = (back + ref_dot_nt(up_low[k], rows_of(w_up, i))).astype(bf16)
            held[pl.ds(2 * k, 2), :, columns] = (
                ref_dot(spread, back).astype(bf16).reshape(2, rows, ff)
            )
            return carry

        lax.fori_loop(0, width // ff, leave, 0)

    def stage_copy(k, stage):
        return pltpu.make_async_copy(
            mix_stage.at[stage], mix_out.at[pl.ds(2 * k, 2)], stage_sem.at[stage]
        )

    def near_copy(side, i):
        return pltpu.make_async_remote_copy(
            src_ref=held.at[pl.ds(((1 - c) * 2 + side) * 2, 2)],
            dst_ref=near.at[pl.ds(side * 2, 2)],
            send_sem=near_send.at[i],
            recv_sem=near_recv.at[i],
            device_id=other_core(),
            device_id_type=MESH,
        )

    def add_near(z):
        mine = held.at[c * 4 + z]

        def add(i, carry):
            here = at(i, 64)
            mine[here] = mine[here] + near[z, here]
            return carry

        lax.fori_loop(0, rows // 64, add, 0)

    half = rows // 2
    first, second = pl.ds(0, half), pl.ds(half, half)
    z = {
        "own": h * 2 + l,
        "partner": h * 2 + 1 - l,
        "cross": (1 - h) * 2 + 1 - l,
        "far": (1 - h) * 2 + l,
    }

    def block_at(which, part):
        return held.at[c * 4 + z[which], part]

    order = [(1 - c) * 2 + h, (1 - c) * 2 + 1 - h, c * 2 + 1 - h, c * 2 + h]
    expert(order[0], 0)
    near_copy(h, 0).start()
    stage_copy(order[0], 0).start()
    ring.far()
    ring.shared["cross"].wait_recv()
    ring.shared["far"].wait_recv()
    expert(order[1], 1)
    near_copy(1 - h, 1).start()
    stage_copy(order[1], 1).start()
    stage_copy(order[0], 0).wait()
    expert(order[2], 0)
    stage_copy(order[2], 0).start()
    near_copy(1 - h, 1).wait_recv()
    add_near(z["far"])
    far_partner = lanes.send(block_at("far", first), far.at[0], partner())
    far_cross = lanes.send(block_at("far", second), far.at[1], cross())
    add_near(z["cross"])
    early_cross = lanes.send(block_at("cross", second), nearest.at[1, second], cross())
    stage_copy(order[1], 1).wait()
    expert(order[3], 1)
    stage_copy(order[3], 1).start()
    near_copy(h, 0).wait_recv()
    add_near(z["partner"])
    early_partner = lanes.send(block_at("partner", first), nearest.at[0, first], partner())
    add_near(z["own"])
    sends = []
    gate_own = pltpu.make_async_copy(gate_back.at[me], gate_back_out.at[me], own.at[6])
    gate_own.start()
    for step in COLUMN:
        peer = column_peer(*step)
        to = (peer["c"] * 2 + peer["h"]) * 2 + peer["l"]
        sends.append(lanes.send(gate_back.at[to], gate_back_out.at[me], peer))

    def weight_grad(values, others, target, number):
        part = 384

        def make(i, carry):
            left = values[:, :, at(i, part)].reshape(4 * slots, part)
            grad = ref_dot_tn(left, others[...].reshape(4 * slots, ff)).astype(bf16)
            target[pl.ds(4 * i, 4)] = grad.reshape(4, part // 4, ff)
            return carry

        lax.fori_loop(0, width // part, make, 0)
        copy = pltpu.make_async_copy(target, weight_grads.at[:, number], own.at[1 + number])
        copy.start()
        return copy

    far_partner.wait_recv()
    mine = block_at("cross", first)
    mine[...] = mine[...] + far[0]
    late_cross = lanes.send(mine, nearest.at[1, first], cross())
    far_cross.wait_recv()
    mine = block_at("partner", second)
    mine[...] = mine[...] + far[1]
    late_partner = lanes.send(mine, nearest.at[0, second], partner())
    go("drain")
    grad_copies = [
        weight_grad(picked_grads, hidden_gated, w_down, 2),
        weight_grad(picked, gate_low, w_gate, 0),
        weight_grad(picked, up_low, w_up, 1),
    ]
    for copy in (early_partner, early_cross, late_cross, late_partner):
        copy.wait_recv()

    def finish(i, carry):
        here = at(i, 64)
        total = held[c * 4 + z["own"], here].astype(f32)
        back_out[here, :] = (
            total + nearest[0, here].astype(f32) + nearest[1, here].astype(f32)
        )
        return carry

    lax.fori_loop(0, rows // 64, finish, 0)
    for copy in (early_partner, early_cross, late_cross, late_partner, far_partner, far_cross):
        copy.wait_send()
    for i, side in ((0, h), (1, 1 - h)):
        near_copy(side, i).wait_send()
    for copy in sends + grad_copies + [gate_own]:
        copy.wait()
    stage_copy(order[2], 0).wait()
    stage_copy(order[3], 1).wait()
    ring.drain()


def experts_of_column(rows, gates, grads_all, slots, others, block):
    count, width = rows.shape
    ff = others.shape[3]
    return pl.pallas_call(
        experts_kernel,
        name="experts",
        out_shape=(
            jax.ShapeDtypeStruct((8, count, width), bf16),
            jax.ShapeDtypeStruct((16, 3) + others.shape[2:], bf16),
            jax.ShapeDtypeStruct((count, width), f32),
            jax.ShapeDtypeStruct(gates.shape, f32),
        ),
        in_specs=[VMEM, VMEM, ANY, VMEM, ANY, VMEM],
        out_specs=(HBM, HBM, VMEM, VMEM),
        scratch_shapes=[
            pltpu.VMEM((8, count, width), bf16),
            pltpu.VMEM((8, count, width), bf16),
            pltpu.VMEM((16, width // 16, ff), bf16),
            pltpu.VMEM((16, width // 16, ff), bf16),
            pltpu.VMEM((16, width // 16, ff), bf16),
            pltpu.VMEM((4, SLOTS, width), bf16),
            pltpu.VMEM((4, SLOTS, width), bf16),
            pltpu.VMEM((4, SLOTS, ff), f32),
            pltpu.VMEM((4, SLOTS, ff), bf16),
            pltpu.VMEM((4, SLOTS, ff), bf16),
            pltpu.VMEM((4, SLOTS, ff), bf16),
            pltpu.VMEM((2, 2, count, width), bf16),
            pltpu.VMEM((4, count, width), bf16),
            pltpu.VMEM((2, count // 2, width), bf16),
            pltpu.VMEM((2, count, width), bf16),
            pltpu.VMEM(gates.shape, f32),
            pltpu.VMEM(gates.shape, f32),
        ]
        + lanes_scratch(64)
        + [
            pltpu.SemaphoreType.DMA((7,)),
            pltpu.SemaphoreType.DMA((2,)),
            pltpu.SemaphoreType.DMA((2,)),
            pltpu.SemaphoreType.DMA((2,)),
        ],
        compiler_params=pltpu.CompilerParams(
            collective_id=4, has_side_effects=True, vmem_limit_bytes=60 * 2**20
        ),
    )(rows, gates, grads_all, slots[:, None, :], others, block)


def return_kernel(
    part,
    misc_at,
    in_ref,
    out_ref,
    expert_ref,
    tokens_ref,
    block_ref,
    block_half,
    grads_out,
    misc_out,
    expert_out,
    tokens_out,
    block_out,
    near,
    near_p0,
    rest_p0,
    near_q0,
    near_p1,
    rest_p1,
    near_q1,
    pieces,
    landed,
    misc_landed,
    s_sem,
    r_sem,
    ps,
    pr,
    ms,
    mr,
    own,
):
    c, h, l = place()
    z = h * 2 + l
    me = c * 4 + z
    barrier = pltpu.get_barrier_semaphore()
    pl.semaphore_wait(barrier, greet_column(barrier) + greet_chips(barrier))
    lanes = Lanes(s_sem, r_sem)
    width = near.shape[2]
    half = near.shape[1] // 2
    load = pltpu.make_async_copy(in_ref, near, own.at[4])
    load.start()
    sums = []
    for low, p, q, held in (
        (0, "y", "x", (near_p0, rest_p0, near_q0)),
        (half, "x", "y", (near_p1, rest_p1, near_q1)),
    ):

        def view(index, columns, mine=pl.ds(low, half)):
            return near.at[index, mine, columns]

        def source(index, mine=pl.ds(low, half)):
            return in_ref.at[index, mine]

        sums.append(ChipSum(lanes, view, source, 640, width, p, q, *held))
    for each in sums:
        each.far()
    own_copy = pltpu.make_async_copy(expert_ref.at[me], expert_out.at[me], own.at[0])
    own_copy.start()
    own_tokens = pltpu.make_async_copy(tokens_ref, tokens_out.at[l], own.at[1])
    own_tokens.start()
    own_block = pltpu.make_async_copy(block_ref, block_out.at[l], own.at[2])
    own_block.start()
    count = block_half.shape[0]
    rest = pl.ds(count, count)
    had = pltpu.make_async_copy(block_half, block_out.at[1 - l, pl.ds(0, count)], own.at[3])
    had.start()
    expert_copies = [
        lanes.send(tokens_ref, tokens_out.at[l], partner()),
        lanes.send(block_ref.at[rest], block_out.at[l, rest], partner()),
    ]
    for step in COLUMN:
        peer = column_peer(*step)
        to = (peer["c"] * 2 + peer["h"]) * 2 + peer["l"]
        expert_copies.append(lanes.send(expert_ref.at[to], expert_out.at[me], peer))

    load.wait()
    for each in sums:
        each.joined()
    for each in sums:
        each.plain()
    for each in sums:
        each.far_q()
    for each in sums:
        each.next_q()
    for number, each in enumerate(sums):
        total = each.total()
        for i in range(2):
            pieces[2 * number + i, :part, :width] = total[i * part : (i + 1) * part].astype(bf16)
    for k in range(4):
        pieces[k, :part, width:] = out_ref[k * part : (k + 1) * part, :].astype(bf16)
        pieces[k, part:, :] = jnp.zeros((PAD - part, pieces.shape[2]), bf16)

    def to_owner(target, owner, src, dst, send_sem, recv_sem, asked):
        is_me = (owner["c"] == c) & (owner["h"] == h) & (owner["l"] == l)
        there = pltpu.make_async_remote_copy(
            src_ref=src,
            dst_ref=dst,
            send_sem=send_sem,
            recv_sem=recv_sem,
            device_id=owner,
            device_id_type=MESH,
        )
        here = pltpu.make_async_copy(src, dst, recv_sem)
        pl.when(asked & jnp.logical_not(is_me))(there.start)
        pl.when(asked & is_me)(here.start)
        return asked & jnp.logical_not(is_me), there

    sent = []
    everyone = c < 2
    for target in range(4):
        owner = {"c": target // 2, "h": target % 2, "l": c}
        sent.append(
            to_owner(
                target, owner, pieces.at[target], landed.at[z], ps.at[target], pr.at[z], everyone
            )
        )
    misc = pl.ds(misc_at, MISC)
    for target in range(4):
        owner = {"c": target // 2, "h": target % 2, "l": 1}
        sent.append(
            to_owner(
                target,
                owner,
                pieces.at[target, :, misc],
                misc_landed.at[z],
                ms.at[target],
                mr.at[z],
                c == 0,
            )
        )
    for source in range(4):
        pltpu.make_async_copy(pieces.at[0], landed.at[source], pr.at[source]).wait()

    def summed(ref, columns=slice(None)):
        parts = [ref[i, :, columns].astype(f32)[:part] for i in range(4)]
        return (parts[0] + parts[1]) + (parts[2] + parts[3])

    grads_out[...] = summed(landed)

    def from_core():
        for source in range(4):
            pltpu.make_async_copy(
                pieces.at[0, :, misc], misc_landed.at[source], mr.at[source]
            ).wait()
        misc_out[...] = summed(misc_landed)

    def from_piece():
        misc_out[...] = summed(landed, misc)

    pl.when(l == 1)(from_core)
    pl.when(l == 0)(from_piece)
    for asked, there in sent:
        pl.when(asked)(there.wait_send)
    for each in sums:
        each.drain()
    own_copy.wait()
    own_tokens.wait()
    own_block.wait()
    had.wait()
    for copy in expert_copies:
        copy.wait()


def return_gradients(grad_in, out_sum, expert_pieces, tokens, block, block_half, part, misc_at):
    width, rows = grad_in.shape[2], grad_in.shape[1]
    full = width + out_sum.shape[1]
    half = rows // 2
    ring = [
        pltpu.VMEM((2, 2, half, width), bf16),
        pltpu.VMEM((2, 4, half, width), bf16),
        pltpu.VMEM((4, half, width), bf16),
    ]
    return pl.pallas_call(
        functools.partial(return_kernel, part, misc_at),
        name="return_gradients",
        out_shape=(
            jax.ShapeDtypeStruct((part, full), f32),
            jax.ShapeDtypeStruct((part, MISC), f32),
            jax.ShapeDtypeStruct(expert_pieces.shape, expert_pieces.dtype),
            jax.ShapeDtypeStruct((2,) + tokens.shape, tokens.dtype),
            jax.ShapeDtypeStruct((2,) + block.shape, block.dtype),
        ),
        in_specs=[ANY] + [VMEM] * 5,
        out_specs=(VMEM, VMEM, HBM, HBM, HBM),
        scratch_shapes=[pltpu.VMEM((16, rows, width), bf16)]
        + ring
        + ring
        + [
            pltpu.VMEM((4, PAD, full), bf16),
            pltpu.VMEM((4, PAD, full), bf16),
            pltpu.VMEM((4, PAD, MISC), bf16),
        ]
        + lanes_scratch(50)
        + [
            pltpu.SemaphoreType.DMA((4,)),
            pltpu.SemaphoreType.DMA((4,)),
            pltpu.SemaphoreType.DMA((4,)),
            pltpu.SemaphoreType.DMA((4,)),
            pltpu.SemaphoreType.DMA((5,)),
        ],
        compiler_params=pltpu.CompilerParams(
            collective_id=7, has_side_effects=True, vmem_limit_bytes=62 * 2**20
        ),
    )(grad_in, out_sum, expert_pieces, tokens, block, block_half)


def body(
    tokens,
    segments,
    routes,
    attn_gain,
    w_query,
    key_matrix,
    value_matrix,
    w_output,
    mix_gain,
    w_router,
    w_gate,
    w_up,
    w_down,
    block_cotangent,
):
    c, h, l = place()
    model_width = tokens.shape[2]
    rows = tokens.shape[1] // 2
    experts, part, ff_half = w_gate.shape
    q_half = w_query.shape[1]

    kv_width = key_matrix.shape[1]
    in_width = q_half + 2 * kv_width + MISC
    halves = (2, rows, model_width)
    tables = [jnp.asarray(table) for table in rope_tables(segments.shape[1])]
    (
        w_attn,
        grads_all,
        slots,
        others_full,
        expert_block,
        normed_in,
        q,
        kv,
        attended,
        lse,
        residual,
        normed_mix,
        gates,
    ) = attention(
        (w_query, key_matrix, value_matrix, w_output.T, w_router),
        (attn_gain[None], mix_gain[None]),
        (w_gate, w_up, w_down),
        block_cotangent.reshape(halves),
        tokens.reshape(halves),
        routes[0].T,
        segments,
        tables,
        part,
    )
    w_attn = w_attn.reshape(2, model_width, in_width + q_half)
    mix_parts, expert_grads, mix_back, gate_back = experts_of_column(
        normed_mix, gates, grads_all, slots.reshape(4, 2 * rows), others_full, expert_block
    )
    grad_in, out_sum, tokens_back, block_out, block_half, pieces = attention_back(
        mix_back,
        gate_back,
        gates,
        normed_mix,
        residual,
        tokens.reshape(halves),
        block_cotangent.reshape(halves),
        normed_in,
        attended,
        q,
        kv,
        lse,
        *tables,
        segments,
        w_attn,
        mix_parts,
        expert_grads,
    )

    returned, misc_back, expert_back, tokens_back, block_out = return_gradients(
        grad_in,
        out_sum,
        pieces,
        tokens_back,
        block_out,
        block_half,
        part,
        in_width - MISC,
    )
    expert_back = expert_back[:, :, :part].astype(f32)
    return (
        block_out.reshape(1, 2 * rows, model_width),
        tokens_back.reshape(1, 2 * rows, model_width).astype(f32),
        misc_back[:, experts],
        returned[:, :q_half],
        returned[:, q_half : q_half + kv_width],
        returned[:, q_half + kv_width : q_half + 2 * kv_width],
        returned[:, in_width:].T,
        misc_back[:, experts + 1],
        misc_back[:, :experts],
        expert_back[:, 0],
        expert_back[:, 1],
        expert_back[:, 2],
    )


def solution(mesh):
    split = Mesh(mesh.devices.reshape(4, 4, 2, 2, 2), ("x", "y", "c", "h", "l"))
    fsdp = ("x", "y", "c")
    owner = ("x", "y", "c", "h")
    return jax.shard_map(
        body,
        mesh=split,
        in_specs=(
            P(fsdp, "h", None),
            P(fsdp, None),
            P(fsdp, "h", None),
            P(owner),
            P(owner, "l"),
            P(owner, "l"),
            P(owner, "l"),
            P("l", owner),
            P(owner),
            P(owner, None),
            P(None, owner, "l"),
            P(None, owner, "l"),
            P(None, owner, "l"),
            P(fsdp, "h", None),
        ),
        out_specs=(
            P(fsdp, "h", None),
            P(fsdp, "h", None),
            P(owner),
            P(owner, "l"),
            P(owner, "l"),
            P(owner, "l"),
            P("l", owner),
            P(owner),
            P(owner, None),
            P(None, owner, "l"),
            P(None, owner, "l"),
            P(None, owner, "l"),
        ),
        check_vma=False,
    )
```
